32 devices in a mesh: prow: 4 (over x, core), pcol: 8 (over z, y).
Axes of the slice: x: 2, y: 2, z: 4, core: 2. Of those that a mesh axis runs over, the one named last changes fastest.
Arguments:
- matrix: bfloat16 [5, 2048, 2, 4096], P(None, 'prow', None, 'pcol'), may hold values from -6 to 6
- pivots: int32 [2, 512], replicated, may hold values from 0 to 10239, as said below
- lower_inverse: bfloat16 [2, 512, 512], replicated, as said below
- upper_inverse: bfloat16 [2, 512, 512], replicated, as said below
Outputs:
- factored: bfloat16 [5, 2048, 2, 4096], P(None, 'prow', None, 'pcol')
The draws below stay inside these ranges and needn't reach their ends.
Inputs may be any that keep to these rules, and one draw needn't show every extreme that they name: `pivots`: for panel k, entry i is either k * 512 + i (the row stays) or a row from (k + 1) * 512 on; the entries of one panel are distinct; entry 511 of each panel is 10239, and entry 0 of panel 0 is 0. Each lower_inverse[k] is unit lower triangular. Each upper_inverse[k] is upper triangular with a positive diagonal.
All inputs are finite; a program needn't handle non-finite values.
Results may differ from the reference program's by a relative error of at most 0.0084.
Values may be sent and summed in bfloat16 or wider, within the bound.
No kernel may reach another device: no remote copies, remote signals or barrier semaphores. Data moves between devices by JAX's collectives and lax.ppermute only.
A program may use at most 128 MiB of HBM per device.

```python
import math
import jax
import jax.numpy as jnp
from jax import lax

NB = 512
CB_DEV = 2
RB_DEV = 5
STEPS = 2
RSPAN = 2048
CSPAN = 4096
ROWS = 10240
ORDER = 8192


def draw_pivots(key, part):
    picked_rows = []
    for panel_step in range(STEPS):
        panel_key = jax.random.fold_in(key, panel_step)
        begin_row = (panel_step + 1) * NB
        shuffled = jax.random.permutation(jax.random.fold_in(panel_key, 1), ROWS - begin_row)[:NB] + begin_row
        last_place = jnp.argmax(shuffled == ROWS - 1)
        shuffled = shuffled.at[last_place].set(shuffled[NB - 1]).at[NB - 1].set(ROWS - 1)
        staying = jax.random.randint(jax.random.fold_in(panel_key, 2), (NB,), 0, 4) == 0
        if panel_step == 0:
            staying = staying.at[0].set(True)
        staying = staying.at[NB - 1].set(False)
        own_rows = panel_step * NB + jnp.arange(NB)
        picked_rows.append(jnp.where(staying, own_rows, shuffled))
    return jnp.stack(picked_rows).astype(jnp.int32)


def draw_lower_inverse(key, part):
    noise = jax.random.normal(key, (STEPS, NB, NB), jnp.float32)
    strict = jnp.tril(noise * (0.5 / math.sqrt(NB)), -1)
    return (strict + jnp.eye(NB, dtype=jnp.float32)).astype(jnp.bfloat16)


def draw_upper_inverse(key, part):
    noise_key = jax.random.fold_in(key, 11)
    scale_key = jax.random.fold_in(key, 12)
    noise = jax.random.normal(noise_key, (STEPS, NB, NB), jnp.float32)
    diagonal = jnp.exp(jax.random.uniform(scale_key, (STEPS, NB), jnp.float32, math.log(0.5), math.log(2.0)))
    strict = jnp.triu(noise * (0.5 / NB), 1)
    full = strict + (diagonal / math.sqrt(NB))[:, :, None] * jnp.eye(NB, dtype=jnp.float32)
    return full.astype(jnp.bfloat16)


def shard_levels(rng, shape, split, low, top_value):
    def one(dim, blocks):
        draws = jax.random.uniform(jax.random.fold_in(jax.random.fold_in(rng, 6), dim), (blocks,), jnp.float32, low / len(split), top_value / len(split))
        return jnp.repeat(jnp.exp(draws), shape[dim] // blocks).reshape((-1,) + (1,) * (len(shape) - dim - 1))

    factor_of = one(*split[0])
    for cut in split[1:]:
        factor_of = factor_of * one(*cut)
    return factor_of


def gaussian(stream_key, extent, scale, bound, shards=(), held_as=jnp.bfloat16):
    level = shard_levels(stream_key, extent, shards, -0.22, 0.18) if shards else 1.0
    entries = jax.random.normal(stream_key, extent, jnp.float32) * scale * level
    return jnp.minimum(jnp.maximum(entries, -bound), bound).astype(held_as)


def setup_inputs(seed: int = 0) -> dict:
    streams_of = jax.random.split(jax.random.key(seed), 5)
    return {
        "matrix": gaussian(streams_of[0], (RB_DEV, RSPAN, CB_DEV, CSPAN), 1.0, 6.0, ((1, 4), (3, 8))),
        "pivots": draw_pivots(jax.random.fold_in(streams_of[4], 71), 0),
        "lower_inverse": draw_lower_inverse(jax.random.fold_in(streams_of[4], 71), 0),
        "upper_inverse": draw_upper_inverse(jax.random.fold_in(streams_of[4], 71), 0),
    }


def reference(matrix, pivots, lower_inverse, upper_inverse):
    dense = matrix.reshape(ROWS, ORDER)
    for panel_step in range(STEPS):
        top_start = panel_step * NB
        next_start = top_start + NB
        top_index = top_start + jnp.arange(NB, dtype=jnp.int32)
        pivot_index = pivots[panel_step]
        top_values = dense[top_index]
        pivot_values = dense[pivot_index]
        dense = dense.at[pivot_index].set(top_values).at[top_index].set(pivot_values)
        factor = jnp.dot(dense[next_start:, top_start:next_start], upper_inverse[panel_step],
                         preferred_element_type=jnp.float32).astype(jnp.bfloat16)
        top_product = jnp.dot(lower_inverse[panel_step], dense[top_start:next_start, next_start:],
                              preferred_element_type=jnp.float32).astype(jnp.bfloat16)
        dense = dense.at[next_start:, top_start:next_start].set(factor)
        dense = dense.at[top_start:next_start, next_start:].set(top_product)
        upper_wide = top_product.astype(jnp.float32)

        def update_block(block_index, current):
            row_begin = (block_index * NB).astype(jnp.int32)
            row_slab = lax.dynamic_slice_in_dim(current, row_begin, NB, 0)
            factor_rows = lax.dynamic_slice_in_dim(factor, (row_begin - next_start).astype(jnp.int32), NB, 0)
            change = jnp.dot(factor_rows.astype(jnp.float32), upper_wide, preferred_element_type=jnp.float32)
            refreshed = (row_slab[:, next_start:].astype(jnp.float32) - change).astype(jnp.bfloat16)
            return lax.dynamic_update_slice_in_dim(current, row_slab.at[:, next_start:].set(refreshed), row_begin, 0)

        dense = lax.fori_loop(panel_step + 1, ROWS // NB, update_block, dense)
    return dense.reshape(matrix.shape)
```

```python
import functools

import jax
import jax.numpy as jnp
from jax import lax
from jax.experimental import pallas as pl
from jax.experimental.pallas import tpu as pltpu
from jax.sharding import PartitionSpec as P

BF16 = jnp.bfloat16
F32 = jnp.float32
VMEM_LIMIT = 48 * 1024 * 1024


def swapped(pivot_list, top_start, rows):
    tops = top_start + jnp.arange(pivot_list.shape[0], dtype=jnp.int32)
    at_top = (rows[:, None] == tops[None, :]).astype(jnp.int32)
    at_pivot = (rows[:, None] == pivot_list[None, :]).astype(jnp.int32)
    return rows + jnp.sum((at_top - at_pivot) * (pivot_list - tops)[None, :], axis=1)


def dot(a, b):
    return jnp.dot(a, b, preferred_element_type=F32)


def gather_kernel(keep_index, send_index, tiles, keep, send):
    def copy(i, carry):
        keep[i] = tiles[keep_index[i]]
        send[i] = tiles[send_index[i]]
        return carry

    lax.fori_loop(0, keep.shape[0], copy, 0, unroll=8)


def gather_rows(keep_index, send_index, tiles):
    count = keep_index.shape[0]
    shape = jax.ShapeDtypeStruct((count,) + tiles.shape[1:], tiles.dtype)
    smem = pl.BlockSpec(memory_space=pltpu.SMEM)
    vmem = pl.BlockSpec(memory_space=pltpu.VMEM)
    return pl.pallas_call(
        gather_kernel,
        out_shape=(shape, shape),
        in_specs=[smem, smem, vmem],
        out_specs=(vmem, vmem),
        compiler_params=pltpu.CompilerParams(vmem_limit_bytes=VMEM_LIMIT),
    )(keep_index, send_index, tiles)


def scatter_kernel(*refs):
    sources = (len(refs) - 2) // 2
    indices, values = refs[:sources], refs[sources : 2 * sources]
    tiles, out = refs[2 * sources], refs[2 * sources + 1]
    out[0 : tiles.shape[0]] = tiles[...]
    for index, value in zip(indices, values):

        def copy(i, carry, index=index, value=value):
            out[index[i]] = value[i]
            return carry

        lax.fori_loop(0, value.shape[0], copy, 0, unroll=8)


def scatter_rows(indices, values, tiles):
    smem = pl.BlockSpec(memory_space=pltpu.SMEM)
    vmem = pl.BlockSpec(memory_space=pltpu.VMEM)
    rows = tiles.shape[0] + 8
    return pl.pallas_call(
        scatter_kernel,
        out_shape=jax.ShapeDtypeStruct((rows,) + tiles.shape[1:], tiles.dtype),
        in_specs=[smem] * len(indices) + [vmem] * (len(values) + 1),
        out_specs=vmem,
        compiler_params=pltpu.CompilerParams(vmem_limit_bytes=VMEM_LIMIT),
    )(*indices, *values, tiles)


def prep_kernel(meta, first, second, head0, head1, lower, upper, up0, up1, up0_panel, top):
    half = first.shape[1]
    core, column = meta[1], meta[2]
    odd = lax.rem(column, 2) == 1

    def rows_of(block, j):
        wanted_first = odd if block == 0 else jnp.logical_not(odd)
        low_a, high_a = first[core, :, j, :], first[1 - core, :, j, :]
        low_b, high_b = second[core, :, j, :], second[1 - core, :, j, :]
        low = jnp.where(wanted_first, low_a.astype(F32), low_b.astype(F32))
        high = jnp.where(wanted_first, high_a.astype(F32), high_b.astype(F32))
        return jnp.concatenate([low, high], axis=0)

    nb = 2 * half
    cb = first.shape[2]
    up0_panel[...] = dot(lower[0], head0[...]).astype(BF16)
    factor = dot(head1[...], upper[0]).astype(BF16)
    for j in range(cb):
        cols = slice(j * nb, (j + 1) * nb)
        old = rows_of(0, j)
        product = dot(lower[0], old.astype(BF16))
        in_panel = (column == 0) if j == 0 else False
        next_panel = (column == 1) if j == 0 else False
        if j == 0:
            top[0:nb, j, :] = jnp.where(in_panel, old, product).astype(BF16)
            product = jnp.where(in_panel, 0.0, product)
        else:
            top[0:nb, j, :] = product.astype(BF16)
        product = product.astype(BF16)
        up0[:, cols] = product
        updated = (rows_of(1, j) - dot(factor, product)).astype(BF16)
        last = dot(lower[1], updated)
        if j == 0:
            kept = jnp.where(next_panel, updated.astype(F32), last)
            kept = jnp.where(in_panel, factor.astype(F32), kept)
            top[nb : 2 * nb, j, :] = kept.astype(BF16)
            last = jnp.where(jnp.logical_or(in_panel, next_panel), 0.0, last)
        else:
            top[nb : 2 * nb, j, :] = last.astype(BF16)
        up1[:, cols] = last.astype(BF16)


def prep(meta, first, second, head0, head1, lower, upper):
    _, half, cb, nb = first.shape
    smem = pl.BlockSpec(memory_space=pltpu.SMEM)
    vmem = pl.BlockSpec(memory_space=pltpu.VMEM)
    return pl.pallas_call(
        prep_kernel,
        out_shape=(
            jax.ShapeDtypeStruct((nb, cb * nb), BF16),
            jax.ShapeDtypeStruct((nb, cb * nb), BF16),
            jax.ShapeDtypeStruct((nb, nb), BF16),
            jax.ShapeDtypeStruct((2 * nb, cb, nb), BF16),
        ),
        in_specs=[smem] + [vmem] * 6,
        out_specs=(vmem,) * 4,
        compiler_params=pltpu.CompilerParams(vmem_limit_bytes=VMEM_LIMIT),
    )(meta, first, second, head0, head1, lower, upper)


def update_kernel(
    per_block, meta, position, panel0, panel1, tiles, old_mine, old_sibling, upper,
    up0, up1, up0_panel, top, out,
):
    row, column, row_devices = meta[0], meta[2], meta[3]
    step = pl.program_id(0)
    chunk, cb, nb = out.shape
    block = step // per_block * row_devices + row

    @pl.when(block < 2)
    def _():
        begin = block * nb + lax.rem(step, per_block) * chunk
        out[...] = top[pl.ds(begin, chunk)]

    @pl.when(block >= 2)
    def _():
        place = position[...]
        moved = place >= 0
        slots = lax.broadcasted_iota(jnp.int32, (chunk, 2 * nb), 1)
        pick = jnp.where(slots == place, 1.0, 0.0).astype(BF16)
        fixed = []
        for k, panel in enumerate((panel0, panel1)):
            brought = dot(pick[:, :nb], old_mine[k]) + dot(pick[:, nb:], old_sibling[k])
            fixed.append(jnp.where(moved, brought, panel[0, 0].astype(F32)))
        factor0 = dot(fixed[0].astype(BF16), upper[0]).astype(BF16)
        below = (fixed[1] - dot(factor0, up0_panel[...])).astype(BF16)
        factor1 = dot(below, upper[1]).astype(BF16)
        for j in range(cb):
            cols = slice(j * nb, (j + 1) * nb)
            value = tiles[:, j, :].astype(F32) - dot(factor0, up0[:, cols])
            value = value.astype(BF16).astype(F32) - dot(factor1, up1[:, cols])
            if j == 0:
                value = jnp.where(column == 0, factor0.astype(F32), value)
                value = jnp.where(column == 1, factor1.astype(F32), value)
            out[:, j, :] = value.astype(BF16)


def update(meta, position, panels, skip, tiles, old_mine, old_sibling, upper, up0, up1, up0_panel, top, rows):
    chunk, nb = panels.shape[2:]
    cb = tiles.shape[1]
    whole = lambda a: pl.BlockSpec(a.shape, lambda s: (0,) * a.ndim)
    return pl.pallas_call(
        functools.partial(update_kernel, nb // chunk),
        grid=(rows // chunk,),
        out_shape=jax.ShapeDtypeStruct((rows, cb, nb), BF16),
        in_specs=[
            pl.BlockSpec(memory_space=pltpu.SMEM),
            pl.BlockSpec((chunk, 1), lambda s: (s, 0)),
            pl.BlockSpec((1, 1, chunk, nb), lambda s: (0, s + skip, 0, 0)),
            pl.BlockSpec((1, 1, chunk, nb), lambda s: (1, s + skip, 0, 0)),
            pl.BlockSpec((chunk, cb, nb), lambda s: (s, 0, 0)),
            whole(old_mine), whole(old_sibling), whole(upper), whole(up0), whole(up1), whole(up0_panel), whole(top),
        ],
        out_specs=pl.BlockSpec((chunk, cb, nb), lambda s: (s, 0, 0)),
        compiler_params=pltpu.CompilerParams(vmem_limit_bytes=VMEM_LIMIT),
    )(meta, position, panels, panels, tiles, old_mine, old_sibling, upper, up0, up1, up0_panel, top)


def body(matrix, pivots, lower_inverse, upper_inverse):
    rb, nb, cb, _ = matrix.shape
    rows = rb * nb
    row_devices = lax.axis_size("prow")
    col_devices = lax.axis_size("pcol")
    chips = row_devices // 2
    line = col_devices // 2
    row = lax.axis_index("prow").astype(jnp.int32)
    column = lax.axis_index("pcol").astype(jnp.int32)
    core, chip = row % 2, row // 2
    place_in_line, side = column // 2, column % 2
    meta = jnp.stack([row, core, column, jnp.int32(row_devices)])
    tiles = matrix.reshape(rows, cb, nb)

    sibling = [(r, r ^ 1) for r in range(row_devices)]
    neighbour = [(c, c ^ 1) for c in range(col_devices)]
    onward = [(c, c + 2) for c in range(col_devices - 2)]

    chunk = nb // 2
    per_block = nb // chunk
    pieces = rows // chunk
    skip = line - 1
    panels = jnp.zeros((2, pieces + 2 * skip, chunk, nb), BF16)
    held = tiles[0:chunk, 0, :]
    after_block = None
    for step in range(pieces + line - 1):
        if step:
            held = lax.ppermute(held, "pcol", onward)
            if step < pieces:
                own = tiles[step * chunk : (step + 1) * chunk, 0, :]
                held = jnp.where(place_in_line == 0, own, held)
        other = lax.ppermute(held, "pcol", neighbour)
        slot = step - place_in_line + skip
        panels = lax.dynamic_update_slice(panels, held[None, None], (side, slot, 0, 0))
        panels = lax.dynamic_update_slice(panels, other[None, None], (1 - side, slot, 0, 0))
        if step == per_block - 1 + skip:
            after_block = panels[:, skip : skip + per_block].reshape(2, nb, nb)

    old_mine = after_block
    for hop in range(1, chips):
        came = lax.ppermute(after_block, "prow", [(0, 2 * hop), (1, 2 * hop + 1)])
        old_mine = jnp.where(chip == hop, came, old_mine)
    old_sibling = lax.ppermute(old_mine, "prow", sibling)

    def source_of(index):
        return swapped(pivots[0], 0, swapped(pivots[1], nb, index))

    def target_of(index):
        return swapped(pivots[1], nb, swapped(pivots[0], 0, index))

    def holder(index):
        return index // nb % row_devices

    def local(index):
        return index // (nb * row_devices) * nb + index % nb

    def placed(index, valid):
        mine = valid & (holder(index) == row) & (index >= 2 * nb)
        return jnp.where(mine, local(index), rows)

    half = nb // 2
    indices, values = [], []
    new_top = []
    head = None
    for turn in range(2):
        begin = jnp.where((side == 0) == (turn == 0), nb, 0)
        kept_slots = begin + core * half + jnp.arange(half, dtype=jnp.int32)
        sent_slots = begin + (1 - core) * half + jnp.arange(half, dtype=jnp.int32)
        source_all = source_of(jnp.concatenate([kept_slots, sent_slots]))
        source_kept, source_sent = source_all[:half], source_all[half:]
        second_all = source_of(source_all)
        on_chip = holder(source_all) // 2 == chip
        wanted = jnp.where(on_chip, source_all, second_all)
        here = local(wanted)
        keep, send = gather_rows(here[:half], here[half:], tiles)
        from_sibling = lax.ppermute(send, "prow", sibling)
        is_mine = (holder(wanted[:half]) == row)[:, None, None]
        joined = jnp.where(is_mine, keep, from_sibling)
        top_here, brought = joined, None
        for hop in range(1, chips):
            came = lax.ppermute(
                joined, "prow", [(r, (r + 2 * hop) % row_devices) for r in range(row_devices)]
            )
            from_chip = (chip - hop) % chips
            theirs = (holder(source_kept) // 2 == from_chip)[:, None, None]
            top_here = jnp.where(theirs, came, top_here)
            brought = came if brought is None else jnp.where(from_chip == 0, came, brought)
        if brought is None:
            brought = joined
        both = jnp.stack([top_here, brought])
        theirs = lax.ppermute(both, "prow", sibling)
        new_top.append(jnp.stack([top_here, theirs[0]]))
        away = chip != 0
        for value, source in ((brought, source_kept), (theirs[1], source_sent)):
            indices.append(placed(source, away))
            values.append(value)
        if turn == 0:
            part = nb // row_devices
            full = jnp.concatenate([top_here[:, 0, :], theirs[0][:, 0, :]])
            at = (row * part + core * half) % nb
            head = lax.dynamic_slice(full, (at, 0), (part, nb))

    block0 = tiles[:nb]
    sibling_block0 = lax.ppermute(block0, "prow", sibling)
    tops = jnp.arange(nb, dtype=jnp.int32)
    for value, first_row in ((block0, core * nb), (sibling_block0, (1 - core) * nb)):
        indices.append(placed(target_of(first_row + tops), chip == 0))
        values.append(value)
    moved_tiles = scatter_rows(indices, values, tiles)

    for _ in range(line - 1):
        head = jnp.where(place_in_line == 0, head, lax.ppermute(head, "pcol", onward))
    head_other = lax.ppermute(head, "pcol", neighbour)
    head = jnp.where(side == 1, jnp.stack([head, head_other]), jnp.stack([head_other, head]))
    heads = jnp.zeros((2, row_devices) + head.shape[1:], BF16)
    around = [(chip, head)]
    for hop in range(1, chips):
        came = lax.ppermute(head, "prow", [(r, (r + 2 * hop) % row_devices) for r in range(row_devices)])
        around.append(((chip - hop) % chips, came))
    for at, piece in around:
        heads = lax.dynamic_update_slice(heads, piece[:, None], (0, 2 * at + core, 0, 0))
    packed = jnp.stack([piece for _, piece in around])
    packed = lax.ppermute(packed, "prow", sibling)
    for i, (at, _) in enumerate(around):
        heads = lax.dynamic_update_slice(heads, packed[i][:, None], (0, 2 * at + 1 - core, 0, 0))
    heads = heads.reshape(2, nb, nb)

    up0, up1, up0_panel, top = prep(meta, new_top[0], new_top[1], heads[0], heads[1], lower_inverse, upper_inverse)

    slot = jnp.arange(rows, dtype=jnp.int32)
    mine = (slot // nb * row_devices + row) * nb + slot % nb
    source = source_of(mine)
    same_core = source // nb == core
    position = jnp.where(same_core, source % nb, nb + source % nb)
    position = jnp.where((source < 2 * nb) & (mine >= 2 * nb), position, -1)
    result = update(
        meta, position[:, None], panels, skip, moved_tiles, old_mine, old_sibling, upper_inverse,
        up0, up1, up0_panel, top, rows,
    )
    return result.reshape(matrix.shape)


def solution(mesh):
    placed = (P(None, "prow", None, "pcol"), P(), P(), P())
    return jax.shard_map(
        body, mesh=mesh, in_specs=placed, out_specs=P(None, "prow", None, "pcol"), check_vma=False
    )
```

```python
import functools

import jax
import jax.numpy as jnp
from jax import lax
from jax.experimental import pallas as pl
from jax.experimental.pallas import tpu as pltpu
from jax.sharding import PartitionSpec as P

BF16 = jnp.bfloat16
F32 = jnp.float32
I32 = jnp.int32
SMEM = pl.BlockSpec(memory_space=pltpu.SMEM)
VMEM = pl.BlockSpec(memory_space=pltpu.VMEM)
PARAMS = pltpu.CompilerParams(vmem_limit_bytes=48 * 1024 * 1024)


def dot(a, b):
    return jnp.dot(a, b, preferred_element_type=F32)


def flat(rows):
    return rows.reshape(rows.shape[0], rows.shape[1] * rows.shape[2])


def index_kernel(nb, rows, meta, pivots, fetch, join, arrive, goal, hops):
    row, core, row_devices = meta[0], meta[1], meta[3]
    chip, chips = row // 2, row_devices // 2
    slots = lax.broadcasted_iota(I32, (1, 2 * nb), 1)

    def swapped(panel, index):
        def add(i, total):
            begin = pl.multiple_of(i * 8, 8)
            pivot = pivots[pl.ds(begin, 8), panel : panel + 1]
            top = panel * nb + begin + lax.broadcasted_iota(I32, (8, 1), 0)
            step = pivot - top
            total = total + jnp.where(index == top, step, 0)
            return total - jnp.where(index == pivot, step, 0)

        total = lax.fori_loop(0, nb // 8, add, jnp.zeros((8, 2 * nb), I32), unroll=4)
        return index + jnp.sum(total, axis=0, keepdims=True)

    def source_of(index):
        return swapped(0, swapped(1, index))

    def holder(index):
        return lax.rem(lax.div(index, nb), row_devices)

    def local(index):
        return lax.div(index, nb * row_devices) * nb + lax.rem(index, nb)

    def placed(index):
        mine = (holder(index) == row) & (index >= 2 * nb)
        return jnp.where(mine, local(index), rows)

    source = source_of(slots)
    second = source_of(source)
    target = swapped(1, swapped(0, slots))
    from_chip = lax.div(holder(source), 2)
    wanted = jnp.where(from_chip == chip, source, second)
    fetch[...] = local(wanted)
    join[...] = jnp.where(holder(wanted) == row, lax.rem(slots, nb), nb)
    arrive[...] = placed(source)
    goal[...] = placed(target)
    hops[...] = lax.rem(chip + chips - from_chip, chips)


def make_indices(meta, pivots, nb, rows):
    steps = pivots.shape[0]
    shape = jax.ShapeDtypeStruct((1, steps * nb), I32)
    return pl.pallas_call(
        functools.partial(index_kernel, nb, rows),
        out_shape=(shape,) * 5,
        in_specs=[SMEM, VMEM],
        out_specs=(VMEM,) * 5,
        compiler_params=PARAMS,
    )(meta, pivots.T)


def split_kernel(tiles, *panels):
    nb = panels[0].shape[0]
    for b, panel in enumerate(panels):
        panel[...] = flat(tiles[b * nb : (b + 1) * nb])[:, :nb]


def split_panels(tiles, nb):
    count = tiles.shape[0] // nb
    return pl.pallas_call(
        split_kernel,
        out_shape=(jax.ShapeDtypeStruct((nb, nb), BF16),) * count,
        in_specs=[VMEM],
        out_specs=(VMEM,) * count,
        compiler_params=PARAMS,
    )(tiles)


def send_kernel(meta, fetch, tiles, send, block0):
    count = send.shape[0]
    begin = (1 - meta[1]) * count

    def copy(i, carry):
        send[i] = tiles[fetch[0, begin + i]]
        return carry

    lax.fori_loop(0, count, copy, 0, unroll=16)
    block0[...] = tiles[0:count]


def gather_sent(meta, fetch, tiles, nb):
    shape = jax.ShapeDtypeStruct((nb,) + tiles.shape[1:], BF16)
    return pl.pallas_call(
        send_kernel,
        out_shape=(shape, shape),
        in_specs=[SMEM, SMEM, VMEM],
        out_specs=(VMEM, VMEM),
        compiler_params=PARAMS,
    )(meta, fetch, tiles)


def join_kernel(meta, fetch, join, tiles, came, joined, work):
    count = came.shape[0]
    begin = meta[1] * count
    work[0:count] = came[...]

    def copy(i, carry):
        work[join[0, begin + i]] = tiles[fetch[0, begin + i]]
        return carry

    lax.fori_loop(0, count, copy, 0, unroll=16)
    joined[...] = work[0:count]


def join_rows(meta, fetch, join, tiles, came):
    nb = came.shape[0]
    return pl.pallas_call(
        join_kernel,
        out_shape=jax.ShapeDtypeStruct(came.shape, BF16),
        in_specs=[SMEM, SMEM, SMEM, VMEM, VMEM],
        out_specs=VMEM,
        scratch_shapes=[pltpu.VMEM((nb + 8,) + came.shape[1:], BF16)],
        compiler_params=PARAMS,
    )(meta, fetch, join, tiles, came)


def scatter_kernel(meta, arrive, goal, came, came_sibling, old, old_sibling, tiles, out):
    core, chip = meta[1], meta[0] // 2
    count = old.shape[0]
    out[0 : tiles.shape[0]] = tiles[...]

    def scatter(index, values, begin):
        def copy(i, carry):
            out[index[0, begin + i]] = values[i]
            return carry

        lax.fori_loop(0, count, copy, 0, unroll=16)

    @pl.when(chip == 0)
    def _():
        scatter(goal, old, core * count)
        scatter(goal, old_sibling, (1 - core) * count)

    @pl.when(chip != 0)
    def _():
        scatter(arrive, came, core * count)
        scatter(arrive, came_sibling, (1 - core) * count)


def scatter_rows(meta, arrive, goal, came, came_sibling, old, old_sibling, tiles):
    rows = tiles.shape[0] + 8
    return pl.pallas_call(
        scatter_kernel,
        out_shape=jax.ShapeDtypeStruct((rows,) + tiles.shape[1:], BF16),
        in_specs=[SMEM] * 3 + [VMEM] * 5,
        out_specs=VMEM,
        compiler_params=PARAMS,
    )(meta, arrive, goal, came, came_sibling, old, old_sibling, tiles)


def choose(hop, choices):
    value = flat(choices[0]).astype(F32)
    for h, other in enumerate(choices[1:], 1):
        value = jnp.where(hop == h, flat(other).astype(F32), value)
    return value.astype(BF16)


def head_kernel(meta, hops, *refs):
    *choices, out = refs
    part = out.shape[0]
    nb = hops.shape[0] // 2
    core, begin = meta[1], meta[0] // 2 * part
    hop = hops[pl.ds(core * nb + begin, part)]
    out[...] = choose(hop, [c[pl.ds(begin, part)] for c in choices])[:, : out.shape[1]]


def head_part(meta, hops, choices, part):
    nb = choices[0].shape[2]
    return pl.pallas_call(
        head_kernel,
        out_shape=jax.ShapeDtypeStruct((part, nb), BF16),
        in_specs=[SMEM] + [VMEM] * (1 + len(choices)),
        out_specs=VMEM,
        compiler_params=PARAMS,
    )(meta, hops, *choices)


def prep_kernel(chips, meta, hops, lower, upper, *refs):
    mine, sibling = refs[:chips], refs[chips : 2 * chips]
    heads, heads_sibling = refs[2 * chips : 3 * chips], refs[3 * chips : 4 * chips]
    up0, up1, up0_panel, top, fresh, head = refs[4 * chips :]
    core, column, chip = meta[1], meta[2], meta[0] // 2
    nb = head.shape[1]
    part = heads[0].shape[0]
    for who, choices in ((core, mine), (1 - core, sibling)):
        fresh[who] = choose(hops[pl.ds(who * nb, nb)], [c[0:nb] for c in choices])
    for who, pieces in ((core, heads), (1 - core, heads_sibling)):
        for h, piece in enumerate(pieces):
            head[who, pl.ds(lax.rem(chip + chips - h, chips) * part, part)] = piece[...]
    up0_panel[...] = dot(lower[0], head[0]).astype(BF16)
    factor = dot(head[1], upper[0]).astype(BF16)
    in_panel, next_panel = column == 0, column == 1
    tops = [[], []]
    for j in range(fresh.shape[2] // nb):
        cols = slice(j * nb, (j + 1) * nb)
        product = dot(lower[0], fresh[0, :, cols])
        shown = product
        if j == 0:
            shown = jnp.where(in_panel, fresh[0, :, cols].astype(F32), product)
            product = jnp.where(in_panel, 0.0, product)
        product = product.astype(BF16)
        up0[:, cols] = product
        updated = (fresh[1, :, cols].astype(F32) - dot(factor, product)).astype(BF16)
        last = dot(lower[1], updated)
        kept = last
        if j == 0:
            kept = jnp.where(next_panel, updated.astype(F32), kept)
            kept = jnp.where(in_panel, factor.astype(F32), kept)
            last = jnp.where(in_panel | next_panel, 0.0, last)
        up1[:, cols] = last.astype(BF16)
        tops[0].append(shown.astype(BF16))
        tops[1].append(kept.astype(BF16))
    for k in range(2):
        top[k * nb : (k + 1) * nb] = jnp.concatenate(tops[k], axis=1).reshape(nb, len(tops[k]), nb)


def prep(meta, hops, lower, upper, mine, sibling, heads, heads_sibling):
    cb, nb = mine[0].shape[1:]
    chips = len(mine)
    return pl.pallas_call(
        functools.partial(prep_kernel, chips),
        out_shape=(
            jax.ShapeDtypeStruct((nb, cb * nb), BF16),
            jax.ShapeDtypeStruct((nb, cb * nb), BF16),
            jax.ShapeDtypeStruct((nb, nb), BF16),
            jax.ShapeDtypeStruct((2 * nb, cb, nb), BF16),
        ),
        in_specs=[SMEM] + [VMEM] * (3 + 4 * chips),
        out_specs=(VMEM,) * 4,
        scratch_shapes=[pltpu.VMEM((2, nb, cb * nb), BF16), pltpu.VMEM((2, nb, nb), BF16)],
        compiler_params=PARAMS,
    )(meta, hops, lower, upper, *mine, *sibling, *heads, *heads_sibling)


def update_kernel(
    block, meta, goal, held, other, tiles, old, old_sibling, upper, up0, up1, up0_panel, top, *rest
):
    out = rest[-1]
    row, core, column = meta[0], meta[1], meta[2]
    side = lax.rem(column, 2)
    chunk, cb, nb = out.shape
    begin = pl.program_id(0) * chunk

    def from_top():
        out[...] = top[pl.ds(row * nb + begin, chunk)]

    def from_factors():
        here = block * nb + begin + lax.broadcasted_iota(I32, (chunk, nb), 0)
        pick = jnp.where(here == goal[pl.ds(core, 1), :], 1.0, 0.0)
        pick_sibling = jnp.where(here == goal[pl.ds(1 - core, 1), :], 1.0, 0.0)
        moved = jnp.sum(pick + pick_sibling, axis=1, keepdims=True) > 0.5
        pick, pick_sibling = pick.astype(BF16), pick_sibling.astype(BF16)
        mine, theirs = held[...].astype(F32), other[...].astype(F32)
        raw = (jnp.where(side == 0, mine, theirs), jnp.where(side == 0, theirs, mine))
        panels = []
        for k in range(2):
            which = lax.rem(k + side, 2)
            brought = dot(pick, old[which]) + dot(pick_sibling, old_sibling[which])
            panels.append(jnp.where(moved, brought, raw[k]))
        factor0 = dot(panels[0].astype(BF16), upper[0]).astype(BF16)
        below = (panels[1] - dot(factor0, up0_panel[...])).astype(BF16)
        factor1 = dot(below, upper[1]).astype(BF16)
        values = flat(tiles[...])
        results = []
        for j in range(cb):
            cols = slice(j * nb, (j + 1) * nb)
            value = values[:, cols].astype(F32) - dot(factor0, up0[:, cols])
            value = value.astype(BF16).astype(F32) - dot(factor1, up1[:, cols])
            if j == 0:
                value = jnp.where(column == 0, factor0.astype(F32), value)
                value = jnp.where(column == 1, factor1.astype(F32), value)
            results.append(value.astype(BF16))
        out[...] = jnp.concatenate(results, axis=1).reshape(chunk, cb, nb)

    if block == 0:
        pl.when(row < 2)(from_top)
        pl.when(row >= 2)(from_factors)
    else:
        from_factors()


def update(block, meta, goal, held, other, tiles, old, old_sibling, upper, up0, up1, up0_panel, top, rows, done):
    nb = held.shape[0]
    chunk = nb // 2
    cb = tiles.shape[1]
    whole = lambda a: pl.BlockSpec(a.shape, lambda s: (0,) * a.ndim)
    at_block = lambda s: (block * (nb // chunk) + s, 0, 0)
    operands = [meta, goal, held, other, tiles, old, old_sibling, upper, up0, up1, up0_panel, top]
    in_specs = [
        SMEM,
        whole(goal),
        pl.BlockSpec((chunk, nb), lambda s: (s, 0)),
        pl.BlockSpec((chunk, nb), lambda s: (s, 0)),
        pl.BlockSpec((chunk, cb, nb), at_block),
    ] + [whole(a) for a in operands[5:]]
    aliases = {}
    if done is not None:
        aliases = {len(operands): 0}
        operands.append(done)
        in_specs.append(pl.BlockSpec(memory_space=pl.ANY))
    steps = nb // chunk
    return pl.pallas_call(
        functools.partial(update_kernel, block),
        grid=(steps,),
        out_shape=jax.ShapeDtypeStruct((rows, cb, nb), BF16),
        in_specs=in_specs,
        out_specs=pl.BlockSpec((chunk, cb, nb), at_block),
        input_output_aliases=aliases,
        compiler_params=PARAMS,
        cost_estimate=pl.CostEstimate(
            flops=2 * nb**3 * (7 + 2 * cb), bytes_accessed=16 * nb * nb * 2, transcendentals=0
        ),
    )(*operands)


def body(matrix, pivots, lower_inverse, upper_inverse):
    rb, nb, cb, _ = matrix.shape
    rows = rb * nb
    row_devices = lax.axis_size("prow")
    col_devices = lax.axis_size("pcol")
    chips = row_devices // 2
    line = col_devices // 2
    row = lax.axis_index("prow").astype(I32)
    column = lax.axis_index("pcol").astype(I32)
    core, chip = row % 2, row // 2
    place = column // 2
    meta = jnp.stack([row, core, column, jnp.int32(row_devices)])
    tiles = matrix.reshape(rows, cb, nb)

    sibling = [(r, r ^ 1) for r in range(row_devices)]
    neighbour = [(c, c ^ 1) for c in range(col_devices)]

    def chip_hop(h):
        return [(r, (r + 2 * h) % row_devices) for r in range(row_devices)]

    def line_hop(h):
        return [(2 * h - 2, 2 * h), (2 * h - 1, 2 * h + 1)]

    def along_line(value, axes, hop_pairs):
        held = value
        for h in range(1, line):
            value = lax.ppermute(value, axes, hop_pairs(h))
            held = jnp.where(place == h, value, held)
        return held

    own = split_panels(tiles, nb)
    hops_done = [list(own)]
    for h in range(1, line):
        came = []
        for b in range(rb):
            sent = hops_done[-1][b]
            if b >= 2:
                sent, _ = lax.optimization_barrier((sent, came[b - 2]))
            came.append(lax.ppermute(sent, "pcol", line_hop(h)))
        hops_done.append(came)
    held, other = [], []
    for b in range(rb):
        value = own[b]
        for h in range(1, line):
            value = jnp.where(place == h, hops_done[h][b], value)
        held.append(value)
        other.append(lax.ppermute(value, "pcol", neighbour))

    fetch, join, arrive, goal, hops = make_indices(meta, pivots, nb, rows)
    hops = hops.reshape(2 * nb, 1)
    send, block0 = gather_sent(meta, fetch, tiles, nb)
    from_sibling = lax.ppermute(send, "prow", sibling)
    joined = join_rows(meta, fetch, join, tiles, from_sibling)
    mine = [joined] + [lax.ppermute(joined, "prow", chip_hop(h)) for h in range(1, chips)]
    block0_sibling = lax.ppermute(block0, "prow", sibling)
    theirs = [lax.ppermute(value, "prow", sibling) for value in mine]

    part = nb // chips
    head = head_part(meta, hops, mine, part)
    flat_index = lambda r, c: r * col_devices + c
    senders = [[r for r in range(row_devices) if r % 2 != s] for s in range(2)]

    def head_pairs(h):
        return [(flat_index(r, a), flat_index(r, b)) for a, b in line_hop(h) for r in senders[a % 2]]

    both = ("prow", "pcol")
    head = along_line(head, both, head_pairs)
    swap_pairs = [(flat_index(r, c), flat_index(r, c ^ 1)) for c in range(col_devices) for r in senders[c % 2]]
    head = jnp.where(column % 2 != core, head, lax.ppermute(head, both, swap_pairs))
    heads = [head] + [lax.ppermute(head, "prow", chip_hop(h)) for h in range(1, chips)]
    heads_sibling = [lax.ppermute(value, "prow", sibling) for value in heads]
    up0, up1, up0_panel, top = prep(
        meta, hops, lower_inverse, upper_inverse, mine, theirs, heads, heads_sibling
    )

    def from_first_chip(values):
        value = values[-1]
        for h in range(1, chips - 1):
            value = jnp.where(chip == h, values[h], value)
        return value

    moved_tiles = scatter_rows(
        meta, arrive, goal, from_first_chip(mine), from_first_chip(theirs), block0, block0_sibling, tiles
    )

    old = jnp.stack([held[0], other[0]])
    first_old = old
    for h in range(1, chips):
        came = lax.ppermute(first_old, "prow", [(0, 2 * h), (1, 2 * h + 1)])
        old = jnp.where(chip == h, came, old)
    old_sibling = lax.ppermute(old, "prow", sibling)

    goal = goal.reshape(2, nb)
    result = None
    for b in range(rb):
        result = update(
            b, meta, goal, held[b], other[b], moved_tiles, old, old_sibling, upper_inverse,
            up0, up1, up0_panel, top, rows, result,
        )
    return result.reshape(matrix.shape)


def solution(mesh):
    placed = (P(None, "prow", None, "pcol"), P(), P(), P())
    return jax.shard_map(
        body, mesh=mesh, in_specs=placed, out_specs=P(None, "prow", None, "pcol"), check_vma=False
    )
```

```python
import functools

import jax
import jax.numpy as jnp
from jax import lax
from jax.experimental import pallas as pl
from jax.experimental.pallas import tpu as pltpu
from jax.sharding import PartitionSpec as P

BF16 = jnp.bfloat16
F32 = jnp.float32
I32 = jnp.int32
SMEM = pl.BlockSpec(memory_space=pltpu.SMEM)
VMEM = pl.BlockSpec(memory_space=pltpu.VMEM)
PARAMS = pltpu.CompilerParams(vmem_limit_bytes=20 * 1024 * 1024)


def dot(a, b):
    return jnp.dot(a, b, preferred_element_type=F32)


def flat(rows):
    return rows.reshape(rows.shape[0], rows.shape[1] * rows.shape[2])


def index_kernel(nb, rows, meta, pivots, spread, fetch, join, arrive, goal, hops):
    row, row_devices = meta[0], meta[3]
    chip, chips = row // 2, row_devices // 2
    lanes = spread.shape[2]
    tiles = nb // lanes
    slot = lax.broadcasted_iota(I32, (1, nb), 1)
    pivot0, pivot1 = pivots[0:1, :], pivots[1:2, :]

    def lookup(keys, entry, value):
        parts = [keys[:, t * lanes : (t + 1) * lanes] for t in range(tiles)]

        def add(i, totals):
            begin = pl.multiple_of(i * 8, 8)
            at = begin + lax.broadcasted_iota(I32, (8, lanes), 0)
            here, give = entry(begin, at), value(begin, at)
            return tuple(t + jnp.where(p == here, give, 0) for t, p in zip(totals, parts))

        zero = jnp.zeros((8, lanes), I32)
        totals = lax.fori_loop(0, nb // 8, add, (zero,) * tiles, unroll=8)
        return jnp.concatenate([jnp.sum(t, axis=0, keepdims=True) for t in totals], axis=1)

    def pivot_of(panel):
        return lambda begin, at: spread[panel, pl.ds(begin, 8), :]

    place = lambda begin, at: at + 1
    in_pivots0 = lookup(pivot1, pivot_of(0), place)
    in_pivots1 = lookup(pivot0, pivot_of(1), place)
    top1_in_pivots0 = lookup(nb + slot, pivot_of(0), place)
    over_top1 = lookup(pivot0, lambda begin, at: nb + at, pivot_of(1))
    chained = lookup(nb + in_pivots1 - 1, pivot_of(0), place)

    source0 = pivot0
    source1 = jnp.where(in_pivots0 > 0, in_pivots0 - 1, pivot1)
    second0 = jnp.where(in_pivots1 > 0, jnp.where(chained > 0, chained - 1, nb + in_pivots1 - 1), slot)
    second1 = jnp.where(top1_in_pivots0 > 0, top1_in_pivots0 - 1, nb + slot)
    target0 = jnp.where(over_top1 > 0, over_top1, jnp.where(in_pivots1 > 0, nb + in_pivots1 - 1, pivot0))
    target1 = jnp.where(top1_in_pivots0 > 0, top1_in_pivots0 - 1, pivot1)

    def holder(index):
        return lax.rem(lax.div(index, nb), row_devices)

    def local(index):
        return lax.div(index, nb * row_devices) * nb + lax.rem(index, nb)

    def placed(index):
        mine = (holder(index) == row) & (index >= 2 * nb)
        return jnp.where(mine, local(index), rows)

    for k, (source, second, target) in enumerate(((source0, second0, target0), (source1, second1, target1))):
        from_chip = lax.div(holder(source), 2)
        wanted = jnp.where(from_chip == chip, source, second)
        at = (slice(None), slice(k * nb, (k + 1) * nb))
        fetch[at] = local(wanted)
        join[at] = jnp.where(holder(wanted) == row, slot, nb)
        arrive[at] = placed(source)
        goal[at] = placed(target)
        hops[at] = lax.rem(chip + chips - from_chip, chips)


def make_indices(meta, pivots, nb, rows):
    steps = pivots.shape[0]
    shape = jax.ShapeDtypeStruct((1, steps * nb), I32)
    lanes = min(nb, 128)
    spread = jnp.broadcast_to(pivots[:, :, None], (steps, nb, lanes))
    return pl.pallas_call(
        functools.partial(index_kernel, nb, rows),
        out_shape=(shape,) * 5,
        in_specs=[SMEM, VMEM, VMEM],
        out_specs=(VMEM,) * 5,
        compiler_params=PARAMS,
    )(meta, pivots, spread)


def split_kernel(tiles, panel):
    panel[...] = flat(tiles[...])[:, : panel.shape[1]]


def split_panels(tiles):
    rows, cb, nb = tiles.shape
    return pl.pallas_call(
        split_kernel,
        grid=(rows // nb,),
        out_shape=jax.ShapeDtypeStruct((rows, nb), BF16),
        in_specs=[pl.BlockSpec((nb, cb, nb), lambda s: (s, 0, 0))],
        out_specs=pl.BlockSpec((nb, nb), lambda s: (s, 0)),
        compiler_params=PARAMS,
    )(tiles)


def send_kernel(meta, fetch, tiles, send, block0):
    count = send.shape[0]
    begin = (1 - meta[1]) * count

    def copy(i, carry):
        send[i] = tiles[fetch[0, begin + i]]
        return carry

    lax.fori_loop(0, count, copy, 0, unroll=16)
    block0[...] = tiles[0:count]


def gather_sent(meta, fetch, tiles, nb):
    shape = jax.ShapeDtypeStruct((nb,) + tiles.shape[1:], BF16)
    return pl.pallas_call(
        send_kernel,
        out_shape=(shape, shape),
        in_specs=[SMEM, SMEM, VMEM],
        out_specs=(VMEM, VMEM),
        compiler_params=PARAMS,
    )(meta, fetch, tiles)


def join_kernel(meta, fetch, join, tiles, came, joined, work):
    count = came.shape[0]
    begin = meta[1] * count
    work[0:count] = came[...]

    def copy(i, carry):
        work[join[0, begin + i]] = tiles[fetch[0, begin + i]]
        return carry

    lax.fori_loop(0, count, copy, 0, unroll=16)
    joined[...] = work[0:count]


def join_rows(meta, fetch, join, tiles, came):
    nb = came.shape[0]
    return pl.pallas_call(
        join_kernel,
        out_shape=jax.ShapeDtypeStruct(came.shape, BF16),
        in_specs=[SMEM, SMEM, SMEM, VMEM, VMEM],
        out_specs=VMEM,
        scratch_shapes=[pltpu.VMEM((nb + 8,) + came.shape[1:], BF16)],
        compiler_params=PARAMS,
    )(meta, fetch, join, tiles, came)


def scatter_kernel(meta, arrive, goal, came, came_sibling, old, old_sibling, tiles, out):
    core, chip = meta[1], meta[0] // 2
    count = old.shape[0]
    out[0 : tiles.shape[0]] = tiles[...]

    def scatter(index, values, begin):
        def copy(i, carry):
            out[index[0, begin + i]] = values[i]
            return carry

        lax.fori_loop(0, count, copy, 0, unroll=16)

    @pl.when(chip == 0)
    def _():
        scatter(goal, old, core * count)
        scatter(goal, old_sibling, (1 - core) * count)

    @pl.when(chip != 0)
    def _():
        scatter(arrive, came, core * count)
        scatter(arrive, came_sibling, (1 - core) * count)


def scatter_rows(meta, arrive, goal, came, came_sibling, old, old_sibling, tiles):
    rows = tiles.shape[0] + 8
    return pl.pallas_call(
        scatter_kernel,
        out_shape=jax.ShapeDtypeStruct((rows,) + tiles.shape[1:], BF16),
        in_specs=[SMEM] * 3 + [VMEM] * 5,
        out_specs=VMEM,
        compiler_params=PARAMS,
    )(meta, arrive, goal, came, came_sibling, old, old_sibling, tiles)


def choose(hop, choices):
    value = flat(choices[0]).astype(F32)
    for h, other in enumerate(choices[1:], 1):
        value = jnp.where(hop == h, flat(other).astype(F32), value)
    return value.astype(BF16)


def head_kernel(chips, meta, hops, *refs):
    out = refs[-1]
    part = out.shape[0]
    nb = hops.shape[0] // 2
    core = meta[1]
    needed = 1 - lax.rem(meta[2], 2)
    begin = meta[0] * part
    hop = hops[pl.ds(needed * nb + begin, part)]

    def take(choices):
        out[...] = choose(hop, [c[pl.ds(begin, part)] for c in choices])[:, : out.shape[1]]

    pl.when(core == needed)(lambda: take(refs[:chips]))
    pl.when(core != needed)(lambda: take(refs[chips : 2 * chips]))


def head_part(meta, hops, mine, sibling, part):
    nb = mine[0].shape[2]
    return pl.pallas_call(
        functools.partial(head_kernel, len(mine)),
        out_shape=jax.ShapeDtypeStruct((part, nb), BF16),
        in_specs=[SMEM] + [VMEM] * (1 + 2 * len(mine)),
        out_specs=VMEM,
        compiler_params=PARAMS,
    )(meta, hops, *mine, *sibling)


def prep_kernel(chips, meta, hops, lower, upper, *refs):
    mine, sibling = refs[:chips], refs[chips : 2 * chips]
    heads, heads_sibling = refs[2 * chips : 3 * chips], refs[3 * chips : 4 * chips]
    up0, up1, up0_panel, top, fresh, head = refs[4 * chips :]
    core, column, chip = meta[1], meta[2], meta[0] // 2
    nb = head.shape[1]
    part = heads[0].shape[1]
    side = lax.rem(column, 2)
    for who, choices in ((core, mine), (1 - core, sibling)):
        fresh[who] = choose(hops[pl.ds(who * nb, nb)], [c[0:nb] for c in choices])
    for who, pieces in ((core, heads), (1 - core, heads_sibling)):
        for h, piece in enumerate(pieces):
            at = pl.ds((2 * lax.rem(chip + chips - h, chips) + who) * part, part)
            head[1 - side, at] = piece[0]
            head[side, at] = piece[1]
    up0_panel[...] = dot(lower[0], head[0]).astype(BF16)
    factor = dot(head[1], upper[0]).astype(BF16)
    in_panel, next_panel = column == 0, column == 1
    tops = [[], []]
    for j in range(fresh.shape[2] // nb):
        cols = slice(j * nb, (j + 1) * nb)
        product = dot(lower[0], fresh[0, :, cols])
        shown = product
        if j == 0:
            shown = jnp.where(in_panel, fresh[0, :, cols].astype(F32), product)
            product = jnp.where(in_panel, 0.0, product)
        product = product.astype(BF16)
        up0[:, cols] = product
        updated = (fresh[1, :, cols].astype(F32) - dot(factor, product)).astype(BF16)
        last = dot(lower[1], updated)
        kept = last
        if j == 0:
            kept = jnp.where(next_panel, updated.astype(F32), kept)
            kept = jnp.where(in_panel, factor.astype(F32), kept)
            last = jnp.where(in_panel | next_panel, 0.0, last)
        up1[:, cols] = last.astype(BF16)
        tops[0].append(shown.astype(BF16))
        tops[1].append(kept.astype(BF16))
    for k in range(2):
        top[k * nb : (k + 1) * nb] = jnp.concatenate(tops[k], axis=1).reshape(nb, len(tops[k]), nb)


def prep(meta, hops, lower, upper, mine, sibling, heads, heads_sibling):
    cb, nb = mine[0].shape[1:]
    chips = len(mine)
    return pl.pallas_call(
        functools.partial(prep_kernel, chips),
        out_shape=(
            jax.ShapeDtypeStruct((nb, cb * nb), BF16),
            jax.ShapeDtypeStruct((nb, cb * nb), BF16),
            jax.ShapeDtypeStruct((nb, nb), BF16),
            jax.ShapeDtypeStruct((2 * nb, cb, nb), BF16),
        ),
        in_specs=[SMEM] + [VMEM] * (3 + 4 * chips),
        out_specs=(VMEM,) * 4,
        scratch_shapes=[pltpu.VMEM((2, nb, cb * nb), BF16), pltpu.VMEM((2, nb, nb), BF16)],
        compiler_params=PARAMS,
    )(meta, hops, lower, upper, *mine, *sibling, *heads, *heads_sibling)


def update_kernel(
    step, pieces, meta, goal, held, other, old, old_sibling, upper, up0, up1, up0_panel, tiles, top, *rest
):
    out, block, result, in_sem, out_sem = rest[-5:]
    row, core, column, row_devices = meta[0], meta[1], meta[2], meta[3]
    side, place = lax.rem(column, 2), lax.div(column, 2)
    chunk, cb, nb = block.shape
    per_block = nb // chunk
    piece = step - place
    begin = pl.multiple_of(piece * chunk, chunk)
    panel_row = lax.div(piece, per_block) * row_devices + row

    def fetch_top():
        copy = pltpu.make_async_copy(top.at[pl.ds(panel_row * nb + begin, chunk)], result, in_sem)
        copy.start()
        copy.wait()

    def from_factors():
        copy = pltpu.make_async_copy(tiles.at[pl.ds(begin, chunk)], block, in_sem)
        copy.start()
        here = begin + lax.broadcasted_iota(I32, (chunk, nb), 0)
        pick = jnp.where(here == goal[pl.ds(core, 1), :], 1.0, 0.0)
        pick_sibling = jnp.where(here == goal[pl.ds(1 - core, 1), :], 1.0, 0.0)
        moved = jnp.sum(pick + pick_sibling, axis=1, keepdims=True) > 0.5
        pick, pick_sibling = pick.astype(BF16), pick_sibling.astype(BF16)
        mine, theirs = held[...].astype(F32), other[...].astype(F32)
        raw = (jnp.where(side == 0, mine, theirs), jnp.where(side == 0, theirs, mine))
        panels = []
        for k in range(2):
            which = lax.rem(k + side, 2)
            brought = dot(pick, old[which]) + dot(pick_sibling, old_sibling[which])
            panels.append(jnp.where(moved, brought, raw[k]))
        factor0 = dot(panels[0].astype(BF16), upper[0]).astype(BF16)
        below = (panels[1] - dot(factor0, up0_panel[...])).astype(BF16)
        factor1 = dot(below, upper[1]).astype(BF16)
        copy.wait()
        values = flat(block[...])
        results = []
        for j in range(cb):
            cols = slice(j * nb, (j + 1) * nb)
            value = values[:, cols].astype(F32) - dot(factor0, up0[:, cols])
            value = value.astype(BF16).astype(F32) - dot(factor1, up1[:, cols])
            if j == 0:
                value = jnp.where(column == 0, factor0.astype(F32), value)
                value = jnp.where(column == 1, factor1.astype(F32), value)
            results.append(value.astype(BF16))
        result[...] = jnp.concatenate(results, axis=1).reshape(chunk, cb, nb)

    @pl.when((piece >= 0) & (piece < pieces))
    def _():
        pl.when(panel_row < 2)(fetch_top)
        pl.when(panel_row >= 2)(from_factors)
        copy = pltpu.make_async_copy(result, out.at[pl.ds(begin, chunk)], out_sem)
        copy.start()
        copy.wait()


def update(step, pieces, meta, goal, held, other, old, old_sibling, upper, up0, up1, up0_panel, tiles, top, done):
    chunk, nb = held.shape
    cb = tiles.shape[1]
    operands = [meta, goal, held, other, old, old_sibling, upper, up0, up1, up0_panel, tiles, top]
    anywhere = pl.BlockSpec(memory_space=pl.ANY)
    in_specs = [SMEM] + [VMEM] * 9 + [anywhere] * 2
    aliases = {}
    if done is not None:
        aliases = {len(operands): 0}
        operands.append(done)
        in_specs.append(anywhere)
    return pl.pallas_call(
        functools.partial(update_kernel, step, pieces),
        out_shape=jax.ShapeDtypeStruct((pieces * chunk, cb, nb), BF16),
        in_specs=in_specs,
        out_specs=anywhere,
        scratch_shapes=[
            pltpu.VMEM((chunk, cb, nb), BF16),
            pltpu.VMEM((chunk, cb, nb), BF16),
            pltpu.SemaphoreType.DMA,
            pltpu.SemaphoreType.DMA,
        ],
        input_output_aliases=aliases,
        compiler_params=PARAMS,
        cost_estimate=pl.CostEstimate(
            flops=2 * chunk * nb * nb * (7 + 2 * cb), bytes_accessed=8 * chunk * nb, transcendentals=0
        ),
    )(*operands)


def body(matrix, pivots, lower_inverse, upper_inverse):
    rb, nb, cb, _ = matrix.shape
    rows = rb * nb
    row_devices = lax.axis_size("prow")
    col_devices = lax.axis_size("pcol")
    chips = row_devices // 2
    line = col_devices // 2
    row = lax.axis_index("prow").astype(I32)
    column = lax.axis_index("pcol").astype(I32)
    core, chip = row % 2, row // 2
    place = column // 2
    meta = jnp.stack([row, core, column, jnp.int32(row_devices)])
    tiles = matrix.reshape(rows, cb, nb)

    sibling = [(r, r ^ 1) for r in range(row_devices)]
    neighbour = [(c, c ^ 1) for c in range(col_devices)]

    def chip_hop(h):
        return [(r, (r + 2 * h) % row_devices) for r in range(row_devices)]

    def line_hop(h):
        return [(c, (c + 2 * h) % col_devices) for c in range(col_devices)]

    def by_place(values):
        value = values[0]
        for h, entry in enumerate(values[1:], 1):
            value = jnp.where(place == h, entry, value)
        return value

    own = split_panels(tiles)
    chunk = nb // 2
    pieces = rows // chunk
    held, other = [], []
    for step in range(pieces + line - 1):
        mine = own[step * chunk : (step + 1) * chunk] if step < pieces else None
        if step:
            came = lax.ppermute(held[-1], "pcol", line_hop(1))
            mine = came if mine is None else jnp.where(place == 0, mine, came)
        held.append(mine)
        other.append(lax.ppermute(mine, "pcol", neighbour))

    fetch, join, arrive, goal, hops = make_indices(meta, pivots, nb, rows)
    hops = hops.reshape(2 * nb, 1)
    send, block0 = gather_sent(meta, fetch, tiles, nb)
    from_sibling = lax.ppermute(send, "prow", sibling)
    joined = join_rows(meta, fetch, join, tiles, from_sibling)
    mine = [joined] + [lax.ppermute(joined, "prow", chip_hop(h)) for h in range(1, chips)]
    block0_sibling = lax.ppermute(block0, "prow", sibling)
    theirs = [lax.ppermute(value, "prow", sibling) for value in mine]

    head = head_part(meta, hops, mine, theirs, nb // row_devices)
    from_line = [head]
    for h in range(1, line):
        from_line.append(lax.ppermute(head, "pcol", [(0, 2 * h), (1, 2 * h + 1)]))
    head = by_place(from_line)
    head = jnp.stack([head, lax.ppermute(head, "pcol", neighbour)])
    heads = [head] + [lax.ppermute(head, "prow", chip_hop(h)) for h in range(1, chips)]
    heads_sibling = [lax.ppermute(value, "prow", sibling) for value in heads]
    up0, up1, up0_panel, top = prep(
        meta, hops, lower_inverse, upper_inverse, mine, theirs, heads, heads_sibling
    )

    def from_first_chip(values):
        value = values[-1]
        for h in range(1, chips - 1):
            value = jnp.where(chip == h, values[h], value)
        return value

    moved_tiles = scatter_rows(
        meta, arrive, goal, from_first_chip(mine), from_first_chip(theirs), block0, block0_sibling, tiles
    )

    old = jnp.stack([
        jnp.concatenate([by_place([values[p + h] for h in range(line)]) for p in range(nb // chunk)])
        for values in (held, other)
    ])
    first_old = old
    for h in range(1, chips):
        came = lax.ppermute(first_old, "prow", [(0, 2 * h), (1, 2 * h + 1)])
        old = jnp.where(chip == h, came, old)
    old_sibling = lax.ppermute(old, "prow", sibling)

    goal = goal.reshape(2, nb)
    result = None
    for step in range(pieces + line - 1):
        result = update(
            step, pieces, meta, goal, held[step], other[step], old, old_sibling, upper_inverse,
            up0, up1, up0_panel, moved_tiles, top, result,
        )
    return result.reshape(matrix.shape)


def solution(mesh):
    placed = (P(None, "prow", None, "pcol"), P(), P(), P())
    return jax.shard_map(
        body, mesh=mesh, in_specs=placed, out_specs=P(None, "prow", None, "pcol"), check_vma=False
    )
```

```python
import functools

import jax
import jax.numpy as jnp
from jax import lax
from jax.experimental import pallas as pl
from jax.experimental.pallas import tpu as pltpu
from jax.sharding import PartitionSpec as P

BF16 = jnp.bfloat16
F32 = jnp.float32
I32 = jnp.int32
SMEM = pl.BlockSpec(memory_space=pltpu.SMEM)
VMEM = pl.BlockSpec(memory_space=pltpu.VMEM)
ANY = pl.BlockSpec(memory_space=pl.ANY)
DMA = pltpu.SemaphoreType.DMA


def dot(a, b):
    return jnp.dot(a, b, preferred_element_type=F32)


def flat(rows):
    return rows.reshape(rows.shape[0], rows.shape[1] * rows.shape[2])


def bf16(*shape):
    return jax.ShapeDtypeStruct(shape, BF16)


def call(kernel, operands, outs, after=(), scratch=(), aliases=None, flops=0, moved=0):
    count = len(operands)

    def ordered(*refs):
        kernel(*refs[:count], *refs[count + len(after) :])

    return pl.pallas_call(
        ordered,
        out_shape=tuple(shape for shape, _ in outs),
        in_specs=[spec for _, spec in operands] + [ANY] * len(after),
        out_specs=tuple(spec for _, spec in outs),
        scratch_shapes=list(scratch),
        input_output_aliases=aliases or {},
        compiler_params=pltpu.CompilerParams(vmem_limit_bytes=24 * 1024 * 1024),
        cost_estimate=pl.CostEstimate(flops=flops, bytes_accessed=moved, transcendentals=0),
    )(*[array for array, _ in operands], *after)


def fill_indices(nb, rows, meta, pivots, spread, fetch, join, arrive, goal, hops):
    row, row_devices = meta[0], meta[3]
    chip, chips = row // 2, row_devices // 2
    lanes = spread.shape[2]
    tiles = nb // lanes
    slot = lax.broadcasted_iota(I32, (1, nb), 1)
    pivot0, pivot1 = pivots[0:1, :], pivots[1:2, :]

    def lookup(keys, entry, value):
        parts = [keys[:, t * lanes : (t + 1) * lanes] for t in range(tiles)]

        def add(i, totals):
            begin = pl.multiple_of(i * 8, 8)
            at = begin + lax.broadcasted_iota(I32, (8, lanes), 0)
            here, give = entry(begin, at), value(begin, at)
            return tuple(t + jnp.where(p == here, give, 0) for t, p in zip(totals, parts))

        zero = jnp.zeros((8, lanes), I32)
        totals = lax.fori_loop(0, nb // 8, add, (zero,) * tiles, unroll=8)
        return jnp.concatenate([jnp.sum(t, axis=0, keepdims=True) for t in totals], axis=1)

    def pivot_of(panel):
        return lambda begin, at: spread[panel, pl.ds(begin, 8), :]

    place = lambda begin, at: at + 1
    in_pivots0 = lookup(pivot1, pivot_of(0), place)
    in_pivots1 = lookup(pivot0, pivot_of(1), place)
    top1_in_pivots0 = lookup(nb + slot, pivot_of(0), place)
    over_top1 = lookup(pivot0, lambda begin, at: nb + at, pivot_of(1))
    chained = lookup(nb + in_pivots1 - 1, pivot_of(0), place)

    source0 = pivot0
    source1 = jnp.where(in_pivots0 > 0, in_pivots0 - 1, pivot1)
    second0 = jnp.where(in_pivots1 > 0, jnp.where(chained > 0, chained - 1, nb + in_pivots1 - 1), slot)
    second1 = jnp.where(top1_in_pivots0 > 0, top1_in_pivots0 - 1, nb + slot)
    target0 = jnp.where(over_top1 > 0, over_top1, jnp.where(in_pivots1 > 0, nb + in_pivots1 - 1, pivot0))
    target1 = jnp.where(top1_in_pivots0 > 0, top1_in_pivots0 - 1, pivot1)

    def holder(index):
        return lax.rem(lax.div(index, nb), row_devices)

    def local(index):
        return lax.div(index, nb * row_devices) * nb + lax.rem(index, nb)

    def placed(index):
        mine = (holder(index) == row) & (index >= 2 * nb)
        return jnp.where(mine, local(index), rows)

    for k, (source, second, target) in enumerate(((source0, second0, target0), (source1, second1, target1))):
        from_chip = lax.div(holder(source), 2)
        wanted = jnp.where(from_chip == chip, source, second)
        at = (slice(k, k + 1), slice(None))
        fetch[at] = local(wanted)
        join[at] = jnp.where(holder(wanted) == row, slot, nb)
        arrive[at] = placed(source)
        goal[at] = placed(target)
        hops[at] = lax.rem(chip + chips - from_chip, chips)


def copy_rows(count, target, target_at, origin, origin_at):
    def copy(i, carry):
        target[target_at(i)] = origin[origin_at(i)]
        return carry

    lax.fori_loop(0, count, copy, 0, unroll=16)


def split_kernel(tiles, *pieces):
    chunk, nb = pieces[0].shape
    for i, piece in enumerate(pieces):
        piece[...] = flat(tiles[i * chunk : (i + 1) * chunk])[:, :nb]


def gather_kernel(
    meta, pivots, spread, tiles, send, keep, block0, join, arrive, goal, hops,
    loaded, fetch, fetch_table, load_sem, table_sem,
):
    nb = send.shape[0]
    core = meta[1]
    load = pltpu.make_async_copy(tiles, loaded, load_sem)
    load.start()
    fill_indices(nb, tiles.shape[0], meta, pivots, spread, fetch, join, arrive, goal, hops)
    table = pltpu.make_async_copy(fetch, fetch_table, table_sem)
    table.start()
    table.wait()
    load.wait()
    copy_rows(nb, send, lambda i: i, loaded, lambda i: fetch_table[1 - core, i])
    copy_rows(nb, keep, lambda i: i, loaded, lambda i: fetch_table[core, i])
    block0[...] = loaded[0:nb]


def join_kernel(meta, join, keep, came, joined, work):
    count = came.shape[0]
    core = meta[1]
    work[0:count] = came[...]
    copy_rows(count, work, lambda i: join[core, i], keep, lambda i: i)
    joined[...] = work[0:count]


def scatter_kernel(meta, arrive, goal, came, came_sibling, old, old_sibling, tiles, out, work, sem):
    core, chip = meta[1], meta[0] // 2
    count, rows = old.shape[0], tiles.shape[0]
    load = pltpu.make_async_copy(tiles, work.at[pl.ds(0, rows)], sem)
    load.start()
    load.wait()

    def scatter(table, values, k):
        copy_rows(count, work, lambda i: table[k, i], values, lambda i: i)

    @pl.when(chip == 0)
    def _():
        scatter(goal, old, core)
        scatter(goal, old_sibling, 1 - core)

    @pl.when(chip != 0)
    def _():
        scatter(arrive, came, core)
        scatter(arrive, came_sibling, 1 - core)

    store = pltpu.make_async_copy(work.at[pl.ds(0, rows)], out, sem)
    store.start()
    store.wait()


def relay_kernel(meta, came, own, held):
    place = lax.div(meta[2], 2)

    @pl.when(place == 0)
    def _():
        held[...] = own[...]

    @pl.when(place != 0)
    def _():
        held[...] = came[...]


def pass_kernel(came, held):
    held[...] = came[...]


def old_kernel(line, meta, *refs):
    held, other, old = refs[: len(refs) // 2], refs[len(refs) // 2 : -1], refs[-1]
    place = lax.div(meta[2], 2)
    chunk = held[0].shape[0]
    for h in range(line):

        @pl.when(place == h)
        def _(h=h):
            for p in range(old.shape[1] // chunk):
                old[0, p * chunk : (p + 1) * chunk] = held[p + h][...]
                old[1, p * chunk : (p + 1) * chunk] = other[p + h][...]


def by_chip_kernel(meta, *refs):
    out = refs[-1]
    for h, choice in enumerate(refs[:-1]):

        @pl.when(meta[0] // 2 == h)
        def _(choice=choice):
            out[...] = choice[...]


def by_place_kernel(meta, *refs):
    out = refs[-1]
    for h, choice in enumerate(refs[:-1]):

        @pl.when(lax.div(meta[2], 2) == h)
        def _(choice=choice):
            out[...] = choice[...]


def by_side_kernel(meta, mine, swapped, out):
    needed = 1 - lax.rem(meta[2], 2)

    @pl.when(meta[1] == needed)
    def _():
        out[...] = mine[...]

    @pl.when(meta[1] != needed)
    def _():
        out[...] = swapped[...]


def choose(hop, choices):
    value = flat(choices[0]).astype(F32)
    for h, other in enumerate(choices[1:], 1):
        value = jnp.where(hop == h, flat(other).astype(F32), value)
    return value.astype(BF16)


def fresh_kernel(chips, meta, hops, *refs):
    choices, (fresh, head, brought) = refs[:chips], refs[chips:]
    nb, part = fresh.shape[0], head.shape[0]
    core, chip = meta[1], meta[0] // 2
    fresh[...] = choose(hops[pl.ds(core * nb, nb)], [c[...] for c in choices])
    head[...] = fresh[pl.ds(pl.multiple_of(chip * part, part), part), :nb]
    if chips == 1:
        brought[...] = choices[0][...]
    for h in range(1, chips):

        @pl.when((chip == h) | ((chip == 0) & (h == 1)))
        def _(h=h):
            brought[...] = choices[h][...]


def raw(columns, nb):
    joined = jnp.concatenate(columns, axis=1)
    return joined.reshape(joined.shape[0], len(columns), nb)


def prep0_kernel(meta, lower, fresh, fresh_sibling, up0, top, work):
    core, column = meta[1], meta[2]
    nb = fresh.shape[0]

    @pl.when(core == 0)
    def _():
        work[...] = fresh[...]

    @pl.when(core != 0)
    def _():
        work[...] = fresh_sibling[...]

    shown = []
    for j in range(work.shape[1] // nb):
        cols = slice(j * nb, (j + 1) * nb)
        product = dot(lower[0], work[:, cols])
        show = product
        if j == 0:
            show = jnp.where(column == 0, work[:, cols].astype(F32), product)
            product = jnp.where(column == 0, 0.0, product)
        up0[:, cols] = product.astype(BF16)
        shown.append(show.astype(BF16))
    top[...] = raw(shown, nb)


def prep1_kernel(chips, meta, lower, upper, fresh, fresh_sibling, up0, *refs):
    heads, heads_sibling = refs[:chips], refs[chips : 2 * chips]
    up1, up0_panel, top, work, head = refs[2 * chips :]
    core, column, chip = meta[1], meta[2], meta[0] // 2
    nb, part = fresh.shape[0], heads[0].shape[0]
    for who, pieces in ((core, heads), (1 - core, heads_sibling)):
        for h, piece in enumerate(pieces):
            at = pl.multiple_of(lax.rem(chip + chips - h, chips) * part, part)
            head[who, pl.ds(at, part)] = piece[...]

    @pl.when(core == 1)
    def _():
        work[...] = fresh[...]

    @pl.when(core != 1)
    def _():
        work[...] = fresh_sibling[...]

    up0_panel[...] = dot(lower[0], head[0]).astype(BF16)
    factor = dot(head[1], upper[0]).astype(BF16)
    in_panel, next_panel = column == 0, column == 1
    shown = []
    for j in range(work.shape[1] // nb):
        cols = slice(j * nb, (j + 1) * nb)
        updated = (work[:, cols].astype(F32) - dot(factor, up0[:, cols])).astype(BF16)
        last = dot(lower[1], updated)
        show = last
        if j == 0:
            show = jnp.where(next_panel, updated.astype(F32), show)
            show = jnp.where(in_panel, factor.astype(F32), show)
            last = jnp.where(in_panel | next_panel, 0.0, last)
        up1[:, cols] = last.astype(BF16)
        shown.append(show.astype(BF16))
    top[...] = raw(shown, nb)


def update_kernel(
    first, count, line, meta, goal, old, old_sibling, upper, up0, up1, up0_panel, tiles, top0, top1, *rest
):
    spans = count + line - 1
    held, other = rest[:spans], rest[spans : 2 * spans]
    out, token, panels, block, result, panel_sem, block_sem, out_sem = rest[-8:]
    row, core, column, row_devices = meta[0], meta[1], meta[2], meta[3]
    side, place = lax.rem(column, 2), lax.div(column, 2)
    _, chunk, cb, nb = block.shape
    per_block = nb // chunk
    rows_of = lambda i: pl.ds((first + i) * chunk, chunk)

    def block_copy(i):
        return pltpu.make_async_copy(tiles.at[rows_of(i)], block.at[i], block_sem.at[i])

    def panel_copy(i, h, which):
        source = (held, other)[which][i + h]
        return pltpu.make_async_copy(source, panels.at[i, lax.rem(side + which, 2)], panel_sem.at[i, which])

    for i in range(count):
        block_copy(i).start()
        for h in range(line):

            @pl.when(place == h)
            def _(h=h, i=i):
                panel_copy(i, h, 0).start()
                panel_copy(i, h, 1).start()

    def from_factors(i):
        here = (first + i) * chunk + lax.broadcasted_iota(I32, (chunk, nb), 0)
        pick = jnp.where(here == goal[pl.ds(core, 1), :], 1.0, 0.0)
        pick_sibling = jnp.where(here == goal[pl.ds(1 - core, 1), :], 1.0, 0.0)
        moved = jnp.sum(pick + pick_sibling, axis=1, keepdims=True) > 0.5
        pick, pick_sibling = pick.astype(BF16), pick_sibling.astype(BF16)
        whole = []
        for k in range(2):
            which = lax.rem(k + side, 2)
            brought = dot(pick, old[which]) + dot(pick_sibling, old_sibling[which])
            whole.append(jnp.where(moved, brought, panels[i, k].astype(F32)))
        factor0 = dot(whole[0].astype(BF16), upper[0]).astype(BF16)
        below = (whole[1] - dot(factor0, up0_panel[...])).astype(BF16)
        factor1 = dot(below, upper[1]).astype(BF16)
        values = flat(block[i])
        columns = []
        for j in range(cb):
            cols = slice(j * nb, (j + 1) * nb)
            value = values[:, cols].astype(F32) - dot(factor0, up0[:, cols])
            value = value.astype(BF16).astype(F32) - dot(factor1, up1[:, cols])
            if j == 0:
                value = jnp.where(column == 0, factor0.astype(F32), value)
                value = jnp.where(column == 1, factor1.astype(F32), value)
            columns.append(value.astype(BF16))
        result[i] = raw(columns, nb)

    def out_copy(i):
        return pltpu.make_async_copy(result.at[i], out.at[rows_of(i)], out_sem.at[i])

    for i in range(count):
        block_copy(i).wait()
        panel_copy(i, 0, 0).wait()
        panel_copy(i, 0, 1).wait()
    for i in range(count):
        panel_row = (first + i) // per_block * row_devices + row
        if first + i < per_block:
            inside = pl.ds((first + i) * chunk, chunk)

            @pl.when(panel_row == 0)
            def _(i=i, inside=inside):
                copy = pltpu.make_async_copy(top0.at[inside], result.at[i], block_sem.at[i])
                copy.start()
                copy.wait()

            @pl.when(panel_row == 1)
            def _(i=i, inside=inside):
                copy = pltpu.make_async_copy(top1.at[inside], result.at[i], block_sem.at[i])
                copy.start()
                copy.wait()

            pl.when(panel_row >= 2)(functools.partial(from_factors, i))
        else:
            from_factors(i)
        out_copy(i).start()
    token[...] = jnp.zeros(token.shape, F32)
    for i in range(count):
        out_copy(i).wait()


def body(matrix, pivots, lower, upper):
    rb, nb, cb, _ = matrix.shape
    rows = rb * nb
    chunk = nb // 2
    pieces = rows // chunk
    row_devices = lax.axis_size("prow")
    col_devices = lax.axis_size("pcol")
    chips, line = row_devices // 2, col_devices // 2
    row = lax.axis_index("prow").astype(I32)
    column = lax.axis_index("pcol").astype(I32)
    meta = jnp.stack([row, row % 2, column, jnp.int32(row_devices)])
    tiles = matrix.reshape(rows, cb, nb)

    def to_sibling(value):
        return lax.ppermute(value, "prow", [(r, r ^ 1) for r in range(row_devices)])

    def to_neighbour(value):
        return lax.ppermute(value, "pcol", [(c, c ^ 1) for c in range(col_devices)])

    def to_chip(value, h):
        return lax.ppermute(value, "prow", [(r, (r + 2 * h) % row_devices) for r in range(row_devices)])

    def to_next(value):
        return lax.ppermute(value, "pcol", [(c, (c + 2) % col_devices) for c in range(col_devices)])

    order = []

    def run(kernel, operands, outs, also=(), **kwargs):
        after = tuple(order[-1:]) + tuple(also)
        results = call(kernel, operands, outs, after=after, **kwargs)
        order.append(results[-1])
        return results

    state = {}
    own = run(split_kernel, [(tiles, VMEM)], [(bf16(chunk, nb), VMEM)] * pieces)
    held, other, came = [], [], None

    def advance(step):
        nonlocal came
        if step == 0:
            piece = own[0]
        else:
            also = (other[step - 2],) if step >= 2 else ()
            out = [(bf16(chunk, nb), VMEM)]
            if step < pieces:
                operands = [(meta, SMEM), (came, VMEM), (own[step], VMEM)]
                (piece,) = run(relay_kernel, operands, out, also)
            else:
                (piece,) = run(pass_kernel, [(came, VMEM)], out, also)
        held.append(piece)
        if step < pieces + line - 2:
            came = to_next(piece)
        other.append(to_neighbour(piece))

    def gather():
        lanes = min(nb, 128)
        spread = jnp.broadcast_to(pivots[:, :, None], (2, nb, lanes))
        table = jax.ShapeDtypeStruct((2, nb), I32)
        send, keep, block0, join, arrive, goal, hops = run(
            gather_kernel,
            [(meta, SMEM), (pivots, VMEM), (spread, VMEM), (tiles, ANY)],
            [(bf16(nb, cb, nb), VMEM)] * 3 + [(table, VMEM)] * 4,
            scratch=[
                pltpu.VMEM(tiles.shape, BF16), pltpu.VMEM((2, nb), I32), pltpu.SMEM((2, nb), I32), DMA, DMA,
            ],
        )
        state.update(keep=keep, block0=block0, join=join, arrive=arrive, goal=goal)
        state["hops"] = hops.reshape(2 * nb, 1)
        state["sent"] = to_sibling(send)
        state["block0_sibling"] = to_sibling(block0)

    def join():
        (joined,) = run(
            join_kernel,
            [(meta, SMEM), (state["join"], SMEM), (state["keep"], VMEM), (state["sent"], VMEM)],
            [(bf16(nb, cb, nb), VMEM)],
            scratch=[pltpu.VMEM((nb + 8, cb, nb), BF16)],
        )
        state["choices"] = [joined] + [to_chip(joined, h) for h in range(1, chips)]

    flat_index = lambda r, c: r * col_devices + c
    both = ("prow", "pcol")
    part = nb // chips

    def fresh():
        new, head, brought = run(
            functools.partial(fresh_kernel, chips),
            [(meta, SMEM), (state["hops"], VMEM)] + [(c, VMEM) for c in state["choices"]],
            [(bf16(nb, cb * nb), VMEM), (bf16(part, nb), VMEM), (bf16(nb, cb, nb), VMEM)],
        )
        state["head"] = [head]
        for h in range(1, line):
            pairs = [
                (flat_index(r, c), flat_index(r, c + 2 * h))
                for c in range(2) for r in range(row_devices) if r % 2 != c
            ]
            state["head"].append(lax.ppermute(head, both, pairs))
        state["brought"] = (brought, to_sibling(brought))
        state["fresh"] = (new, to_sibling(new))

    def old():
        spans = range(nb // chunk + line - 1)
        (mine,) = run(
            functools.partial(old_kernel, line),
            [(meta, SMEM)] + [(held[i], VMEM) for i in spans] + [(other[i], VMEM) for i in spans],
            [(bf16(2, nb, nb), VMEM)],
        )
        state["old"] = [mine] + [to_chip(mine, h) for h in range(1, chips)]

    def old_here():
        (mine,) = run(
            by_chip_kernel, [(meta, SMEM)] + [(v, VMEM) for v in state["old"]], [(bf16(2, nb, nb), VMEM)]
        )
        state["old"] = (mine, to_sibling(mine))

    def head_here():
        (mine,) = run(
            by_place_kernel, [(meta, SMEM)] + [(v, VMEM) for v in state["head"]], [(bf16(part, nb), VMEM)]
        )
        pairs = [
            (flat_index(r, c), flat_index(r, c ^ 1))
            for c in range(col_devices) for r in range(row_devices) if r % 2 != c % 2
        ]
        state["head"] = (mine, lax.ppermute(mine, both, pairs))

    def head_around():
        (mine,) = run(
            by_side_kernel, [(meta, SMEM)] + [(v, VMEM) for v in state["head"]], [(bf16(part, nb), VMEM)]
        )
        heads = [mine] + [to_chip(mine, h) for h in range(1, chips)]
        state["heads"] = heads + [to_sibling(v) for v in heads]

    def scatter():
        sources = state["brought"] + (state["block0"], state["block0_sibling"])
        (state["moved"],) = run(
            scatter_kernel,
            [(meta, SMEM), (state["arrive"], SMEM), (state["goal"], SMEM)]
            + [(v, VMEM) for v in sources] + [(tiles, ANY)],
            [(bf16(rows, cb, nb), ANY)],
            scratch=[pltpu.VMEM((rows + 8, cb, nb), BF16), DMA],
        )

    def prep0():
        state["up0"], state["top0"] = run(
            prep0_kernel,
            [(meta, SMEM), (lower, VMEM)] + [(v, VMEM) for v in state["fresh"]],
            [(bf16(nb, cb * nb), VMEM), (bf16(nb, cb, nb), VMEM)],
            scratch=[pltpu.VMEM((nb, cb * nb), BF16)],
        )

    def prep1():
        state["up1"], state["up0_panel"], state["top1"] = run(
            functools.partial(prep1_kernel, chips),
            [(meta, SMEM), (lower, VMEM), (upper, VMEM)] + [(v, VMEM) for v in state["fresh"]]
            + [(state["up0"], VMEM)] + [(v, VMEM) for v in state["heads"]],
            [(bf16(nb, cb * nb), VMEM), (bf16(nb, nb), VMEM), (bf16(nb, cb, nb), VMEM)],
            scratch=[pltpu.VMEM((nb, cb * nb), BF16), pltpu.VMEM((2, nb, nb), BF16)],
        )

    def update(first, count):
        spans = range(first, first + count + line - 1)
        operands = [(meta, SMEM), (state["goal"], VMEM)] + [(v, VMEM) for v in state["old"]] + [(upper, VMEM)]
        operands += [(state[name], VMEM) for name in ("up0", "up1", "up0_panel")]
        operands += [(state[name], ANY) for name in ("moved", "top0", "top1")]
        operands += [(held[i], ANY) for i in spans] + [(other[i], ANY) for i in spans]
        aliases = {}
        if "result" in state:
            aliases = {len(operands): 0}
            operands.append((state["result"], ANY))
        state["result"], _ = run(
            functools.partial(update_kernel, first, count, line),
            operands,
            [(bf16(rows, cb, nb), ANY), (jax.ShapeDtypeStruct((8, 128), F32), VMEM)],
            scratch=[
                pltpu.VMEM((count, 2, chunk, nb), BF16),
                pltpu.VMEM((count, chunk, cb, nb), BF16),
                pltpu.VMEM((count, chunk, cb, nb), BF16),
                DMA((count, 2)), DMA((count,)), DMA((count,)),
            ],
            aliases=aliases,
            flops=2 * count * chunk * nb * nb * (7 + 2 * cb),
        )

    plan = [(0, gather), (1, join), (5, fresh), (max(5, line), old), (6, head_here), (6, scatter), (7, head_around)]
    plan += [(7, prep0), (8, old_here), (9, prep1)]
    group = 2
    for first in range(0, pieces, group):
        count = min(group, pieces - first)
        plan.append((max(9 + first // group, first + count + line - 2), functools.partial(update, first, count)))
    last = pieces + line - 2
    for step in range(last + 1):
        advance(step)
        while plan and (plan[0][0] <= step or step == last):
            plan.pop(0)[1]()
    return state["result"].reshape(matrix.shape)


def solution(mesh):
    placed = (P(None, "prow", None, "pcol"), P(), P(), P())
    return jax.shard_map(
        body, mesh=mesh, in_specs=placed, out_specs=P(None, "prow", None, "pcol"), check_vma=False
    )
```

```python
import functools

import jax
import jax.numpy as jnp
from jax import lax
from jax.experimental import pallas as pl
from jax.experimental.pallas import tpu as pltpu
from jax.sharding import PartitionSpec as P

BF16 = jnp.bfloat16
F32 = jnp.float32
I32 = jnp.int32
SMEM = pl.BlockSpec(memory_space=pltpu.SMEM)
VMEM = pl.BlockSpec(memory_space=pltpu.VMEM)
ANY = pl.BlockSpec(memory_space=pl.ANY)
DMA = pltpu.SemaphoreType.DMA


def dot(a, b):
    return jnp.dot(a, b, preferred_element_type=F32)


def flat(rows):
    return rows.reshape(rows.shape[0], rows.shape[1] * rows.shape[2])


def bf16(*shape):
    return jax.ShapeDtypeStruct(shape, BF16)


def call(kernel, operands, outs, after=(), scratch=(), aliases=None, us=1.0, mib=8):
    count = len(operands)

    def ordered(*refs):
        kernel(*refs[:count], *refs[count + len(after) :])

    return pl.pallas_call(
        ordered,
        out_shape=tuple(shape for shape, _ in outs),
        in_specs=[spec for _, spec in operands] + [ANY] * len(after),
        out_specs=tuple(spec for _, spec in outs),
        scratch_shapes=list(scratch),
        input_output_aliases=aliases or {},
        compiler_params=pltpu.CompilerParams(vmem_limit_bytes=mib * 1024 * 1024),
        cost_estimate=pl.CostEstimate(flops=int(us * 1.1e9), bytes_accessed=0, transcendentals=0),
    )(*[array for array, _ in operands], *after)


def fill_indices(nb, rows, meta, pivots, spread, fetch, join, arrive, goal, hops):
    row, row_devices = meta[0], meta[3]
    chip, chips = row // 2, row_devices // 2
    lanes = spread.shape[2]
    tiles = nb // lanes
    slot = lax.broadcasted_iota(I32, (1, nb), 1)
    pivot0, pivot1 = pivots[0:1, :], pivots[1:2, :]

    def lookup(keys, entry, value):
        parts = [keys[:, t * lanes : (t + 1) * lanes] for t in range(tiles)]

        def add(i, totals):
            begin = pl.multiple_of(i * 8, 8)
            at = begin + lax.broadcasted_iota(I32, (8, lanes), 0)
            here, give = entry(begin, at), value(begin, at)
            return tuple(t + jnp.where(p == here, give, 0) for t, p in zip(totals, parts))

        zero = jnp.zeros((8, lanes), I32)
        totals = lax.fori_loop(0, nb // 8, add, (zero,) * tiles, unroll=8)
        return jnp.concatenate([jnp.sum(t, axis=0, keepdims=True) for t in totals], axis=1)

    def pivot_of(panel):
        return lambda begin, at: spread[panel, pl.ds(begin, 8), :]

    place = lambda begin, at: at + 1
    in_pivots0 = lookup(pivot1, pivot_of(0), place)
    in_pivots1 = lookup(pivot0, pivot_of(1), place)
    top1_in_pivots0 = lookup(nb + slot, pivot_of(0), place)
    over_top1 = lookup(pivot0, lambda begin, at: nb + at, pivot_of(1))
    chained = lookup(nb + in_pivots1 - 1, pivot_of(0), place)

    source0 = pivot0
    source1 = jnp.where(in_pivots0 > 0, in_pivots0 - 1, pivot1)
    second0 = jnp.where(in_pivots1 > 0, jnp.where(chained > 0, chained - 1, nb + in_pivots1 - 1), slot)
    second1 = jnp.where(top1_in_pivots0 > 0, top1_in_pivots0 - 1, nb + slot)
    target0 = jnp.where(over_top1 > 0, over_top1, jnp.where(in_pivots1 > 0, nb + in_pivots1 - 1, pivot0))
    target1 = jnp.where(top1_in_pivots0 > 0, top1_in_pivots0 - 1, pivot1)

    def holder(index):
        return lax.rem(lax.div(index, nb), row_devices)

    def local(index):
        return lax.div(index, nb * row_devices) * nb + lax.rem(index, nb)

    def placed(index):
        mine = (holder(index) == row) & (index >= 2 * nb)
        return jnp.where(mine, local(index), rows)

    for k, (source, second, target) in enumerate(((source0, second0, target0), (source1, second1, target1))):
        from_chip = lax.div(holder(source), 2)
        wanted = jnp.where(from_chip == chip, source, second)
        at = (slice(k, k + 1), slice(None))
        fetch[at] = local(wanted)
        join[at] = jnp.where(holder(wanted) == row, slot, nb)
        arrive[at] = placed(source)
        goal[at] = placed(target)
        hops[at] = lax.rem(chip + chips - from_chip, chips)


def copy_rows(count, target, target_at, origin, origin_at):
    def copy(i, carry):
        target[target_at(i)] = origin[origin_at(i)]
        return carry

    lax.fori_loop(0, count, copy, 0, unroll=16)


def first_kernel(tiles, piece, work, sem):
    load = pltpu.make_async_copy(tiles.at[pl.ds(0, piece.shape[0])], work, sem)
    load.start()
    load.wait()
    piece[...] = flat(work[...])[:, : piece.shape[1]]


def gather_kernel(meta, pivots, spread, tiles, *refs):
    *pieces, loaded, send, keep, block0, join, arrive, goal, hops, fetch, fetch_table, load_sem, table_sem = refs
    chunk, nb = pieces[0].shape
    rows = tiles.shape[0]
    core = meta[1]
    load = pltpu.make_async_copy(tiles, loaded.at[pl.ds(0, rows)], load_sem)
    load.start()
    fill_indices(nb, rows, meta, pivots, spread, fetch, join, arrive, goal, hops)
    table = pltpu.make_async_copy(fetch, fetch_table, table_sem)
    table.start()
    table.wait()
    load.wait()
    for i, piece in enumerate(pieces, 1):
        piece[...] = flat(loaded[i * chunk : (i + 1) * chunk])[:, :nb]
    copy_rows(nb, send, lambda i: i, loaded, lambda i: fetch_table[1 - core, i])
    copy_rows(nb, keep, lambda i: i, loaded, lambda i: fetch_table[core, i])
    block0[...] = loaded[0:nb]


def join_kernel(meta, join, keep, came, joined, work):
    count = came.shape[0]
    core = meta[1]
    work[0:count] = came[...]
    copy_rows(count, work, lambda i: join[core, i], keep, lambda i: i)
    joined[...] = work[0:count]


def scatter_kernel(meta, arrive, goal, came, came_sibling, old, old_sibling, tiles, out):
    core, chip = meta[1], meta[0] // 2
    count = old.shape[0]
    out[...] = tiles[...]

    def scatter(table, values, k):
        copy_rows(count, out, lambda i: table[k, i], values, lambda i: i)

    @pl.when(chip == 0)
    def _():
        scatter(goal, old, core)
        scatter(goal, old_sibling, 1 - core)

    @pl.when(chip != 0)
    def _():
        scatter(arrive, came, core)
        scatter(arrive, came_sibling, 1 - core)


def relay_kernel(meta, came, own, held):
    place = lax.div(meta[2], 2)

    @pl.when(place == 0)
    def _():
        held[...] = own[...]

    @pl.when(place != 0)
    def _():
        held[...] = came[...]


def pass_kernel(came, held):
    held[...] = came[...]


def old_kernel(*refs):
    *pieces, old = refs
    chunk = pieces[0].shape[0]
    half = len(pieces) // 2
    for i, piece in enumerate(pieces):
        at = i % half * chunk
        old[i // half, at : at + chunk] = piece[...]


def by_chip_kernel(meta, *refs):
    out = refs[-1]
    for h, choice in enumerate(refs[:-1]):

        @pl.when(meta[0] // 2 == h)
        def _(choice=choice):
            out[...] = choice[...]


def by_place_kernel(meta, *refs):
    out = refs[-1]
    for h, choice in enumerate(refs[:-1]):

        @pl.when(lax.div(meta[2], 2) == h)
        def _(choice=choice):
            out[...] = choice[...]


def head_kernel(meta, fresh, fresh_sibling, head):
    needed = 1 - lax.rem(meta[2], 2)
    half, nb = head.shape
    at = pl.ds(pl.multiple_of(meta[1] * half, half), half)

    @pl.when(meta[1] == needed)
    def _():
        head[...] = fresh[at, :nb]

    @pl.when(meta[1] != needed)
    def _():
        head[...] = fresh_sibling[at, :nb]


def choose(hop, choices):
    value = flat(choices[0]).astype(F32)
    for h, other in enumerate(choices[1:], 1):
        value = jnp.where(hop == h, flat(other).astype(F32), value)
    return value.astype(BF16)


def fresh_kernel(chips, meta, hops, *refs):
    choices, (fresh, brought) = refs[:chips], refs[chips:]
    nb = fresh.shape[0]
    core, chip = meta[1], meta[0] // 2
    hop = jnp.broadcast_to(hops[pl.ds(core, 1), :], (8, nb)).T[:, 0:1]
    fresh[...] = choose(hop, [c[...] for c in choices])
    if chips == 1:
        brought[...] = choices[0][...]
    for h in range(1, chips):

        @pl.when((chip == h) | ((chip == 0) & (h == 1)))
        def _(h=h):
            brought[...] = choices[h][...]


def raw(columns, nb):
    joined = jnp.concatenate(columns, axis=1)
    return joined.reshape(joined.shape[0], len(columns), nb)


def prep0_kernel(meta, lower, fresh, fresh_sibling, up0, top, work):
    core, column = meta[1], meta[2]
    nb = fresh.shape[0]

    @pl.when(core == 0)
    def _():
        work[...] = fresh[...]

    @pl.when(core != 0)
    def _():
        work[...] = fresh_sibling[...]

    shown = []
    for j in range(work.shape[1] // nb):
        cols = slice(j * nb, (j + 1) * nb)
        product = dot(lower[0], work[:, cols])
        show = product
        if j == 0:
            show = jnp.where(column == 0, work[:, cols].astype(F32), product)
            product = jnp.where(column == 0, 0.0, product)
        up0[:, cols] = product.astype(BF16)
        shown.append(show.astype(BF16))
    top[...] = raw(shown, nb)


def prep1_kernel(meta, lower, upper, fresh, fresh_sibling, up0, *refs):
    mine, mine_sibling, other, other_sibling, up1, up0_panel, top, work, head = refs
    core, column = meta[1], meta[2]
    side = lax.rem(column, 2)
    nb, half = fresh.shape[0], mine.shape[0]
    for which, who, piece in (
        (1 - side, core, mine), (1 - side, 1 - core, mine_sibling), (side, core, other), (side, 1 - core, other_sibling)
    ):
        head[which, pl.ds(pl.multiple_of(who * half, half), half)] = piece[...]

    @pl.when(core == 1)
    def _():
        work[...] = fresh[...]

    @pl.when(core != 1)
    def _():
        work[...] = fresh_sibling[...]

    up0_panel[...] = dot(lower[0], head[0]).astype(BF16)
    factor = dot(head[1], upper[0]).astype(BF16)
    in_panel, next_panel = column == 0, column == 1
    shown = []
    for j in range(work.shape[1] // nb):
        cols = slice(j * nb, (j + 1) * nb)
        updated = (work[:, cols].astype(F32) - dot(factor, up0[:, cols])).astype(BF16)
        last = dot(lower[1], updated)
        show = last
        if j == 0:
            show = jnp.where(next_panel, updated.astype(F32), show)
            show = jnp.where(in_panel, factor.astype(F32), show)
            last = jnp.where(in_panel | next_panel, 0.0, last)
        up1[:, cols] = last.astype(BF16)
        shown.append(show.astype(BF16))
    top[...] = raw(shown, nb)


def update_kernel(first, count, meta, goal, old, old_sibling, upper, up0, up1, up0_panel, tiles, top0, top1, *rest):
    held, other = rest[:count], rest[count : 2 * count]
    out, token, block, result, block_sem, out_sem = rest[-6:]
    row, core, column, row_devices = meta[0], meta[1], meta[2], meta[3]
    side = lax.rem(column, 2)
    _, chunk, cb, nb = block.shape
    per_block = nb // chunk
    rows_of = lambda i: pl.ds((first + i) * chunk, chunk)

    def block_copy(i):
        return pltpu.make_async_copy(tiles.at[rows_of(i)], block.at[i], block_sem.at[i])

    for i in range(count):
        block_copy(i).start()

    def from_factors(i):
        here = (first + i) * chunk + lax.broadcasted_iota(I32, (chunk, nb), 0)
        pick = jnp.where(here == goal[pl.ds(core, 1), :], 1.0, 0.0)
        pick_sibling = jnp.where(here == goal[pl.ds(1 - core, 1), :], 1.0, 0.0)
        moved = jnp.sum(pick + pick_sibling, axis=1, keepdims=True) > 0.5
        pick, pick_sibling = pick.astype(BF16), pick_sibling.astype(BF16)
        even = side == 0
        sent = (jnp.where(even, held[i][...], other[i][...]), jnp.where(even, other[i][...], held[i][...]))
        whole = []
        for k in range(2):
            which = lax.rem(k + side, 2)
            brought = dot(pick, old[which]) + dot(pick_sibling, old_sibling[which])
            whole.append(jnp.where(moved, brought, sent[k].astype(F32)))
        factor0 = dot(whole[0].astype(BF16), upper[0]).astype(BF16)
        below = (whole[1] - dot(factor0, up0_panel[...])).astype(BF16)
        factor1 = dot(below, upper[1]).astype(BF16)
        block_copy(i).wait()
        values = flat(block[i])
        columns = []
        for j in range(cb):
            cols = slice(j * nb, (j + 1) * nb)
            value = values[:, cols].astype(F32) - dot(factor0, up0[:, cols])
            value = value.astype(BF16).astype(F32) - dot(factor1, up1[:, cols])
            columns.append(value.astype(BF16))
        result[i] = raw(columns, nb)

        def panel_column(factor):
            result[i] = raw([factor] + columns[1:], nb)

        pl.when(column == 0)(lambda: panel_column(factor0))
        pl.when(column == 1)(lambda: panel_column(factor1))

    def out_copy(i):
        return pltpu.make_async_copy(result.at[i], out.at[rows_of(i)], out_sem.at[i])

    for i in range(count):
        panel_row = (first + i) // per_block * row_devices + row
        if first + i < per_block:
            inside = pl.ds((first + i) * chunk, chunk)

            def from_top(top, i=i, inside=inside):
                block_copy(i).wait()
                copy = pltpu.make_async_copy(top.at[inside], result.at[i], block_sem.at[i])
                copy.start()
                copy.wait()

            pl.when(panel_row == 0)(lambda: from_top(top0))
            pl.when(panel_row == 1)(lambda: from_top(top1))
            pl.when(panel_row >= 2)(functools.partial(from_factors, i))
        else:
            from_factors(i)
        out_copy(i).start()
    token[...] = jnp.zeros(token.shape, F32)
    for i in range(count):
        out_copy(i).wait()


def body(matrix, pivots, lower, upper):
    rb, nb, cb, _ = matrix.shape
    rows = rb * nb
    chunk = nb // 2
    pieces = rows // chunk
    row_devices = lax.axis_size("prow")
    col_devices = lax.axis_size("pcol")
    chips, line = row_devices // 2, col_devices // 2
    row = lax.axis_index("prow").astype(I32)
    column = lax.axis_index("pcol").astype(I32)
    meta = jnp.stack([row, row % 2, column, jnp.int32(row_devices)])
    tiles = matrix.reshape(rows, cb, nb)

    def to_sibling(value):
        return lax.ppermute(value, "prow", [(r, r ^ 1) for r in range(row_devices)])

    def to_neighbour(value):
        return lax.ppermute(value, "pcol", [(c, c ^ 1) for c in range(col_devices)])

    def to_chip(value, h):
        return lax.ppermute(value, "prow", [(r, (r + 2 * h) % row_devices) for r in range(row_devices)])

    def along(value, begin):
        partner = lambda p: p + 1 if (p - begin) % 2 == 0 else p - 1
        pairs = [(p, partner(p)) for p in range(line) if 0 <= partner(p) < line]
        return lax.ppermute(value, "pcol", [(2 * p + y, 2 * q + y) for p, q in pairs for y in range(2)])

    order = []

    def run(kernel, operands, outs, also=(), **kwargs):
        after = tuple(order[-1:]) + tuple(also)
        results = call(kernel, operands, outs, after=after, **kwargs)
        order.append(results[-1])
        return results

    lag = 3
    even_turns = pieces + lag * ((line - 2) // 2)
    odd_turns = pieces + lag * ((line - 3) // 2) if line > 2 else 0
    last_turn = max(even_turns, odd_turns)
    behind = last_turn - pieces
    piece_out = [(bf16(chunk, nb), VMEM)]
    own, even_came, odd_came, held, other = [], [], [], [], []
    state = {}

    def turn(k):
        if k == 0:
            own.extend(run(
                first_kernel, [(tiles, ANY)], piece_out, scratch=[pltpu.VMEM((chunk, cb, nb), BF16), DMA]
            ))
        if k < even_turns:
            also = (even_came[k - 2],) if k >= 2 else ()
            if k >= pieces:
                (value,) = run(pass_kernel, [(odd_came[k - lag], VMEM)], piece_out, also, us=0.6)
            elif k >= lag and odd_turns:
                operands = [(meta, SMEM), (odd_came[k - lag], VMEM), (own[k], VMEM)]
                (value,) = run(relay_kernel, operands, piece_out, also, us=0.6)
            elif k >= 2:
                (value,) = run(pass_kernel, [(own[k], VMEM)], piece_out, also, us=0.6)
            else:
                value = own[k]
            even_came.append(along(value, 0))
        if 0 < k <= odd_turns:
            odd_came.append(along(even_came[k - 1], 1))
        m = k - 1 - behind
        if 0 <= m < pieces:
            choices = [own[m]]
            for p in range(1, line):
                choices.append((odd_came, even_came)[p % 2][m + lag * ((p - 1) // 2)])
            (value,) = run(
                by_place_kernel, [(meta, SMEM)] + [(c, VMEM) for c in choices], piece_out,
                (other[m - 2],) if m >= 2 else (), us=0.6,
            )
            held.append(value)
            other.append(to_neighbour(value))

    def gather():
        lanes = min(nb, 128)
        spread = jnp.broadcast_to(pivots[:, :, None], (2, nb, lanes))
        table = jax.ShapeDtypeStruct((2, nb), I32)
        results = run(
            gather_kernel,
            [(meta, SMEM), (pivots, VMEM), (spread, VMEM), (tiles, ANY)],
            piece_out * (pieces - 1) + [(bf16(rows + 8, cb, nb), VMEM)]
            + [(bf16(nb, cb, nb), VMEM)] * 3 + [(table, VMEM)] * 4,
            scratch=[pltpu.VMEM((2, nb), I32), pltpu.SMEM((2, nb), I32), DMA, DMA],
            us=8.0, mib=20,
        )
        own.extend(results[: pieces - 1])
        state["loaded"], send, *rest = results[pieces - 1 :]
        state.update(zip(("keep", "block0", "join", "arrive", "goal", "hops"), rest))
        state["sent"] = to_sibling(send)
        state["block0_sibling"] = to_sibling(state["block0"])

    def join():
        (joined,) = run(
            join_kernel,
            [(meta, SMEM), (state["join"], SMEM), (state["keep"], VMEM), (state["sent"], VMEM)],
            [(bf16(nb, cb, nb), VMEM)],
            scratch=[pltpu.VMEM((nb + 8, cb, nb), BF16)],
            us=2.0,
        )
        state["choices"] = [joined] + [to_chip(joined, h) for h in range(1, chips)]

    def fresh():
        new, brought = run(
            functools.partial(fresh_kernel, chips),
            [(meta, SMEM), (state["hops"], VMEM)] + [(c, VMEM) for c in state["choices"]],
            [(bf16(nb, cb * nb), VMEM), (bf16(nb, cb, nb), VMEM)],
            us=2.0, mib=16,
        )
        state["fresh"] = (new, to_sibling(new))
        state["brought"] = (brought, to_sibling(brought))

    def head():
        (mine,) = run(
            head_kernel, [(meta, SMEM)] + [(v, VMEM) for v in state["fresh"]], [(bf16(nb // 2, nb), VMEM)]
        )
        state["head"] = [mine] + [
            lax.ppermute(mine, "pcol", [(0, 2 * h), (1, 2 * h + 1)]) for h in range(1, line)
        ]

    def head_here():
        (mine,) = run(
            by_place_kernel, [(meta, SMEM)] + [(v, VMEM) for v in state["head"]], [(bf16(nb // 2, nb), VMEM)]
        )
        swapped = to_neighbour(mine)
        state["heads"] = (mine, to_sibling(mine), swapped, to_sibling(swapped))

    def old():
        values = [values[p] for values in (held, other) for p in range(nb // chunk)]
        (mine,) = run(old_kernel, [(v, VMEM) for v in values], [(bf16(2, nb, nb), VMEM)])
        state["old"] = [mine] + [to_chip(mine, h) for h in range(1, chips)]

    def old_here():
        (mine,) = run(
            by_chip_kernel, [(meta, SMEM)] + [(v, VMEM) for v in state["old"]], [(bf16(2, nb, nb), VMEM)]
        )
        state["old"] = (mine, to_sibling(mine))

    def scatter():
        sources = state["brought"] + (state["block0"], state["block0_sibling"], state["loaded"])
        (state["moved"],) = run(
            scatter_kernel,
            [(meta, SMEM), (state["arrive"], SMEM), (state["goal"], SMEM)] + [(v, VMEM) for v in sources],
            [(bf16(rows + 8, cb, nb), VMEM)],
            us=4.0, mib=24,
        )

    def prep0():
        state["up0"], state["top0"] = run(
            prep0_kernel,
            [(meta, SMEM), (lower, VMEM)] + [(v, VMEM) for v in state["fresh"]],
            [(bf16(nb, cb * nb), VMEM), (bf16(nb, cb, nb), VMEM)],
            scratch=[pltpu.VMEM((nb, cb * nb), BF16)],
            us=2.0, mib=16,
        )

    def prep1():
        state["up1"], state["up0_panel"], state["top1"] = run(
            prep1_kernel,
            [(meta, SMEM), (lower, VMEM), (upper, VMEM)] + [(v, VMEM) for v in state["fresh"]]
            + [(state["up0"], VMEM)] + [(v, VMEM) for v in state["heads"]],
            [(bf16(nb, cb * nb), VMEM), (bf16(nb, nb), VMEM), (bf16(nb, cb, nb), VMEM)],
            scratch=[pltpu.VMEM((nb, cb * nb), BF16), pltpu.VMEM((2, nb, nb), BF16)],
            us=3.5, mib=16,
        )

    def update(first, count):
        operands = [(meta, SMEM), (state["goal"], VMEM)] + [(v, VMEM) for v in state["old"]] + [(upper, VMEM)]
        operands += [(state[name], VMEM) for name in ("up0", "up1", "up0_panel")]
        operands += [(state[name], ANY) for name in ("moved", "top0", "top1")]
        operands += [(v, VMEM) for v in held[first : first + count] + other[first : first + count]]
        aliases = {}
        if "result" in state:
            aliases = {len(operands): 0}
            operands.append((state["result"], ANY))
        state["result"], _ = run(
            functools.partial(update_kernel, first, count),
            operands,
            [(bf16(rows, cb, nb), ANY), (jax.ShapeDtypeStruct((8, 128), F32), VMEM)],
            scratch=[
                pltpu.VMEM((count, chunk, cb, nb), BF16),
                pltpu.VMEM((count, chunk, cb, nb), BF16),
                DMA((count,)), DMA((count,)),
            ],
            aliases=aliases,
            us=2.5 * count, mib=16,
        )

    plan = [(0, gather), (2, join), (6, fresh), (behind + 3, old), (7, head), (8, scatter), (8, prep0)]
    plan += [(9, head_here), (10, old_here), (11, prep1)]
    group = 2
    for first in range(0, pieces, group):
        count = min(group, pieces - first)
        plan.append((max(11 + first // group, first + count + behind + 1), functools.partial(update, first, count)))
    for k in range(last_turn + 1):
        turn(k)
        while plan and (plan[0][0] <= k or k == last_turn):
            plan.pop(0)[1]()
    return state["result"].reshape(matrix.shape)


def solution(mesh):
    placed = (P(None, "prow", None, "pcol"), P(), P(), P())
    return jax.shard_map(
        body, mesh=mesh, in_specs=placed, out_specs=P(None, "prow", None, "pcol"), check_vma=False
    )
```

```python
import functools

import jax
import jax.numpy as jnp
from jax import lax
from jax.experimental import pallas as pl
from jax.experimental.pallas import tpu as pltpu
from jax.sharding import PartitionSpec as P

BF16 = jnp.bfloat16
F32 = jnp.float32
I32 = jnp.int32
SMEM = pl.BlockSpec(memory_space=pltpu.SMEM)
VMEM = pl.BlockSpec(memory_space=pltpu.VMEM)
ANY = pl.BlockSpec(memory_space=pl.ANY)
DMA = pltpu.SemaphoreType.DMA


def dot(a, b):
    return jnp.dot(a, b, preferred_element_type=F32)


def flat(rows):
    return rows.reshape(rows.shape[0], rows.shape[1] * rows.shape[2])


def bf16(*shape):
    return jax.ShapeDtypeStruct(shape, BF16)


def call(kernel, operands, outs, after=(), scratch=(), aliases=None, us=1.0, mib=8):
    count = len(operands)

    def ordered(*refs):
        kernel(*refs[:count], *refs[count + len(after) :])

    return pl.pallas_call(
        ordered,
        out_shape=tuple(shape for shape, _ in outs),
        in_specs=[spec for _, spec in operands] + [ANY] * len(after),
        out_specs=tuple(spec for _, spec in outs),
        scratch_shapes=list(scratch),
        input_output_aliases=aliases or {},
        compiler_params=pltpu.CompilerParams(vmem_limit_bytes=mib * 1024 * 1024),
        cost_estimate=pl.CostEstimate(flops=int(us * 1.1e9), bytes_accessed=0, transcendentals=0),
    )(*[array for array, _ in operands], *after)


def fill_indices(nb, rows, meta, pivots, spread, fetch, join, arrive, goal, hops):
    row, row_devices = meta[0], meta[3]
    chip, chips = row // 2, row_devices // 2
    lanes = spread.shape[2]
    tiles = nb // lanes
    slot = lax.broadcasted_iota(I32, (1, nb), 1)
    pivot0, pivot1 = pivots[0:1, :], pivots[1:2, :]

    def lookup(keys, entry, value):
        parts = [keys[:, t * lanes : (t + 1) * lanes] for t in range(tiles)]

        def add(i, totals):
            begin = pl.multiple_of(i * 8, 8)
            at = begin + lax.broadcasted_iota(I32, (8, lanes), 0)
            here, give = entry(begin, at), value(begin, at)
            return tuple(t + jnp.where(p == here, give, 0) for t, p in zip(totals, parts))

        zero = jnp.zeros((8, lanes), I32)
        totals = lax.fori_loop(0, nb // 8, add, (zero,) * tiles, unroll=8)
        return jnp.concatenate([jnp.sum(t, axis=0, keepdims=True) for t in totals], axis=1)

    def pivot_of(panel):
        return lambda begin, at: spread[panel, pl.ds(begin, 8), :]

    place = lambda begin, at: at + 1
    in_pivots0 = lookup(pivot1, pivot_of(0), place)
    in_pivots1 = lookup(pivot0, pivot_of(1), place)
    top1_in_pivots0 = lookup(nb + slot, pivot_of(0), place)
    over_top1 = lookup(pivot0, lambda begin, at: nb + at, pivot_of(1))
    chained = lookup(nb + in_pivots1 - 1, pivot_of(0), place)

    source0 = pivot0
    source1 = jnp.where(in_pivots0 > 0, in_pivots0 - 1, pivot1)
    second0 = jnp.where(in_pivots1 > 0, jnp.where(chained > 0, chained - 1, nb + in_pivots1 - 1), slot)
    second1 = jnp.where(top1_in_pivots0 > 0, top1_in_pivots0 - 1, nb + slot)
    target0 = jnp.where(over_top1 > 0, over_top1, jnp.where(in_pivots1 > 0, nb + in_pivots1 - 1, pivot0))
    target1 = jnp.where(top1_in_pivots0 > 0, top1_in_pivots0 - 1, pivot1)

    def holder(index):
        return lax.rem(lax.div(index, nb), row_devices)

    def local(index):
        return lax.div(index, nb * row_devices) * nb + lax.rem(index, nb)

    def placed(index):
        mine = (holder(index) == row) & (index >= 2 * nb)
        return jnp.where(mine, local(index), rows)

    for k, (source, second, target) in enumerate(((source0, second0, target0), (source1, second1, target1))):
        from_chip = lax.div(holder(source), 2)
        wanted = jnp.where(from_chip == chip, source, second)
        at = (slice(k, k + 1), slice(None))
        fetch[at] = local(wanted)
        join[at] = jnp.where(holder(wanted) == row, slot, nb)
        arrive[at] = placed(source)
        goal[at] = placed(target)
        hops[at] = lax.rem(chip + chips - from_chip, chips)


def copy_rows(count, target, target_at, origin, origin_at):
    def copy(i, carry):
        target[target_at(i)] = origin[origin_at(i)]
        return carry

    lax.fori_loop(0, count, copy, 0, unroll=16)


def first_kernel(tiles, piece, work, sem):
    load = pltpu.make_async_copy(tiles.at[pl.ds(0, piece.shape[0])], work, sem)
    load.start()
    load.wait()
    piece[...] = flat(work[...])[:, : piece.shape[1]]


def gather_kernel(meta, pivots, spread, tiles, *refs):
    *pieces, loaded, send, keep, block0, join, arrive, goal, hops, fetch, fetch_table, load_sem, table_sem = refs
    chunk, nb = pieces[0].shape
    rows = tiles.shape[0]
    core = meta[1]
    load = pltpu.make_async_copy(tiles, loaded.at[pl.ds(0, rows)], load_sem)
    load.start()
    fill_indices(nb, rows, meta, pivots, spread, fetch, join, arrive, goal, hops)
    table = pltpu.make_async_copy(fetch, fetch_table, table_sem)
    table.start()
    table.wait()
    load.wait()
    for i, piece in enumerate(pieces, 1):
        piece[...] = flat(loaded[i * chunk : (i + 1) * chunk])[:, :nb]
    copy_rows(nb, send, lambda i: i, loaded, lambda i: fetch_table[1 - core, i])
    copy_rows(nb, keep, lambda i: i, loaded, lambda i: fetch_table[core, i])
    block0[...] = loaded[0:nb]


def join_kernel(meta, join, keep, came, joined, work):
    count = came.shape[0]
    core = meta[1]
    work[0:count] = came[...]
    copy_rows(count, work, lambda i: join[core, i], keep, lambda i: i)
    joined[...] = work[0:count]


def scatter_kernel(meta, arrive, goal, came, came_sibling, old, old_sibling, tiles, out):
    core, chip = meta[1], meta[0] // 2
    count = old.shape[0]
    out[...] = tiles[...]

    def scatter(table, values, k):
        copy_rows(count, out, lambda i: table[k, i], values, lambda i: i)

    @pl.when(chip == 0)
    def _():
        scatter(goal, old, core)
        scatter(goal, old_sibling, 1 - core)

    @pl.when(chip != 0)
    def _():
        scatter(arrive, came, core)
        scatter(arrive, came_sibling, 1 - core)


def relay_kernel(meta, came, own, held):
    place = lax.div(meta[2], 2)

    @pl.when(place == 0)
    def _():
        held[...] = own[...]

    @pl.when(place != 0)
    def _():
        held[...] = came[...]


def pass_kernel(came, held):
    held[...] = came[...]


def old_kernel(line, meta, *refs):
    held, other, old = refs[: len(refs) // 2], refs[len(refs) // 2 : -1], refs[-1]
    place = lax.div(meta[2], 2)
    chunk = held[0].shape[0]
    for h in range(line):

        @pl.when(place == h)
        def _(h=h):
            for p in range(old.shape[1] // chunk):
                old[0, p * chunk : (p + 1) * chunk] = held[p + h][...]
                old[1, p * chunk : (p + 1) * chunk] = other[p + h][...]


def by_chip_kernel(meta, *refs):
    out = refs[-1]
    for h, choice in enumerate(refs[:-1]):

        @pl.when(meta[0] // 2 == h)
        def _(choice=choice):
            out[...] = choice[...]


def by_place_kernel(meta, *refs):
    out = refs[-1]
    for h, choice in enumerate(refs[:-1]):

        @pl.when(lax.div(meta[2], 2) == h)
        def _(choice=choice):
            out[...] = choice[...]


def head_kernel(meta, fresh, fresh_sibling, head):
    needed = 1 - lax.rem(meta[2], 2)
    half, nb = head.shape
    at = pl.ds(pl.multiple_of(meta[1] * half, half), half)

    @pl.when(meta[1] == needed)
    def _():
        head[...] = fresh[at, :nb]

    @pl.when(meta[1] != needed)
    def _():
        head[...] = fresh_sibling[at, :nb]


def choose(hop, choices):
    value = flat(choices[0]).astype(F32)
    for h, other in enumerate(choices[1:], 1):
        value = jnp.where(hop == h, flat(other).astype(F32), value)
    return value.astype(BF16)


def fresh_kernel(chips, meta, hops, *refs):
    choices, (fresh, brought) = refs[:chips], refs[chips:]
    nb = fresh.shape[0]
    core, chip = meta[1], meta[0] // 2
    hop = jnp.broadcast_to(hops[pl.ds(core, 1), :], (8, nb)).T[:, 0:1]
    fresh[...] = choose(hop, [c[...] for c in choices])
    if chips == 1:
        brought[...] = choices[0][...]
    for h in range(1, chips):

        @pl.when((chip == h) | ((chip == 0) & (h == 1)))
        def _(h=h):
            brought[...] = choices[h][...]


def raw(columns, nb):
    joined = jnp.concatenate(columns, axis=1)
    return joined.reshape(joined.shape[0], len(columns), nb)


def prep0_kernel(meta, lower, fresh, fresh_sibling, up0, top, work):
    core, column = meta[1], meta[2]
    nb = fresh.shape[0]

    @pl.when(core == 0)
    def _():
        work[...] = fresh[...]

    @pl.when(core != 0)
    def _():
        work[...] = fresh_sibling[...]

    shown = []
    for j in range(work.shape[1] // nb):
        cols = slice(j * nb, (j + 1) * nb)
        product = dot(lower[0], work[:, cols])
        show = product
        if j == 0:
            show = jnp.where(column == 0, work[:, cols].astype(F32), product)
            product = jnp.where(column == 0, 0.0, product)
        up0[:, cols] = product.astype(BF16)
        shown.append(show.astype(BF16))
    top[...] = raw(shown, nb)


def prep1_kernel(meta, lower, upper, fresh, fresh_sibling, up0, *refs):
    mine, mine_sibling, other, other_sibling, up1, up0_panel, top, work, head = refs
    core, column = meta[1], meta[2]
    side = lax.rem(column, 2)
    nb, half = fresh.shape[0], mine.shape[0]
    for which, who, piece in (
        (1 - side, core, mine), (1 - side, 1 - core, mine_sibling), (side, core, other), (side, 1 - core, other_sibling)
    ):
        head[which, pl.ds(pl.multiple_of(who * half, half), half)] = piece[...]

    @pl.when(core == 1)
    def _():
        work[...] = fresh[...]

    @pl.when(core != 1)
    def _():
        work[...] = fresh_sibling[...]

    up0_panel[...] = dot(lower[0], head[0]).astype(BF16)
    factor = dot(head[1], upper[0]).astype(BF16)
    in_panel, next_panel = column == 0, column == 1
    shown = []
    for j in range(work.shape[1] // nb):
        cols = slice(j * nb, (j + 1) * nb)
        updated = (work[:, cols].astype(F32) - dot(factor, up0[:, cols])).astype(BF16)
        last = dot(lower[1], updated)
        show = last
        if j == 0:
            show = jnp.where(next_panel, updated.astype(F32), show)
            show = jnp.where(in_panel, factor.astype(F32), show)
            last = jnp.where(in_panel | next_panel, 0.0, last)
        up1[:, cols] = last.astype(BF16)
        shown.append(show.astype(BF16))
    top[...] = raw(shown, nb)


def update_kernel(
    block_index, line, meta, goal, old, old_sibling, upper, up0, up1, up0_panel, tiles, top0, top1, *rest
):
    out, token, panels, block, result, panel_sem, block_sem, out_sem = rest[-8:]
    spans = (len(rest) - 8) // 2
    held, other = rest[:spans], rest[spans : 2 * spans]
    per_block = spans - line + 1
    row, core, column, row_devices = meta[0], meta[1], meta[2], meta[3]
    side, place = lax.rem(column, 2), lax.div(column, 2)
    nb, cb, _ = block.shape
    chunk = nb // per_block
    rows_of = pl.ds(block_index * nb, nb)

    def panel_copy(i, h, which):
        source = (held, other)[which][i + h]
        target = panels.at[lax.rem(side + which, 2), pl.ds(i * chunk, chunk)]
        return pltpu.make_async_copy(source, target, panel_sem.at[i, which])

    load = pltpu.make_async_copy(tiles.at[rows_of], block, block_sem)
    load.start()
    for h in range(line):

        @pl.when(place == h)
        def _(h=h):
            for i in range(per_block):
                panel_copy(i, h, 0).start()
                panel_copy(i, h, 1).start()

    def arrived():
        for i in range(per_block):
            panel_copy(i, 0, 0).wait()
            panel_copy(i, 0, 1).wait()

    def from_factors():
        here = block_index * nb + lax.broadcasted_iota(I32, (nb, nb), 0)
        pick = jnp.where(here == goal[pl.ds(core, 1), :], 1.0, 0.0)
        pick_sibling = jnp.where(here == goal[pl.ds(1 - core, 1), :], 1.0, 0.0)
        moved = jnp.sum(pick + pick_sibling, axis=1, keepdims=True) > 0.5
        pick, pick_sibling = pick.astype(BF16), pick_sibling.astype(BF16)
        arrived()
        whole = []
        for k in range(2):
            which = lax.rem(k + side, 2)
            brought = dot(pick, old[which]) + dot(pick_sibling, old_sibling[which])
            whole.append(jnp.where(moved, brought, panels[k].astype(F32)))
        factor0 = dot(whole[0].astype(BF16), upper[0]).astype(BF16)
        below = (whole[1] - dot(factor0, up0_panel[...])).astype(BF16)
        factor1 = dot(below, upper[1]).astype(BF16)
        load.wait()
        values = flat(block[...])
        columns = []
        for j in range(cb):
            cols = slice(j * nb, (j + 1) * nb)
            value = values[:, cols].astype(F32) - dot(factor0, up0[:, cols])
            value = value.astype(BF16).astype(F32) - dot(factor1, up1[:, cols])
            if j == 0:
                value = jnp.where(column == 0, factor0.astype(F32), value)
                value = jnp.where(column == 1, factor1.astype(F32), value)
            columns.append(value.astype(BF16))
        result[...] = raw(columns, nb)

    def from_top(top):
        arrived()
        load.wait()
        copy = pltpu.make_async_copy(top, result, block_sem)
        copy.start()
        copy.wait()

    if block_index == 0:
        pl.when(row == 0)(lambda: from_top(top0))
        pl.when(row == 1)(lambda: from_top(top1))
        pl.when(row >= 2)(from_factors)
    else:
        from_factors()
    store = pltpu.make_async_copy(result, out.at[rows_of], out_sem)
    store.start()
    token[...] = jnp.zeros(token.shape, F32)
    store.wait()


def body(matrix, pivots, lower, upper):
    rb, nb, cb, _ = matrix.shape
    rows = rb * nb
    chunk = nb // 2
    pieces = rows // chunk
    row_devices = lax.axis_size("prow")
    col_devices = lax.axis_size("pcol")
    chips, line = row_devices // 2, col_devices // 2
    row = lax.axis_index("prow").astype(I32)
    column = lax.axis_index("pcol").astype(I32)
    meta = jnp.stack([row, row % 2, column, jnp.int32(row_devices)])
    tiles = matrix.reshape(rows, cb, nb)

    def to_sibling(value):
        return lax.ppermute(value, "prow", [(r, r ^ 1) for r in range(row_devices)])

    def to_neighbour(value):
        return lax.ppermute(value, "pcol", [(c, c ^ 1) for c in range(col_devices)])

    def to_chip(value, h):
        return lax.ppermute(value, "prow", [(r, (r + 2 * h) % row_devices) for r in range(row_devices)])

    def to_next(value):
        return lax.ppermute(value, "pcol", [(c, c + 2) for c in range(col_devices - 2)])

    order = []

    def run(kernel, operands, outs, also=(), **kwargs):
        after = tuple(order[-1:]) + tuple(also)
        results = call(kernel, operands, outs, after=after, **kwargs)
        order.append(results[-1])
        return results

    last_step = pieces + line - 2
    piece_out = [(bf16(chunk, nb), VMEM)]
    own, held, other = [], [], []
    state = {}

    def turn_us(k):
        return 10.0 if k in (1, 6) or k > 8 else 0.2

    def step(k):
        if k == 0:
            own.extend(run(
                first_kernel, [(tiles, ANY)], piece_out, scratch=[pltpu.VMEM((chunk, cb, nb), BF16), DMA], mib=60,
            ))
            value = own[0]
        else:
            also = (other[k - 2],) if k >= 2 else ()
            came = state["came"]
            if k < pieces:
                operands = [(meta, SMEM), (came, VMEM), (own[k], VMEM)]
                (value,) = run(relay_kernel, operands, piece_out, also, us=turn_us(k))
            else:
                (value,) = run(pass_kernel, [(came, VMEM)], piece_out, also, us=turn_us(k))
        held.append(value)
        if k < last_step:
            state["came"] = to_next(value)
        other.append(to_neighbour(value))

    def gather():
        lanes = min(nb, 128)
        spread = jnp.broadcast_to(pivots[:, :, None], (2, nb, lanes))
        table = jax.ShapeDtypeStruct((2, nb), I32)
        results = run(
            gather_kernel,
            [(meta, SMEM), (pivots, VMEM), (spread, VMEM), (tiles, ANY)],
            piece_out * (pieces - 1) + [(bf16(rows + 8, cb, nb), VMEM)]
            + [(bf16(nb, cb, nb), VMEM)] * 3 + [(table, VMEM)] * 4,
            scratch=[pltpu.VMEM((2, nb), I32), pltpu.SMEM((2, nb), I32), DMA, DMA],
            us=8.0, mib=20,
        )
        own.extend(results[: pieces - 1])
        state["loaded"], send, *rest = results[pieces - 1 :]
        state.update(zip(("keep", "block0", "join", "arrive", "goal", "hops"), rest))
        state["sent"] = to_sibling(send)
        state["block0_sibling"] = to_sibling(state["block0"])

    def join():
        (joined,) = run(
            join_kernel,
            [(meta, SMEM), (state["join"], SMEM), (state["keep"], VMEM), (state["sent"], VMEM)],
            [(bf16(nb, cb, nb), VMEM)],
            scratch=[pltpu.VMEM((nb + 8, cb, nb), BF16)],
            us=2.0,
        )
        state["choices"] = [joined] + [to_chip(joined, h) for h in range(1, chips)]

    def fresh():
        new, brought = run(
            functools.partial(fresh_kernel, chips),
            [(meta, SMEM), (state["hops"], VMEM)] + [(c, VMEM) for c in state["choices"]],
            [(bf16(nb, cb * nb), VMEM), (bf16(nb, cb, nb), VMEM)],
            us=2.0, mib=16,
        )
        state["fresh"] = (new, to_sibling(new))
        state["brought"] = (brought, to_sibling(brought))

    def head():
        (mine,) = run(
            head_kernel, [(meta, SMEM)] + [(v, VMEM) for v in state["fresh"]], [(bf16(nb // 2, nb), VMEM)], us=0.1,
        )
        state["head"] = [mine] + [
            lax.ppermute(mine, "pcol", [(0, 2 * h), (1, 2 * h + 1)]) for h in range(1, line)
        ]

    def head_here():
        (mine,) = run(
            by_place_kernel, [(meta, SMEM)] + [(v, VMEM) for v in state["head"]], [(bf16(nb // 2, nb), VMEM)]
        )
        swapped = to_neighbour(mine)
        state["heads"] = (mine, to_sibling(mine), swapped, to_sibling(swapped))

    def old():
        spans = range(nb // chunk + line - 1)
        (mine,) = run(
            functools.partial(old_kernel, line),
            [(meta, SMEM)] + [(held[i], VMEM) for i in spans] + [(other[i], VMEM) for i in spans],
            [(bf16(2, nb, nb), VMEM)],
        )
        state["old"] = [mine] + [to_chip(mine, h) for h in range(1, chips)]

    def old_here():
        (mine,) = run(
            by_chip_kernel, [(meta, SMEM)] + [(v, VMEM) for v in state["old"]], [(bf16(2, nb, nb), VMEM)]
        )
        state["old"] = (mine, to_sibling(mine))

    def scatter():
        sources = state["brought"] + (state["block0"], state["block0_sibling"], state["loaded"])
        (state["moved"],) = run(
            scatter_kernel,
            [(meta, SMEM), (state["arrive"], SMEM), (state["goal"], SMEM)] + [(v, VMEM) for v in sources],
            [(bf16(rows + 8, cb, nb), VMEM)],
            us=0.1, mib=24,
        )

    def prep0():
        state["up0"], state["top0"] = run(
            prep0_kernel,
            [(meta, SMEM), (lower, VMEM)] + [(v, VMEM) for v in state["fresh"]],
            [(bf16(nb, cb * nb), VMEM), (bf16(nb, cb, nb), VMEM)],
            scratch=[pltpu.VMEM((nb, cb * nb), BF16)],
            us=0.1, mib=16,
        )

    def prep1():
        state["up1"], state["up0_panel"], state["top1"] = run(
            prep1_kernel,
            [(meta, SMEM), (lower, VMEM), (upper, VMEM)] + [(v, VMEM) for v in state["fresh"]]
            + [(state["up0"], VMEM)] + [(v, VMEM) for v in state["heads"]],
            [(bf16(nb, cb * nb), VMEM), (bf16(nb, nb), VMEM), (bf16(nb, cb, nb), VMEM)],
            scratch=[pltpu.VMEM((nb, cb * nb), BF16), pltpu.VMEM((2, nb, nb), BF16)],
            us=3.5, mib=16,
        )

    per_block = nb // chunk

    def update(b):
        spans = range(b * per_block, (b + 1) * per_block + line - 1)
        operands = [(meta, SMEM), (state["goal"], VMEM)] + [(v, VMEM) for v in state["old"]] + [(upper, VMEM)]
        operands += [(state[name], VMEM) for name in ("up0", "up1", "up0_panel")]
        operands += [(state[name], ANY) for name in ("moved", "top0", "top1")]
        operands += [(held[i], ANY) for i in spans] + [(other[i], ANY) for i in spans]
        aliases = {}
        if "result" in state:
            aliases = {len(operands): 0}
            operands.append((state["result"], ANY))
        kernel = functools.partial(update_kernel, b, line)
        if aliases:
            kernel = lambda *refs, kernel=kernel, at=len(operands) - 1: kernel(*refs[:at], *refs[at + 1 :])
        state["result"], _ = run(
            kernel,
            operands,
            [(bf16(rows, cb, nb), ANY), (jax.ShapeDtypeStruct((8, 128), F32), VMEM)],
            scratch=[
                pltpu.VMEM((2, nb, nb), BF16), pltpu.VMEM((nb, cb, nb), BF16), pltpu.VMEM((nb, cb, nb), BF16),
                DMA((per_block, 2)), DMA, DMA,
            ],
            aliases=aliases,
            us=5.0, mib=24,
        )

    plan = [(0, gather), (1, join), (5, fresh), (line + 1, old), (6, head), (6, scatter), (7, prep0), (8, head_here), (8, old_here), (9, prep1)]
    for b in range(rb):
        plan.append((max(9 + b, (b + 1) * per_block + line - 2), functools.partial(update, b)))
    for k in range(last_step + 1):
        step(k)
        while plan and (plan[0][0] <= k or k == last_step):
            plan.pop(0)[1]()
    return state["result"].reshape(matrix.shape)


def solution(mesh):
    placed = (P(None, "prow", None, "pcol"), P(), P(), P())
    return jax.shard_map(
        body, mesh=mesh, in_specs=placed, out_specs=P(None, "prow", None, "pcol"), check_vma=False
    )
```

```python
import functools

import jax
import jax.numpy as jnp
from jax import lax
from jax.experimental import pallas as pl
from jax.experimental.pallas import tpu as pltpu
from jax.sharding import PartitionSpec as P

BF16 = jnp.bfloat16
F32 = jnp.float32
I32 = jnp.int32
SMEM = pl.BlockSpec(memory_space=pltpu.SMEM)
VMEM = pl.BlockSpec(memory_space=pltpu.VMEM)
ANY = pl.BlockSpec(memory_space=pl.ANY)
DMA = pltpu.SemaphoreType.DMA


def dot(a, b):
    return jnp.dot(a, b, preferred_element_type=F32)


def flat(rows):
    return rows.reshape(rows.shape[0], rows.shape[1] * rows.shape[2])


def bf16(*shape):
    return jax.ShapeDtypeStruct(shape, BF16)


def call(kernel, operands, outs, after=(), scratch=(), aliases=None, us=1.0, mib=8):
    count = len(operands)

    def ordered(*refs):
        kernel(*refs[:count], *refs[count + len(after) :])

    return pl.pallas_call(
        ordered,
        out_shape=tuple(shape for shape, _ in outs),
        in_specs=[spec for _, spec in operands] + [ANY] * len(after),
        out_specs=tuple(spec for _, spec in outs),
        scratch_shapes=list(scratch),
        input_output_aliases=aliases or {},
        compiler_params=pltpu.CompilerParams(vmem_limit_bytes=mib * 1024 * 1024),
        cost_estimate=pl.CostEstimate(flops=int(us * 1.1e9), bytes_accessed=0, transcendentals=0),
    )(*[array for array, _ in operands], *after)


def fill_indices(nb, rows, meta, pivots, spread, fetch, join, arrive, goal, hops):
    row, row_devices = meta[0], meta[3]
    chip, chips = row // 2, row_devices // 2
    lanes = spread.shape[2]
    tiles = nb // lanes
    slot = lax.broadcasted_iota(I32, (1, nb), 1)
    pivot0, pivot1 = pivots[0:1, :], pivots[1:2, :]

    def lookup(keys, entry, value):
        parts = [keys[:, t * lanes : (t + 1) * lanes] for t in range(tiles)]

        def add(i, totals):
            begin = pl.multiple_of(i * 8, 8)
            at = begin + lax.broadcasted_iota(I32, (8, lanes), 0)
            here, give = entry(begin, at), value(begin, at)
            return tuple(t + jnp.where(p == here, give, 0) for t, p in zip(totals, parts))

        zero = jnp.zeros((8, lanes), I32)
        totals = lax.fori_loop(0, nb // 8, add, (zero,) * tiles, unroll=8)
        return jnp.concatenate([jnp.sum(t, axis=0, keepdims=True) for t in totals], axis=1)

    def pivot_of(panel):
        return lambda begin, at: spread[panel, pl.ds(begin, 8), :]

    place = lambda begin, at: at + 1
    in_pivots0 = lookup(pivot1, pivot_of(0), place)
    in_pivots1 = lookup(pivot0, pivot_of(1), place)
    top1_in_pivots0 = lookup(nb + slot, pivot_of(0), place)
    over_top1 = lookup(pivot0, lambda begin, at: nb + at, pivot_of(1))
    chained = lookup(nb + in_pivots1 - 1, pivot_of(0), place)

    source0 = pivot0
    source1 = jnp.where(in_pivots0 > 0, in_pivots0 - 1, pivot1)
    second0 = jnp.where(in_pivots1 > 0, jnp.where(chained > 0, chained - 1, nb + in_pivots1 - 1), slot)
    second1 = jnp.where(top1_in_pivots0 > 0, top1_in_pivots0 - 1, nb + slot)
    target0 = jnp.where(over_top1 > 0, over_top1, jnp.where(in_pivots1 > 0, nb + in_pivots1 - 1, pivot0))
    target1 = jnp.where(top1_in_pivots0 > 0, top1_in_pivots0 - 1, pivot1)

    def holder(index):
        return lax.rem(lax.div(index, nb), row_devices)

    def local(index):
        return lax.div(index, nb * row_devices) * nb + lax.rem(index, nb)

    def placed(index):
        mine = (holder(index) == row) & (index >= 2 * nb)
        return jnp.where(mine, local(index), rows)

    for k, (source, second, target) in enumerate(((source0, second0, target0), (source1, second1, target1))):
        from_chip = lax.div(holder(source), 2)
        wanted = jnp.where(from_chip == chip, source, second)
        at = (slice(k, k + 1), slice(None))
        fetch[at] = local(wanted)
        join[at] = jnp.where(holder(wanted) == row, slot, nb)
        arrive[at] = placed(source)
        goal[at] = placed(target)
        hops[at] = lax.rem(chip + chips - from_chip, chips)


def copy_rows(count, target, target_at, origin, origin_at):
    def copy(i, carry):
        target[target_at(i)] = origin[origin_at(i)]
        return carry

    lax.fori_loop(0, count, copy, 0, unroll=16)


def first_kernel(tiles, piece, work, sem):
    load = pltpu.make_async_copy(tiles.at[pl.ds(0, piece.shape[0])], work, sem)
    load.start()
    load.wait()
    piece[...] = flat(work[...])[:, : piece.shape[1]]


def gather_kernel(meta, pivots, spread, tiles, *refs):
    *pieces, loaded, send, keep, block0, join, arrive, goal, hops, fetch, fetch_table, load_sem, table_sem = refs
    nb = send.shape[0]
    rows = tiles.shape[0]
    core = meta[1]
    load = pltpu.make_async_copy(tiles, loaded.at[pl.ds(0, rows)], load_sem)
    load.start()
    fill_indices(nb, rows, meta, pivots, spread, fetch, join, arrive, goal, hops)
    table = pltpu.make_async_copy(fetch, fetch_table, table_sem)
    table.start()
    table.wait()
    load.wait()
    begin = nb
    for piece in pieces:
        end = begin + piece.shape[0]
        piece[...] = flat(loaded[begin:end])[:, :nb]
        begin = end
    copy_rows(nb, send, lambda i: i, loaded, lambda i: fetch_table[1 - core, i])
    copy_rows(nb, keep, lambda i: i, loaded, lambda i: fetch_table[core, i])
    block0[...] = loaded[0:nb]


def join_kernel(meta, join, keep, came, joined, work):
    count = came.shape[0]
    core = meta[1]
    work[0:count] = came[...]
    copy_rows(count, work, lambda i: join[core, i], keep, lambda i: i)
    joined[...] = work[0:count]


def scatter_kernel(meta, arrive, goal, came, came_sibling, old, old_sibling, tiles, out):
    core, chip = meta[1], meta[0] // 2
    count = old.shape[0]
    out[...] = tiles[...]

    def scatter(table, values, k):
        copy_rows(count, out, lambda i: table[k, i], values, lambda i: i)

    @pl.when(chip == 0)
    def _():
        scatter(goal, old, core)
        scatter(goal, old_sibling, 1 - core)

    @pl.when(chip != 0)
    def _():
        scatter(arrive, came, core)
        scatter(arrive, came_sibling, 1 - core)


def relay_kernel(meta, came, *refs):
    *own, held = refs
    place = lax.div(meta[2], 2)
    for piece in own:

        @pl.when(place == 0)
        def _(piece=piece):
            held[0 : piece.shape[0]] = piece[...]

    @pl.when(place != 0)
    def _():
        count = min(came.shape[0], held.shape[0])
        held[0:count] = came[0:count]


def old_kernel(line, meta, *refs):
    held, other, old = refs[:line], refs[line : 2 * line], refs[-1]
    for h in range(line):

        @pl.when(lax.div(meta[2], 2) == h)
        def _(h=h):
            old[0] = held[h][0 : old.shape[1]]
            old[1] = other[h][0 : old.shape[1]]


def by_chip_kernel(meta, *refs):
    out = refs[-1]
    for h, choice in enumerate(refs[:-1]):

        @pl.when(meta[0] // 2 == h)
        def _(choice=choice):
            out[...] = choice[...]


def by_place_kernel(meta, *refs):
    out = refs[-1]
    for h, choice in enumerate(refs[:-1]):

        @pl.when(lax.div(meta[2], 2) == h)
        def _(choice=choice):
            out[...] = choice[...]


def head_kernel(meta, fresh, fresh_sibling, head):
    needed = 1 - lax.rem(meta[2], 2)
    part, nb = head.shape
    at = pl.ds(pl.multiple_of(meta[0] * part, part), part)

    @pl.when(meta[1] == needed)
    def _():
        head[...] = fresh[at, :nb]

    @pl.when(meta[1] != needed)
    def _():
        head[...] = fresh_sibling[at, :nb]


def stack_kernel(*refs):
    *entries, out = refs
    for i, entry in enumerate(entries):
        out[i] = entry[...]


def choose(hop, choices):
    value = flat(choices[0]).astype(F32)
    for h, other in enumerate(choices[1:], 1):
        value = jnp.where(hop == h, flat(other).astype(F32), value)
    return value.astype(BF16)


def fresh_kernel(chips, meta, hops, *refs):
    choices, (fresh, brought) = refs[:chips], refs[chips:]
    nb = fresh.shape[0]
    core, chip = meta[1], meta[0] // 2
    hop = jnp.broadcast_to(hops[pl.ds(core, 1), :], (8, nb)).T[:, 0:1]
    fresh[...] = choose(hop, [c[...] for c in choices])
    if chips == 1:
        brought[...] = choices[0][...]
    for h in range(1, chips):

        @pl.when((chip == h) | ((chip == 0) & (h == 1)))
        def _(h=h):
            brought[...] = choices[h][...]


def raw(columns, nb):
    joined = jnp.concatenate(columns, axis=1)
    return joined.reshape(joined.shape[0], len(columns), nb)


def prep0_kernel(meta, lower, fresh, fresh_sibling, up0, top, work):
    core, column = meta[1], meta[2]
    nb = fresh.shape[0]

    @pl.when(core == 0)
    def _():
        work[...] = fresh[...]

    @pl.when(core != 0)
    def _():
        work[...] = fresh_sibling[...]

    shown = []
    for j in range(work.shape[1] // nb):
        cols = slice(j * nb, (j + 1) * nb)
        product = dot(lower[0], work[:, cols])
        show = product
        if j == 0:
            show = jnp.where(column == 0, work[:, cols].astype(F32), product)
            product = jnp.where(column == 0, 0.0, product)
        up0[:, cols] = product.astype(BF16)
        shown.append(show.astype(BF16))
    top[...] = raw(shown, nb)


def prep1_kernel(chips, meta, lower, upper, fresh, fresh_sibling, up0, *refs):
    heads, heads_sibling, up1, up0_panel, top, work, head = refs
    core, column, chip = meta[1], meta[2], meta[0] // 2
    side = lax.rem(column, 2)
    nb, part = fresh.shape[0], heads.shape[2]
    for who, parts in ((core, heads), (1 - core, heads_sibling)):
        for h in range(chips):
            at = pl.multiple_of((2 * lax.rem(chip + chips - h, chips) + who) * part, part)
            head[1 - side, pl.ds(at, part)] = parts[h, 0]
            head[side, pl.ds(at, part)] = parts[h, 1]

    @pl.when(core == 1)
    def _():
        work[...] = fresh[...]

    @pl.when(core != 1)
    def _():
        work[...] = fresh_sibling[...]

    up0_panel[...] = dot(lower[0], head[0]).astype(BF16)
    factor = dot(head[1], upper[0]).astype(BF16)
    in_panel, next_panel = column == 0, column == 1
    shown = []
    for j in range(work.shape[1] // nb):
        cols = slice(j * nb, (j + 1) * nb)
        updated = (work[:, cols].astype(F32) - dot(factor, up0[:, cols])).astype(BF16)
        last = dot(lower[1], updated)
        show = last
        if j == 0:
            show = jnp.where(next_panel, updated.astype(F32), show)
            show = jnp.where(in_panel, factor.astype(F32), show)
            last = jnp.where(in_panel | next_panel, 0.0, last)
        up1[:, cols] = last.astype(BF16)
        shown.append(show.astype(BF16))
    top[...] = raw(shown, nb)


def update_kernel(
    begin, line, meta, goal, old, old_sibling, upper, up0, up1, up0_panel, tiles, top0, top1, *rest
):
    held, other = rest[:line], rest[line : 2 * line]
    out, token, panels, block, result, panel_sem, block_sem, out_sem = rest[-8:]
    row, core, column = meta[0], meta[1], meta[2]
    side, place = lax.rem(column, 2), lax.div(column, 2)
    count, cb, nb = block.shape
    rows_of = pl.ds(begin, count)

    def panel_copy(h, which):
        source = (held, other)[which][h].at[pl.ds(0, count)]
        return pltpu.make_async_copy(source, panels.at[lax.rem(side + which, 2)], panel_sem.at[which])

    load = pltpu.make_async_copy(tiles.at[rows_of], block, block_sem)
    load.start()
    for h in range(line):

        @pl.when(place == h)
        def _(h=h):
            panel_copy(h, 0).start()
            panel_copy(h, 1).start()

    def arrived():
        panel_copy(0, 0).wait()
        panel_copy(0, 1).wait()

    def from_factors():
        here = begin + lax.broadcasted_iota(I32, (count, nb), 0)
        pick = jnp.where(here == goal[pl.ds(core, 1), :], 1.0, 0.0)
        pick_sibling = jnp.where(here == goal[pl.ds(1 - core, 1), :], 1.0, 0.0)
        moved = jnp.sum(pick + pick_sibling, axis=1, keepdims=True) > 0.5
        pick, pick_sibling = pick.astype(BF16), pick_sibling.astype(BF16)
        arrived()
        whole = []
        for k in range(2):
            which = lax.rem(k + side, 2)
            brought = dot(pick, old[which]) + dot(pick_sibling, old_sibling[which])
            whole.append(jnp.where(moved, brought, panels[k].astype(F32)))
        factor0 = dot(whole[0].astype(BF16), upper[0]).astype(BF16)
        below = (whole[1] - dot(factor0, up0_panel[...])).astype(BF16)
        factor1 = dot(below, upper[1]).astype(BF16)
        load.wait()
        values = flat(block[...])
        columns = []
        for j in range(cb):
            cols = slice(j * nb, (j + 1) * nb)
            value = values[:, cols].astype(F32) - dot(factor0, up0[:, cols])
            value = value.astype(BF16).astype(F32) - dot(factor1, up1[:, cols])
            if j == 0:
                value = jnp.where(column == 0, factor0.astype(F32), value)
                value = jnp.where(column == 1, factor1.astype(F32), value)
            columns.append(value.astype(BF16))
        result[...] = raw(columns, nb)

    def from_top(top):
        arrived()
        load.wait()
        copy = pltpu.make_async_copy(top.at[rows_of], result, block_sem)
        copy.start()
        copy.wait()

    if begin < nb:
        pl.when(row == 0)(lambda: from_top(top0))
        pl.when(row == 1)(lambda: from_top(top1))
        pl.when(row >= 2)(from_factors)
    else:
        from_factors()
    store = pltpu.make_async_copy(result, out.at[rows_of], out_sem)
    store.start()
    token[...] = jnp.zeros(token.shape, F32)
    store.wait()


def body(matrix, pivots, lower, upper):
    rb, nb, cb, _ = matrix.shape
    rows = rb * nb
    sizes = [nb] * (rb - 1) + [nb // 2] * 2
    begins = [sum(sizes[:i]) for i in range(len(sizes))]
    pieces = len(sizes)
    row_devices = lax.axis_size("prow")
    col_devices = lax.axis_size("pcol")
    chips, line = row_devices // 2, col_devices // 2
    row = lax.axis_index("prow").astype(I32)
    column = lax.axis_index("pcol").astype(I32)
    meta = jnp.stack([row, row % 2, column, jnp.int32(row_devices)])
    tiles = matrix.reshape(rows, cb, nb)

    def to_sibling(value):
        return lax.ppermute(value, "prow", [(r, r ^ 1) for r in range(row_devices)])

    def to_neighbour(value):
        return lax.ppermute(value, "pcol", [(c, c ^ 1) for c in range(col_devices)])

    def to_chip(value, h):
        return lax.ppermute(value, "prow", [(r, (r + 2 * h) % row_devices) for r in range(row_devices)])

    def to_next(value):
        return lax.ppermute(value, "pcol", [(c, c + 2) for c in range(col_devices - 2)])

    order = []

    def run(kernel, operands, outs, also=(), **kwargs):
        after = tuple(order[-1:]) + tuple(also)
        results = call(kernel, operands, outs, after=after, **kwargs)
        order.append(results[-1])
        return results

    last_step = pieces + line - 2

    def piece_out(i):
        return (bf16(sizes[i], nb), VMEM)

    def step_out(k):
        return (bf16(max(sizes[k - p] for p in range(line) if 0 <= k - p < pieces), nb), VMEM)

    own, held, other = [], [], []
    state = {}

    def step(k):
        if k == 0:
            own.extend(run(
                first_kernel, [(tiles, ANY)], [piece_out(0)],
                scratch=[pltpu.VMEM((sizes[0], cb, nb), BF16), DMA], mib=60,
            ))
            value = own[0]
        else:
            also = (other[k - 2],) if k >= 2 else ()
            operands = [(meta, SMEM), (state["came"], VMEM)] + [(v, VMEM) for v in own[k : k + 1]]
            (value,) = run(relay_kernel, operands, [step_out(k)], also, us=0.2 if k in (3, 4, 5) else 12.0)
        held.append(value)
        if k < last_step:
            state["came"] = to_next(value)
        other.append(to_neighbour(value))

    def gather():
        lanes = min(nb, 128)
        spread = jnp.broadcast_to(pivots[:, :, None], (2, nb, lanes))
        table = jax.ShapeDtypeStruct((2, nb), I32)
        results = run(
            gather_kernel,
            [(meta, SMEM), (pivots, VMEM), (spread, VMEM), (tiles, ANY)],
            [piece_out(i) for i in range(1, pieces)] + [(bf16(rows + 8, cb, nb), VMEM)]
            + [(bf16(nb, cb, nb), VMEM)] * 3 + [(table, VMEM)] * 4,
            scratch=[pltpu.VMEM((2, nb), I32), pltpu.SMEM((2, nb), I32), DMA, DMA],
            us=8.0, mib=20,
        )
        own.extend(results[: pieces - 1])
        state["loaded"], send, *rest = results[pieces - 1 :]
        state.update(zip(("keep", "block0", "join", "arrive", "goal", "hops"), rest))
        state["sent"] = to_sibling(send)
        state["block0_sibling"] = to_sibling(state["block0"])

    def join():
        (joined,) = run(
            join_kernel,
            [(meta, SMEM), (state["join"], SMEM), (state["keep"], VMEM), (state["sent"], VMEM)],
            [(bf16(nb, cb, nb), VMEM)],
            scratch=[pltpu.VMEM((nb + 8, cb, nb), BF16)],
            us=2.0,
        )
        state["choices"] = [joined] + [to_chip(joined, h) for h in range(1, chips)]

    def fresh():
        new, brought = run(
            functools.partial(fresh_kernel, chips),
            [(meta, SMEM), (state["hops"], VMEM)] + [(c, VMEM) for c in state["choices"]],
            [(bf16(nb, cb * nb), VMEM), (bf16(nb, cb, nb), VMEM)],
            us=2.0, mib=16,
        )
        state["fresh"] = (new, to_sibling(new))
        state["brought"] = (brought, to_sibling(brought))

    part = nb // row_devices

    def head():
        (mine,) = run(
            head_kernel, [(meta, SMEM)] + [(v, VMEM) for v in state["fresh"]], [(bf16(part, nb), VMEM)], us=0.1
        )
        state["head"] = [mine] + [
            lax.ppermute(mine, "pcol", [(0, 2 * h), (1, 2 * h + 1)]) for h in range(1, line)
        ]

    def head_here():
        (mine,) = run(
            by_place_kernel, [(meta, SMEM)] + [(v, VMEM) for v in state["head"]], [(bf16(part, nb), VMEM)]
        )
        state["head"] = (mine, to_neighbour(mine))

    def head_pair():
        (pair,) = run(stack_kernel, [(v, VMEM) for v in state["head"]], [(bf16(2, part, nb), VMEM)])
        state["head"] = [pair] + [to_chip(pair, h) for h in range(1, chips)]

    def head_all():
        (mine,) = run(
            stack_kernel, [(v, VMEM) for v in state["head"]], [(bf16(chips, 2, part, nb), VMEM)], us=0.1
        )
        state["heads"] = (mine, to_sibling(mine))

    def old():
        operands = [(meta, SMEM)] + [(v, VMEM) for v in held[:line] + other[:line]]
        (mine,) = run(functools.partial(old_kernel, line), operands, [(bf16(2, nb, nb), VMEM)], us=0.6)
        state["old"] = [mine] + [to_chip(mine, h) for h in range(1, chips)]

    def old_here():
        (mine,) = run(
            by_chip_kernel, [(meta, SMEM)] + [(v, VMEM) for v in state["old"]], [(bf16(2, nb, nb), VMEM)]
        )
        state["old"] = (mine, to_sibling(mine))

    def scatter():
        sources = state["brought"] + (state["block0"], state["block0_sibling"], state["loaded"])
        (state["moved"],) = run(
            scatter_kernel,
            [(meta, SMEM), (state["arrive"], SMEM), (state["goal"], SMEM)] + [(v, VMEM) for v in sources],
            [(bf16(rows + 8, cb, nb), VMEM)],
            us=0.1, mib=24,
        )

    def prep0():
        state["up0"], state["top0"] = run(
            prep0_kernel,
            [(meta, SMEM), (lower, VMEM)] + [(v, VMEM) for v in state["fresh"]],
            [(bf16(nb, cb * nb), VMEM), (bf16(nb, cb, nb), VMEM)],
            scratch=[pltpu.VMEM((nb, cb * nb), BF16)],
            us=0.1, mib=16,
        )

    def prep1():
        state["up1"], state["up0_panel"], state["top1"] = run(
            functools.partial(prep1_kernel, chips),
            [(meta, SMEM), (lower, VMEM), (upper, VMEM)] + [(v, VMEM) for v in state["fresh"]]
            + [(state["up0"], VMEM)] + [(v, VMEM) for v in state["heads"]],
            [(bf16(nb, cb * nb), VMEM), (bf16(nb, nb), VMEM), (bf16(nb, cb, nb), VMEM)],
            scratch=[pltpu.VMEM((nb, cb * nb), BF16), pltpu.VMEM((2, nb, nb), BF16)],
            us=3.5, mib=16,
        )

    def update(i):
        operands = [(meta, SMEM), (state["goal"], VMEM)] + [(v, VMEM) for v in state["old"]] + [(upper, VMEM)]
        operands += [(state[name], VMEM) for name in ("up0", "up1", "up0_panel")]
        operands += [(state[name], ANY) for name in ("moved", "top0", "top1")]
        operands += [(v, ANY) for v in held[i : i + line] + other[i : i + line]]
        aliases = {}
        if "result" in state:
            aliases = {len(operands): 0}
            operands.append((state["result"], ANY))
        count = sizes[i]
        state["result"], _ = run(
            functools.partial(update_kernel, begins[i], line),
            operands,
            [(bf16(rows, cb, nb), ANY), (jax.ShapeDtypeStruct((8, 128), F32), VMEM)],
            scratch=[
                pltpu.VMEM((2, count, nb), BF16), pltpu.VMEM((count, cb, nb), BF16),
                pltpu.VMEM((count, cb, nb), BF16), DMA((2,)), DMA, DMA,
            ],
            aliases=aliases,
            us=5.0, mib=24,
        )

    plan = [(0, gather), (1, join), (3, fresh), (line - 1, old), (3, head), (4, head_here), (4, head_pair), (5, old_here), (5, head_all), (5, scatter), (5, prep0), (5, prep1)]
    for i in range(pieces):
        plan.append((max(6 + i, i + line - 1), functools.partial(update, i)))
    for k in range(last_step + 1):
        step(k)
        while plan and (plan[0][0] <= k or k == last_step):
            plan.pop(0)[1]()
    return state["result"].reshape(matrix.shape)


def solution(mesh):
    placed = (P(None, "prow", None, "pcol"), P(), P(), P())
    return jax.shard_map(
        body, mesh=mesh, in_specs=placed, out_specs=P(None, "prow", None, "pcol"), check_vma=False
    )
```

```python
import functools

import jax
import jax.numpy as jnp
from jax import lax
from jax.experimental import pallas as pl
from jax.experimental.pallas import tpu as pltpu
from jax.sharding import PartitionSpec as P

BF16 = jnp.bfloat16
F32 = jnp.float32
I32 = jnp.int32
SMEM = pl.BlockSpec(memory_space=pltpu.SMEM)
VMEM = pl.BlockSpec(memory_space=pltpu.VMEM)
ANY = pl.BlockSpec(memory_space=pl.ANY)
DMA = pltpu.SemaphoreType.DMA


def dot(a, b):
    return jnp.dot(a, b, preferred_element_type=F32)


def flat(rows):
    return rows.reshape(rows.shape[0], rows.shape[1] * rows.shape[2])


def bf16(*shape):
    return jax.ShapeDtypeStruct(shape, BF16)


def call(kernel, operands, outs, after=(), scratch=(), aliases=None, us=1.0, mib=8):
    count = len(operands)

    def ordered(*refs):
        kernel(*refs[:count], *refs[count + len(after) :])

    return pl.pallas_call(
        ordered,
        out_shape=tuple(shape for shape, _ in outs),
        in_specs=[spec for _, spec in operands] + [ANY] * len(after),
        out_specs=tuple(spec for _, spec in outs),
        scratch_shapes=list(scratch),
        input_output_aliases=aliases or {},
        compiler_params=pltpu.CompilerParams(vmem_limit_bytes=mib * 1024 * 1024),
        cost_estimate=pl.CostEstimate(flops=int(us * 1.1e9), bytes_accessed=0, transcendentals=0),
    )(*[array for array, _ in operands], *after)


def fill_indices(nb, rows, meta, pivots, spread, fetch, join, arrive, goal, hops):
    row, row_devices = meta[0], meta[3]
    chip, chips = row // 2, row_devices // 2
    lanes = spread.shape[2]
    tiles = nb // lanes
    slot = lax.broadcasted_iota(I32, (1, nb), 1)
    pivot0, pivot1 = pivots[0:1, :], pivots[1:2, :]

    def lookup(keys, entry, value):
        parts = [keys[:, t * lanes : (t + 1) * lanes] for t in range(tiles)]

        def add(i, totals):
            begin = pl.multiple_of(i * 8, 8)
            at = begin + lax.broadcasted_iota(I32, (8, lanes), 0)
            here, give = entry(begin, at), value(begin, at)
            return tuple(t + jnp.where(p == here, give, 0) for t, p in zip(totals, parts))

        zero = jnp.zeros((8, lanes), I32)
        totals = lax.fori_loop(0, nb // 8, add, (zero,) * tiles, unroll=8)
        return jnp.concatenate([jnp.sum(t, axis=0, keepdims=True) for t in totals], axis=1)

    def pivot_of(panel):
        return lambda begin, at: spread[panel, pl.ds(begin, 8), :]

    place = lambda begin, at: at + 1
    in_pivots0 = lookup(pivot1, pivot_of(0), place)
    in_pivots1 = lookup(pivot0, pivot_of(1), place)
    top1_in_pivots0 = lookup(nb + slot, pivot_of(0), place)
    over_top1 = lookup(pivot0, lambda begin, at: nb + at, pivot_of(1))
    chained = lookup(nb + in_pivots1 - 1, pivot_of(0), place)

    source0 = pivot0
    source1 = jnp.where(in_pivots0 > 0, in_pivots0 - 1, pivot1)
    second0 = jnp.where(in_pivots1 > 0, jnp.where(chained > 0, chained - 1, nb + in_pivots1 - 1), slot)
    second1 = jnp.where(top1_in_pivots0 > 0, top1_in_pivots0 - 1, nb + slot)
    target0 = jnp.where(over_top1 > 0, over_top1, jnp.where(in_pivots1 > 0, nb + in_pivots1 - 1, pivot0))
    target1 = jnp.where(top1_in_pivots0 > 0, top1_in_pivots0 - 1, pivot1)

    def holder(index):
        return lax.rem(lax.div(index, nb), row_devices)

    def local(index):
        return lax.div(index, nb * row_devices) * nb + lax.rem(index, nb)

    def placed(index):
        mine = (holder(index) == row) & (index >= 2 * nb)
        return jnp.where(mine, local(index), rows)

    for k, (source, second, target) in enumerate(((source0, second0, target0), (source1, second1, target1))):
        from_chip = lax.div(holder(source), 2)
        wanted = jnp.where(from_chip == chip, source, second)
        at = (slice(k, k + 1), slice(None))
        fetch[at] = local(wanted)
        join[at] = jnp.where(holder(wanted) == row, slot, nb)
        arrive[at] = placed(source)
        goal[at] = placed(target)
        hops[at] = lax.rem(chip + chips - from_chip, chips)


def copy_rows(count, target, target_at, origin, origin_at):
    def copy(i, carry):
        target[target_at(i)] = origin[origin_at(i)]
        return carry

    lax.fori_loop(0, count, copy, 0, unroll=16)


def first_kernel(tiles, piece, work, sem):
    load = pltpu.make_async_copy(tiles.at[pl.ds(0, piece.shape[0])], work, sem)
    load.start()
    load.wait()
    piece[...] = flat(work[...])[:, : piece.shape[1]]


def gather_kernel(meta, pivots, spread, tiles, *refs):
    *pieces, loaded, send, keep, block0, join, arrive, goal, hops, fetch, fetch_table, load_sem, table_sem = refs
    nb = send.shape[0]
    rows = tiles.shape[0]
    core = meta[1]
    load = pltpu.make_async_copy(tiles, loaded.at[pl.ds(0, rows)], load_sem)
    load.start()
    fill_indices(nb, rows, meta, pivots, spread, fetch, join, arrive, goal, hops)
    table = pltpu.make_async_copy(fetch, fetch_table, table_sem)
    table.start()
    table.wait()
    load.wait()
    begin = nb
    for piece in pieces:
        end = begin + piece.shape[0]
        piece[...] = flat(loaded[begin:end])[:, :nb]
        begin = end
    copy_rows(nb, send, lambda i: i, loaded, lambda i: fetch_table[1 - core, i])
    copy_rows(nb, keep, lambda i: i, loaded, lambda i: fetch_table[core, i])
    block0[...] = loaded[0:nb]


def join_kernel(meta, join, keep, came, joined, work):
    count = came.shape[0]
    core = meta[1]
    work[0:count] = came[...]
    copy_rows(count, work, lambda i: join[core, i], keep, lambda i: i)
    joined[...] = work[0:count]


def scatter_kernel(meta, arrive, goal, came, came_sibling, old, old_sibling, tiles, out):
    core, chip = meta[1], meta[0] // 2
    count = old.shape[0]
    out[...] = tiles[...]

    def scatter(table, values, k):
        copy_rows(count, out, lambda i: table[k, i], values, lambda i: i)

    @pl.when(chip == 0)
    def _():
        scatter(goal, old, core)
        scatter(goal, old_sibling, 1 - core)

    @pl.when(chip != 0)
    def _():
        scatter(arrive, came, core)
        scatter(arrive, came_sibling, 1 - core)


def relay_kernel(meta, came, *refs):
    *own, sent = refs
    place = lax.div(meta[2], 2)
    for piece in own:

        @pl.when(place == 0)
        def _(piece=piece):
            sent[0 : piece.shape[0]] = piece[...]

    @pl.when(place != 0)
    def _():
        count = min(came.shape[0], sent.shape[0])
        sent[0:count] = came[0:count]


def old_kernel(meta, *refs):
    *choices, old = refs
    for h in range(len(choices) // 2):

        @pl.when(meta[0] // 2 == h)
        def _(h=h):
            old[0] = choices[2 * h][...]
            old[1] = choices[2 * h + 1][...]


def by_place_kernel(meta, *refs):
    out = refs[-1]
    for h, choice in enumerate(refs[:-1]):

        @pl.when(lax.div(meta[2], 2) == h)
        def _(choice=choice):
            out[...] = choice[0 : out.shape[0]]


def head_kernel(meta, fresh, fresh_sibling, head):
    needed = 1 - lax.rem(meta[2], 2)
    half, nb = head.shape
    at = pl.ds(pl.multiple_of(meta[1] * half, half), half)

    @pl.when(meta[1] == needed)
    def _():
        head[...] = fresh[at, :nb]

    @pl.when(meta[1] != needed)
    def _():
        head[...] = fresh_sibling[at, :nb]


def choose(hop, choices):
    value = flat(choices[0]).astype(F32)
    for h, other in enumerate(choices[1:], 1):
        value = jnp.where(hop == h, flat(other).astype(F32), value)
    return value.astype(BF16)


def fresh_kernel(chips, meta, hops, *refs):
    choices, (fresh, brought) = refs[:chips], refs[chips:]
    nb = fresh.shape[0]
    core, chip = meta[1], meta[0] // 2
    hop = jnp.broadcast_to(hops[pl.ds(core, 1), :], (8, nb)).T[:, 0:1]
    fresh[...] = choose(hop, [c[...] for c in choices])
    if chips == 1:
        brought[...] = choices[0][...]
    for h in range(1, chips):

        @pl.when((chip == h) | ((chip == 0) & (h == 1)))
        def _(h=h):
            brought[...] = choices[h][...]


def raw(columns, nb):
    joined = jnp.concatenate(columns, axis=1)
    return joined.reshape(joined.shape[0], len(columns), nb)


def prep0_kernel(meta, lower, fresh, fresh_sibling, up0, top, work):
    core, column = meta[1], meta[2]
    nb = fresh.shape[0]

    @pl.when(core == 0)
    def _():
        work[...] = fresh[...]

    @pl.when(core != 0)
    def _():
        work[...] = fresh_sibling[...]

    shown = []
    for j in range(work.shape[1] // nb):
        cols = slice(j * nb, (j + 1) * nb)
        product = dot(lower[0], work[:, cols])
        show = product
        if j == 0:
            show = jnp.where(column == 0, work[:, cols].astype(F32), product)
            product = jnp.where(column == 0, 0.0, product)
        up0[:, cols] = product.astype(BF16)
        shown.append(show.astype(BF16))
    top[...] = raw(shown, nb)


def prep1_kernel(meta, lower, upper, fresh, fresh_sibling, up0, *refs):
    mine, mine_sibling, other, other_sibling, up1, up0_panel, top, work, head = refs
    core, column = meta[1], meta[2]
    side = lax.rem(column, 2)
    nb, half = fresh.shape[0], mine.shape[0]
    for which, who, piece in (
        (1 - side, core, mine), (1 - side, 1 - core, mine_sibling), (side, core, other), (side, 1 - core, other_sibling)
    ):
        head[which, pl.ds(pl.multiple_of(who * half, half), half)] = piece[...]

    @pl.when(core == 1)
    def _():
        work[...] = fresh[...]

    @pl.when(core != 1)
    def _():
        work[...] = fresh_sibling[...]

    up0_panel[...] = dot(lower[0], head[0]).astype(BF16)
    factor = dot(head[1], upper[0]).astype(BF16)
    in_panel, next_panel = column == 0, column == 1
    shown = []
    for j in range(work.shape[1] // nb):
        cols = slice(j * nb, (j + 1) * nb)
        updated = (work[:, cols].astype(F32) - dot(factor, up0[:, cols])).astype(BF16)
        last = dot(lower[1], updated)
        show = last
        if j == 0:
            show = jnp.where(next_panel, updated.astype(F32), show)
            show = jnp.where(in_panel, factor.astype(F32), show)
            last = jnp.where(in_panel | next_panel, 0.0, last)
        up1[:, cols] = last.astype(BF16)
        shown.append(show.astype(BF16))
    top[...] = raw(shown, nb)


def update_kernel(
    begin, meta, goal, old, old_sibling, upper, up0, up1, up0_panel, tiles, top0, top1, *rest
):
    held, other = rest[:2]
    out, token, panels, block, result, panel_sem, block_sem, out_sem = rest[-8:]
    row, core, column = meta[0], meta[1], meta[2]
    side = lax.rem(column, 2)
    count, cb, nb = block.shape
    rows_of = pl.ds(begin, count)

    def panel_copy(which):
        return pltpu.make_async_copy(
            (held, other)[which], panels.at[lax.rem(side + which, 2)], panel_sem.at[which]
        )

    load = pltpu.make_async_copy(tiles.at[rows_of], block, block_sem)
    load.start()
    panel_copy(0).start()
    panel_copy(1).start()

    def arrived():
        panel_copy(0).wait()
        panel_copy(1).wait()

    def from_factors():
        here = begin + lax.broadcasted_iota(I32, (count, nb), 0)
        pick = jnp.where(here == goal[pl.ds(core, 1), :], 1.0, 0.0)
        pick_sibling = jnp.where(here == goal[pl.ds(1 - core, 1), :], 1.0, 0.0)
        moved = jnp.sum(pick + pick_sibling, axis=1, keepdims=True) > 0.5
        pick, pick_sibling = pick.astype(BF16), pick_sibling.astype(BF16)
        arrived()
        whole = []
        for k in range(2):
            which = lax.rem(k + side, 2)
            brought = dot(pick, old[which]) + dot(pick_sibling, old_sibling[which])
            whole.append(jnp.where(moved, brought, panels[k].astype(F32)))
        factor0 = dot(whole[0].astype(BF16), upper[0]).astype(BF16)
        below = (whole[1] - dot(factor0, up0_panel[...])).astype(BF16)
        factor1 = dot(below, upper[1]).astype(BF16)
        load.wait()
        values = flat(block[...])
        columns = []
        for j in range(cb):
            cols = slice(j * nb, (j + 1) * nb)
            value = values[:, cols].astype(F32) - dot(factor0, up0[:, cols])
            value = value.astype(BF16).astype(F32) - dot(factor1, up1[:, cols])
            if j == 0:
                value = jnp.where(column == 0, factor0.astype(F32), value)
                value = jnp.where(column == 1, factor1.astype(F32), value)
            columns.append(value.astype(BF16))
        result[...] = raw(columns, nb)

    def from_top(top):
        arrived()
        load.wait()
        copy = pltpu.make_async_copy(top.at[rows_of], result, block_sem)
        copy.start()
        copy.wait()

    if begin < nb:
        pl.when(row == 0)(lambda: from_top(top0))
        pl.when(row == 1)(lambda: from_top(top1))
        pl.when(row >= 2)(from_factors)
    else:
        from_factors()
    store = pltpu.make_async_copy(result, out.at[rows_of], out_sem)
    store.start()
    token[...] = jnp.zeros(token.shape, F32)
    store.wait()


def body(matrix, pivots, lower, upper):
    rb, nb, cb, _ = matrix.shape
    rows = rb * nb
    sizes = [nb] * (rb - 1) + [nb // 2] * 2
    begins = [sum(sizes[:i]) for i in range(len(sizes))]
    pieces = len(sizes)
    row_devices = lax.axis_size("prow")
    col_devices = lax.axis_size("pcol")
    chips, line = row_devices // 2, col_devices // 2
    row = lax.axis_index("prow").astype(I32)
    column = lax.axis_index("pcol").astype(I32)
    meta = jnp.stack([row, row % 2, column, jnp.int32(row_devices)])
    tiles = matrix.reshape(rows, cb, nb)

    def to_sibling(value):
        return lax.ppermute(value, "prow", [(r, r ^ 1) for r in range(row_devices)])

    def to_neighbour(value):
        return lax.ppermute(value, "pcol", [(c, c ^ 1) for c in range(col_devices)])

    def to_chip(value, h):
        return lax.ppermute(value, "prow", [(r, (r + 2 * h) % row_devices) for r in range(row_devices)])

    def along(value, begin):
        pairs = [(p, (p + (1 if (p - begin) % 2 == 0 else -1)) % line) for p in range(line)]
        return lax.ppermute(value, "pcol", [(2 * p + y, 2 * q + y) for p, q in pairs for y in range(2)])

    order = []

    def run(kernel, operands, outs, also=(), **kwargs):
        after = tuple(order[-1:]) + tuple(also)
        results = call(kernel, operands, outs, after=after, **kwargs)
        order.append(results[-1])
        return results

    lag = 2
    behind = lag * ((line - 2) // 2)
    even_turns = pieces + behind
    odd_turns = pieces + lag * ((line - 3) // 2) if line > 2 else 0
    last_turn = pieces + behind

    def piece_out(i):
        return (bf16(sizes[i], nb), VMEM)

    def even_out(k):
        return (bf16(max(sizes[k - h] for h in range(0, behind + 1, lag) if 0 <= k - h < pieces), nb), VMEM)

    own, even_came, odd_came, held, other = [], [], [], [], []
    state = {}
    awaited = []

    def wait(k, value):
        awaited.append((k, value))
        return value

    def due(k):
        values = [value for at, value in awaited if at <= k]
        awaited[:] = [entry for entry in awaited if entry[0] > k]
        return values

    def turn(k):
        state["turn"] = k
        if k == 0:
            own.extend(run(
                first_kernel, [(tiles, ANY)], [piece_out(0)],
                scratch=[pltpu.VMEM((sizes[0], cb, nb), BF16), DMA], mib=60,
            ))
        if k < even_turns:
            if k == 0:
                value = own[0]
            else:
                also = due(k)
                operands = [(meta, SMEM)]
                if k >= lag and odd_turns:
                    operands += [(odd_came[k - lag], VMEM)] + [(v, VMEM) for v in own[k : k + 1]]
                else:
                    operands += [(own[k], VMEM), (own[k], VMEM)]
                (value,) = run(relay_kernel, operands, [even_out(k)], also, us=0.2 if k in (2, 4, 5) else 12.0)
            even_came.append(wait(k + 1, along(value, 0)))
        if 0 < k <= odd_turns:
            carried = [sizes[k - 1 - h] for h in range(0, behind, lag) if 0 <= k - 1 - h < pieces]
            odd_came.append(wait(k + 1, along(even_came[k - 1][: max(carried)], 1)))
        m = k - 1 - behind
        if 0 <= m < pieces:
            choices = [own[m]]
            for p in range(1, line):
                choices.append((odd_came, even_came)[p % 2][m + lag * ((p - 1) // 2)])
            (value,) = run(
                by_place_kernel, [(meta, SMEM)] + [(c, VMEM) for c in choices], [piece_out(m)],
                due(k) if k >= even_turns else (), us=0.2 if k in (2, 4, 5) else 12.0 if k >= even_turns else 0.6,
            )
            held.append(value)
            other.append(wait(k + 1, to_neighbour(value)))

    def gather():
        lanes = min(nb, 128)
        spread = jnp.broadcast_to(pivots[:, :, None], (2, nb, lanes))
        table = jax.ShapeDtypeStruct((2, nb), I32)
        results = run(
            gather_kernel,
            [(meta, SMEM), (pivots, VMEM), (spread, VMEM), (tiles, ANY)],
            [piece_out(i) for i in range(1, pieces)] + [(bf16(rows + 8, cb, nb), VMEM)]
            + [(bf16(nb, cb, nb), VMEM)] * 3 + [(table, VMEM)] * 4,
            scratch=[pltpu.VMEM((2, nb), I32), pltpu.SMEM((2, nb), I32), DMA, DMA],
            us=8.0, mib=20,
        )
        own.extend(results[: pieces - 1])
        state["loaded"], send, *rest = results[pieces - 1 :]
        state.update(zip(("keep", "block0", "join", "arrive", "goal", "hops"), rest))
        state["sent"] = to_sibling(send)
        state["block0_sibling"] = wait(state["turn"] + 2, to_sibling(state["block0"]))

    def join():
        (joined,) = run(
            join_kernel,
            [(meta, SMEM), (state["join"], SMEM), (state["keep"], VMEM), (state["sent"], VMEM)],
            [(bf16(nb, cb, nb), VMEM)],
            scratch=[pltpu.VMEM((nb + 8, cb, nb), BF16)],
            us=2.0,
        )
        state["choices"] = [joined] + [wait(state["turn"] + 2, to_chip(joined, h)) for h in range(1, chips)]

    def fresh():
        new, brought = run(
            functools.partial(fresh_kernel, chips),
            [(meta, SMEM), (state["hops"], VMEM)] + [(c, VMEM) for c in state["choices"]],
            [(bf16(nb, cb * nb), VMEM), (bf16(nb, cb, nb), VMEM)],
            us=2.0, mib=16,
        )
        state["fresh"] = (new, wait(state["turn"] + 1, to_sibling(new)))
        state["brought"] = (brought, wait(state["turn"] + 1, to_sibling(brought)))

    def head():
        (mine,) = run(
            head_kernel, [(meta, SMEM)] + [(v, VMEM) for v in state["fresh"]], [(bf16(nb // 2, nb), VMEM)], us=0.1
        )
        state["head"] = [mine] + [
            wait(state["turn"] + 1, lax.ppermute(mine, "pcol", [(0, 2 * h), (1, 2 * h + 1)])) for h in range(1, line)
        ]

    def head_here():
        (mine,) = run(
            by_place_kernel, [(meta, SMEM)] + [(v, VMEM) for v in state["head"]], [(bf16(nb // 2, nb), VMEM)]
        )
        swapped = to_neighbour(mine)
        state["heads"] = [mine, to_sibling(mine), swapped, to_sibling(swapped)]
        wait(state["turn"] + 1, state["heads"][1])
        wait(state["turn"] + 1, state["heads"][3])

    def old_here():
        first = [(held[0], other[0])]
        first += zip(state["held_x"], state["other_x"])
        (mine,) = run(
            old_kernel, [(meta, SMEM)] + [(v, VMEM) for pair in first for v in pair], [(bf16(2, nb, nb), VMEM)],
            us=0.6,
        )
        state["old"] = (mine, wait(state["turn"] + 1, to_sibling(mine)))

    def old_held():
        state["held_x"] = [wait(state["turn"] + 3, to_chip(held[0], h)) for h in range(1, chips)]

    def old_other():
        state["other_x"] = [wait(state["turn"] + 2, to_chip(other[0], h)) for h in range(1, chips)]

    def scatter():
        sources = state["brought"] + (state["block0"], state["block0_sibling"], state["loaded"])
        (state["moved"],) = run(
            scatter_kernel,
            [(meta, SMEM), (state["arrive"], SMEM), (state["goal"], SMEM)] + [(v, VMEM) for v in sources],
            [(bf16(rows + 8, cb, nb), VMEM)],
            us=0.1, mib=24,
        )

    def prep0():
        state["up0"], state["top0"] = run(
            prep0_kernel,
            [(meta, SMEM), (lower, VMEM)] + [(v, VMEM) for v in state["fresh"]],
            [(bf16(nb, cb * nb), VMEM), (bf16(nb, cb, nb), VMEM)],
            scratch=[pltpu.VMEM((nb, cb * nb), BF16)],
            us=0.1, mib=16,
        )

    def prep1():
        state["up1"], state["up0_panel"], state["top1"] = run(
            prep1_kernel,
            [(meta, SMEM), (lower, VMEM), (upper, VMEM)] + [(v, VMEM) for v in state["fresh"]]
            + [(state["up0"], VMEM)] + [(v, VMEM) for v in state["heads"]],
            [(bf16(nb, cb * nb), VMEM), (bf16(nb, nb), VMEM), (bf16(nb, cb, nb), VMEM)],
            scratch=[pltpu.VMEM((nb, cb * nb), BF16), pltpu.VMEM((2, nb, nb), BF16)],
            us=3.5, mib=16,
        )

    def update(i):
        operands = [(meta, SMEM), (state["goal"], VMEM)] + [(v, VMEM) for v in state["old"]] + [(upper, VMEM)]
        operands += [(state[name], VMEM) for name in ("up0", "up1", "up0_panel")]
        operands += [(state[name], ANY) for name in ("moved", "top0", "top1")]
        operands += [(held[i], ANY), (other[i], ANY)]
        aliases = {}
        if "result" in state:
            aliases = {len(operands): 0}
            operands.append((state["result"], ANY))
        count = sizes[i]
        state["result"], _ = run(
            functools.partial(update_kernel, begins[i]),
            operands,
            [(bf16(rows, cb, nb), ANY), (jax.ShapeDtypeStruct((8, 128), F32), VMEM)],
            scratch=[
                pltpu.VMEM((2, count, nb), BF16), pltpu.VMEM((count, cb, nb), BF16),
                pltpu.VMEM((count, cb, nb), BF16), DMA((2,)), DMA, DMA,
            ],
            aliases=aliases,
            us=5.0, mib=24,
        )

    plan = [(0, gather), (1, join), (behind + 1, old_held), (3, fresh), (4, head), (behind + 2, old_other), (4, scatter), (5, head_here), (5, prep0), (6, old_here), (6, prep1)]
    for i in range(pieces):
        plan.append((max(6 + i // 2, i + behind + 2), functools.partial(update, i)))
    for k in range(last_turn + 1):
        turn(k)
        while plan and (plan[0][0] <= k or k == last_turn):
            plan.pop(0)[1]()
    return state["result"].reshape(matrix.shape)


def solution(mesh):
    placed = (P(None, "prow", None, "pcol"), P(), P(), P())
    return jax.shard_map(
        body, mesh=mesh, in_specs=placed, out_specs=P(None, "prow", None, "pcol"), check_vma=False
    )
```

```python
import functools

import jax
import jax.numpy as jnp
from jax import lax
from jax.experimental import pallas as pl
from jax.experimental.pallas import tpu as pltpu
from jax.sharding import PartitionSpec as P

BF16 = jnp.bfloat16
F32 = jnp.float32
I32 = jnp.int32
SMEM = pl.BlockSpec(memory_space=pltpu.SMEM)
VMEM = pl.BlockSpec(memory_space=pltpu.VMEM)
ANY = pl.BlockSpec(memory_space=pl.ANY)
DMA = pltpu.SemaphoreType.DMA


def dot(a, b):
    return jnp.dot(a, b, preferred_element_type=F32)


def flat(rows):
    return rows.reshape(rows.shape[0], rows.shape[1] * rows.shape[2])


def bf16(*shape):
    return jax.ShapeDtypeStruct(shape, BF16)


def call(kernel, operands, outs, after=(), scratch=(), aliases=None, us=1.0, mib=8):
    count = len(operands)

    def ordered(*refs):
        kernel(*refs[:count], *refs[count + len(after) :])

    return pl.pallas_call(
        ordered,
        out_shape=tuple(shape for shape, _ in outs),
        in_specs=[spec for _, spec in operands] + [ANY] * len(after),
        out_specs=tuple(spec for _, spec in outs),
        scratch_shapes=list(scratch),
        input_output_aliases=aliases or {},
        compiler_params=pltpu.CompilerParams(vmem_limit_bytes=mib * 1024 * 1024),
        cost_estimate=pl.CostEstimate(flops=int(us * 1.1e9), bytes_accessed=0, transcendentals=0),
    )(*[array for array, _ in operands], *after)


def fill_indices(nb, rows, meta, pivots, spread, fetch, join, arrive, goal, hops):
    row, row_devices = meta[0], meta[3]
    chip, chips = row // 2, row_devices // 2
    lanes = spread.shape[2]
    tiles = nb // lanes
    slot = lax.broadcasted_iota(I32, (1, nb), 1)
    pivot0, pivot1 = pivots[0:1, :], pivots[1:2, :]

    def lookup(keys, entry, value):
        parts = [keys[:, t * lanes : (t + 1) * lanes] for t in range(tiles)]

        def add(i, totals):
            begin = pl.multiple_of(i * 8, 8)
            at = begin + lax.broadcasted_iota(I32, (8, lanes), 0)
            here, give = entry(begin, at), value(begin, at)
            return tuple(t + jnp.where(p == here, give, 0) for t, p in zip(totals, parts))

        zero = jnp.zeros((8, lanes), I32)
        totals = lax.fori_loop(0, nb // 8, add, (zero,) * tiles, unroll=8)
        return jnp.concatenate([jnp.sum(t, axis=0, keepdims=True) for t in totals], axis=1)

    def pivot_of(panel):
        return lambda begin, at: spread[panel, pl.ds(begin, 8), :]

    place = lambda begin, at: at + 1
    in_pivots0 = lookup(pivot1, pivot_of(0), place)
    in_pivots1 = lookup(pivot0, pivot_of(1), place)
    top1_in_pivots0 = lookup(nb + slot, pivot_of(0), place)
    over_top1 = lookup(pivot0, lambda begin, at: nb + at, pivot_of(1))
    chained = lookup(nb + in_pivots1 - 1, pivot_of(0), place)

    source0 = pivot0
    source1 = jnp.where(in_pivots0 > 0, in_pivots0 - 1, pivot1)
    second0 = jnp.where(in_pivots1 > 0, jnp.where(chained > 0, chained - 1, nb + in_pivots1 - 1), slot)
    second1 = jnp.where(top1_in_pivots0 > 0, top1_in_pivots0 - 1, nb + slot)
    target0 = jnp.where(over_top1 > 0, over_top1, jnp.where(in_pivots1 > 0, nb + in_pivots1 - 1, pivot0))
    target1 = jnp.where(top1_in_pivots0 > 0, top1_in_pivots0 - 1, pivot1)

    def holder(index):
        return lax.rem(lax.div(index, nb), row_devices)

    def local(index):
        return lax.div(index, nb * row_devices) * nb + lax.rem(index, nb)

    def placed(index):
        mine = (holder(index) == row) & (index >= 2 * nb)
        return jnp.where(mine, local(index), rows)

    for k, (source, second, target) in enumerate(((source0, second0, target0), (source1, second1, target1))):
        from_chip = lax.div(holder(source), 2)
        wanted = jnp.where(from_chip == chip, source, second)
        at = (slice(k, k + 1), slice(None))
        fetch[at] = local(wanted)
        join[at] = jnp.where(holder(wanted) == row, lax.rem(slot, nb // 2), nb // 2)
        arrive[at] = placed(source)
        goal[at] = placed(target)
        hops[at] = lax.rem(chip + chips - from_chip, chips)


def copy_rows(count, target, target_at, origin, origin_at):
    def copy(i, carry):
        target[target_at(i)] = origin[origin_at(i)]
        return carry

    lax.fori_loop(0, count, copy, 0, unroll=16)


def first_kernel(tiles, piece, work, sem):
    load = pltpu.make_async_copy(tiles.at[pl.ds(0, piece.shape[0])], work, sem)
    load.start()
    load.wait()
    piece[...] = flat(work[...])[:, : piece.shape[1]]


def gather_kernel(meta, pivots, spread, tiles, *refs):
    *pieces, loaded, send, keep, block0, join, arrive, goal, hops, fetch, fetch_table, load_sem, table_sem = refs
    nb = send.shape[0]
    rows = tiles.shape[0]
    core = meta[1]
    load = pltpu.make_async_copy(tiles, loaded.at[pl.ds(0, rows)], load_sem)
    load.start()
    fill_indices(nb, rows, meta, pivots, spread, fetch, join, arrive, goal, hops)
    table = pltpu.make_async_copy(fetch, fetch_table, table_sem)
    table.start()
    table.wait()
    load.wait()
    begin = nb
    for piece in pieces:
        end = begin + piece.shape[0]
        piece[...] = flat(loaded[begin:end])[:, :nb]
        begin = end
    half, side = nb // 2, lax.rem(meta[2], 2)
    for turn, b in enumerate((1 - side, side)):
        to = lambda i, turn=turn: turn * half + i
        copy_rows(half, send, to, loaded, lambda i, b=b: fetch_table[b, (1 - core) * half + i])
        copy_rows(half, keep, to, loaded, lambda i, b=b: fetch_table[b, core * half + i])
    block0[...] = loaded[0:nb]


def join_kernel(meta, join, keep, came, joined0, joined1, work0, work1):
    half = joined0.shape[0]
    core, side = meta[1], lax.rem(meta[2], 2)
    for turn, (b, work, joined) in enumerate(((1 - side, work0, joined0), (side, work1, joined1))):
        work[0:half] = came[turn * half : (turn + 1) * half]
        copy_rows(
            half, work, lambda i, b=b: join[b, core * half + i], keep, lambda i, turn=turn: turn * half + i
        )
        joined[...] = work[0:half]


def scatter_kernel(meta, arrive, goal, *refs):
    *came, old, old_sibling, tiles, out = refs
    core, side, chip = meta[1], lax.rem(meta[2], 2), meta[0] // 2
    nb = old.shape[0]
    half = nb // 2
    out[...] = tiles[...]

    @pl.when(chip == 0)
    def _():
        copy_rows(nb, out, lambda i: goal[core, i], old, lambda i: i)
        copy_rows(nb, out, lambda i: goal[1 - core, i], old_sibling, lambda i: i)

    @pl.when(chip != 0)
    def _():
        for turn, b in enumerate((1 - side, side)):
            for values, who in ((came[2 * turn], core), (came[2 * turn + 1], 1 - core)):
                copy_rows(half, out, lambda i, b=b, who=who: arrive[b, who * half + i], values, lambda i: i)


def relay_kernel(meta, came, *refs):
    *own, held = refs
    place = lax.div(meta[2], 2)
    for piece in own:

        @pl.when(place == 0)
        def _(piece=piece):
            held[0 : piece.shape[0]] = piece[...]

    @pl.when(place != 0)
    def _():
        count = min(came.shape[0], held.shape[0])
        held[0:count] = came[0:count]


def old_kernel(line, meta, *refs):
    *choices, old = refs
    for h in range(line):

        @pl.when(lax.div(meta[2], 2) == h)
        def _(h=h):
            old[...] = choices[h][0 : old.shape[0]]


def by_chip_kernel(meta, *refs):
    *choices, out = refs
    for h in range(len(choices) // 2):

        @pl.when(meta[0] // 2 == h)
        def _(h=h):
            out[0] = choices[2 * h][...]
            out[1] = choices[2 * h + 1][...]


def choose(hop, choices):
    value = flat(choices[0]).astype(F32)
    for h, other in enumerate(choices[1:], 1):
        value = jnp.where(hop == h, flat(other).astype(F32), value)
    return value.astype(BF16)


def fresh_kernel(turn, chips, meta, hops, *refs):
    choices, (fresh, brought, *head) = refs[:chips], refs[chips:]
    half = fresh.shape[0]
    core, side, chip = meta[1], lax.rem(meta[2], 2), meta[0] // 2
    b = side if turn else 1 - side
    hop = jnp.broadcast_to(hops[pl.ds(b, 1), :], (8, 2 * half)).T[:, 0:1]
    hop = jnp.where(core == 0, hop[:half], hop[half:])
    fresh[...] = choose(hop, [c[...] for c in choices])
    if head:
        part, nb = head[0].shape
        head[0][...] = fresh[pl.ds(pl.multiple_of(chip * part, part), part), :nb]
    if chips == 1:
        brought[...] = choices[0][...]
    for h in range(1, chips):

        @pl.when((chip == h) | ((chip == 0) & (h == 1)))
        def _(h=h):
            brought[...] = choices[h][...]


def assemble(meta, b, fresh, work):
    core, side = meta[1], lax.rem(meta[2], 2)
    half = work.shape[0] // 2
    for turn, which in enumerate((1 - side, side)):

        @pl.when(which == b)
        def _(turn=turn):
            work[pl.ds(pl.multiple_of(core * half, half), half)] = fresh[2 * turn][...]
            work[pl.ds(pl.multiple_of((1 - core) * half, half), half)] = fresh[2 * turn + 1][...]


def raw(columns, nb):
    joined = jnp.concatenate(columns, axis=1)
    return joined.reshape(joined.shape[0], len(columns), nb)


def prep0_kernel(meta, lower, *refs):
    *fresh, up0, top, work = refs
    column = meta[2]
    nb = work.shape[0]
    assemble(meta, 0, fresh, work)
    shown = []
    for j in range(work.shape[1] // nb):
        cols = slice(j * nb, (j + 1) * nb)
        product = dot(lower[0], work[:, cols])
        show = product
        if j == 0:
            show = jnp.where(column == 0, work[:, cols].astype(F32), product)
            product = jnp.where(column == 0, 0.0, product)
        up0[:, cols] = product.astype(BF16)
        shown.append(show.astype(BF16))
    top[...] = raw(shown, nb)


def prep1_kernel(meta, lower, upper, up0, heads, *refs):
    *fresh, up1, up0_panel, top, work, head = refs
    column = meta[2]
    row_devices, _, part, nb = heads.shape
    for r in range(row_devices):
        at = (r % 2 * (row_devices // 2) + r // 2) * part
        head[1, at : at + part] = heads[r, 0]
        head[0, at : at + part] = heads[r, 1]
    assemble(meta, 1, fresh, work)
    up0_panel[...] = dot(lower[0], head[0]).astype(BF16)
    factor = dot(head[1], upper[0]).astype(BF16)
    in_panel, next_panel = column == 0, column == 1
    shown = []
    for j in range(work.shape[1] // nb):
        cols = slice(j * nb, (j + 1) * nb)
        updated = (work[:, cols].astype(F32) - dot(factor, up0[:, cols])).astype(BF16)
        last = dot(lower[1], updated)
        show = last
        if j == 0:
            show = jnp.where(next_panel, updated.astype(F32), show)
            show = jnp.where(in_panel, factor.astype(F32), show)
            last = jnp.where(in_panel | next_panel, 0.0, last)
        up1[:, cols] = last.astype(BF16)
        shown.append(show.astype(BF16))
    top[...] = raw(shown, nb)


def update_kernel(
    begin, line, meta, goal, old, old_sibling, upper, up0, up1, up0_panel, tiles, top0, top1, *rest
):
    held, other = rest[:line], rest[line : 2 * line]
    out, token, panels, block, result, panel_sem, block_sem, out_sem = rest[-8:]
    row, core, column = meta[0], meta[1], meta[2]
    side, place = lax.rem(column, 2), lax.div(column, 2)
    count, cb, nb = block.shape
    rows_of = pl.ds(begin, count)

    def panel_copy(h, which):
        source = (held, other)[which][h].at[pl.ds(0, count)]
        return pltpu.make_async_copy(source, panels.at[lax.rem(side + which, 2)], panel_sem.at[which])

    load = pltpu.make_async_copy(tiles.at[rows_of], block, block_sem)
    load.start()
    for h in range(line):

        @pl.when(place == h)
        def _(h=h):
            panel_copy(h, 0).start()
            panel_copy(h, 1).start()

    def arrived():
        panel_copy(0, 0).wait()
        panel_copy(0, 1).wait()

    def from_factors():
        here = begin + lax.broadcasted_iota(I32, (count, nb), 0)
        pick = jnp.where(here == goal[pl.ds(core, 1), :], 1.0, 0.0)
        pick_sibling = jnp.where(here == goal[pl.ds(1 - core, 1), :], 1.0, 0.0)
        moved = jnp.sum(pick + pick_sibling, axis=1, keepdims=True) > 0.5
        pick, pick_sibling = pick.astype(BF16), pick_sibling.astype(BF16)
        arrived()
        whole = []
        for k in range(2):
            which = lax.rem(k + side, 2)
            brought = dot(pick, old[which]) + dot(pick_sibling, old_sibling[which])
            whole.append(jnp.where(moved, brought, panels[k].astype(F32)))
        factor0 = dot(whole[0].astype(BF16), upper[0]).astype(BF16)
        below = (whole[1] - dot(factor0, up0_panel[...])).astype(BF16)
        factor1 = dot(below, upper[1]).astype(BF16)
        load.wait()
        values = flat(block[...])
        columns = []
        for j in range(cb):
            cols = slice(j * nb, (j + 1) * nb)
            value = values[:, cols].astype(F32) - dot(factor0, up0[:, cols])
            value = value.astype(BF16).astype(F32) - dot(factor1, up1[:, cols])
            if j == 0:
                value = jnp.where(column == 0, factor0.astype(F32), value)
                value = jnp.where(column == 1, factor1.astype(F32), value)
            columns.append(value.astype(BF16))
        result[...] = raw(columns, nb)

    def from_top(top):
        arrived()
        load.wait()
        copy = pltpu.make_async_copy(top.at[rows_of], result, block_sem)
        copy.start()
        copy.wait()

    if begin < nb:
        pl.when(row == 0)(lambda: from_top(top0))
        pl.when(row == 1)(lambda: from_top(top1))
        pl.when(row >= 2)(from_factors)
    else:
        from_factors()
    store = pltpu.make_async_copy(result, out.at[rows_of], out_sem)
    store.start()
    token[...] = jnp.zeros(token.shape, F32)
    store.wait()


def body(matrix, pivots, lower, upper):
    rb, nb, cb, _ = matrix.shape
    rows = rb * nb
    sizes = [nb] * (rb - 1) + [nb // 2] * 2
    begins = [sum(sizes[:i]) for i in range(len(sizes))]
    pieces = len(sizes)
    row_devices = lax.axis_size("prow")
    col_devices = lax.axis_size("pcol")
    chips, line = row_devices // 2, col_devices // 2
    row = lax.axis_index("prow").astype(I32)
    column = lax.axis_index("pcol").astype(I32)
    meta = jnp.stack([row, row % 2, column, jnp.int32(row_devices)])
    tiles = matrix.reshape(rows, cb, nb)

    def to_sibling(value):
        return lax.ppermute(value, "prow", [(r, r ^ 1) for r in range(row_devices)])

    def to_neighbour(value):
        return lax.ppermute(value, "pcol", [(c, c ^ 1) for c in range(col_devices)])

    def to_chip(value, h):
        return lax.ppermute(value, "prow", [(r, (r + 2 * h) % row_devices) for r in range(row_devices)])

    def to_next(value):
        return lax.ppermute(value, "pcol", [(c, c + 2) for c in range(col_devices - 2)])

    order = []

    def run(kernel, operands, outs, also=(), **kwargs):
        after = tuple(order[-1:]) + tuple(also)
        results = call(kernel, operands, outs, after=after, **kwargs)
        order.append(results[-1])
        return results

    last_step = pieces + line - 2

    def piece_out(i):
        return (bf16(sizes[i], nb), VMEM)

    def step_out(k):
        return (bf16(max(sizes[k - p] for p in range(line) if 0 <= k - p < pieces), nb), VMEM)

    own, held, other = [], [], []
    state = {}

    def step(k):
        if k == 0:
            own.extend(run(
                first_kernel, [(tiles, ANY)], [piece_out(0)],
                scratch=[pltpu.VMEM((sizes[0], cb, nb), BF16), DMA], mib=60,
            ))
            value = own[0]
        else:
            also = [other[k - 1]] + state.pop('awaited', [])
            operands = [(meta, SMEM), (state["came"], VMEM)] + [(v, VMEM) for v in own[k : k + 1]]
            (value,) = run(relay_kernel, operands, [step_out(k)], also, us=0.2 if k in (2, 3, 5) else 12.0)
        held.append(value)
        if k < last_step:
            state["came"] = to_next(value)
        other.append(to_neighbour(value))

    def gather():
        lanes = min(nb, 128)
        spread = jnp.broadcast_to(pivots[:, :, None], (2, nb, lanes))
        table = jax.ShapeDtypeStruct((2, nb), I32)
        results = run(
            gather_kernel,
            [(meta, SMEM), (pivots, VMEM), (spread, VMEM), (tiles, ANY)],
            [piece_out(i) for i in range(1, pieces)] + [(bf16(rows + 8, cb, nb), VMEM)]
            + [(bf16(nb, cb, nb), VMEM)] * 3 + [(table, VMEM)] * 4,
            scratch=[pltpu.VMEM((2, nb), I32), pltpu.SMEM((2, nb), I32), DMA, DMA],
            us=8.0, mib=20,
        )
        own.extend(results[: pieces - 1])
        state["loaded"], send, *rest = results[pieces - 1 :]
        state.update(zip(("keep", "block0", "join", "arrive", "goal", "hops"), rest))
        state["sent"] = to_sibling(send)
        state["block0_sibling"] = to_sibling(state["block0"])

    half = nb // 2
    part = half // chips

    def join():
        joined = run(
            join_kernel,
            [(meta, SMEM), (state["join"], SMEM), (state["keep"], VMEM), (state["sent"], VMEM)],
            [(bf16(half, cb, nb), VMEM)] * 2,
            scratch=[pltpu.VMEM((half + 8, cb, nb), BF16)] * 2,
            us=2.0,
        )
        state["choices"] = [[v] + [to_chip(v, h) for h in range(1, chips)] for v in joined]
        state["fresh"], state["brought"] = [], []

    def fresh(turn):
        new, brought, *head = run(
            functools.partial(fresh_kernel, turn, chips),
            [(meta, SMEM), (state["hops"], VMEM)] + [(c, VMEM) for c in state["choices"][turn]],
            [(bf16(half, cb * nb), VMEM), (bf16(half, cb, nb), VMEM)]
            + [(bf16(part, nb), VMEM)] * (1 - turn),
            us=1.5, mib=16,
        )
        state["fresh"] += [new, to_sibling(new)]
        state["brought"] += [brought, to_sibling(brought)]
        if head:
            parts = lax.all_gather(head[0], "pcol")[:2]
            state["heads"] = lax.all_gather(parts, "prow")

    def old(values, name):
        operands = [(meta, SMEM)] + [(v, VMEM) for v in values[:line]]
        (mine,) = run(functools.partial(old_kernel, line), operands, [(bf16(nb, nb), VMEM)], us=0.1)
        state[name] = [mine] + [to_chip(mine, h) for h in range(1, chips)]
        state["awaited"] = state.get("awaited", []) + state[name][1:]

    def old_here():
        choices = [v for pair in zip(state["old_held"], state["old_other"]) for v in pair]
        (mine,) = run(
            by_chip_kernel, [(meta, SMEM)] + [(v, VMEM) for v in choices], [(bf16(2, nb, nb), VMEM)], us=0.1
        )
        state["old"] = (mine, to_sibling(mine))

    def scatter():
        sources = state["brought"] + [state["block0"], state["block0_sibling"], state["loaded"]]
        (state["moved"],) = run(
            scatter_kernel,
            [(meta, SMEM), (state["arrive"], SMEM), (state["goal"], SMEM)] + [(v, VMEM) for v in sources],
            [(bf16(rows + 8, cb, nb), VMEM)],
            us=0.1, mib=24,
        )

    def prep0():
        state["up0"], state["top0"] = run(
            prep0_kernel,
            [(meta, SMEM), (lower, VMEM)] + [(v, VMEM) for v in state["fresh"]],
            [(bf16(nb, cb * nb), VMEM), (bf16(nb, cb, nb), VMEM)],
            scratch=[pltpu.VMEM((nb, cb * nb), BF16)],
            us=2.0, mib=16,
        )

    def prep1():
        state["up1"], state["up0_panel"], state["top1"] = run(
            prep1_kernel,
            [(meta, SMEM), (lower, VMEM), (upper, VMEM), (state["up0"], VMEM), (state["heads"], VMEM)]
            + [(v, VMEM) for v in state["fresh"]],
            [(bf16(nb, cb * nb), VMEM), (bf16(nb, nb), VMEM), (bf16(nb, cb, nb), VMEM)],
            scratch=[pltpu.VMEM((nb, cb * nb), BF16), pltpu.VMEM((2, nb, nb), BF16)],
            us=3.5, mib=16,
        )

    def update(i):
        operands = [(meta, SMEM), (state["goal"], VMEM)] + [(v, VMEM) for v in state["old"]] + [(upper, VMEM)]
        operands += [(state[name], VMEM) for name in ("up0", "up1", "up0_panel")]
        operands += [(state[name], ANY) for name in ("moved", "top0", "top1")]
        operands += [(v, ANY) for v in held[i : i + line] + other[i : i + line]]
        aliases = {}
        if "result" in state:
            aliases = {len(operands): 0}
            operands.append((state["result"], ANY))
        count = sizes[i]
        state["result"], _ = run(
            functools.partial(update_kernel, begins[i], line),
            operands,
            [(bf16(rows, cb, nb), ANY), (jax.ShapeDtypeStruct((8, 128), F32), VMEM)],
            scratch=[
                pltpu.VMEM((2, count, nb), BF16), pltpu.VMEM((count, cb, nb), BF16),
                pltpu.VMEM((count, cb, nb), BF16), DMA((2,)), DMA, DMA,
            ],
            aliases=aliases,
            us=5.0, mib=24,
        )

    plan = [(0, gather), (1, join), (2, functools.partial(fresh, 0)), (3, functools.partial(fresh, 1)), (line - 1, functools.partial(old, held, "old_held")), (line, functools.partial(old, other, "old_other")), (4, scatter), (4, prep0), (5, prep1), (5, old_here)]
    for i in range(pieces):
        plan.append((max((5, 5, 6, 7, 8, 8)[min(i, 5)], i + line - 1), functools.partial(update, i)))
    for k in range(last_step + 1):
        step(k)
        while plan and (plan[0][0] <= k or k == last_step):
            plan.pop(0)[1]()
    return state["result"].reshape(matrix.shape)


def solution(mesh):
    placed = (P(None, "prow", None, "pcol"), P(), P(), P())
    return jax.shard_map(
        body, mesh=mesh, in_specs=placed, out_specs=P(None, "prow", None, "pcol"), check_vma=False
    )
```

```python
import functools

import jax
import jax.numpy as jnp
from jax import lax
from jax.experimental import pallas as pl
from jax.experimental.pallas import tpu as pltpu
from jax.sharding import PartitionSpec as P

BF16 = jnp.bfloat16
F32 = jnp.float32
I32 = jnp.int32
SMEM = pl.BlockSpec(memory_space=pltpu.SMEM)
VMEM = pl.BlockSpec(memory_space=pltpu.VMEM)
ANY = pl.BlockSpec(memory_space=pl.ANY)
DMA = pltpu.SemaphoreType.DMA


def dot(a, b):
    return jnp.dot(a, b, preferred_element_type=F32)


def flat(rows):
    return rows.reshape(rows.shape[0], rows.shape[1] * rows.shape[2])


def bf16(*shape):
    return jax.ShapeDtypeStruct(shape, BF16)


def call(kernel, operands, outs, after=(), scratch=(), aliases=None, us=1.0, mib=8):
    count = len(operands)

    def ordered(*refs):
        kernel(*refs[:count], *refs[count + len(after) :])

    return pl.pallas_call(
        ordered,
        out_shape=tuple(shape for shape, _ in outs),
        in_specs=[spec for _, spec in operands] + [ANY] * len(after),
        out_specs=tuple(spec for _, spec in outs),
        scratch_shapes=list(scratch),
        input_output_aliases=aliases or {},
        compiler_params=pltpu.CompilerParams(vmem_limit_bytes=mib * 1024 * 1024),
        cost_estimate=pl.CostEstimate(flops=int(us * 1.1e9), bytes_accessed=0, transcendentals=0),
    )(*[array for array, _ in operands], *after)


def fill_indices(nb, rows, meta, pivots, spread, fetch, join, arrive, goal, hops):
    row, row_devices = meta[0], meta[3]
    chip, chips = row // 2, row_devices // 2
    lanes = spread.shape[2]
    tiles = nb // lanes
    slot = lax.broadcasted_iota(I32, (1, nb), 1)
    pivot0, pivot1 = pivots[0:1, :], pivots[1:2, :]

    def lookup(keys, entry, value):
        parts = [keys[:, t * lanes : (t + 1) * lanes] for t in range(tiles)]

        def add(i, totals):
            begin = pl.multiple_of(i * 8, 8)
            at = begin + lax.broadcasted_iota(I32, (8, lanes), 0)
            here, give = entry(begin, at), value(begin, at)
            return tuple(t + jnp.where(p == here, give, 0) for t, p in zip(totals, parts))

        zero = jnp.zeros((8, lanes), I32)
        totals = lax.fori_loop(0, nb // 8, add, (zero,) * tiles, unroll=8)
        return jnp.concatenate([jnp.sum(t, axis=0, keepdims=True) for t in totals], axis=1)

    def pivot_of(panel):
        return lambda begin, at: spread[panel, pl.ds(begin, 8), :]

    place = lambda begin, at: at + 1
    in_pivots0 = lookup(pivot1, pivot_of(0), place)
    in_pivots1 = lookup(pivot0, pivot_of(1), place)
    top1_in_pivots0 = lookup(nb + slot, pivot_of(0), place)
    over_top1 = lookup(pivot0, lambda begin, at: nb + at, pivot_of(1))
    chained = lookup(nb + in_pivots1 - 1, pivot_of(0), place)

    source0 = pivot0
    source1 = jnp.where(in_pivots0 > 0, in_pivots0 - 1, pivot1)
    second0 = jnp.where(in_pivots1 > 0, jnp.where(chained > 0, chained - 1, nb + in_pivots1 - 1), slot)
    second1 = jnp.where(top1_in_pivots0 > 0, top1_in_pivots0 - 1, nb + slot)
    target0 = jnp.where(over_top1 > 0, over_top1, jnp.where(in_pivots1 > 0, nb + in_pivots1 - 1, pivot0))
    target1 = jnp.where(top1_in_pivots0 > 0, top1_in_pivots0 - 1, pivot1)

    def holder(index):
        return lax.rem(lax.div(index, nb), row_devices)

    def local(index):
        return lax.div(index, nb * row_devices) * nb + lax.rem(index, nb)

    def placed(index):
        mine = (holder(index) == row) & (index >= 2 * nb)
        return jnp.where(mine, local(index), rows)

    for k, (source, second, target) in enumerate(((source0, second0, target0), (source1, second1, target1))):
        from_chip = lax.div(holder(source), 2)
        wanted = jnp.where(from_chip == chip, source, second)
        at = (slice(k, k + 1), slice(None))
        fetch[at] = local(wanted)
        join[at] = jnp.where(holder(wanted) == row, lax.rem(slot, nb // 2), nb // 2)
        arrive[at] = placed(source)
        goal[at] = placed(target)
        hops[at] = lax.rem(chip + chips - from_chip, chips)


def copy_rows(count, target, target_at, origin, origin_at):
    def copy(i, carry):
        target[target_at(i)] = origin[origin_at(i)]
        return carry

    lax.fori_loop(0, count, copy, 0, unroll=16)


def first_kernel(tiles, piece, work, sem):
    load = pltpu.make_async_copy(tiles.at[pl.ds(0, piece.shape[0])], work, sem)
    load.start()
    load.wait()
    piece[...] = flat(work[...])[:, : piece.shape[1]]


def gather_kernel(meta, pivots, spread, tiles, *refs):
    *pieces, loaded, send, keep, block0, join, arrive, goal, hops, fetch, fetch_table, load_sem, table_sem = refs
    nb = send.shape[0]
    rows = tiles.shape[0]
    core = meta[1]
    load = pltpu.make_async_copy(tiles, loaded.at[pl.ds(0, rows)], load_sem)
    load.start()
    fill_indices(nb, rows, meta, pivots, spread, fetch, join, arrive, goal, hops)
    table = pltpu.make_async_copy(fetch, fetch_table, table_sem)
    table.start()
    table.wait()
    load.wait()
    begin = nb
    for piece in pieces:
        end = begin + piece.shape[0]
        piece[...] = flat(loaded[begin:end])[:, :nb]
        begin = end
    half, side = nb // 2, lax.rem(meta[2], 2)
    for turn, b in enumerate((1 - side, side)):
        to = lambda i, turn=turn: turn * half + i
        copy_rows(half, send, to, loaded, lambda i, b=b: fetch_table[b, (1 - core) * half + i])
        copy_rows(half, keep, to, loaded, lambda i, b=b: fetch_table[b, core * half + i])
    block0[...] = loaded[0:nb]


def join_kernel(meta, join, keep, came, joined0, joined1, work0, work1):
    half = joined0.shape[0]
    core, side = meta[1], lax.rem(meta[2], 2)
    for turn, (b, work, joined) in enumerate(((1 - side, work0, joined0), (side, work1, joined1))):
        work[0:half] = came[turn * half : (turn + 1) * half]
        copy_rows(
            half, work, lambda i, b=b: join[b, core * half + i], keep, lambda i, turn=turn: turn * half + i
        )
        joined[...] = work[0:half]


def scatter_kernel(meta, arrive, goal, *refs):
    *came, old, old_sibling, tiles, out = refs
    core, side, chip = meta[1], lax.rem(meta[2], 2), meta[0] // 2
    nb = old.shape[0]
    half = nb // 2
    out[...] = tiles[...]

    @pl.when(chip == 0)
    def _():
        copy_rows(nb, out, lambda i: goal[core, i], old, lambda i: i)
        copy_rows(nb, out, lambda i: goal[1 - core, i], old_sibling, lambda i: i)

    @pl.when(chip != 0)
    def _():
        for turn, b in enumerate((1 - side, side)):
            for values, who in ((came[2 * turn], core), (came[2 * turn + 1], 1 - core)):
                copy_rows(half, out, lambda i, b=b, who=who: arrive[b, who * half + i], values, lambda i: i)


def relay_kernel(meta, came, *refs):
    *own, held = refs
    place = lax.div(meta[2], 2)
    for piece in own:

        @pl.when(place == 0)
        def _(piece=piece):
            held[0 : piece.shape[0]] = piece[...]

    @pl.when(place != 0)
    def _():
        count = min(came.shape[0], held.shape[0])
        held[0:count] = came[0:count]


def old_kernel(line, meta, *refs):
    *choices, old = refs
    for h in range(line):

        @pl.when(lax.div(meta[2], 2) == h)
        def _(h=h):
            old[...] = choices[h][0 : old.shape[0]]


def by_chip_kernel(meta, *refs):
    *choices, out = refs
    for h in range(len(choices) // 2):

        @pl.when(meta[0] // 2 == h)
        def _(h=h):
            out[0] = choices[2 * h][...]
            out[1] = choices[2 * h + 1][...]


def by_place_kernel(meta, *refs):
    out = refs[-1]
    for h, choice in enumerate(refs[:-1]):

        @pl.when(lax.div(meta[2], 2) == h)
        def _(choice=choice):
            out[...] = choice[...]


def stack_kernel(*refs):
    *entries, out = refs
    for i, entry in enumerate(entries):
        out[i] = entry[...]


def choose(hop, choices):
    value = flat(choices[0]).astype(F32)
    for h, other in enumerate(choices[1:], 1):
        value = jnp.where(hop == h, flat(other).astype(F32), value)
    return value.astype(BF16)


def fresh_kernel(turn, chips, meta, hops, *refs):
    choices, (fresh, brought, *head) = refs[:chips], refs[chips:]
    half = fresh.shape[0]
    core, side, chip = meta[1], lax.rem(meta[2], 2), meta[0] // 2
    b = side if turn else 1 - side
    hop = jnp.broadcast_to(hops[pl.ds(b, 1), :], (8, 2 * half)).T[:, 0:1]
    hop = jnp.where(core == 0, hop[:half], hop[half:])
    fresh[...] = choose(hop, [c[...] for c in choices])
    if head:
        part, nb = head[0].shape
        head[0][...] = fresh[pl.ds(pl.multiple_of(chip * part, part), part), :nb]
    if chips == 1:
        brought[...] = choices[0][...]
    for h in range(1, chips):

        @pl.when((chip == h) | ((chip == 0) & (h == 1)))
        def _(h=h):
            brought[...] = choices[h][...]


def assemble(meta, b, fresh, work):
    core, side = meta[1], lax.rem(meta[2], 2)
    half = work.shape[0] // 2
    for turn, which in enumerate((1 - side, side)):

        @pl.when(which == b)
        def _(turn=turn):
            work[pl.ds(pl.multiple_of(core * half, half), half)] = fresh[2 * turn][...]
            work[pl.ds(pl.multiple_of((1 - core) * half, half), half)] = fresh[2 * turn + 1][...]


def raw(columns, nb):
    joined = jnp.concatenate(columns, axis=1)
    return joined.reshape(joined.shape[0], len(columns), nb)


def prep0_kernel(meta, lower, *refs):
    *fresh, up0, top, work = refs
    column = meta[2]
    nb = work.shape[0]
    assemble(meta, 0, fresh, work)
    shown = []
    for j in range(work.shape[1] // nb):
        cols = slice(j * nb, (j + 1) * nb)
        product = dot(lower[0], work[:, cols])
        show = product
        if j == 0:
            show = jnp.where(column == 0, work[:, cols].astype(F32), product)
            product = jnp.where(column == 0, 0.0, product)
        up0[:, cols] = product.astype(BF16)
        shown.append(show.astype(BF16))
    top[...] = raw(shown, nb)


def prep1_kernel(chips, meta, lower, upper, up0, heads, heads_sibling, *refs):
    *fresh, up1, up0_panel, top, work, head = refs
    core, column, chip = meta[1], meta[2], meta[0] // 2
    side = lax.rem(column, 2)
    nb, part = work.shape[0], heads.shape[2]
    for who, parts in ((core, heads), (1 - core, heads_sibling)):
        for h in range(chips):
            at = pl.multiple_of((who * chips + lax.rem(chip + chips - h, chips)) * part, part)
            head[1 - side, pl.ds(at, part)] = parts[h, 0]
            head[side, pl.ds(at, part)] = parts[h, 1]
    assemble(meta, 1, fresh, work)
    up0_panel[...] = dot(lower[0], head[0]).astype(BF16)
    factor = dot(head[1], upper[0]).astype(BF16)
    in_panel, next_panel = column == 0, column == 1
    shown = []
    for j in range(work.shape[1] // nb):
        cols = slice(j * nb, (j + 1) * nb)
        updated = (work[:, cols].astype(F32) - dot(factor, up0[:, cols])).astype(BF16)
        last = dot(lower[1], updated)
        show = last
        if j == 0:
            show = jnp.where(next_panel, updated.astype(F32), show)
            show = jnp.where(in_panel, factor.astype(F32), show)
            last = jnp.where(in_panel | next_panel, 0.0, last)
        up1[:, cols] = last.astype(BF16)
        shown.append(show.astype(BF16))
    top[...] = raw(shown, nb)


def update_kernel(
    begin, line, meta, goal, old, old_sibling, upper, up0, up1, up0_panel, tiles, top0, top1, *rest
):
    held, other = rest[:line], rest[line : 2 * line]
    out, token, panels, block, result, panel_sem, block_sem, out_sem = rest[-8:]
    row, core, column = meta[0], meta[1], meta[2]
    side, place = lax.rem(column, 2), lax.div(column, 2)
    count, cb, nb = block.shape
    rows_of = pl.ds(begin, count)

    def panel_copy(h, which):
        source = (held, other)[which][h].at[pl.ds(0, count)]
        return pltpu.make_async_copy(source, panels.at[lax.rem(side + which, 2)], panel_sem.at[which])

    load = pltpu.make_async_copy(tiles.at[rows_of], block, block_sem)
    load.start()
    for h in range(line):

        @pl.when(place == h)
        def _(h=h):
            panel_copy(h, 0).start()
            panel_copy(h, 1).start()

    def arrived():
        panel_copy(0, 0).wait()
        panel_copy(0, 1).wait()

    def from_factors():
        here = begin + lax.broadcasted_iota(I32, (count, nb), 0)
        pick = jnp.where(here == goal[pl.ds(core, 1), :], 1.0, 0.0)
        pick_sibling = jnp.where(here == goal[pl.ds(1 - core, 1), :], 1.0, 0.0)
        moved = jnp.sum(pick + pick_sibling, axis=1, keepdims=True) > 0.5
        pick, pick_sibling = pick.astype(BF16), pick_sibling.astype(BF16)
        arrived()
        whole = []
        for k in range(2):
            which = lax.rem(k + side, 2)
            brought = dot(pick, old[which]) + dot(pick_sibling, old_sibling[which])
            whole.append(jnp.where(moved, brought, panels[k].astype(F32)))
        factor0 = dot(whole[0].astype(BF16), upper[0]).astype(BF16)
        below = (whole[1] - dot(factor0, up0_panel[...])).astype(BF16)
        factor1 = dot(below, upper[1]).astype(BF16)
        load.wait()
        values = flat(block[...])
        columns = []
        for j in range(cb):
            cols = slice(j * nb, (j + 1) * nb)
            value = values[:, cols].astype(F32) - dot(factor0, up0[:, cols])
            value = value.astype(BF16).astype(F32) - dot(factor1, up1[:, cols])
            if j == 0:
                value = jnp.where(column == 0, factor0.astype(F32), value)
                value = jnp.where(column == 1, factor1.astype(F32), value)
            columns.append(value.astype(BF16))
        result[...] = raw(columns, nb)

    def from_top(top):
        arrived()
        load.wait()
        copy = pltpu.make_async_copy(top.at[rows_of], result, block_sem)
        copy.start()
        copy.wait()

    if begin < nb:
        pl.when(row == 0)(lambda: from_top(top0))
        pl.when(row == 1)(lambda: from_top(top1))
        pl.when(row >= 2)(from_factors)
    else:
        from_factors()
    store = pltpu.make_async_copy(result, out.at[rows_of], out_sem)
    store.start()
    token[...] = jnp.zeros(token.shape, F32)
    store.wait()


def body(matrix, pivots, lower, upper):
    rb, nb, cb, _ = matrix.shape
    rows = rb * nb
    sizes = [nb] * (rb - 1) + [nb // 2] * 2
    begins = [sum(sizes[:i]) for i in range(len(sizes))]
    pieces = len(sizes)
    row_devices = lax.axis_size("prow")
    col_devices = lax.axis_size("pcol")
    chips, line = row_devices // 2, col_devices // 2
    row = lax.axis_index("prow").astype(I32)
    column = lax.axis_index("pcol").astype(I32)
    meta = jnp.stack([row, row % 2, column, jnp.int32(row_devices)])
    tiles = matrix.reshape(rows, cb, nb)

    def to_sibling(value):
        return lax.ppermute(value, "prow", [(r, r ^ 1) for r in range(row_devices)])

    def to_neighbour(value):
        return lax.ppermute(value, "pcol", [(c, c ^ 1) for c in range(col_devices)])

    def to_chip(value, h):
        return lax.ppermute(value, "prow", [(r, (r + 2 * h) % row_devices) for r in range(row_devices)])

    def to_next(value):
        return lax.ppermute(value, "pcol", [(c, c + 2) for c in range(col_devices - 2)])

    order = []

    def run(kernel, operands, outs, also=(), **kwargs):
        after = tuple(order[-1:]) + tuple(also)
        results = call(kernel, operands, outs, after=after, **kwargs)
        order.append(results[-1])
        return results

    last_step = pieces + line - 2

    def piece_out(i):
        return (bf16(sizes[i], nb), VMEM)

    def step_out(k):
        return (bf16(max(sizes[k - p] for p in range(line) if 0 <= k - p < pieces), nb), VMEM)

    own, held, other = [], [], []
    state = {}

    def step(k):
        if k == 0:
            own.extend(run(
                first_kernel, [(tiles, ANY)], [piece_out(0)],
                scratch=[pltpu.VMEM((sizes[0], cb, nb), BF16), DMA], mib=60,
            ))
            value = own[0]
        else:
            also = [other[k - 1]] + state.pop('awaited', [])
            operands = [(meta, SMEM), (state["came"], VMEM)] + [(v, VMEM) for v in own[k : k + 1]]
            (value,) = run(relay_kernel, operands, [step_out(k)], also, us=0.2 if k in (2, 3, 5) else 12.0)
        held.append(value)
        if k < last_step:
            state["came"] = to_next(value)
        other.append(to_neighbour(value))

    def gather():
        lanes = min(nb, 128)
        spread = jnp.broadcast_to(pivots[:, :, None], (2, nb, lanes))
        table = jax.ShapeDtypeStruct((2, nb), I32)
        results = run(
            gather_kernel,
            [(meta, SMEM), (pivots, VMEM), (spread, VMEM), (tiles, ANY)],
            [piece_out(i) for i in range(1, pieces)] + [(bf16(rows + 8, cb, nb), VMEM)]
            + [(bf16(nb, cb, nb), VMEM)] * 3 + [(table, VMEM)] * 4,
            scratch=[pltpu.VMEM((2, nb), I32), pltpu.SMEM((2, nb), I32), DMA, DMA],
            us=8.0, mib=20,
        )
        own.extend(results[: pieces - 1])
        state["loaded"], send, *rest = results[pieces - 1 :]
        state.update(zip(("keep", "block0", "join", "arrive", "goal", "hops"), rest))
        state["sent"] = to_sibling(send)
        state["block0_sibling"] = to_sibling(state["block0"])
        state["awaited"] = [state["block0_sibling"]]

    half = nb // 2
    part = half // chips

    def join():
        joined = run(
            join_kernel,
            [(meta, SMEM), (state["join"], SMEM), (state["keep"], VMEM), (state["sent"], VMEM)],
            [(bf16(half, cb, nb), VMEM)] * 2,
            scratch=[pltpu.VMEM((half + 8, cb, nb), BF16)] * 2,
            us=2.0,
        )
        state["choices"] = [[v] + [to_chip(v, h) for h in range(1, chips)] for v in joined]
        state["fresh"], state["brought"] = [], []

    def fresh(turn):
        new, brought, *head = run(
            functools.partial(fresh_kernel, turn, chips),
            [(meta, SMEM), (state["hops"], VMEM)] + [(c, VMEM) for c in state["choices"][turn]],
            [(bf16(half, cb * nb), VMEM), (bf16(half, cb, nb), VMEM)]
            + [(bf16(part, nb), VMEM)] * (1 - turn),
            us=1.5, mib=16,
        )
        state["fresh"] += [new, to_sibling(new)]
        state["brought"] += [brought, to_sibling(brought)]
        if head:
            state["head"] = head + [
                lax.ppermute(head[0], "pcol", [(0, 2 * h), (1, 2 * h + 1)]) for h in range(1, line)
            ]
            state["awaited"] = state.get("awaited", []) + state["head"][1:]

    def head_here():
        (mine,) = run(
            by_place_kernel, [(meta, SMEM)] + [(v, VMEM) for v in state["head"]], [(bf16(part, nb), VMEM)], us=0.1
        )
        state["head"] = (mine, to_neighbour(mine))

    def head_pair():
        (pair,) = run(stack_kernel, [(v, VMEM) for v in state["head"]], [(bf16(2, part, nb), VMEM)], us=0.1)
        state["head"] = [pair] + [to_chip(pair, h) for h in range(1, chips)]

    def head_all():
        (mine,) = run(
            stack_kernel, [(v, VMEM) for v in state["head"]], [(bf16(chips, 2, part, nb), VMEM)], us=0.1
        )
        state["heads"] = (mine, to_sibling(mine))

    def old(values, name):
        operands = [(meta, SMEM)] + [(v, VMEM) for v in values[:line]]
        (mine,) = run(functools.partial(old_kernel, line), operands, [(bf16(nb, nb), VMEM)], us=0.1)
        state[name] = [mine] + [to_chip(mine, h) for h in range(1, chips)]
        state["awaited"] = state.get("awaited", []) + state[name][1:]

    def old_here():
        choices = [v for pair in zip(state["old_held"], state["old_other"]) for v in pair]
        (mine,) = run(
            by_chip_kernel, [(meta, SMEM)] + [(v, VMEM) for v in choices], [(bf16(2, nb, nb), VMEM)], us=0.1
        )
        state["old"] = (mine, to_sibling(mine))

    def scatter():
        sources = state["brought"] + [state["block0"], state["block0_sibling"], state["loaded"]]
        (state["moved"],) = run(
            scatter_kernel,
            [(meta, SMEM), (state["arrive"], SMEM), (state["goal"], SMEM)] + [(v, VMEM) for v in sources],
            [(bf16(rows + 8, cb, nb), VMEM)],
            us=0.1, mib=24,
        )

    def prep0():
        state["up0"], state["top0"] = run(
            prep0_kernel,
            [(meta, SMEM), (lower, VMEM)] + [(v, VMEM) for v in state["fresh"]],
            [(bf16(nb, cb * nb), VMEM), (bf16(nb, cb, nb), VMEM)],
            scratch=[pltpu.VMEM((nb, cb * nb), BF16)],
            us=2.0, mib=16,
        )

    def prep1():
        state["up1"], state["up0_panel"], state["top1"] = run(
            functools.partial(prep1_kernel, chips),
            [(meta, SMEM), (lower, VMEM), (upper, VMEM), (state["up0"], VMEM)]
            + [(v, VMEM) for v in state["heads"]] + [(v, VMEM) for v in state["fresh"]],
            [(bf16(nb, cb * nb), VMEM), (bf16(nb, nb), VMEM), (bf16(nb, cb, nb), VMEM)],
            scratch=[pltpu.VMEM((nb, cb * nb), BF16), pltpu.VMEM((2, nb, nb), BF16)],
            us=3.5, mib=16,
        )

    def update(i):
        operands = [(meta, SMEM), (state["goal"], VMEM)] + [(v, VMEM) for v in state["old"]] + [(upper, VMEM)]
        operands += [(state[name], VMEM) for name in ("up0", "up1", "up0_panel")]
        operands += [(state[name], ANY) for name in ("moved", "top0", "top1")]
        operands += [(v, ANY) for v in held[i : i + line] + other[i : i + line]]
        aliases = {}
        if "result" in state:
            aliases = {len(operands): 0}
            operands.append((state["result"], ANY))
        count = sizes[i]
        state["result"], _ = run(
            functools.partial(update_kernel, begins[i], line),
            operands,
            [(bf16(rows, cb, nb), ANY), (jax.ShapeDtypeStruct((8, 128), F32), VMEM)],
            scratch=[
                pltpu.VMEM((2, count, nb), BF16), pltpu.VMEM((count, cb, nb), BF16),
                pltpu.VMEM((count, cb, nb), BF16), DMA((2,)), DMA, DMA,
            ],
            aliases=aliases,
            us=5.0, mib=24,
        )

    plan = [(0, gather), (1, join), (2, functools.partial(fresh, 0)), (3, head_here), (line - 1, functools.partial(old, held, "old_held")), (3, head_pair), (3, functools.partial(fresh, 1)), (line, functools.partial(old, other, "old_other")), (4, head_all), (4, scatter), (4, prep0), (5, prep1), (5, old_here)]
    for i in range(pieces):
        plan.append((max((5, 5, 6, 7, 8, 8)[min(i, 5)], i + line - 1), functools.partial(update, i)))
    for k in range(last_step + 1):
        step(k)
        while plan and (plan[0][0] <= k or k == last_step):
            plan.pop(0)[1]()
    return state["result"].reshape(matrix.shape)


def solution(mesh):
    placed = (P(None, "prow", None, "pcol"), P(), P(), P())
    return jax.shard_map(
        body, mesh=mesh, in_specs=placed, out_specs=P(None, "prow", None, "pcol"), check_vma=False
    )
```

```python
import functools

import jax
import jax.numpy as jnp
from jax import lax
from jax.experimental import pallas as pl
from jax.experimental.pallas import tpu as pltpu
from jax.sharding import PartitionSpec as P

BF16 = jnp.bfloat16
F32 = jnp.float32
I32 = jnp.int32
SMEM = pl.BlockSpec(memory_space=pltpu.SMEM)
VMEM = pl.BlockSpec(memory_space=pltpu.VMEM)
ANY = pl.BlockSpec(memory_space=pl.ANY)
DMA = pltpu.SemaphoreType.DMA


def dot(a, b):
    return jnp.dot(a, b, preferred_element_type=F32)


def flat(rows):
    return rows.reshape(rows.shape[0], rows.shape[1] * rows.shape[2])


def bf16(*shape):
    return jax.ShapeDtypeStruct(shape, BF16)


def call(kernel, operands, outs, after=(), scratch=(), aliases=None, us=1.0, mib=8):
    count = len(operands)

    def ordered(*refs):
        kernel(*refs[:count], *refs[count + len(after) :])

    return pl.pallas_call(
        ordered,
        out_shape=tuple(shape for shape, _ in outs),
        in_specs=[spec for _, spec in operands] + [ANY] * len(after),
        out_specs=tuple(spec for _, spec in outs),
        scratch_shapes=list(scratch),
        input_output_aliases=aliases or {},
        compiler_params=pltpu.CompilerParams(vmem_limit_bytes=mib * 1024 * 1024),
        cost_estimate=pl.CostEstimate(flops=int(us * 1.1e9), bytes_accessed=0, transcendentals=0),
    )(*[array for array, _ in operands], *after)


def fill_indices(nb, rows, meta, pivots, spread, fetch, join, arrive, goal, hops):
    row, row_devices = meta[0], meta[3]
    chip, chips = row // 2, row_devices // 2
    lanes = spread.shape[2]
    tiles = nb // lanes
    slot = lax.broadcasted_iota(I32, (1, nb), 1)
    pivot0, pivot1 = pivots[0:1, :], pivots[1:2, :]

    def lookup(keys, entry, value):
        parts = [keys[:, t * lanes : (t + 1) * lanes] for t in range(tiles)]

        def add(i, totals):
            begin = pl.multiple_of(i * 8, 8)
            at = begin + lax.broadcasted_iota(I32, (8, lanes), 0)
            here, give = entry(begin, at), value(begin, at)
            return tuple(t + jnp.where(p == here, give, 0) for t, p in zip(totals, parts))

        zero = jnp.zeros((8, lanes), I32)
        totals = lax.fori_loop(0, nb // 8, add, (zero,) * tiles, unroll=8)
        return jnp.concatenate([jnp.sum(t, axis=0, keepdims=True) for t in totals], axis=1)

    def pivot_of(panel):
        return lambda begin, at: spread[panel, pl.ds(begin, 8), :]

    place = lambda begin, at: at + 1
    in_pivots0 = lookup(pivot1, pivot_of(0), place)
    in_pivots1 = lookup(pivot0, pivot_of(1), place)
    top1_in_pivots0 = lookup(nb + slot, pivot_of(0), place)
    over_top1 = lookup(pivot0, lambda begin, at: nb + at, pivot_of(1))
    chained = lookup(nb + in_pivots1 - 1, pivot_of(0), place)

    source0 = pivot0
    source1 = jnp.where(in_pivots0 > 0, in_pivots0 - 1, pivot1)
    second0 = jnp.where(in_pivots1 > 0, jnp.where(chained > 0, chained - 1, nb + in_pivots1 - 1), slot)
    second1 = jnp.where(top1_in_pivots0 > 0, top1_in_pivots0 - 1, nb + slot)
    target0 = jnp.where(over_top1 > 0, over_top1, jnp.where(in_pivots1 > 0, nb + in_pivots1 - 1, pivot0))
    target1 = jnp.where(top1_in_pivots0 > 0, top1_in_pivots0 - 1, pivot1)

    def holder(index):
        return lax.rem(lax.div(index, nb), row_devices)

    def local(index):
        return lax.div(index, nb * row_devices) * nb + lax.rem(index, nb)

    def placed(index):
        mine = (holder(index) == row) & (index >= 2 * nb)
        return jnp.where(mine, local(index), rows)

    for k, (source, second, target) in enumerate(((source0, second0, target0), (source1, second1, target1))):
        from_chip = lax.div(holder(source), 2)
        wanted = jnp.where(from_chip == chip, source, second)
        at = (slice(k, k + 1), slice(None))
        fetch[at] = local(wanted)
        join[at] = jnp.where(holder(wanted) == row, lax.rem(slot, nb // 2), nb // 2)
        arrive[at] = placed(source)
        goal[at] = placed(target)
        hops[at] = lax.rem(chip + chips - from_chip, chips)


def copy_rows(count, target, target_at, origin, origin_at):
    def copy(i, carry):
        target[target_at(i)] = origin[origin_at(i)]
        return carry

    lax.fori_loop(0, count, copy, 0, unroll=16)


def first_kernel(tiles, piece, work, sem):
    load = pltpu.make_async_copy(tiles.at[pl.ds(0, piece.shape[0])], work, sem)
    load.start()
    load.wait()
    piece[...] = flat(work[...])[:, : piece.shape[1]]


def gather_kernel(meta, pivots, spread, tiles, *refs):
    *pieces, loaded, send, keep, block0, join, arrive, goal, hops, fetch, fetch_table, load_sem, table_sem = refs
    nb = send.shape[0]
    rows = tiles.shape[0]
    core = meta[1]
    load = pltpu.make_async_copy(tiles, loaded.at[pl.ds(0, rows)], load_sem)
    load.start()
    fill_indices(nb, rows, meta, pivots, spread, fetch, join, arrive, goal, hops)
    table = pltpu.make_async_copy(fetch, fetch_table, table_sem)
    table.start()
    table.wait()
    load.wait()
    begin = nb
    for piece in pieces:
        end = begin + piece.shape[0]
        piece[...] = flat(loaded[begin:end])[:, :nb]
        begin = end
    half, side = nb // 2, lax.rem(meta[2], 2)
    for turn, b in enumerate((1 - side, side)):
        to = lambda i, turn=turn: turn * half + i
        copy_rows(half, send, to, loaded, lambda i, b=b: fetch_table[b, (1 - core) * half + i])
        copy_rows(half, keep, to, loaded, lambda i, b=b: fetch_table[b, core * half + i])
    block0[...] = loaded[0:nb]


def join_kernel(meta, join, keep, came, joined0, joined1, work0, work1):
    half = joined0.shape[0]
    core, side = meta[1], lax.rem(meta[2], 2)
    for turn, (b, work, joined) in enumerate(((1 - side, work0, joined0), (side, work1, joined1))):
        work[0:half] = came[turn * half : (turn + 1) * half]
        copy_rows(
            half, work, lambda i, b=b: join[b, core * half + i], keep, lambda i, turn=turn: turn * half + i
        )
        joined[...] = work[0:half]


def scatter_kernel(meta, arrive, goal, *refs):
    *came, old, old_sibling, tiles, out = refs
    core, side, chip = meta[1], lax.rem(meta[2], 2), meta[0] // 2
    nb = old.shape[0]
    half = nb // 2
    out[...] = tiles[...]

    @pl.when(chip == 0)
    def _():
        copy_rows(nb, out, lambda i: goal[core, i], old, lambda i: i)
        copy_rows(nb, out, lambda i: goal[1 - core, i], old_sibling, lambda i: i)

    @pl.when(chip != 0)
    def _():
        for turn, b in enumerate((1 - side, side)):
            for values, who in ((came[2 * turn], core), (came[2 * turn + 1], 1 - core)):
                copy_rows(half, out, lambda i, b=b, who=who: arrive[b, who * half + i], values, lambda i: i)


def relay_kernel(meta, came, *refs):
    *own, held = refs
    place = lax.div(meta[2], 2)
    for piece in own:

        @pl.when(place == 0)
        def _(piece=piece):
            held[0 : piece.shape[0]] = piece[...]

    @pl.when(place != 0)
    def _():
        count = min(came.shape[0], held.shape[0])
        held[0:count] = came[0:count]


def old_kernel(line, meta, *refs):
    *choices, old = refs
    for h in range(line):

        @pl.when(lax.div(meta[2], 2) == h)
        def _(h=h):
            old[...] = choices[h][0 : old.shape[0]]


def by_chip_kernel(meta, *refs):
    *choices, out = refs
    for h in range(len(choices) // 2):

        @pl.when(meta[0] // 2 == h)
        def _(h=h):
            out[0] = choices[2 * h][...]
            out[1] = choices[2 * h + 1][...]


def by_place_kernel(meta, *refs):
    out = refs[-1]
    for h, choice in enumerate(refs[:-1]):

        @pl.when(lax.div(meta[2], 2) == h)
        def _(choice=choice):
            out[...] = choice[...]


def stack_kernel(*refs):
    *entries, out = refs
    for i, entry in enumerate(entries):
        out[i] = entry[...]


def choose(hop, choices):
    value = flat(choices[0]).astype(F32)
    for h, other in enumerate(choices[1:], 1):
        value = jnp.where(hop == h, flat(other).astype(F32), value)
    return value.astype(BF16)


def fresh_kernel(turn, chips, meta, hops, *refs):
    choices, (fresh, brought, *head) = refs[:chips], refs[chips:]
    half = fresh.shape[0]
    core, side, chip = meta[1], lax.rem(meta[2], 2), meta[0] // 2
    b = side if turn else 1 - side
    hop = jnp.broadcast_to(hops[pl.ds(b, 1), :], (8, 2 * half)).T[:, 0:1]
    hop = jnp.where(core == 0, hop[:half], hop[half:])
    fresh[...] = choose(hop, [c[...] for c in choices])
    if head:
        part, nb = head[0].shape
        head[0][...] = fresh[pl.ds(pl.multiple_of(chip * part, part), part), :nb]
    if chips == 1:
        brought[...] = choices[0][...]
    for h in range(1, chips):

        @pl.when((chip == h) | ((chip == 0) & (h == 1)))
        def _(h=h):
            brought[...] = choices[h][...]


def assemble(meta, b, fresh, work):
    core, side = meta[1], lax.rem(meta[2], 2)
    half = work.shape[0] // 2
    for turn, which in enumerate((1 - side, side)):

        @pl.when(which == b)
        def _(turn=turn):
            work[pl.ds(pl.multiple_of(core * half, half), half)] = fresh[2 * turn][...]
            work[pl.ds(pl.multiple_of((1 - core) * half, half), half)] = fresh[2 * turn + 1][...]


def raw(columns, nb):
    joined = jnp.concatenate(columns, axis=1)
    return joined.reshape(joined.shape[0], len(columns), nb)


def prep0_kernel(meta, lower, *refs):
    *fresh, up0, top, work = refs
    column = meta[2]
    nb = work.shape[0]
    assemble(meta, 0, fresh, work)
    shown = []
    for j in range(work.shape[1] // nb):
        cols = slice(j * nb, (j + 1) * nb)
        product = dot(lower[0], work[:, cols])
        show = product
        if j == 0:
            show = jnp.where(column == 0, work[:, cols].astype(F32), product)
            product = jnp.where(column == 0, 0.0, product)
        up0[:, cols] = product.astype(BF16)
        shown.append(show.astype(BF16))
    top[...] = raw(shown, nb)


def prep1_kernel(chips, meta, lower, upper, up0, heads, heads_sibling, *refs):
    *fresh, up1, up0_panel, top, work, head = refs
    core, column, chip = meta[1], meta[2], meta[0] // 2
    side = lax.rem(column, 2)
    nb, part = work.shape[0], heads.shape[2]
    for who, parts in ((core, heads), (1 - core, heads_sibling)):
        for h in range(chips):
            at = pl.multiple_of((who * chips + lax.rem(chip + chips - h, chips)) * part, part)
            head[1 - side, pl.ds(at, part)] = parts[h, 0]
            head[side, pl.ds(at, part)] = parts[h, 1]
    assemble(meta, 1, fresh, work)
    up0_panel[...] = dot(lower[0], head[0]).astype(BF16)
    factor = dot(head[1], upper[0]).astype(BF16)
    in_panel, next_panel = column == 0, column == 1
    shown = []
    for j in range(work.shape[1] // nb):
        cols = slice(j * nb, (j + 1) * nb)
        updated = (work[:, cols].astype(F32) - dot(factor, up0[:, cols])).astype(BF16)
        last = dot(lower[1], updated)
        show = last
        if j == 0:
            show = jnp.where(next_panel, updated.astype(F32), show)
            show = jnp.where(in_panel, factor.astype(F32), show)
            last = jnp.where(in_panel | next_panel, 0.0, last)
        up1[:, cols] = last.astype(BF16)
        shown.append(show.astype(BF16))
    top[...] = raw(shown, nb)


def update_kernel(
    begin, line, meta, goal, old, old_sibling, upper, up0, up1, up0_panel, tiles, top0, top1, *rest
):
    held, other = rest[:line], rest[line : 2 * line]
    out, token, panels, block, result, panel_sem, block_sem, out_sem = rest[-8:]
    row, core, column = meta[0], meta[1], meta[2]
    side, place = lax.rem(column, 2), lax.div(column, 2)
    count, cb, nb = block.shape
    rows_of = pl.ds(begin, count)

    def panel_copy(h, which):
        source = (held, other)[which][h].at[pl.ds(0, count)]
        return pltpu.make_async_copy(source, panels.at[lax.rem(side + which, 2)], panel_sem.at[which])

    load = pltpu.make_async_copy(tiles.at[rows_of], block, block_sem)
    load.start()
    for h in range(line):

        @pl.when(place == h)
        def _(h=h):
            panel_copy(h, 0).start()
            panel_copy(h, 1).start()

    def arrived():
        panel_copy(0, 0).wait()
        panel_copy(0, 1).wait()

    def from_factors():
        here = begin + lax.broadcasted_iota(I32, (count, nb), 0)
        pick = jnp.where(here == goal[pl.ds(core, 1), :], 1.0, 0.0)
        pick_sibling = jnp.where(here == goal[pl.ds(1 - core, 1), :], 1.0, 0.0)
        moved = jnp.sum(pick + pick_sibling, axis=1, keepdims=True) > 0.5
        pick, pick_sibling = pick.astype(BF16), pick_sibling.astype(BF16)
        arrived()
        whole = []
        for k in range(2):
            which = lax.rem(k + side, 2)
            brought = dot(pick, old[which]) + dot(pick_sibling, old_sibling[which])
            whole.append(jnp.where(moved, brought, panels[k].astype(F32)))
        factor0 = dot(whole[0].astype(BF16), upper[0]).astype(BF16)
        below = (whole[1] - dot(factor0, up0_panel[...])).astype(BF16)
        factor1 = dot(below, upper[1]).astype(BF16)
        load.wait()
        values = flat(block[...])
        columns = []
        for j in range(cb):
            cols = slice(j * nb, (j + 1) * nb)
            value = values[:, cols].astype(F32) - dot(factor0, up0[:, cols])
            value = value.astype(BF16).astype(F32) - dot(factor1, up1[:, cols])
            if j == 0:
                value = jnp.where(column == 0, factor0.astype(F32), value)
                value = jnp.where(column == 1, factor1.astype(F32), value)
            columns.append(value.astype(BF16))
        result[...] = raw(columns, nb)

    def from_top(top):
        arrived()
        load.wait()
        copy = pltpu.make_async_copy(top.at[rows_of], result, block_sem)
        copy.start()
        copy.wait()

    if begin < nb:
        pl.when(row == 0)(lambda: from_top(top0))
        pl.when(row == 1)(lambda: from_top(top1))
        pl.when(row >= 2)(from_factors)
    else:
        from_factors()
    store = pltpu.make_async_copy(result, out.at[rows_of], out_sem)
    store.start()
    token[...] = jnp.zeros(token.shape, F32)
    store.wait()


def body(matrix, pivots, lower, upper):
    rb, nb, cb, _ = matrix.shape
    rows = rb * nb
    sizes = [nb] * (rb - 1) + [nb // 2] * 2
    begins = [sum(sizes[:i]) for i in range(len(sizes))]
    pieces = len(sizes)
    row_devices = lax.axis_size("prow")
    col_devices = lax.axis_size("pcol")
    chips, line = row_devices // 2, col_devices // 2
    row = lax.axis_index("prow").astype(I32)
    column = lax.axis_index("pcol").astype(I32)
    meta = jnp.stack([row, row % 2, column, jnp.int32(row_devices)])
    tiles = matrix.reshape(rows, cb, nb)

    def to_sibling(value):
        return lax.ppermute(value, "prow", [(r, r ^ 1) for r in range(row_devices)])

    def to_neighbour(value):
        return lax.ppermute(value, "pcol", [(c, c ^ 1) for c in range(col_devices)])

    def to_chip(value, h):
        return lax.ppermute(value, "prow", [(r, (r + 2 * h) % row_devices) for r in range(row_devices)])

    def to_next(value):
        return lax.ppermute(value, "pcol", [(c, c + 2) for c in range(col_devices - 2)])

    order = []

    def run(kernel, operands, outs, also=(), **kwargs):
        after = tuple(order[-1:]) + tuple(also)
        results = call(kernel, operands, outs, after=after, **kwargs)
        order.append(results[-1])
        return results

    last_step = pieces + line - 2

    def piece_out(i):
        return (bf16(sizes[i], nb), VMEM)

    def step_out(k):
        return (bf16(max(sizes[k - p] for p in range(line) if 0 <= k - p < pieces), nb), VMEM)

    own, held, other = [], [], []
    state = {}

    def step(k):
        if k == 0:
            own.extend(run(
                first_kernel, [(tiles, ANY)], [piece_out(0)],
                scratch=[pltpu.VMEM((sizes[0], cb, nb), BF16), DMA], mib=60,
            ))
            value = own[0]
        else:
            also = [other[k - 1]] + state.pop('awaited', [])
            operands = [(meta, SMEM), (state["came"], VMEM)] + [(v, VMEM) for v in own[k : k + 1]]
            (value,) = run(relay_kernel, operands, [step_out(k)], also, us=0.2 if k in (2, 3, 5) else 12.0)
        held.append(value)
        if k < last_step:
            sent = max(sizes[k - p] for p in range(line - 1) if 0 <= k - p < pieces)
            state["came"] = to_next(value[:sent])
        other.append(to_neighbour(value))

    def gather():
        lanes = min(nb, 128)
        spread = jnp.broadcast_to(pivots[:, :, None], (2, nb, lanes))
        table = jax.ShapeDtypeStruct((2, nb), I32)
        results = run(
            gather_kernel,
            [(meta, SMEM), (pivots, VMEM), (spread, VMEM), (tiles, ANY)],
            [piece_out(i) for i in range(1, pieces)] + [(bf16(rows + 8, cb, nb), VMEM)]
            + [(bf16(nb, cb, nb), VMEM)] * 3 + [(table, VMEM)] * 4,
            scratch=[pltpu.VMEM((2, nb), I32), pltpu.SMEM((2, nb), I32), DMA, DMA],
            us=8.0, mib=20,
        )
        own.extend(results[: pieces - 1])
        state["loaded"], send, *rest = results[pieces - 1 :]
        state.update(zip(("keep", "block0", "join", "arrive", "goal", "hops"), rest))
        state["sent"] = to_sibling(send)
        state["block0_sibling"] = to_sibling(state["block0"])

    half = nb // 2
    part = half // chips

    def join():
        joined = run(
            join_kernel,
            [(meta, SMEM), (state["join"], SMEM), (state["keep"], VMEM), (state["sent"], VMEM)],
            [(bf16(half, cb, nb), VMEM)] * 2,
            scratch=[pltpu.VMEM((half + 8, cb, nb), BF16)] * 2,
            us=2.0,
        )
        state["choices"] = [[v] + [to_chip(v, h) for h in range(1, chips)] for v in joined]
        state["fresh"], state["brought"] = [], []
        state["awaited"] = [state["block0_sibling"]]

    def fresh(turn):
        new, brought, *head = run(
            functools.partial(fresh_kernel, turn, chips),
            [(meta, SMEM), (state["hops"], VMEM)] + [(c, VMEM) for c in state["choices"][turn]],
            [(bf16(half, cb * nb), VMEM), (bf16(half, cb, nb), VMEM)]
            + [(bf16(part, nb), VMEM)] * (1 - turn),
            us=1.5, mib=16,
        )
        state["fresh"] += [new, to_sibling(new)]
        state["brought"] += [brought, to_sibling(brought)]
        if head:
            state["head"] = head + [
                lax.ppermute(head[0], "pcol", [(0, 2 * h), (1, 2 * h + 1)]) for h in range(1, line)
            ]
            state["awaited"] = state.get("awaited", []) + state["head"][1:]

    def head_here():
        (mine,) = run(
            by_place_kernel, [(meta, SMEM)] + [(v, VMEM) for v in state["head"]], [(bf16(part, nb), VMEM)], us=0.1
        )
        state["head"] = (mine, to_neighbour(mine))

    def head_pair():
        (pair,) = run(stack_kernel, [(v, VMEM) for v in state["head"]], [(bf16(2, part, nb), VMEM)], us=0.1)
        state["head"] = [pair] + [to_chip(pair, h) for h in range(1, chips)]

    def head_all():
        (mine,) = run(
            stack_kernel, [(v, VMEM) for v in state["head"]], [(bf16(chips, 2, part, nb), VMEM)], us=0.1
        )
        state["heads"] = (mine, to_sibling(mine))

    def old(values, name):
        operands = [(meta, SMEM)] + [(v, VMEM) for v in values[:line]]
        (mine,) = run(functools.partial(old_kernel, line), operands, [(bf16(nb, nb), VMEM)], us=0.1)
        state[name] = [mine] + [to_chip(mine, h) for h in range(1, chips)]
        if name == "old_held":
            state["awaited"] = state.get("awaited", []) + state[name][1:]

    def old_here():
        choices = [v for pair in zip(state["old_held"], state["old_other"]) for v in pair]
        (mine,) = run(
            by_chip_kernel, [(meta, SMEM)] + [(v, VMEM) for v in choices], [(bf16(2, nb, nb), VMEM)], us=0.1
        )
        state["old"] = (mine, to_sibling(mine))

    def scatter():
        sources = state["brought"] + [state["block0"], state["block0_sibling"], state["loaded"]]
        (state["moved"],) = run(
            scatter_kernel,
            [(meta, SMEM), (state["arrive"], SMEM), (state["goal"], SMEM)] + [(v, VMEM) for v in sources],
            [(bf16(rows + 8, cb, nb), VMEM)],
            us=0.1, mib=24,
        )

    def prep0():
        state["up0"], state["top0"] = run(
            prep0_kernel,
            [(meta, SMEM), (lower, VMEM)] + [(v, VMEM) for v in state["fresh"]],
            [(bf16(nb, cb * nb), VMEM), (bf16(nb, cb, nb), VMEM)],
            scratch=[pltpu.VMEM((nb, cb * nb), BF16)],
            us=2.0, mib=16,
        )

    def prep1():
        state["up1"], state["up0_panel"], state["top1"] = run(
            functools.partial(prep1_kernel, chips),
            [(meta, SMEM), (lower, VMEM), (upper, VMEM), (state["up0"], VMEM)]
            + [(v, VMEM) for v in state["heads"]] + [(v, VMEM) for v in state["fresh"]],
            [(bf16(nb, cb * nb), VMEM), (bf16(nb, nb), VMEM), (bf16(nb, cb, nb), VMEM)],
            scratch=[pltpu.VMEM((nb, cb * nb), BF16), pltpu.VMEM((2, nb, nb), BF16)],
            us=3.5, mib=16,
        )

    def update(i):
        operands = [(meta, SMEM), (state["goal"], VMEM)] + [(v, VMEM) for v in state["old"]] + [(upper, VMEM)]
        operands += [(state[name], VMEM) for name in ("up0", "up1", "up0_panel")]
        operands += [(state[name], ANY) for name in ("moved", "top0", "top1")]
        operands += [(v, ANY) for v in held[i : i + line] + other[i : i + line]]
        aliases = {}
        if "result" in state:
            aliases = {len(operands): 0}
            operands.append((state["result"], ANY))
        count = sizes[i]
        state["result"], _ = run(
            functools.partial(update_kernel, begins[i], line),
            operands,
            [(bf16(rows, cb, nb), ANY), (jax.ShapeDtypeStruct((8, 128), F32), VMEM)],
            scratch=[
                pltpu.VMEM((2, count, nb), BF16), pltpu.VMEM((count, cb, nb), BF16),
                pltpu.VMEM((count, cb, nb), BF16), DMA((2,)), DMA, DMA,
            ],
            aliases=aliases,
            us=5.0, mib=24,
        )

    plan = [(0, gather), (1, join), (2, functools.partial(fresh, 0)), (3, head_here), (line - 1, functools.partial(old, held, "old_held")), (3, head_pair), (3, functools.partial(fresh, 1)), (line, functools.partial(old, other, "old_other")), (4, head_all), (4, scatter), (4, prep0), (5, prep1), (5, old_here)]
    for i in range(pieces):
        plan.append((max((6, 6, 7, 7, 8, 8)[min(i, 5)], i + line - 1), functools.partial(update, i)))
    for k in range(last_step + 1):
        step(k)
        while plan and (plan[0][0] <= k or k == last_step):
            plan.pop(0)[1]()
    return state["result"].reshape(matrix.shape)


def solution(mesh):
    placed = (P(None, "prow", None, "pcol"), P(), P(), P())
    return jax.shard_map(
        body, mesh=mesh, in_specs=placed, out_specs=P(None, "prow", None, "pcol"), check_vma=False
    )
```

```python
import functools

import jax
import jax.numpy as jnp
from jax import lax
from jax.experimental import pallas as pl
from jax.experimental.pallas import tpu as pltpu
from jax.sharding import PartitionSpec as P

BF16 = jnp.bfloat16
F32 = jnp.float32
I32 = jnp.int32
SMEM = pl.BlockSpec(memory_space=pltpu.SMEM)
VMEM = pl.BlockSpec(memory_space=pltpu.VMEM)
ANY = pl.BlockSpec(memory_space=pl.ANY)
DMA = pltpu.SemaphoreType.DMA


def dot(a, b):
    return jnp.dot(a, b, preferred_element_type=F32)


def flat(rows):
    return rows.reshape(rows.shape[0], rows.shape[1] * rows.shape[2])


def bf16(*shape):
    return jax.ShapeDtypeStruct(shape, BF16)


def call(kernel, operands, outs, after=(), scratch=(), aliases=None, us=1.0, mib=8):
    count = len(operands)

    def ordered(*refs):
        kernel(*refs[:count], *refs[count + len(after) :])

    return pl.pallas_call(
        ordered,
        out_shape=tuple(shape for shape, _ in outs),
        in_specs=[spec for _, spec in operands] + [ANY] * len(after),
        out_specs=tuple(spec for _, spec in outs),
        scratch_shapes=list(scratch),
        input_output_aliases=aliases or {},
        compiler_params=pltpu.CompilerParams(vmem_limit_bytes=mib * 1024 * 1024),
        cost_estimate=pl.CostEstimate(flops=int(us * 1.1e9), bytes_accessed=0, transcendentals=0),
    )(*[array for array, _ in operands], *after)


def fill_indices(nb, rows, meta, pivots, spread, fetch, join, arrive, goal, hops):
    row, row_devices = meta[0], meta[3]
    chip, chips = row // 2, row_devices // 2
    lanes = spread.shape[2]
    tiles = nb // lanes
    slot = lax.broadcasted_iota(I32, (1, nb), 1)
    pivot0, pivot1 = pivots[0:1, :], pivots[1:2, :]

    def lookup(keys, entry, value):
        parts = [keys[:, t * lanes : (t + 1) * lanes] for t in range(tiles)]

        def add(i, totals):
            begin = pl.multiple_of(i * 8, 8)
            at = begin + lax.broadcasted_iota(I32, (8, lanes), 0)
            here, give = entry(begin, at), value(begin, at)
            return tuple(t + jnp.where(p == here, give, 0) for t, p in zip(totals, parts))

        zero = jnp.zeros((8, lanes), I32)
        totals = lax.fori_loop(0, nb // 8, add, (zero,) * tiles, unroll=8)
        return jnp.concatenate([jnp.sum(t, axis=0, keepdims=True) for t in totals], axis=1)

    def pivot_of(panel):
        return lambda begin, at: spread[panel, pl.ds(begin, 8), :]

    place = lambda begin, at: at + 1
    in_pivots0 = lookup(pivot1, pivot_of(0), place)
    in_pivots1 = lookup(pivot0, pivot_of(1), place)
    top1_in_pivots0 = lookup(nb + slot, pivot_of(0), place)
    over_top1 = lookup(pivot0, lambda begin, at: nb + at, pivot_of(1))
    chained = lookup(nb + in_pivots1 - 1, pivot_of(0), place)

    source0 = pivot0
    source1 = jnp.where(in_pivots0 > 0, in_pivots0 - 1, pivot1)
    second0 = jnp.where(in_pivots1 > 0, jnp.where(chained > 0, chained - 1, nb + in_pivots1 - 1), slot)
    second1 = jnp.where(top1_in_pivots0 > 0, top1_in_pivots0 - 1, nb + slot)
    target0 = jnp.where(over_top1 > 0, over_top1, jnp.where(in_pivots1 > 0, nb + in_pivots1 - 1, pivot0))
    target1 = jnp.where(top1_in_pivots0 > 0, top1_in_pivots0 - 1, pivot1)

    def holder(index):
        return lax.rem(lax.div(index, nb), row_devices)

    def local(index):
        return lax.div(index, nb * row_devices) * nb + lax.rem(index, nb)

    def placed(index):
        mine = (holder(index) == row) & (index >= 2 * nb)
        return jnp.where(mine, local(index), rows)

    for k, (source, second, target) in enumerate(((source0, second0, target0), (source1, second1, target1))):
        from_chip = lax.div(holder(source), 2)
        wanted = jnp.where(from_chip == chip, source, second)
        at = (slice(k, k + 1), slice(None))
        fetch[at] = local(wanted)
        join[at] = jnp.where(holder(wanted) == row, lax.rem(slot, nb // 2), nb // 2)
        arrive[at] = placed(source)
        goal[at] = placed(target)
        hops[at] = lax.rem(chip + chips - from_chip, chips)


def copy_rows(count, target, target_at, origin, origin_at):
    def copy(i, carry):
        target[target_at(i)] = origin[origin_at(i)]
        return carry

    lax.fori_loop(0, count, copy, 0, unroll=16)


def first_kernel(tiles, piece, work, sem):
    load = pltpu.make_async_copy(tiles.at[pl.ds(0, piece.shape[0])], work, sem)
    load.start()
    load.wait()
    piece[...] = flat(work[...])[:, : piece.shape[1]]


def gather_kernel(meta, pivots, spread, tiles, *refs):
    *pieces, loaded, send, keep, block0, join, arrive, goal, hops, fetch, fetch_table, load_sem, table_sem = refs
    nb = send.shape[0]
    rows = tiles.shape[0]
    core = meta[1]
    load = pltpu.make_async_copy(tiles, loaded.at[pl.ds(0, rows)], load_sem)
    load.start()
    fill_indices(nb, rows, meta, pivots, spread, fetch, join, arrive, goal, hops)
    table = pltpu.make_async_copy(fetch, fetch_table, table_sem)
    table.start()
    table.wait()
    load.wait()
    begin = nb
    for piece in pieces:
        end = begin + piece.shape[0]
        piece[...] = flat(loaded[begin:end])[:, :nb]
        begin = end
    half, side = nb // 2, lax.rem(meta[2], 2)
    for turn, b in enumerate((1 - side, side)):
        to = lambda i, turn=turn: turn * half + i
        copy_rows(half, send, to, loaded, lambda i, b=b: fetch_table[b, (1 - core) * half + i])
        copy_rows(half, keep, to, loaded, lambda i, b=b: fetch_table[b, core * half + i])
    block0[...] = loaded[0:nb]


def join_kernel(meta, join, keep, came, joined0, joined1, work0, work1):
    half = joined0.shape[0]
    core, side = meta[1], lax.rem(meta[2], 2)
    for turn, (b, work, joined) in enumerate(((1 - side, work0, joined0), (side, work1, joined1))):
        work[0:half] = came[turn * half : (turn + 1) * half]
        copy_rows(
            half, work, lambda i, b=b: join[b, core * half + i], keep, lambda i, turn=turn: turn * half + i
        )
        joined[...] = work[0:half]


def scatter_kernel(meta, arrive, goal, *refs):
    *came, old, old_sibling, tiles, out = refs
    core, side, chip = meta[1], lax.rem(meta[2], 2), meta[0] // 2
    nb = old.shape[0]
    half = nb // 2
    out[...] = tiles[...]

    @pl.when(chip == 0)
    def _():
        copy_rows(nb, out, lambda i: goal[core, i], old, lambda i: i)
        copy_rows(nb, out, lambda i: goal[1 - core, i], old_sibling, lambda i: i)

    @pl.when(chip != 0)
    def _():
        for turn, b in enumerate((1 - side, side)):
            for values, who in ((came[2 * turn], core), (came[2 * turn + 1], 1 - core)):
                copy_rows(half, out, lambda i, b=b, who=who: arrive[b, who * half + i], values, lambda i: i)


def relay_kernel(meta, came, *refs):
    *own, held = refs
    place = lax.div(meta[2], 2)
    for piece in own:

        @pl.when(place == 0)
        def _(piece=piece):
            held[0 : piece.shape[0]] = piece[...]

    @pl.when(place != 0)
    def _():
        count = min(came.shape[0], held.shape[0])
        held[0:count] = came[0:count]


def old_kernel(line, meta, *refs):
    *choices, old = refs
    for h in range(line):

        @pl.when(lax.div(meta[2], 2) == h)
        def _(h=h):
            old[...] = choices[h][0 : old.shape[0]]


def by_chip_kernel(meta, *refs):
    *choices, out = refs
    for h in range(len(choices) // 2):

        @pl.when(meta[0] // 2 == h)
        def _(h=h):
            out[0] = choices[2 * h][...]
            out[1] = choices[2 * h + 1][...]


def by_place_kernel(meta, *refs):
    out = refs[-1]
    for h, choice in enumerate(refs[:-1]):

        @pl.when(lax.div(meta[2], 2) == h)
        def _(choice=choice):
            out[...] = choice[...]


def stack_kernel(*refs):
    *entries, out = refs
    for i, entry in enumerate(entries):
        out[i] = entry[...]


def choose(hop, choices):
    value = flat(choices[0]).astype(F32)
    for h, other in enumerate(choices[1:], 1):
        value = jnp.where(hop == h, flat(other).astype(F32), value)
    return value.astype(BF16)


def fresh_kernel(turn, chips, meta, hops, *refs):
    choices, (fresh, brought, *head) = refs[:chips], refs[chips:]
    half = fresh.shape[0]
    core, side, chip = meta[1], lax.rem(meta[2], 2), meta[0] // 2
    b = side if turn else 1 - side
    hop = jnp.broadcast_to(hops[pl.ds(b, 1), :], (8, 2 * half)).T[:, 0:1]
    hop = jnp.where(core == 0, hop[:half], hop[half:])
    fresh[...] = choose(hop, [c[...] for c in choices])
    if head:
        part, nb = head[0].shape
        head[0][...] = fresh[pl.ds(pl.multiple_of(chip * part, part), part), :nb]
    if chips == 1:
        brought[...] = choices[0][...]
    for h in range(1, chips):

        @pl.when((chip == h) | ((chip == 0) & (h == 1)))
        def _(h=h):
            brought[...] = choices[h][...]


def assemble(meta, b, fresh, work):
    core, side = meta[1], lax.rem(meta[2], 2)
    half = work.shape[0] // 2
    for turn, which in enumerate((1 - side, side)):

        @pl.when(which == b)
        def _(turn=turn):
            work[pl.ds(pl.multiple_of(core * half, half), half)] = fresh[2 * turn][...]
            work[pl.ds(pl.multiple_of((1 - core) * half, half), half)] = fresh[2 * turn + 1][...]


def raw(columns, nb):
    joined = jnp.concatenate(columns, axis=1)
    return joined.reshape(joined.shape[0], len(columns), nb)


def prep0_kernel(meta, lower, *refs):
    *fresh, up0, top, work = refs
    column = meta[2]
    nb = work.shape[0]
    assemble(meta, 0, fresh, work)
    shown = []
    for j in range(work.shape[1] // nb):
        cols = slice(j * nb, (j + 1) * nb)
        product = dot(lower[0], work[:, cols])
        show = product
        if j == 0:
            show = jnp.where(column == 0, work[:, cols].astype(F32), product)
            product = jnp.where(column == 0, 0.0, product)
        up0[:, cols] = product.astype(BF16)
        shown.append(show.astype(BF16))
    top[...] = raw(shown, nb)


def prep1_kernel(chips, meta, lower, upper, up0, heads, heads_sibling, *refs):
    *fresh, up1, up0_panel, top, work, head = refs
    core, column, chip = meta[1], meta[2], meta[0] // 2
    side = lax.rem(column, 2)
    nb, part = work.shape[0], heads.shape[2]
    for who, parts in ((core, heads), (1 - core, heads_sibling)):
        for h in range(chips):
            at = pl.multiple_of((who * chips + lax.rem(chip + chips - h, chips)) * part, part)
            head[1 - side, pl.ds(at, part)] = parts[h, 0]
            head[side, pl.ds(at, part)] = parts[h, 1]
    assemble(meta, 1, fresh, work)
    up0_panel[...] = dot(lower[0], head[0]).astype(BF16)
    factor = dot(head[1], upper[0]).astype(BF16)
    in_panel, next_panel = column == 0, column == 1
    shown = []
    for j in range(work.shape[1] // nb):
        cols = slice(j * nb, (j + 1) * nb)
        updated = (work[:, cols].astype(F32) - dot(factor, up0[:, cols])).astype(BF16)
        last = dot(lower[1], updated)
        show = last
        if j == 0:
            show = jnp.where(next_panel, updated.astype(F32), show)
            show = jnp.where(in_panel, factor.astype(F32), show)
            last = jnp.where(in_panel | next_panel, 0.0, last)
        up1[:, cols] = last.astype(BF16)
        shown.append(show.astype(BF16))
    top[...] = raw(shown, nb)


def update_kernel(
    begin, line, meta, goal, old, old_sibling, upper, up0, up1, up0_panel, tiles, top0, top1, *rest
):
    held, other = rest[:line], rest[line : 2 * line]
    out, token, panels, block, result, panel_sem, block_sem, out_sem = rest[-8:]
    row, core, column = meta[0], meta[1], meta[2]
    side, place = lax.rem(column, 2), lax.div(column, 2)
    count, cb, nb = block.shape
    rows_of = pl.ds(begin, count)

    def panel_copy(h, which):
        source = (held, other)[which][h].at[pl.ds(0, count)]
        return pltpu.make_async_copy(source, panels.at[lax.rem(side + which, 2)], panel_sem.at[which])

    load = pltpu.make_async_copy(tiles.at[rows_of], block, block_sem)
    load.start()
    for h in range(line):

        @pl.when(place == h)
        def _(h=h):
            panel_copy(h, 0).start()
            panel_copy(h, 1).start()

    def arrived():
        panel_copy(0, 0).wait()
        panel_copy(0, 1).wait()

    def from_factors():
        here = begin + lax.broadcasted_iota(I32, (count, nb), 0)
        pick = jnp.where(here == goal[pl.ds(core, 1), :], 1.0, 0.0)
        pick_sibling = jnp.where(here == goal[pl.ds(1 - core, 1), :], 1.0, 0.0)
        moved = jnp.sum(pick + pick_sibling, axis=1, keepdims=True) > 0.5
        pick, pick_sibling = pick.astype(BF16), pick_sibling.astype(BF16)
        arrived()
        whole = []
        for k in range(2):
            which = lax.rem(k + side, 2)
            brought = dot(pick, old[which]) + dot(pick_sibling, old_sibling[which])
            whole.append(jnp.where(moved, brought, panels[k].astype(F32)))
        factor0 = dot(whole[0].astype(BF16), upper[0]).astype(BF16)
        below = (whole[1] - dot(factor0, up0_panel[...])).astype(BF16)
        factor1 = dot(below, upper[1]).astype(BF16)
        load.wait()
        values = flat(block[...])
        columns = []
        for j in range(cb):
            cols = slice(j * nb, (j + 1) * nb)
            value = values[:, cols].astype(F32) - dot(factor0, up0[:, cols])
            value = value.astype(BF16).astype(F32) - dot(factor1, up1[:, cols])
            if j == 0:
                value = jnp.where(column == 0, factor0.astype(F32), value)
                value = jnp.where(column == 1, factor1.astype(F32), value)
            columns.append(value.astype(BF16))
        result[...] = raw(columns, nb)

    def from_top(top):
        arrived()
        load.wait()
        copy = pltpu.make_async_copy(top.at[rows_of], result, block_sem)
        copy.start()
        copy.wait()

    if begin < nb:
        pl.when(row == 0)(lambda: from_top(top0))
        pl.when(row == 1)(lambda: from_top(top1))
        pl.when(row >= 2)(from_factors)
    else:
        from_factors()
    store = pltpu.make_async_copy(result, out.at[rows_of], out_sem)
    store.start()
    token[...] = jnp.zeros(token.shape, F32)
    store.wait()


def body(matrix, pivots, lower, upper):
    rb, nb, cb, _ = matrix.shape
    rows = rb * nb
    sizes = [nb] * (rb - 1) + [nb // 2] * 2
    begins = [sum(sizes[:i]) for i in range(len(sizes))]
    pieces = len(sizes)
    row_devices = lax.axis_size("prow")
    col_devices = lax.axis_size("pcol")
    chips, line = row_devices // 2, col_devices // 2
    row = lax.axis_index("prow").astype(I32)
    column = lax.axis_index("pcol").astype(I32)
    meta = jnp.stack([row, row % 2, column, jnp.int32(row_devices)])
    tiles = matrix.reshape(rows, cb, nb)

    def to_sibling(value):
        return lax.ppermute(value, "prow", [(r, r ^ 1) for r in range(row_devices)])

    def to_neighbour(value):
        return lax.ppermute(value, "pcol", [(c, c ^ 1) for c in range(col_devices)])

    def to_chip(value, h):
        return lax.ppermute(value, "prow", [(r, (r + 2 * h) % row_devices) for r in range(row_devices)])

    def to_next(value):
        return lax.ppermute(value, "pcol", [(c, c + 2) for c in range(col_devices - 2)])

    order = []

    def run(kernel, operands, outs, also=(), **kwargs):
        after = tuple(order[-1:]) + tuple(also)
        results = call(kernel, operands, outs, after=after, **kwargs)
        order.append(results[-1])
        return results

    last_step = pieces + line - 2

    def piece_out(i):
        return (bf16(sizes[i], nb), VMEM)

    def step_out(k):
        return (bf16(max(sizes[k - p] for p in range(line) if 0 <= k - p < pieces), nb), VMEM)

    own, held, other = [], [], []
    state = {}

    def step(k):
        if k == 0:
            own.extend(run(
                first_kernel, [(tiles, ANY)], [piece_out(0)],
                scratch=[pltpu.VMEM((sizes[0], cb, nb), BF16), DMA], mib=60,
            ))
            value = own[0]
        else:
            also = [other[k - 1]] + state.pop('awaited', [])
            operands = [(meta, SMEM), (state["came"], VMEM)] + [(v, VMEM) for v in own[k : k + 1]]
            (value,) = run(relay_kernel, operands, [step_out(k)], also, us=0.2 if k in (2, 3, 5) else 12.0)
        held.append(value)
        if k < last_step:
            sent = max(sizes[k - p] for p in range(line - 1) if 0 <= k - p < pieces)
            state["came"] = to_next(value[:sent])
        other.append(to_neighbour(value))

    def gather():
        lanes = min(nb, 128)
        spread = jnp.broadcast_to(pivots[:, :, None], (2, nb, lanes))
        table = jax.ShapeDtypeStruct((2, nb), I32)
        results = run(
            gather_kernel,
            [(meta, SMEM), (pivots, VMEM), (spread, VMEM), (tiles, ANY)],
            [piece_out(i) for i in range(1, pieces)] + [(bf16(rows + 8, cb, nb), VMEM)]
            + [(bf16(nb, cb, nb), VMEM)] * 3 + [(table, VMEM)] * 4,
            scratch=[pltpu.VMEM((2, nb), I32), pltpu.SMEM((2, nb), I32), DMA, DMA],
            us=8.0, mib=20,
        )
        own.extend(results[: pieces - 1])
        state["loaded"], send, *rest = results[pieces - 1 :]
        state.update(zip(("keep", "block0", "join", "arrive", "goal", "hops"), rest))
        state["sent"] = to_sibling(send)
        state["block0_sibling"] = to_sibling(state["block0"])

    half = nb // 2
    part = half // chips

    def join():
        joined = run(
            join_kernel,
            [(meta, SMEM), (state["join"], SMEM), (state["keep"], VMEM), (state["sent"], VMEM)],
            [(bf16(half, cb, nb), VMEM)] * 2,
            scratch=[pltpu.VMEM((half + 8, cb, nb), BF16)] * 2,
            us=2.0,
        )
        state["choices"] = [[v] + [to_chip(v, h) for h in range(1, chips)] for v in joined]
        state["fresh"], state["brought"] = [], []
        state["awaited"] = [state["block0_sibling"]]

    def fresh(turn):
        new, brought, *head = run(
            functools.partial(fresh_kernel, turn, chips),
            [(meta, SMEM), (state["hops"], VMEM)] + [(c, VMEM) for c in state["choices"][turn]],
            [(bf16(half, cb * nb), VMEM), (bf16(half, cb, nb), VMEM)]
            + [(bf16(part, nb), VMEM)] * (1 - turn),
            us=1.5, mib=16,
        )
        state["fresh"] += [new, to_sibling(new)]
        state["brought"] += [brought, to_sibling(brought)]
        if head:
            state["head"] = head + [
                lax.ppermute(head[0], "pcol", [(0, 2 * h), (1, 2 * h + 1)]) for h in range(1, line)
            ]
            state["awaited"] = state.get("awaited", []) + state["head"][1:]

    def head_here():
        (mine,) = run(
            by_place_kernel, [(meta, SMEM)] + [(v, VMEM) for v in state["head"]], [(bf16(part, nb), VMEM)], us=0.1
        )
        state["head"] = (mine, to_neighbour(mine))

    def head_pair():
        (pair,) = run(stack_kernel, [(v, VMEM) for v in state["head"]], [(bf16(2, part, nb), VMEM)], us=0.1)
        state["head"] = [pair] + [to_chip(pair, h) for h in range(1, chips)]

    def head_all():
        (mine,) = run(
            stack_kernel, [(v, VMEM) for v in state["head"]], [(bf16(chips, 2, part, nb), VMEM)], us=0.1
        )
        state["heads"] = (mine, to_sibling(mine))

    def old(values, name):
        operands = [(meta, SMEM)] + [(v, VMEM) for v in values[:line]]
        (mine,) = run(functools.partial(old_kernel, line), operands, [(bf16(nb, nb), VMEM)], us=0.1)
        state[name] = [mine] + [to_chip(mine, h) for h in range(1, chips)]
        if name == "old_held":
            state["awaited"] = state.get("awaited", []) + state[name][1:]

    def old_here():
        choices = [v for pair in zip(state["old_held"], state["old_other"]) for v in pair]
        (mine,) = run(
            by_chip_kernel, [(meta, SMEM)] + [(v, VMEM) for v in choices], [(bf16(2, nb, nb), VMEM)], us=0.1
        )
        state["old"] = (mine, to_sibling(mine))

    def scatter():
        sources = state["brought"] + [state["block0"], state["block0_sibling"], state["loaded"]]
        (state["moved"],) = run(
            scatter_kernel,
            [(meta, SMEM), (state["arrive"], SMEM), (state["goal"], SMEM)] + [(v, VMEM) for v in sources],
            [(bf16(rows + 8, cb, nb), VMEM)],
            us=0.1, mib=24,
        )

    def prep0():
        state["up0"], state["top0"] = run(
            prep0_kernel,
            [(meta, SMEM), (lower, VMEM)] + [(v, VMEM) for v in state["fresh"]],
            [(bf16(nb, cb * nb), VMEM), (bf16(nb, cb, nb), VMEM)],
            scratch=[pltpu.VMEM((nb, cb * nb), BF16)],
            us=2.0, mib=16,
        )

    def prep1():
        state["up1"], state["up0_panel"], state["top1"] = run(
            functools.partial(prep1_kernel, chips),
            [(meta, SMEM), (lower, VMEM), (upper, VMEM), (state["up0"], VMEM)]
            + [(v, VMEM) for v in state["heads"]] + [(v, VMEM) for v in state["fresh"]],
            [(bf16(nb, cb * nb), VMEM), (bf16(nb, nb), VMEM), (bf16(nb, cb, nb), VMEM)],
            scratch=[pltpu.VMEM((nb, cb * nb), BF16), pltpu.VMEM((2, nb, nb), BF16)],
            us=3.5, mib=16,
        )

    def update(i):
        operands = [(meta, SMEM), (state["goal"], VMEM)] + [(v, VMEM) for v in state["old"]] + [(upper, VMEM)]
        operands += [(state[name], VMEM) for name in ("up0", "up1", "up0_panel")]
        operands += [(state[name], ANY) for name in ("moved", "top0", "top1")]
        operands += [(v, ANY) for v in held[i : i + line] + other[i : i + line]]
        aliases = {}
        if "result" in state:
            aliases = {len(operands): 0}
            operands.append((state["result"], ANY))
        count = sizes[i]
        state["result"], _ = run(
            functools.partial(update_kernel, begins[i], line),
            operands,
            [(bf16(rows, cb, nb), ANY), (jax.ShapeDtypeStruct((8, 128), F32), VMEM)],
            scratch=[
                pltpu.VMEM((2, count, nb), BF16), pltpu.VMEM((count, cb, nb), BF16),
                pltpu.VMEM((count, cb, nb), BF16), DMA((2,)), DMA, DMA,
            ],
            aliases=aliases,
            us=5.0, mib=24,
        )

    plan = [(0, gather), (1, join), (2, functools.partial(fresh, 0)), (3, head_here), (line - 1, functools.partial(old, held, "old_held")), (3, head_pair), (3, functools.partial(fresh, 1)), (line, functools.partial(old, other, "old_other")), (4, scatter), (4, prep0), (5, head_all), (5, old_here), (5, prep1)]
    for i in range(pieces):
        plan.append((max((6, 6, 7, 8, 8, 8)[min(i, 5)], i + line - 1), functools.partial(update, i)))
    for k in range(last_step + 1):
        step(k)
        while plan and (plan[0][0] <= k or k == last_step):
            plan.pop(0)[1]()
    return state["result"].reshape(matrix.shape)


def solution(mesh):
    placed = (P(None, "prow", None, "pcol"), P(), P(), P())
    return jax.shard_map(
        body, mesh=mesh, in_specs=placed, out_specs=P(None, "prow", None, "pcol"), check_vma=False
    )
```

```python
import functools

import jax
import jax.numpy as jnp
from jax import lax
from jax.experimental import pallas as pl
from jax.experimental.pallas import tpu as pltpu
from jax.sharding import PartitionSpec as P

BF16 = jnp.bfloat16
F32 = jnp.float32
I32 = jnp.int32
SMEM = pl.BlockSpec(memory_space=pltpu.SMEM)
VMEM = pl.BlockSpec(memory_space=pltpu.VMEM)
ANY = pl.BlockSpec(memory_space=pl.ANY)
DMA = pltpu.SemaphoreType.DMA


def dot(a, b):
    return jnp.dot(a, b, preferred_element_type=F32)


def flat(rows):
    return rows.reshape(rows.shape[0], rows.shape[1] * rows.shape[2])


def bf16(*shape):
    return jax.ShapeDtypeStruct(shape, BF16)


def call(kernel, operands, outs, after=(), scratch=(), aliases=None, us=1.0, mib=8):
    count = len(operands)

    def ordered(*refs):
        kernel(*refs[:count], *refs[count + len(after) :])

    return pl.pallas_call(
        ordered,
        out_shape=tuple(shape for shape, _ in outs),
        in_specs=[spec for _, spec in operands] + [ANY] * len(after),
        out_specs=tuple(spec for _, spec in outs),
        scratch_shapes=list(scratch),
        input_output_aliases=aliases or {},
        compiler_params=pltpu.CompilerParams(vmem_limit_bytes=mib * 1024 * 1024),
        cost_estimate=pl.CostEstimate(flops=int(us * 1.1e9), bytes_accessed=0, transcendentals=0),
    )(*[array for array, _ in operands], *after)


def fill_indices(nb, rows, meta, pivots, spread, fetch, join, arrive, goal, hops):
    row, row_devices = meta[0], meta[3]
    chip, chips = row // 2, row_devices // 2
    lanes = spread.shape[2]
    tiles = nb // lanes
    slot = lax.broadcasted_iota(I32, (1, nb), 1)
    pivot0, pivot1 = pivots[0:1, :], pivots[1:2, :]

    def lookup(keys, entry, value):
        parts = [keys[:, t * lanes : (t + 1) * lanes] for t in range(tiles)]

        def add(i, totals):
            begin = pl.multiple_of(i * 8, 8)
            at = begin + lax.broadcasted_iota(I32, (8, lanes), 0)
            here, give = entry(begin, at), value(begin, at)
            return tuple(t + jnp.where(p == here, give, 0) for t, p in zip(totals, parts))

        zero = jnp.zeros((8, lanes), I32)
        totals = lax.fori_loop(0, nb // 8, add, (zero,) * tiles, unroll=8)
        return jnp.concatenate([jnp.sum(t, axis=0, keepdims=True) for t in totals], axis=1)

    def pivot_of(panel):
        return lambda begin, at: spread[panel, pl.ds(begin, 8), :]

    place = lambda begin, at: at + 1
    in_pivots0 = lookup(pivot1, pivot_of(0), place)
    in_pivots1 = lookup(pivot0, pivot_of(1), place)
    top1_in_pivots0 = lookup(nb + slot, pivot_of(0), place)
    over_top1 = lookup(pivot0, lambda begin, at: nb + at, pivot_of(1))
    chained = lookup(nb + in_pivots1 - 1, pivot_of(0), place)

    source0 = pivot0
    source1 = jnp.where(in_pivots0 > 0, in_pivots0 - 1, pivot1)
    second0 = jnp.where(in_pivots1 > 0, jnp.where(chained > 0, chained - 1, nb + in_pivots1 - 1), slot)
    second1 = jnp.where(top1_in_pivots0 > 0, top1_in_pivots0 - 1, nb + slot)
    target0 = jnp.where(over_top1 > 0, over_top1, jnp.where(in_pivots1 > 0, nb + in_pivots1 - 1, pivot0))
    target1 = jnp.where(top1_in_pivots0 > 0, top1_in_pivots0 - 1, pivot1)

    def holder(index):
        return lax.rem(lax.div(index, nb), row_devices)

    def local(index):
        return lax.div(index, nb * row_devices) * nb + lax.rem(index, nb)

    def placed(index):
        mine = (holder(index) == row) & (index >= 2 * nb)
        return jnp.where(mine, local(index), rows)

    for k, (source, second, target) in enumerate(((source0, second0, target0), (source1, second1, target1))):
        from_chip = lax.div(holder(source), 2)
        wanted = jnp.where(from_chip == chip, source, second)
        at = (slice(k, k + 1), slice(None))
        fetch[at] = local(wanted)
        join[at] = jnp.where(holder(wanted) == row, lax.rem(slot, nb // 2), nb // 2)
        arrive[at] = placed(source)
        goal[at] = placed(target)
        hops[at] = lax.rem(chip + chips - from_chip, chips)


def copy_rows(count, target, target_at, origin, origin_at):
    def copy(i, carry):
        target[target_at(i)] = origin[origin_at(i)]
        return carry

    lax.fori_loop(0, count, copy, 0, unroll=16)


def first_kernel(tiles, piece, work, sem):
    load = pltpu.make_async_copy(tiles.at[pl.ds(0, piece.shape[0])], work, sem)
    load.start()
    load.wait()
    piece[...] = flat(work[...])[:, : piece.shape[1]]


def gather_kernel(meta, pivots, spread, tiles, *refs):
    *pieces, loaded, send, keep, block0, join, arrive, goal, hops, fetch, fetch_table, load_sem, table_sem = refs
    nb = send.shape[0]
    rows = tiles.shape[0]
    core = meta[1]
    load = pltpu.make_async_copy(tiles, loaded.at[pl.ds(0, rows)], load_sem)
    load.start()
    fill_indices(nb, rows, meta, pivots, spread, fetch, join, arrive, goal, hops)
    table = pltpu.make_async_copy(fetch, fetch_table, table_sem)
    table.start()
    table.wait()
    load.wait()
    begin = nb
    for piece in pieces:
        end = begin + piece.shape[0]
        piece[...] = flat(loaded[begin:end])[:, :nb]
        begin = end
    half, side = nb // 2, lax.rem(meta[2], 2)
    for turn, b in enumerate((1 - side, side)):
        to = lambda i, turn=turn: turn * half + i
        copy_rows(half, send, to, loaded, lambda i, b=b: fetch_table[b, (1 - core) * half + i])
        copy_rows(half, keep, to, loaded, lambda i, b=b: fetch_table[b, core * half + i])
    block0[...] = loaded[0:nb]


def join_kernel(meta, join, keep, came, joined0, joined1, work0, work1):
    half = joined0.shape[0]
    core, side = meta[1], lax.rem(meta[2], 2)
    for turn, (b, work, joined) in enumerate(((1 - side, work0, joined0), (side, work1, joined1))):
        work[0:half] = came[turn * half : (turn + 1) * half]
        copy_rows(
            half, work, lambda i, b=b: join[b, core * half + i], keep, lambda i, turn=turn: turn * half + i
        )
        joined[...] = work[0:half]


def scatter_kernel(meta, arrive, goal, *refs):
    *came, old, old_sibling, tiles, out = refs
    core, side, chip = meta[1], lax.rem(meta[2], 2), meta[0] // 2
    nb = old.shape[0]
    half = nb // 2
    out[...] = tiles[...]

    @pl.when(chip == 0)
    def _():
        copy_rows(nb, out, lambda i: goal[core, i], old, lambda i: i)
        copy_rows(nb, out, lambda i: goal[1 - core, i], old_sibling, lambda i: i)

    @pl.when(chip != 0)
    def _():
        for turn, b in enumerate((1 - side, side)):
            for values, who in ((came[2 * turn], core), (came[2 * turn + 1], 1 - core)):
                copy_rows(half, out, lambda i, b=b, who=who: arrive[b, who * half + i], values, lambda i: i)


def relay_kernel(meta, came, *refs):
    *own, held = refs
    place = lax.div(meta[2], 2)
    for piece in own:

        @pl.when(place == 0)
        def _(piece=piece):
            held[0 : piece.shape[0]] = piece[...]

    @pl.when(place != 0)
    def _():
        count = min(came.shape[0], held.shape[0])
        held[0:count] = came[0:count]


def old_kernel(line, meta, *refs):
    *choices, old = refs
    for h in range(line):

        @pl.when(lax.div(meta[2], 2) == h)
        def _(h=h):
            old[...] = choices[h][0 : old.shape[0]]


def by_chip_kernel(meta, *refs):
    *choices, out = refs
    for h in range(len(choices) // 2):

        @pl.when(meta[0] // 2 == h)
        def _(h=h):
            out[0] = choices[2 * h][...]
            out[1] = choices[2 * h + 1][...]


def by_span_kernel(span, meta, mine, came, out):
    first = lax.rem(lax.div(meta[2], 2), 2 * span) == 0

    @pl.when(first)
    def _():
        out[...] = mine[...]

    @pl.when(jnp.logical_not(first))
    def _():
        out[...] = came[...]


def stack_kernel(*refs):
    *entries, out = refs
    for i, entry in enumerate(entries):
        out[i] = entry[...]


def choose(hop, choices):
    value = flat(choices[0]).astype(F32)
    for h, other in enumerate(choices[1:], 1):
        value = jnp.where(hop == h, flat(other).astype(F32), value)
    return value.astype(BF16)


def fresh_kernel(turn, chips, meta, hops, *refs):
    choices, (fresh, brought, *head) = refs[:chips], refs[chips:]
    half = fresh.shape[0]
    core, side, chip = meta[1], lax.rem(meta[2], 2), meta[0] // 2
    b = side if turn else 1 - side
    hop = jnp.broadcast_to(hops[pl.ds(b, 1), :], (8, 2 * half)).T[:, 0:1]
    hop = jnp.where(core == 0, hop[:half], hop[half:])
    fresh[...] = choose(hop, [c[...] for c in choices])
    if head:
        part, nb = head[0].shape
        head[0][...] = fresh[pl.ds(pl.multiple_of(chip * part, part), part), :nb]
    if chips == 1:
        brought[...] = choices[0][...]
    for h in range(1, chips):

        @pl.when((chip == h) | ((chip == 0) & (h == 1)))
        def _(h=h):
            brought[...] = choices[h][...]


def assemble(meta, b, fresh, work):
    core, side = meta[1], lax.rem(meta[2], 2)
    half = work.shape[0] // 2
    for turn, which in enumerate((1 - side, side)):

        @pl.when(which == b)
        def _(turn=turn):
            work[pl.ds(pl.multiple_of(core * half, half), half)] = fresh[2 * turn][...]
            work[pl.ds(pl.multiple_of((1 - core) * half, half), half)] = fresh[2 * turn + 1][...]


def raw(columns, nb):
    joined = jnp.concatenate(columns, axis=1)
    return joined.reshape(joined.shape[0], len(columns), nb)


def prep0_kernel(meta, lower, *refs):
    *fresh, up0, top, work = refs
    column = meta[2]
    nb = work.shape[0]
    assemble(meta, 0, fresh, work)
    shown = []
    for j in range(work.shape[1] // nb):
        cols = slice(j * nb, (j + 1) * nb)
        product = dot(lower[0], work[:, cols])
        show = product
        if j == 0:
            show = jnp.where(column == 0, work[:, cols].astype(F32), product)
            product = jnp.where(column == 0, 0.0, product)
        up0[:, cols] = product.astype(BF16)
        shown.append(show.astype(BF16))
    top[...] = raw(shown, nb)


def prep1_kernel(chips, meta, lower, upper, up0, heads, heads_sibling, *refs):
    *fresh, up1, up0_panel, top, work, head = refs
    core, column, chip = meta[1], meta[2], meta[0] // 2
    side = lax.rem(column, 2)
    nb, part = work.shape[0], heads.shape[2]
    for who, parts in ((core, heads), (1 - core, heads_sibling)):
        for h in range(chips):
            at = pl.multiple_of((who * chips + lax.rem(chip + chips - h, chips)) * part, part)
            head[1 - side, pl.ds(at, part)] = parts[h, 0]
            head[side, pl.ds(at, part)] = parts[h, 1]
    assemble(meta, 1, fresh, work)
    up0_panel[...] = dot(lower[0], head[0]).astype(BF16)
    factor = dot(head[1], upper[0]).astype(BF16)
    in_panel, next_panel = column == 0, column == 1
    shown = []
    for j in range(work.shape[1] // nb):
        cols = slice(j * nb, (j + 1) * nb)
        updated = (work[:, cols].astype(F32) - dot(factor, up0[:, cols])).astype(BF16)
        last = dot(lower[1], updated)
        show = last
        if j == 0:
            show = jnp.where(next_panel, updated.astype(F32), show)
            show = jnp.where(in_panel, factor.astype(F32), show)
            last = jnp.where(in_panel | next_panel, 0.0, last)
        up1[:, cols] = last.astype(BF16)
        shown.append(show.astype(BF16))
    top[...] = raw(shown, nb)


def update_kernel(
    begin, line, meta, goal, old, old_sibling, upper, up0, up1, up0_panel, tiles, top0, top1, *rest
):
    held, other = rest[:line], rest[line : 2 * line]
    out, token, panels, block, result, panel_sem, block_sem, out_sem = rest[-8:]
    row, core, column = meta[0], meta[1], meta[2]
    side, place = lax.rem(column, 2), lax.div(column, 2)
    count, cb, nb = block.shape
    rows_of = pl.ds(begin, count)

    def panel_copy(h, which):
        source = (held, other)[which][h].at[pl.ds(0, count)]
        return pltpu.make_async_copy(source, panels.at[lax.rem(side + which, 2)], panel_sem.at[which])

    load = pltpu.make_async_copy(tiles.at[rows_of], block, block_sem)
    load.start()
    for h in range(line):

        @pl.when(place == h)
        def _(h=h):
            panel_copy(h, 0).start()
            panel_copy(h, 1).start()

    def arrived():
        panel_copy(0, 0).wait()
        panel_copy(0, 1).wait()

    def from_factors():
        here = begin + lax.broadcasted_iota(I32, (count, nb), 0)
        pick = jnp.where(here == goal[pl.ds(core, 1), :], 1.0, 0.0)
        pick_sibling = jnp.where(here == goal[pl.ds(1 - core, 1), :], 1.0, 0.0)
        moved = jnp.sum(pick + pick_sibling, axis=1, keepdims=True) > 0.5
        pick, pick_sibling = pick.astype(BF16), pick_sibling.astype(BF16)
        arrived()
        whole = []
        for k in range(2):
            which = lax.rem(k + side, 2)
            brought = dot(pick, old[which]) + dot(pick_sibling, old_sibling[which])
            whole.append(jnp.where(moved, brought, panels[k].astype(F32)))
        factor0 = dot(whole[0].astype(BF16), upper[0]).astype(BF16)
        below = (whole[1] - dot(factor0, up0_panel[...])).astype(BF16)
        factor1 = dot(below, upper[1]).astype(BF16)
        load.wait()
        values = flat(block[...])
        columns = []
        for j in range(cb):
            cols = slice(j * nb, (j + 1) * nb)
            value = values[:, cols].astype(F32) - dot(factor0, up0[:, cols])
            value = value.astype(BF16).astype(F32) - dot(factor1, up1[:, cols])
            if j == 0:
                value = jnp.where(column == 0, factor0.astype(F32), value)
                value = jnp.where(column == 1, factor1.astype(F32), value)
            columns.append(value.astype(BF16))
        result[...] = raw(columns, nb)

    def from_top(top):
        arrived()
        load.wait()
        copy = pltpu.make_async_copy(top.at[rows_of], result, block_sem)
        copy.start()
        copy.wait()

    if begin < nb:
        pl.when(row == 0)(lambda: from_top(top0))
        pl.when(row == 1)(lambda: from_top(top1))
        pl.when(row >= 2)(from_factors)
    else:
        from_factors()
    store = pltpu.make_async_copy(result, out.at[rows_of], out_sem)
    store.start()
    token[...] = jnp.zeros(token.shape, F32)
    store.wait()


def body(matrix, pivots, lower, upper):
    rb, nb, cb, _ = matrix.shape
    rows = rb * nb
    sizes = [nb] * (rb - 1) + [nb // 2] * 2
    begins = [sum(sizes[:i]) for i in range(len(sizes))]
    pieces = len(sizes)
    row_devices = lax.axis_size("prow")
    col_devices = lax.axis_size("pcol")
    chips, line = row_devices // 2, col_devices // 2
    row = lax.axis_index("prow").astype(I32)
    column = lax.axis_index("pcol").astype(I32)
    meta = jnp.stack([row, row % 2, column, jnp.int32(row_devices)])
    tiles = matrix.reshape(rows, cb, nb)

    def to_sibling(value):
        return lax.ppermute(value, "prow", [(r, r ^ 1) for r in range(row_devices)])

    def to_neighbour(value):
        return lax.ppermute(value, "pcol", [(c, c ^ 1) for c in range(col_devices)])

    def to_chip(value, h):
        return lax.ppermute(value, "prow", [(r, (r + 2 * h) % row_devices) for r in range(row_devices)])

    def to_next(value):
        return lax.ppermute(value, "pcol", [(c, c + 2) for c in range(col_devices - 2)])

    order = []

    def run(kernel, operands, outs, also=(), **kwargs):
        after = tuple(order[-1:]) + tuple(also)
        results = call(kernel, operands, outs, after=after, **kwargs)
        order.append(results[-1])
        return results

    last_step = pieces + line - 2

    def piece_out(i):
        return (bf16(sizes[i], nb), VMEM)

    def step_out(k):
        return (bf16(max(sizes[k - p] for p in range(line) if 0 <= k - p < pieces), nb), VMEM)

    own, held, other = [], [], []
    state = {}

    def step(k):
        if k == 0:
            own.extend(run(
                first_kernel, [(tiles, ANY)], [piece_out(0)],
                scratch=[pltpu.VMEM((sizes[0], cb, nb), BF16), DMA], mib=60,
            ))
            value = own[0]
        else:
            also = [other[k - 1]] + state.pop('awaited', [])
            operands = [(meta, SMEM), (state["came"], VMEM)] + [(v, VMEM) for v in own[k : k + 1]]
            (value,) = run(relay_kernel, operands, [step_out(k)], also, us=0.2 if k in (2, 3, 5) else 12.0)
        held.append(value)
        if k < last_step:
            sent = max(sizes[k - p] for p in range(line - 1) if 0 <= k - p < pieces)
            state["came"] = to_next(value[:sent])
        other.append(to_neighbour(value))

    def gather():
        lanes = min(nb, 128)
        spread = jnp.broadcast_to(pivots[:, :, None], (2, nb, lanes))
        table = jax.ShapeDtypeStruct((2, nb), I32)
        results = run(
            gather_kernel,
            [(meta, SMEM), (pivots, VMEM), (spread, VMEM), (tiles, ANY)],
            [piece_out(i) for i in range(1, pieces)] + [(bf16(rows + 8, cb, nb), VMEM)]
            + [(bf16(nb, cb, nb), VMEM)] * 3 + [(table, VMEM)] * 4,
            scratch=[pltpu.VMEM((2, nb), I32), pltpu.SMEM((2, nb), I32), DMA, DMA],
            us=8.0, mib=20,
        )
        own.extend(results[: pieces - 1])
        state["loaded"], send, *rest = results[pieces - 1 :]
        state.update(zip(("keep", "block0", "join", "arrive", "goal", "hops"), rest))
        state["sent"] = to_sibling(send)
        state["block0_sibling"] = to_sibling(state["block0"])

    half = nb // 2
    part = half // chips

    def join():
        joined = run(
            join_kernel,
            [(meta, SMEM), (state["join"], SMEM), (state["keep"], VMEM), (state["sent"], VMEM)],
            [(bf16(half, cb, nb), VMEM)] * 2,
            scratch=[pltpu.VMEM((half + 8, cb, nb), BF16)] * 2,
            us=2.0,
        )
        state["choices"] = [[v] + [to_chip(v, h) for h in range(1, chips)] for v in joined]
        state["fresh"], state["brought"] = [], []
        state["awaited"] = [state["block0_sibling"]]

    def fresh(turn):
        new, brought, *head = run(
            functools.partial(fresh_kernel, turn, chips),
            [(meta, SMEM), (state["hops"], VMEM)] + [(c, VMEM) for c in state["choices"][turn]],
            [(bf16(half, cb * nb), VMEM), (bf16(half, cb, nb), VMEM)]
            + [(bf16(part, nb), VMEM)] * (1 - turn),
            us=1.5, mib=16,
        )
        state["fresh"] += [new, to_sibling(new)]
        state["brought"] += [brought, to_sibling(brought)]
        if head:
            pass_head(head[0], 0)

    spans = []
    while 2 ** len(spans) < line:
        spans.insert(0, 2 ** len(spans))

    def pass_head(value, i):
        if i == len(spans):
            state["head"] = (value, to_neighbour(value))
            return
        starts = range(0, line - spans[i], 2 * spans[i])
        pairs = [(2 * p + y, 2 * (p + spans[i]) + y) for p in starts for y in range(2)]
        state["head"] = (value, lax.ppermute(value, "pcol", pairs))
        state["awaited"] = state.get("awaited", []) + [state["head"][1]] if i == 0 else []

    def head_next(i):
        (mine,) = run(
            functools.partial(by_span_kernel, spans[i - 1]),
            [(meta, SMEM)] + [(v, VMEM) for v in state["head"]],
            [(bf16(part, nb), VMEM)],
            us=0.1,
        )
        pass_head(mine, i)

    def head_pair():
        (pair,) = run(stack_kernel, [(v, VMEM) for v in state["head"]], [(bf16(2, part, nb), VMEM)], us=0.1)
        state["head"] = [pair] + [to_chip(pair, h) for h in range(1, chips)]

    def head_all():
        (mine,) = run(
            stack_kernel, [(v, VMEM) for v in state["head"]], [(bf16(chips, 2, part, nb), VMEM)], us=0.1
        )
        state["heads"] = (mine, to_sibling(mine))

    def old(values, name):
        operands = [(meta, SMEM)] + [(v, VMEM) for v in values[:line]]
        (mine,) = run(functools.partial(old_kernel, line), operands, [(bf16(nb, nb), VMEM)], us=0.1)
        state[name] = [mine] + [to_chip(mine, h) for h in range(1, chips)]
        if name == "old_held":
            state["awaited"] = state.get("awaited", []) + state[name][1:]

    def old_here():
        choices = [v for pair in zip(state["old_held"], state["old_other"]) for v in pair]
        (mine,) = run(
            by_chip_kernel, [(meta, SMEM)] + [(v, VMEM) for v in choices], [(bf16(2, nb, nb), VMEM)], us=0.1
        )
        state["old"] = (mine, to_sibling(mine))

    def scatter():
        sources = state["brought"] + [state["block0"], state["block0_sibling"], state["loaded"]]
        (state["moved"],) = run(
            scatter_kernel,
            [(meta, SMEM), (state["arrive"], SMEM), (state["goal"], SMEM)] + [(v, VMEM) for v in sources],
            [(bf16(rows + 8, cb, nb), VMEM)],
            us=0.1, mib=24,
        )

    def prep0():
        state["up0"], state["top0"] = run(
            prep0_kernel,
            [(meta, SMEM), (lower, VMEM)] + [(v, VMEM) for v in state["fresh"]],
            [(bf16(nb, cb * nb), VMEM), (bf16(nb, cb, nb), VMEM)],
            scratch=[pltpu.VMEM((nb, cb * nb), BF16)],
            us=2.0, mib=16,
        )

    def prep1():
        state["up1"], state["up0_panel"], state["top1"] = run(
            functools.partial(prep1_kernel, chips),
            [(meta, SMEM), (lower, VMEM), (upper, VMEM), (state["up0"], VMEM)]
            + [(v, VMEM) for v in state["heads"]] + [(v, VMEM) for v in state["fresh"]],
            [(bf16(nb, cb * nb), VMEM), (bf16(nb, nb), VMEM), (bf16(nb, cb, nb), VMEM)],
            scratch=[pltpu.VMEM((nb, cb * nb), BF16), pltpu.VMEM((2, nb, nb), BF16)],
            us=3.5, mib=16,
        )

    def update(i):
        operands = [(meta, SMEM), (state["goal"], VMEM)] + [(v, VMEM) for v in state["old"]] + [(upper, VMEM)]
        operands += [(state[name], VMEM) for name in ("up0", "up1", "up0_panel")]
        operands += [(state[name], ANY) for name in ("moved", "top0", "top1")]
        operands += [(v, ANY) for v in held[i : i + line] + other[i : i + line]]
        aliases = {}
        if "result" in state:
            aliases = {len(operands): 0}
            operands.append((state["result"], ANY))
        count = sizes[i]
        state["result"], _ = run(
            functools.partial(update_kernel, begins[i], line),
            operands,
            [(bf16(rows, cb, nb), ANY), (jax.ShapeDtypeStruct((8, 128), F32), VMEM)],
            scratch=[
                pltpu.VMEM((2, count, nb), BF16), pltpu.VMEM((count, cb, nb), BF16),
                pltpu.VMEM((count, cb, nb), BF16), DMA((2,)), DMA, DMA,
            ],
            aliases=aliases,
            us=5.0, mib=24,
        )

    plan = [(0, gather), (1, join), (2, functools.partial(fresh, 0)), *[(3, functools.partial(head_next, i)) for i in range(1, len(spans))], (line - 1, functools.partial(old, held, "old_held")), (3, functools.partial(fresh, 1)), (3, functools.partial(head_next, len(spans))), (line, functools.partial(old, other, "old_other")), (4, head_pair), (4, scatter), (4, prep0), (5, head_all), (5, old_here), (5, prep1)]
    for i in range(pieces):
        plan.append((max((6, 6, 7, 8, 8, 8)[min(i, 5)], i + line - 1), functools.partial(update, i)))
    for k in range(last_step + 1):
        step(k)
        while plan and (plan[0][0] <= k or k == last_step):
            plan.pop(0)[1]()
    return state["result"].reshape(matrix.shape)


def solution(mesh):
    placed = (P(None, "prow", None, "pcol"), P(), P(), P())
    return jax.shard_map(
        body, mesh=mesh, in_specs=placed, out_specs=P(None, "prow", None, "pcol"), check_vma=False
    )
```

```python
import functools

import jax
import jax.numpy as jnp
from jax import lax
from jax.experimental import pallas as pl
from jax.experimental.pallas import tpu as pltpu
from jax.sharding import PartitionSpec as P

BF16 = jnp.bfloat16
F32 = jnp.float32
I32 = jnp.int32
SMEM = pl.BlockSpec(memory_space=pltpu.SMEM)
VMEM = pl.BlockSpec(memory_space=pltpu.VMEM)
ANY = pl.BlockSpec(memory_space=pl.ANY)
DMA = pltpu.SemaphoreType.DMA


def dot(a, b):
    return jnp.dot(a, b, preferred_element_type=F32)


def flat(rows):
    return rows.reshape(rows.shape[0], rows.shape[1] * rows.shape[2])


def bf16(*shape):
    return jax.ShapeDtypeStruct(shape, BF16)


def call(kernel, operands, outs, after=(), scratch=(), aliases=None, us=1.0, mib=8):
    count = len(operands)

    def ordered(*refs):
        kernel(*refs[:count], *refs[count + len(after) :])

    return pl.pallas_call(
        ordered,
        out_shape=tuple(shape for shape, _ in outs),
        in_specs=[spec for _, spec in operands] + [ANY] * len(after),
        out_specs=tuple(spec for _, spec in outs),
        scratch_shapes=list(scratch),
        input_output_aliases=aliases or {},
        compiler_params=pltpu.CompilerParams(vmem_limit_bytes=mib * 1024 * 1024),
        cost_estimate=pl.CostEstimate(flops=int(us * 1.1e9), bytes_accessed=0, transcendentals=0),
    )(*[array for array, _ in operands], *after)


def fill_indices(nb, rows, meta, pivots, spread, fetch, join, arrive, goal, hops):
    row, row_devices = meta[0], meta[3]
    chip, chips = row // 2, row_devices // 2
    lanes = spread.shape[2]
    tiles = nb // lanes
    slot = lax.broadcasted_iota(I32, (1, nb), 1)
    pivot0, pivot1 = pivots[0:1, :], pivots[1:2, :]

    def lookup(keys, entry, value):
        parts = [keys[:, t * lanes : (t + 1) * lanes] for t in range(tiles)]

        def add(i, totals):
            begin = pl.multiple_of(i * 8, 8)
            at = begin + lax.broadcasted_iota(I32, (8, lanes), 0)
            here, give = entry(begin, at), value(begin, at)
            return tuple(t + jnp.where(p == here, give, 0) for t, p in zip(totals, parts))

        zero = jnp.zeros((8, lanes), I32)
        totals = lax.fori_loop(0, nb // 8, add, (zero,) * tiles, unroll=8)
        return jnp.concatenate([jnp.sum(t, axis=0, keepdims=True) for t in totals], axis=1)

    def pivot_of(panel):
        return lambda begin, at: spread[panel, pl.ds(begin, 8), :]

    place = lambda begin, at: at + 1
    in_pivots0 = lookup(pivot1, pivot_of(0), place)
    in_pivots1 = lookup(pivot0, pivot_of(1), place)
    top1_in_pivots0 = lookup(nb + slot, pivot_of(0), place)
    over_top1 = lookup(pivot0, lambda begin, at: nb + at, pivot_of(1))
    chained = lookup(nb + in_pivots1 - 1, pivot_of(0), place)

    source0 = pivot0
    source1 = jnp.where(in_pivots0 > 0, in_pivots0 - 1, pivot1)
    second0 = jnp.where(in_pivots1 > 0, jnp.where(chained > 0, chained - 1, nb + in_pivots1 - 1), slot)
    second1 = jnp.where(top1_in_pivots0 > 0, top1_in_pivots0 - 1, nb + slot)
    target0 = jnp.where(over_top1 > 0, over_top1, jnp.where(in_pivots1 > 0, nb + in_pivots1 - 1, pivot0))
    target1 = jnp.where(top1_in_pivots0 > 0, top1_in_pivots0 - 1, pivot1)

    def holder(index):
        return lax.rem(lax.div(index, nb), row_devices)

    def local(index):
        return lax.div(index, nb * row_devices) * nb + lax.rem(index, nb)

    def placed(index):
        mine = (holder(index) == row) & (index >= 2 * nb)
        return jnp.where(mine, local(index), rows)

    for k, (source, second, target) in enumerate(((source0, second0, target0), (source1, second1, target1))):
        from_chip = lax.div(holder(source), 2)
        wanted = jnp.where(from_chip == chip, source, second)
        at = (slice(k, k + 1), slice(None))
        fetch[at] = local(wanted)
        join[at] = jnp.where(holder(wanted) == row, lax.rem(slot, nb // 2), nb // 2)
        arrive[at] = placed(source)
        goal[at] = placed(target)
        hops[at] = lax.rem(chip + chips - from_chip, chips)


def copy_rows(count, target, target_at, origin, origin_at):
    def copy(i, carry):
        target[target_at(i)] = origin[origin_at(i)]
        return carry

    lax.fori_loop(0, count, copy, 0, unroll=16)


def first_kernel(tiles, piece, work, sem):
    load = pltpu.make_async_copy(tiles.at[pl.ds(0, piece.shape[0])], work, sem)
    load.start()
    load.wait()
    piece[...] = flat(work[...])[:, : piece.shape[1]]


def gather_kernel(meta, pivots, spread, tiles, *refs):
    *pieces, loaded, send, keep, block0, join, arrive, goal, hops, fetch, fetch_table, load_sem, table_sem = refs
    nb = send.shape[0]
    rows = tiles.shape[0]
    core = meta[1]
    load = pltpu.make_async_copy(tiles, loaded.at[pl.ds(0, rows)], load_sem)
    load.start()
    fill_indices(nb, rows, meta, pivots, spread, fetch, join, arrive, goal, hops)
    table = pltpu.make_async_copy(fetch, fetch_table, table_sem)
    table.start()
    table.wait()
    load.wait()
    begin = nb
    for piece in pieces:
        end = begin + piece.shape[0]
        piece[...] = flat(loaded[begin:end])[:, :nb]
        begin = end
    half, side = nb // 2, lax.rem(meta[2], 2)
    for turn, b in enumerate((1 - side, side)):
        to = lambda i, turn=turn: turn * half + i
        copy_rows(half, send, to, loaded, lambda i, b=b: fetch_table[b, (1 - core) * half + i])
        copy_rows(half, keep, to, loaded, lambda i, b=b: fetch_table[b, core * half + i])
    block0[...] = loaded[0:nb]


def join_kernel(meta, join, keep, came, joined0, joined1, work0, work1):
    half = joined0.shape[0]
    core, side = meta[1], lax.rem(meta[2], 2)
    for turn, (b, work, joined) in enumerate(((1 - side, work0, joined0), (side, work1, joined1))):
        work[0:half] = came[turn * half : (turn + 1) * half]
        copy_rows(
            half, work, lambda i, b=b: join[b, core * half + i], keep, lambda i, turn=turn: turn * half + i
        )
        joined[...] = work[0:half]


def scatter_kernel(meta, arrive, goal, *refs):
    *came, old, old_sibling, tiles, out = refs
    core, side, chip = meta[1], lax.rem(meta[2], 2), meta[0] // 2
    nb = old.shape[0]
    half = nb // 2
    out[...] = tiles[...]

    @pl.when(chip == 0)
    def _():
        copy_rows(nb, out, lambda i: goal[core, i], old, lambda i: i)
        copy_rows(nb, out, lambda i: goal[1 - core, i], old_sibling, lambda i: i)

    @pl.when(chip != 0)
    def _():
        for turn, b in enumerate((1 - side, side)):
            for values, who in ((came[2 * turn], core), (came[2 * turn + 1], 1 - core)):
                copy_rows(half, out, lambda i, b=b, who=who: arrive[b, who * half + i], values, lambda i: i)


def relay_kernel(meta, came, *refs):
    *own, held = refs
    place = lax.div(meta[2], 2)
    for piece in own:

        @pl.when(place == 0)
        def _(piece=piece):
            held[0 : piece.shape[0]] = piece[...]

    @pl.when(place != 0)
    def _():
        count = min(came.shape[0], held.shape[0])
        held[0:count] = came[0:count]


def old_kernel(line, meta, *refs):
    *choices, old = refs
    for h in range(line):

        @pl.when(lax.div(meta[2], 2) == h)
        def _(h=h):
            old[...] = choices[h][0 : old.shape[0]]


def by_chip_kernel(meta, *refs):
    *choices, out = refs
    for h in range(len(choices) // 2):

        @pl.when(meta[0] // 2 == h)
        def _(h=h):
            out[0] = choices[2 * h][...]
            out[1] = choices[2 * h + 1][...]


def by_place_kernel(meta, *refs):
    out = refs[-1]
    for h, choice in enumerate(refs[:-1]):

        @pl.when(lax.div(meta[2], 2) == h)
        def _(choice=choice):
            out[...] = choice[...]


def stack_kernel(*refs):
    *entries, out = refs
    for i, entry in enumerate(entries):
        out[i] = entry[...]


def choose(hop, choices):
    value = flat(choices[0]).astype(F32)
    for h, other in enumerate(choices[1:], 1):
        value = jnp.where(hop == h, flat(other).astype(F32), value)
    return value.astype(BF16)


def fresh_kernel(turn, chips, meta, hops, *refs):
    choices, (fresh, brought, *head) = refs[:chips], refs[chips:]
    half = fresh.shape[0]
    core, side, chip = meta[1], lax.rem(meta[2], 2), meta[0] // 2
    b = side if turn else 1 - side
    hop = jnp.broadcast_to(hops[pl.ds(b, 1), :], (8, 2 * half)).T[:, 0:1]
    hop = jnp.where(core == 0, hop[:half], hop[half:])
    fresh[...] = choose(hop, [c[...] for c in choices])
    if head:
        part, nb = head[0].shape
        head[0][...] = fresh[pl.ds(pl.multiple_of(chip * part, part), part), :nb]
    if chips == 1:
        brought[...] = choices[0][...]
    for h in range(1, chips):

        @pl.when((chip == h) | ((chip == 0) & (h == 1)))
        def _(h=h):
            brought[...] = choices[h][...]


def assemble(meta, b, fresh, work):
    core, side = meta[1], lax.rem(meta[2], 2)
    half = work.shape[0] // 2
    for turn, which in enumerate((1 - side, side)):

        @pl.when(which == b)
        def _(turn=turn):
            work[pl.ds(pl.multiple_of(core * half, half), half)] = fresh[2 * turn][...]
            work[pl.ds(pl.multiple_of((1 - core) * half, half), half)] = fresh[2 * turn + 1][...]


def raw(columns, nb):
    joined = jnp.concatenate(columns, axis=1)
    return joined.reshape(joined.shape[0], len(columns), nb)


def prep0_kernel(meta, lower, *refs):
    *fresh, up0, top, work = refs
    column = meta[2]
    nb = work.shape[0]
    assemble(meta, 0, fresh, work)
    shown = []
    for j in range(work.shape[1] // nb):
        cols = slice(j * nb, (j + 1) * nb)
        product = dot(lower[0], work[:, cols])
        show = product
        if j == 0:
            show = jnp.where(column == 0, work[:, cols].astype(F32), product)
            product = jnp.where(column == 0, 0.0, product)
        up0[:, cols] = product.astype(BF16)
        shown.append(show.astype(BF16))
    top[...] = raw(shown, nb)


def prep1_kernel(chips, meta, lower, upper, up0, heads, heads_sibling, *refs):
    *fresh, up1, up0_panel, top, work, head = refs
    core, column, chip = meta[1], meta[2], meta[0] // 2
    side = lax.rem(column, 2)
    nb, part = work.shape[0], heads.shape[2]
    for who, parts in ((core, heads), (1 - core, heads_sibling)):
        for h in range(chips):
            at = pl.multiple_of((who * chips + lax.rem(chip + chips - h, chips)) * part, part)
            head[1 - side, pl.ds(at, part)] = parts[h, 0]
            head[side, pl.ds(at, part)] = parts[h, 1]
    assemble(meta, 1, fresh, work)
    up0_panel[...] = dot(lower[0], head[0]).astype(BF16)
    factor = dot(head[1], upper[0]).astype(BF16)
    in_panel, next_panel = column == 0, column == 1
    shown = []
    for j in range(work.shape[1] // nb):
        cols = slice(j * nb, (j + 1) * nb)
        updated = (work[:, cols].astype(F32) - dot(factor, up0[:, cols])).astype(BF16)
        last = dot(lower[1], updated)
        show = last
        if j == 0:
            show = jnp.where(next_panel, updated.astype(F32), show)
            show = jnp.where(in_panel, factor.astype(F32), show)
            last = jnp.where(in_panel | next_panel, 0.0, last)
        up1[:, cols] = last.astype(BF16)
        shown.append(show.astype(BF16))
    top[...] = raw(shown, nb)


def update_kernel(
    begin, line, sizes, meta, goal, old, old_sibling, upper, up0, up1, up0_panel, tiles, top0, top1, *rest
):
    spans = len(sizes) * line
    held, other = rest[:spans], rest[spans : 2 * spans]
    out, token, panels, block, result, panel_sem, block_sem, out_sem = rest[-8:]
    row, core, column = meta[0], meta[1], meta[2]
    side, place = lax.rem(column, 2), lax.div(column, 2)
    count, cb, nb = block.shape
    rows_of = pl.ds(begin, count)

    def panel_copy(i, h, which):
        source = (held, other)[which][i * line + h].at[pl.ds(0, sizes[i])]
        target = panels.at[lax.rem(side + which, 2), pl.ds(sum(sizes[:i]), sizes[i])]
        return pltpu.make_async_copy(source, target, panel_sem.at[i, which])

    load = pltpu.make_async_copy(tiles.at[rows_of], block, block_sem)
    load.start()
    for h in range(line):

        @pl.when(place == h)
        def _(h=h):
            for i in range(len(sizes)):
                panel_copy(i, h, 0).start()
                panel_copy(i, h, 1).start()

    def arrived():
        for i in range(len(sizes)):
            panel_copy(i, 0, 0).wait()
            panel_copy(i, 0, 1).wait()

    def from_factors():
        here = begin + lax.broadcasted_iota(I32, (count, nb), 0)
        pick = jnp.where(here == goal[pl.ds(core, 1), :], 1.0, 0.0)
        pick_sibling = jnp.where(here == goal[pl.ds(1 - core, 1), :], 1.0, 0.0)
        moved = jnp.sum(pick + pick_sibling, axis=1, keepdims=True) > 0.5
        pick, pick_sibling = pick.astype(BF16), pick_sibling.astype(BF16)
        arrived()
        whole = []
        for k in range(2):
            which = lax.rem(k + side, 2)
            brought = dot(pick, old[which]) + dot(pick_sibling, old_sibling[which])
            whole.append(jnp.where(moved, brought, panels[k].astype(F32)))
        factor0 = dot(whole[0].astype(BF16), upper[0]).astype(BF16)
        below = (whole[1] - dot(factor0, up0_panel[...])).astype(BF16)
        factor1 = dot(below, upper[1]).astype(BF16)
        load.wait()
        values = flat(block[...])
        columns = []
        for j in range(cb):
            cols = slice(j * nb, (j + 1) * nb)
            value = values[:, cols].astype(F32) - dot(factor0, up0[:, cols])
            value = value.astype(BF16).astype(F32) - dot(factor1, up1[:, cols])
            if j == 0:
                value = jnp.where(column == 0, factor0.astype(F32), value)
                value = jnp.where(column == 1, factor1.astype(F32), value)
            columns.append(value.astype(BF16))
        result[...] = raw(columns, nb)

    def from_top(top):
        arrived()
        load.wait()
        copy = pltpu.make_async_copy(top.at[rows_of], result, block_sem)
        copy.start()
        copy.wait()

    if begin < nb:
        pl.when(row == 0)(lambda: from_top(top0))
        pl.when(row == 1)(lambda: from_top(top1))
        pl.when(row >= 2)(from_factors)
    else:
        from_factors()
    store = pltpu.make_async_copy(result, out.at[rows_of], out_sem)
    store.start()
    token[...] = jnp.zeros(token.shape, F32)
    store.wait()


def body(matrix, pivots, lower, upper):
    rb, nb, cb, _ = matrix.shape
    rows = rb * nb
    sizes = [nb] * (rb - 1) + [nb // 2] * 2
    begins = [sum(sizes[:i]) for i in range(len(sizes))]
    pieces = len(sizes)
    row_devices = lax.axis_size("prow")
    col_devices = lax.axis_size("pcol")
    chips, line = row_devices // 2, col_devices // 2
    row = lax.axis_index("prow").astype(I32)
    column = lax.axis_index("pcol").astype(I32)
    meta = jnp.stack([row, row % 2, column, jnp.int32(row_devices)])
    tiles = matrix.reshape(rows, cb, nb)

    def to_sibling(value):
        return lax.ppermute(value, "prow", [(r, r ^ 1) for r in range(row_devices)])

    def to_neighbour(value):
        return lax.ppermute(value, "pcol", [(c, c ^ 1) for c in range(col_devices)])

    def to_chip(value, h):
        return lax.ppermute(value, "prow", [(r, (r + 2 * h) % row_devices) for r in range(row_devices)])

    def to_next(value):
        return lax.ppermute(value, "pcol", [(c, c + 2) for c in range(col_devices - 2)])

    order = []

    def run(kernel, operands, outs, also=(), **kwargs):
        after = tuple(order[-1:]) + tuple(also)
        results = call(kernel, operands, outs, after=after, **kwargs)
        order.append(results[-1])
        return results

    last_step = pieces + line - 2

    def piece_out(i):
        return (bf16(sizes[i], nb), VMEM)

    def step_out(k):
        return (bf16(max(sizes[k - p] for p in range(line) if 0 <= k - p < pieces), nb), VMEM)

    own, held, other = [], [], []
    state = {}

    def step(k):
        if k == 0:
            own.extend(run(
                first_kernel, [(tiles, ANY)], [piece_out(0)],
                scratch=[pltpu.VMEM((sizes[0], cb, nb), BF16), DMA], mib=60,
            ))
            value = own[0]
        else:
            also = [other[k - 1]] + state.pop('awaited', [])
            operands = [(meta, SMEM), (state["came"], VMEM)] + [(v, VMEM) for v in own[k : k + 1]]
            (value,) = run(relay_kernel, operands, [step_out(k)], also, us=0.2 if k in (2, 3, 5) else 12.0)
        held.append(value)
        if k < last_step:
            sent = max(sizes[k - p] for p in range(line - 1) if 0 <= k - p < pieces)
            state["came"] = to_next(value[:sent])
        other.append(to_neighbour(value))

    def gather():
        lanes = min(nb, 128)
        spread = jnp.broadcast_to(pivots[:, :, None], (2, nb, lanes))
        table = jax.ShapeDtypeStruct((2, nb), I32)
        results = run(
            gather_kernel,
            [(meta, SMEM), (pivots, VMEM), (spread, VMEM), (tiles, ANY)],
            [piece_out(i) for i in range(1, pieces)] + [(bf16(rows + 8, cb, nb), VMEM)]
            + [(bf16(nb, cb, nb), VMEM)] * 3 + [(table, VMEM)] * 4,
            scratch=[pltpu.VMEM((2, nb), I32), pltpu.SMEM((2, nb), I32), DMA, DMA],
            us=8.0, mib=20,
        )
        own.extend(results[: pieces - 1])
        state["loaded"], send, *rest = results[pieces - 1 :]
        state.update(zip(("keep", "block0", "join", "arrive", "goal", "hops"), rest))
        state["sent"] = to_sibling(send)
        state["block0_sibling"] = to_sibling(state["block0"])

    half = nb // 2
    part = half // chips

    def join():
        joined = run(
            join_kernel,
            [(meta, SMEM), (state["join"], SMEM), (state["keep"], VMEM), (state["sent"], VMEM)],
            [(bf16(half, cb, nb), VMEM)] * 2,
            scratch=[pltpu.VMEM((half + 8, cb, nb), BF16)] * 2,
            us=2.0,
        )
        state["choices"] = [[v] + [to_chip(v, h) for h in range(1, chips)] for v in joined]
        state["fresh"], state["brought"] = [], []
        state["awaited"] = [state["block0_sibling"]]

    def fresh(turn):
        new, brought, *head = run(
            functools.partial(fresh_kernel, turn, chips),
            [(meta, SMEM), (state["hops"], VMEM)] + [(c, VMEM) for c in state["choices"][turn]],
            [(bf16(half, cb * nb), VMEM), (bf16(half, cb, nb), VMEM)]
            + [(bf16(part, nb), VMEM)] * (1 - turn),
            us=1.5, mib=16,
        )
        state["fresh"] += [new, to_sibling(new)]
        state["brought"] += [brought, to_sibling(brought)]
        if head:
            state["head"] = head + [
                lax.ppermute(head[0], "pcol", [(0, 2 * h), (1, 2 * h + 1)]) for h in range(1, line)
            ]
            state["awaited"] = state.get("awaited", []) + state["head"][1:]

    def head_here():
        (mine,) = run(
            by_place_kernel, [(meta, SMEM)] + [(v, VMEM) for v in state["head"]], [(bf16(part, nb), VMEM)], us=0.1
        )
        state["head"] = (mine, to_neighbour(mine))

    def head_pair():
        (pair,) = run(stack_kernel, [(v, VMEM) for v in state["head"]], [(bf16(2, part, nb), VMEM)], us=0.1)
        state["head"] = [pair] + [to_chip(pair, h) for h in range(1, chips)]

    def head_all():
        (mine,) = run(
            stack_kernel, [(v, VMEM) for v in state["head"]], [(bf16(chips, 2, part, nb), VMEM)], us=0.1
        )
        state["heads"] = (mine, to_sibling(mine))

    def old(values, name):
        operands = [(meta, SMEM)] + [(v, VMEM) for v in values[:line]]
        (mine,) = run(functools.partial(old_kernel, line), operands, [(bf16(nb, nb), VMEM)], us=0.1)
        state[name] = [mine] + [to_chip(mine, h) for h in range(1, chips)]
        if name == "old_held":
            state["awaited"] = state.get("awaited", []) + state[name][1:]

    def old_here():
        choices = [v for pair in zip(state["old_held"], state["old_other"]) for v in pair]
        (mine,) = run(
            by_chip_kernel, [(meta, SMEM)] + [(v, VMEM) for v in choices], [(bf16(2, nb, nb), VMEM)], us=0.1
        )
        state["old"] = (mine, to_sibling(mine))

    def scatter():
        sources = state["brought"] + [state["block0"], state["block0_sibling"], state["loaded"]]
        (state["moved"],) = run(
            scatter_kernel,
            [(meta, SMEM), (state["arrive"], SMEM), (state["goal"], SMEM)] + [(v, VMEM) for v in sources],
            [(bf16(rows + 8, cb, nb), VMEM)],
            us=0.1, mib=24,
        )

    def prep0():
        state["up0"], state["top0"] = run(
            prep0_kernel,
            [(meta, SMEM), (lower, VMEM)] + [(v, VMEM) for v in state["fresh"]],
            [(bf16(nb, cb * nb), VMEM), (bf16(nb, cb, nb), VMEM)],
            scratch=[pltpu.VMEM((nb, cb * nb), BF16)],
            us=2.0, mib=16,
        )

    def prep1():
        state["up1"], state["up0_panel"], state["top1"] = run(
            functools.partial(prep1_kernel, chips),
            [(meta, SMEM), (lower, VMEM), (upper, VMEM), (state["up0"], VMEM)]
            + [(v, VMEM) for v in state["heads"]] + [(v, VMEM) for v in state["fresh"]],
            [(bf16(nb, cb * nb), VMEM), (bf16(nb, nb), VMEM), (bf16(nb, cb, nb), VMEM)],
            scratch=[pltpu.VMEM((nb, cb * nb), BF16), pltpu.VMEM((2, nb, nb), BF16)],
            us=3.5, mib=16,
        )

    def update(i, group=1):
        operands = [(meta, SMEM), (state["goal"], VMEM)] + [(v, VMEM) for v in state["old"]] + [(upper, VMEM)]
        operands += [(state[name], VMEM) for name in ("up0", "up1", "up0_panel")]
        operands += [(state[name], ANY) for name in ("moved", "top0", "top1")]
        places = [p + h for p in range(i, i + group) for h in range(line)]
        operands += [(values[p], ANY) for values in (held, other) for p in places]
        aliases = {}
        if "result" in state:
            aliases = {len(operands): 0}
            operands.append((state["result"], ANY))
        count = sum(sizes[i : i + group])
        state["result"], _ = run(
            functools.partial(update_kernel, begins[i], line, tuple(sizes[i : i + group])),
            operands,
            [(bf16(rows, cb, nb), ANY), (jax.ShapeDtypeStruct((8, 128), F32), VMEM)],
            scratch=[
                pltpu.VMEM((2, count, nb), BF16), pltpu.VMEM((count, cb, nb), BF16),
                pltpu.VMEM((count, cb, nb), BF16), DMA((group, 2)), DMA, DMA,
            ],
            aliases=aliases,
            us=5.0, mib=24,
        )

    plan = [(0, gather), (1, join), (2, functools.partial(fresh, 0)), (3, head_here), (line - 1, functools.partial(old, held, "old_held")), (3, head_pair), (3, functools.partial(fresh, 1)), (line, functools.partial(old, other, "old_other")), (4, scatter), (4, prep0), (5, head_all), (5, old_here), (5, prep1)]
    for i in range(pieces - 2):
        plan.append((max(6 + i // 2, i + line - 1) if i < 3 else last_step, functools.partial(update, i)))
    plan.append((last_step, functools.partial(update, pieces - 2, 2)))
    for k in range(last_step + 1):
        step(k)
        while plan and (plan[0][0] <= k or k == last_step):
            plan.pop(0)[1]()
    return state["result"].reshape(matrix.shape)


def solution(mesh):
    placed = (P(None, "prow", None, "pcol"), P(), P(), P())
    return jax.shard_map(
        body, mesh=mesh, in_specs=placed, out_specs=P(None, "prow", None, "pcol"), check_vma=False
    )
```

```python
import functools

import jax
import jax.numpy as jnp
from jax import lax
from jax.experimental import pallas as pl
from jax.experimental.pallas import tpu as pltpu
from jax.sharding import PartitionSpec as P

BF16 = jnp.bfloat16
F32 = jnp.float32
I32 = jnp.int32
SMEM = pl.BlockSpec(memory_space=pltpu.SMEM)
VMEM = pl.BlockSpec(memory_space=pltpu.VMEM)
ANY = pl.BlockSpec(memory_space=pl.ANY)
DMA = pltpu.SemaphoreType.DMA


def dot(a, b):
    return jnp.dot(a, b, preferred_element_type=F32)


def flat(rows):
    return rows.reshape(rows.shape[0], rows.shape[1] * rows.shape[2])


def bf16(*shape):
    return jax.ShapeDtypeStruct(shape, BF16)


def call(kernel, operands, outs, after=(), scratch=(), aliases=None, us=1.0, mib=8):
    count = len(operands)

    def ordered(*refs):
        kernel(*refs[:count], *refs[count + len(after) :])

    return pl.pallas_call(
        ordered,
        out_shape=tuple(shape for shape, _ in outs),
        in_specs=[spec for _, spec in operands] + [ANY] * len(after),
        out_specs=tuple(spec for _, spec in outs),
        scratch_shapes=list(scratch),
        input_output_aliases=aliases or {},
        compiler_params=pltpu.CompilerParams(vmem_limit_bytes=mib * 1024 * 1024),
        cost_estimate=pl.CostEstimate(flops=int(us * 1.1e9), bytes_accessed=0, transcendentals=0),
    )(*[array for array, _ in operands], *after)


def fill_indices(nb, rows, meta, pivots, spread, fetch, join, arrive, goal, hops):
    row, row_devices = meta[0], meta[3]
    chip, chips = row // 2, row_devices // 2
    lanes = spread.shape[2]
    tiles = nb // lanes
    slot = lax.broadcasted_iota(I32, (1, nb), 1)
    pivot0, pivot1 = pivots[0:1, :], pivots[1:2, :]

    def lookup(keys, entry, value):
        parts = [keys[:, t * lanes : (t + 1) * lanes] for t in range(tiles)]

        def add(i, totals):
            begin = pl.multiple_of(i * 8, 8)
            at = begin + lax.broadcasted_iota(I32, (8, lanes), 0)
            here, give = entry(begin, at), value(begin, at)
            return tuple(t + jnp.where(p == here, give, 0) for t, p in zip(totals, parts))

        zero = jnp.zeros((8, lanes), I32)
        totals = lax.fori_loop(0, nb // 8, add, (zero,) * tiles, unroll=8)
        return jnp.concatenate([jnp.sum(t, axis=0, keepdims=True) for t in totals], axis=1)

    def pivot_of(panel):
        return lambda begin, at: spread[panel, pl.ds(begin, 8), :]

    place = lambda begin, at: at + 1
    in_pivots0 = lookup(pivot1, pivot_of(0), place)
    in_pivots1 = lookup(pivot0, pivot_of(1), place)
    top1_in_pivots0 = lookup(nb + slot, pivot_of(0), place)
    over_top1 = lookup(pivot0, lambda begin, at: nb + at, pivot_of(1))
    chained = lookup(nb + in_pivots1 - 1, pivot_of(0), place)

    source0 = pivot0
    source1 = jnp.where(in_pivots0 > 0, in_pivots0 - 1, pivot1)
    second0 = jnp.where(in_pivots1 > 0, jnp.where(chained > 0, chained - 1, nb + in_pivots1 - 1), slot)
    second1 = jnp.where(top1_in_pivots0 > 0, top1_in_pivots0 - 1, nb + slot)
    target0 = jnp.where(over_top1 > 0, over_top1, jnp.where(in_pivots1 > 0, nb + in_pivots1 - 1, pivot0))
    target1 = jnp.where(top1_in_pivots0 > 0, top1_in_pivots0 - 1, pivot1)

    def holder(index):
        return lax.rem(lax.div(index, nb), row_devices)

    def local(index):
        return lax.div(index, nb * row_devices) * nb + lax.rem(index, nb)

    def placed(index):
        mine = (holder(index) == row) & (index >= 2 * nb)
        return jnp.where(mine, local(index), rows)

    for k, (source, second, target) in enumerate(((source0, second0, target0), (source1, second1, target1))):
        from_chip = lax.div(holder(source), 2)
        wanted = jnp.where(from_chip == chip, source, second)
        at = (slice(k, k + 1), slice(None))
        fetch[at] = local(wanted)
        join[at] = jnp.where(holder(wanted) == row, lax.rem(slot, nb // 2), nb // 2)
        arrive[at] = placed(source)
        goal[at] = placed(target)
        hops[at] = lax.rem(chip + chips - from_chip, chips)


def copy_rows(count, target, target_at, origin, origin_at):
    def copy(i, carry):
        target[target_at(i)] = origin[origin_at(i)]
        return carry

    lax.fori_loop(0, count, copy, 0, unroll=16)


def first_kernel(tiles, piece, work, sem):
    load = pltpu.make_async_copy(tiles.at[pl.ds(0, piece.shape[0])], work, sem)
    load.start()
    load.wait()
    piece[...] = flat(work[...])[:, : piece.shape[1]]


def gather_kernel(meta, pivots, spread, tiles, *refs):
    *pieces, loaded, send, keep, block0, join, arrive, goal, hops, fetch, fetch_table, load_sem, table_sem = refs
    nb = send.shape[0]
    rows = tiles.shape[0]
    core = meta[1]
    load = pltpu.make_async_copy(tiles, loaded.at[pl.ds(0, rows)], load_sem)
    load.start()
    fill_indices(nb, rows, meta, pivots, spread, fetch, join, arrive, goal, hops)
    table = pltpu.make_async_copy(fetch, fetch_table, table_sem)
    table.start()
    table.wait()
    load.wait()
    begin = nb
    for piece in pieces:
        end = begin + piece.shape[0]
        piece[...] = flat(loaded[begin:end])[:, :nb]
        begin = end
    half, side = nb // 2, lax.rem(meta[2], 2)
    for turn, b in enumerate((1 - side, side)):
        to = lambda i, turn=turn: turn * half + i
        copy_rows(half, send, to, loaded, lambda i, b=b: fetch_table[b, (1 - core) * half + i])
        copy_rows(half, keep, to, loaded, lambda i, b=b: fetch_table[b, core * half + i])
    block0[...] = loaded[0:nb]


def join_kernel(meta, join, keep, came, joined0, joined1, work0, work1):
    half = joined0.shape[0]
    core, side = meta[1], lax.rem(meta[2], 2)
    for turn, (b, work, joined) in enumerate(((1 - side, work0, joined0), (side, work1, joined1))):
        work[0:half] = came[turn * half : (turn + 1) * half]
        copy_rows(
            half, work, lambda i, b=b: join[b, core * half + i], keep, lambda i, turn=turn: turn * half + i
        )
        joined[...] = work[0:half]


def scatter_kernel(meta, arrive, goal, *refs):
    *came, old, old_sibling, tiles, out = refs
    core, side, chip = meta[1], lax.rem(meta[2], 2), meta[0] // 2
    nb = old.shape[0]
    half = nb // 2
    out[...] = tiles[...]

    @pl.when(chip == 0)
    def _():
        copy_rows(nb, out, lambda i: goal[core, i], old, lambda i: i)
        copy_rows(nb, out, lambda i: goal[1 - core, i], old_sibling, lambda i: i)

    @pl.when(chip != 0)
    def _():
        for turn, b in enumerate((1 - side, side)):
            for values, who in ((came[2 * turn], core), (came[2 * turn + 1], 1 - core)):
                copy_rows(half, out, lambda i, b=b, who=who: arrive[b, who * half + i], values, lambda i: i)


def relay_kernel(meta, came, *refs):
    *own, held = refs
    place = lax.div(meta[2], 2)
    for piece in own:

        @pl.when(place == 0)
        def _(piece=piece):
            held[0 : piece.shape[0]] = piece[...]

    @pl.when(place != 0)
    def _():
        count = min(came.shape[0], held.shape[0])
        held[0:count] = came[0:count]


def old_kernel(line, meta, *refs):
    *choices, old = refs
    for h in range(line):

        @pl.when(lax.div(meta[2], 2) == h)
        def _(h=h):
            old[...] = choices[h][0 : old.shape[0]]


def by_chip_kernel(meta, *refs):
    *choices, out = refs
    for h in range(len(choices) // 2):

        @pl.when(meta[0] // 2 == h)
        def _(h=h):
            out[0] = choices[2 * h][...]
            out[1] = choices[2 * h + 1][...]


def by_place_kernel(meta, *refs):
    out = refs[-1]
    for h, choice in enumerate(refs[:-1]):

        @pl.when(lax.div(meta[2], 2) == h)
        def _(choice=choice):
            out[...] = choice[...]


def stack_kernel(*refs):
    *entries, out = refs
    for i, entry in enumerate(entries):
        out[i] = entry[...]


def choose(hop, choices):
    value = flat(choices[0]).astype(F32)
    for h, other in enumerate(choices[1:], 1):
        value = jnp.where(hop == h, flat(other).astype(F32), value)
    return value.astype(BF16)


def fresh_kernel(turn, chips, meta, hops, *refs):
    choices, (fresh, brought, *head) = refs[:chips], refs[chips:]
    half = fresh.shape[0]
    core, side, chip = meta[1], lax.rem(meta[2], 2), meta[0] // 2
    b = side if turn else 1 - side
    hop = jnp.broadcast_to(hops[pl.ds(b, 1), :], (8, 2 * half)).T[:, 0:1]
    hop = jnp.where(core == 0, hop[:half], hop[half:])
    fresh[...] = choose(hop, [c[...] for c in choices])
    if head:
        part, nb = head[0].shape
        head[0][...] = fresh[pl.ds(pl.multiple_of(chip * part, part), part), :nb]
    if chips == 1:
        brought[...] = choices[0][...]
    for h in range(1, chips):

        @pl.when((chip == h) | ((chip == 0) & (h == 1)))
        def _(h=h):
            brought[...] = choices[h][...]


def assemble(meta, b, fresh, work):
    core, side = meta[1], lax.rem(meta[2], 2)
    half = work.shape[0] // 2
    for turn, which in enumerate((1 - side, side)):

        @pl.when(which == b)
        def _(turn=turn):
            work[pl.ds(pl.multiple_of(core * half, half), half)] = fresh[2 * turn][...]
            work[pl.ds(pl.multiple_of((1 - core) * half, half), half)] = fresh[2 * turn + 1][...]


def raw(columns, nb):
    joined = jnp.concatenate(columns, axis=1)
    return joined.reshape(joined.shape[0], len(columns), nb)


def prep0_kernel(meta, lower, *refs):
    *fresh, up0, top, work = refs
    column = meta[2]
    nb = work.shape[0]
    assemble(meta, 0, fresh, work)
    shown = []
    for j in range(work.shape[1] // nb):
        cols = slice(j * nb, (j + 1) * nb)
        product = dot(lower[0], work[:, cols])
        show = product
        if j == 0:
            show = jnp.where(column == 0, work[:, cols].astype(F32), product)
            product = jnp.where(column == 0, 0.0, product)
        up0[:, cols] = product.astype(BF16)
        shown.append(show.astype(BF16))
    top[...] = raw(shown, nb)


def prep1_kernel(chips, meta, lower, upper, up0, heads, heads_sibling, *refs):
    *fresh, up1, up0_panel, top, work, head = refs
    core, column, chip = meta[1], meta[2], meta[0] // 2
    side = lax.rem(column, 2)
    nb, part = work.shape[0], heads.shape[2]
    for who, parts in ((core, heads), (1 - core, heads_sibling)):
        for h in range(chips):
            at = pl.multiple_of((who * chips + lax.rem(chip + chips - h, chips)) * part, part)
            head[1 - side, pl.ds(at, part)] = parts[h, 0]
            head[side, pl.ds(at, part)] = parts[h, 1]
    assemble(meta, 1, fresh, work)
    up0_panel[...] = dot(lower[0], head[0]).astype(BF16)
    factor = dot(head[1], upper[0]).astype(BF16)
    in_panel, next_panel = column == 0, column == 1
    shown = []
    for j in range(work.shape[1] // nb):
        cols = slice(j * nb, (j + 1) * nb)
        updated = (work[:, cols].astype(F32) - dot(factor, up0[:, cols])).astype(BF16)
        last = dot(lower[1], updated)
        show = last
        if j == 0:
            show = jnp.where(next_panel, updated.astype(F32), show)
            show = jnp.where(in_panel, factor.astype(F32), show)
            last = jnp.where(in_panel | next_panel, 0.0, last)
        up1[:, cols] = last.astype(BF16)
        shown.append(show.astype(BF16))
    top[...] = raw(shown, nb)


def update_kernel(
    begin, line, sizes, meta, goal, old, old_sibling, upper, up0, up1, up0_panel, tiles, top0, top1, *rest
):
    spans = len(sizes) * line
    held, other = rest[:spans], rest[spans : 2 * spans]
    out, token, panels, block, result, panel_sem, block_sem, out_sem = rest[-8:]
    row, core, column = meta[0], meta[1], meta[2]
    side, place = lax.rem(column, 2), lax.div(column, 2)
    count, cb, nb = block.shape
    rows_of = pl.ds(begin, count)

    def panel_copy(i, h, which):
        source = (held, other)[which][i * line + h].at[pl.ds(0, sizes[i])]
        target = panels.at[lax.rem(side + which, 2), pl.ds(sum(sizes[:i]), sizes[i])]
        return pltpu.make_async_copy(source, target, panel_sem.at[i, which])

    load = pltpu.make_async_copy(tiles.at[rows_of], block, block_sem)
    load.start()
    for h in range(line):

        @pl.when(place == h)
        def _(h=h):
            for i in range(len(sizes)):
                panel_copy(i, h, 0).start()
                panel_copy(i, h, 1).start()

    def arrived():
        for i in range(len(sizes)):
            panel_copy(i, 0, 0).wait()
            panel_copy(i, 0, 1).wait()

    def from_factors():
        here = begin + lax.broadcasted_iota(I32, (count, nb), 0)
        pick = jnp.where(here == goal[pl.ds(core, 1), :], 1.0, 0.0)
        pick_sibling = jnp.where(here == goal[pl.ds(1 - core, 1), :], 1.0, 0.0)
        moved = jnp.sum(pick + pick_sibling, axis=1, keepdims=True) > 0.5
        pick, pick_sibling = pick.astype(BF16), pick_sibling.astype(BF16)
        arrived()
        whole = []
        for k in range(2):
            which = lax.rem(k + side, 2)
            brought = dot(pick, old[which]) + dot(pick_sibling, old_sibling[which])
            whole.append(jnp.where(moved, brought, panels[k].astype(F32)))
        factor0 = dot(whole[0].astype(BF16), upper[0]).astype(BF16)
        below = (whole[1] - dot(factor0, up0_panel[...])).astype(BF16)
        factor1 = dot(below, upper[1]).astype(BF16)
        load.wait()
        values = flat(block[...])
        columns = []
        for j in range(cb):
            cols = slice(j * nb, (j + 1) * nb)
            value = values[:, cols].astype(F32) - dot(factor0, up0[:, cols])
            value = value.astype(BF16).astype(F32) - dot(factor1, up1[:, cols])
            if j == 0:
                value = jnp.where(column == 0, factor0.astype(F32), value)
                value = jnp.where(column == 1, factor1.astype(F32), value)
            columns.append(value.astype(BF16))
        result[...] = raw(columns, nb)

    def from_top(top):
        arrived()
        load.wait()
        copy = pltpu.make_async_copy(top.at[rows_of], result, block_sem)
        copy.start()
        copy.wait()

    if begin < nb:
        pl.when(row == 0)(lambda: from_top(top0))
        pl.when(row == 1)(lambda: from_top(top1))
        pl.when(row >= 2)(from_factors)
    else:
        from_factors()
    store = pltpu.make_async_copy(result, out.at[rows_of], out_sem)
    store.start()
    token[...] = jnp.zeros(token.shape, F32)
    store.wait()


def body(matrix, pivots, lower, upper):
    rb, nb, cb, _ = matrix.shape
    rows = rb * nb
    sizes = [nb] * (rb - 1) + [nb // 2] * 2
    begins = [sum(sizes[:i]) for i in range(len(sizes))]
    pieces = len(sizes)
    row_devices = lax.axis_size("prow")
    col_devices = lax.axis_size("pcol")
    chips, line = row_devices // 2, col_devices // 2
    row = lax.axis_index("prow").astype(I32)
    column = lax.axis_index("pcol").astype(I32)
    meta = jnp.stack([row, row % 2, column, jnp.int32(row_devices)])
    tiles = matrix.reshape(rows, cb, nb)

    def to_sibling(value):
        return lax.ppermute(value, "prow", [(r, r ^ 1) for r in range(row_devices)])

    def to_neighbour(value):
        return lax.ppermute(value, "pcol", [(c, c ^ 1) for c in range(col_devices)])

    def to_chip(value, h):
        return lax.ppermute(value, "prow", [(r, (r + 2 * h) % row_devices) for r in range(row_devices)])

    def to_next(value):
        return lax.ppermute(value, "pcol", [(c, c + 2) for c in range(col_devices - 2)])

    order = []

    def run(kernel, operands, outs, also=(), **kwargs):
        after = tuple(order[-1:]) + tuple(also)
        results = call(kernel, operands, outs, after=after, **kwargs)
        order.append(results[-1])
        return results

    last_step = pieces + line - 2

    def piece_out(i):
        return (bf16(sizes[i], nb), VMEM)

    def step_out(k):
        return (bf16(max(sizes[k - p] for p in range(line) if 0 <= k - p < pieces), nb), VMEM)

    own, held, other = [], [], []
    state = {}

    def step(k):
        if k == 0:
            own.extend(run(
                first_kernel, [(tiles, ANY)], [piece_out(0)],
                scratch=[pltpu.VMEM((sizes[0], cb, nb), BF16), DMA], mib=60,
            ))
            value = own[0]
        else:
            also = [other[k - 1]] + state.pop('awaited', [])
            operands = [(meta, SMEM), (state["came"], VMEM)] + [(v, VMEM) for v in own[k : k + 1]]
            (value,) = run(relay_kernel, operands, [step_out(k)], also, us=0.2 if k in (2, 3, 5) else 12.0)
        held.append(value)
        if k < last_step:
            sent = max(sizes[k - p] for p in range(line - 1) if 0 <= k - p < pieces)
            state["came"] = to_next(value[:sent])
        other.append(to_neighbour(value))

    def gather():
        lanes = min(nb, 128)
        spread = jnp.broadcast_to(pivots[:, :, None], (2, nb, lanes))
        table = jax.ShapeDtypeStruct((2, nb), I32)
        results = run(
            gather_kernel,
            [(meta, SMEM), (pivots, VMEM), (spread, VMEM), (tiles, ANY)],
            [piece_out(i) for i in range(1, pieces)] + [(bf16(rows + 8, cb, nb), VMEM)]
            + [(bf16(nb, cb, nb), VMEM)] * 3 + [(table, VMEM)] * 4,
            scratch=[pltpu.VMEM((2, nb), I32), pltpu.SMEM((2, nb), I32), DMA, DMA],
            us=8.0, mib=20,
        )
        own.extend(results[: pieces - 1])
        state["loaded"], send, *rest = results[pieces - 1 :]
        state.update(zip(("keep", "block0", "join", "arrive", "goal", "hops"), rest))
        state["sent"] = to_sibling(send)
        state["block0_sibling"] = to_sibling(state["block0"])

    half = nb // 2
    part = half // chips

    def join():
        joined = run(
            join_kernel,
            [(meta, SMEM), (state["join"], SMEM), (state["keep"], VMEM), (state["sent"], VMEM)],
            [(bf16(half, cb, nb), VMEM)] * 2,
            scratch=[pltpu.VMEM((half + 8, cb, nb), BF16)] * 2,
            us=2.0,
        )
        state["choices"] = [[v] + [to_chip(v, h) for h in range(1, chips)] for v in joined]
        state["fresh"], state["brought"] = [], []
        state["awaited"] = [state["block0_sibling"]]

    def fresh(turn):
        new, brought, *head = run(
            functools.partial(fresh_kernel, turn, chips),
            [(meta, SMEM), (state["hops"], VMEM)] + [(c, VMEM) for c in state["choices"][turn]],
            [(bf16(half, cb * nb), VMEM), (bf16(half, cb, nb), VMEM)]
            + [(bf16(part, nb), VMEM)] * (1 - turn),
            us=1.5, mib=16,
        )
        state["fresh"] += [new, to_sibling(new)]
        state["brought"] += [brought, to_sibling(brought)]
        if head:
            state["head"] = head + [
                lax.ppermute(head[0], "pcol", [(0, 2 * h), (1, 2 * h + 1)]) for h in range(1, line)
            ]
            state["awaited"] = state.get("awaited", []) + state["head"][1:]

    def head_here():
        (mine,) = run(
            by_place_kernel, [(meta, SMEM)] + [(v, VMEM) for v in state["head"]], [(bf16(part, nb), VMEM)], us=0.1
        )
        state["head"] = (mine, to_neighbour(mine))

    def head_pair():
        (pair,) = run(stack_kernel, [(v, VMEM) for v in state["head"]], [(bf16(2, part, nb), VMEM)], us=0.1)
        state["head"] = [pair] + [to_chip(pair, h) for h in range(1, chips)]

    def head_all():
        (mine,) = run(
            stack_kernel, [(v, VMEM) for v in state["head"]], [(bf16(chips, 2, part, nb), VMEM)], us=0.1
        )
        state["heads"] = (mine, to_sibling(mine))

    def old(values, name):
        operands = [(meta, SMEM)] + [(v, VMEM) for v in values[:line]]
        (mine,) = run(functools.partial(old_kernel, line), operands, [(bf16(nb, nb), VMEM)], us=0.1)
        state[name] = [mine] + [to_chip(mine, h) for h in range(1, chips)]
        if name == "old_held":
            state["awaited"] = state.get("awaited", []) + state[name][1:]

    def old_here():
        choices = [v for pair in zip(state["old_held"], state["old_other"]) for v in pair]
        (mine,) = run(
            by_chip_kernel, [(meta, SMEM)] + [(v, VMEM) for v in choices], [(bf16(2, nb, nb), VMEM)], us=0.1
        )
        state["old"] = (mine, to_sibling(mine))

    def scatter():
        sources = state["brought"] + [state["block0"], state["block0_sibling"], state["loaded"]]
        (state["moved"],) = run(
            scatter_kernel,
            [(meta, SMEM), (state["arrive"], SMEM), (state["goal"], SMEM)] + [(v, VMEM) for v in sources],
            [(bf16(rows + 8, cb, nb), VMEM)],
            us=0.1, mib=24,
        )

    def prep0():
        state["up0"], state["top0"] = run(
            prep0_kernel,
            [(meta, SMEM), (lower, VMEM)] + [(v, VMEM) for v in state["fresh"]],
            [(bf16(nb, cb * nb), VMEM), (bf16(nb, cb, nb), VMEM)],
            scratch=[pltpu.VMEM((nb, cb * nb), BF16)],
            us=2.0, mib=16,
        )

    def prep1():
        state["up1"], state["up0_panel"], state["top1"] = run(
            functools.partial(prep1_kernel, chips),
            [(meta, SMEM), (lower, VMEM), (upper, VMEM), (state["up0"], VMEM)]
            + [(v, VMEM) for v in state["heads"]] + [(v, VMEM) for v in state["fresh"]],
            [(bf16(nb, cb * nb), VMEM), (bf16(nb, nb), VMEM), (bf16(nb, cb, nb), VMEM)],
            scratch=[pltpu.VMEM((nb, cb * nb), BF16), pltpu.VMEM((2, nb, nb), BF16)],
            us=3.5, mib=16,
        )

    def update(i, group=1):
        operands = [(meta, SMEM), (state["goal"], VMEM)] + [(v, VMEM) for v in state["old"]] + [(upper, VMEM)]
        operands += [(state[name], VMEM) for name in ("up0", "up1", "up0_panel")]
        operands += [(state[name], ANY) for name in ("moved", "top0", "top1")]
        places = [p + h for p in range(i, i + group) for h in range(line)]
        operands += [(values[p], ANY) for values in (held, other) for p in places]
        aliases = {}
        if "result" in state:
            aliases = {len(operands): 0}
            operands.append((state["result"], ANY))
        count = sum(sizes[i : i + group])
        state["result"], _ = run(
            functools.partial(update_kernel, begins[i], line, tuple(sizes[i : i + group])),
            operands,
            [(bf16(rows, cb, nb), ANY), (jax.ShapeDtypeStruct((8, 128), F32), VMEM)],
            scratch=[
                pltpu.VMEM((2, count, nb), BF16), pltpu.VMEM((count, cb, nb), BF16),
                pltpu.VMEM((count, cb, nb), BF16), DMA((group, 2)), DMA, DMA,
            ],
            aliases=aliases,
            us=5.0, mib=24,
        )

    plan = [(0, gather), (1, join), (2, functools.partial(fresh, 0)), (3, head_here), (line - 1, functools.partial(old, held, "old_held")), (3, head_pair), (3, functools.partial(fresh, 1)), (line, functools.partial(old, other, "old_other")), (4, scatter), (4, prep0), (5, head_all), (5, old_here), (5, prep1)]
    for i in range(pieces - 2):
        plan.append((max(5 + i, i + line - 1) if i < 3 else last_step, functools.partial(update, i)))
    plan.append((last_step, functools.partial(update, pieces - 2, 2)))
    for k in range(last_step + 1):
        step(k)
        while plan and (plan[0][0] <= k or k == last_step):
            plan.pop(0)[1]()
    return state["result"].reshape(matrix.shape)


def solution(mesh):
    placed = (P(None, "prow", None, "pcol"), P(), P(), P())
    return jax.shard_map(
        body, mesh=mesh, in_specs=placed, out_specs=P(None, "prow", None, "pcol"), check_vma=False
    )
```

```python
import functools

import jax
import jax.numpy as jnp
from jax import lax
from jax.experimental import pallas as pl
from jax.experimental.pallas import tpu as pltpu
from jax.sharding import PartitionSpec as P

BF16 = jnp.bfloat16
F32 = jnp.float32
I32 = jnp.int32
SMEM = pl.BlockSpec(memory_space=pltpu.SMEM)
VMEM = pl.BlockSpec(memory_space=pltpu.VMEM)
ANY = pl.BlockSpec(memory_space=pl.ANY)
DMA = pltpu.SemaphoreType.DMA


def dot(a, b):
    return jnp.dot(a, b, preferred_element_type=F32)


def flat(rows):
    return rows.reshape(rows.shape[0], rows.shape[1] * rows.shape[2])


def bf16(*shape):
    return jax.ShapeDtypeStruct(shape, BF16)


def call(kernel, operands, outs, after=(), scratch=(), aliases=None, us=1.0, mib=8):
    count = len(operands)

    def ordered(*refs):
        kernel(*refs[:count], *refs[count + len(after) :])

    return pl.pallas_call(
        ordered,
        out_shape=tuple(shape for shape, _ in outs),
        in_specs=[spec for _, spec in operands] + [ANY] * len(after),
        out_specs=tuple(spec for _, spec in outs),
        scratch_shapes=list(scratch),
        input_output_aliases=aliases or {},
        compiler_params=pltpu.CompilerParams(vmem_limit_bytes=mib * 1024 * 1024),
        cost_estimate=pl.CostEstimate(flops=int(us * 1.1e9), bytes_accessed=0, transcendentals=0),
    )(*[array for array, _ in operands], *after)


def fill_indices(nb, rows, meta, pivots, spread, fetch, join, arrive, goal, hops):
    row, row_devices = meta[0], meta[3]
    chip, chips = row // 2, row_devices // 2
    lanes = spread.shape[2]
    tiles = nb // lanes
    slot = lax.broadcasted_iota(I32, (1, nb), 1)
    pivot0, pivot1 = pivots[0:1, :], pivots[1:2, :]

    def lookup(keys, entry, value):
        parts = [keys[:, t * lanes : (t + 1) * lanes] for t in range(tiles)]

        def add(i, totals):
            begin = pl.multiple_of(i * 8, 8)
            at = begin + lax.broadcasted_iota(I32, (8, lanes), 0)
            here, give = entry(begin, at), value(begin, at)
            return tuple(t + jnp.where(p == here, give, 0) for t, p in zip(totals, parts))

        zero = jnp.zeros((8, lanes), I32)
        totals = lax.fori_loop(0, nb // 8, add, (zero,) * tiles, unroll=8)
        return jnp.concatenate([jnp.sum(t, axis=0, keepdims=True) for t in totals], axis=1)

    def pivot_of(panel):
        return lambda begin, at: spread[panel, pl.ds(begin, 8), :]

    place = lambda begin, at: at + 1
    in_pivots0 = lookup(pivot1, pivot_of(0), place)
    in_pivots1 = lookup(pivot0, pivot_of(1), place)
    top1_in_pivots0 = lookup(nb + slot, pivot_of(0), place)
    over_top1 = lookup(pivot0, lambda begin, at: nb + at, pivot_of(1))
    chained = lookup(nb + in_pivots1 - 1, pivot_of(0), place)

    source0 = pivot0
    source1 = jnp.where(in_pivots0 > 0, in_pivots0 - 1, pivot1)
    second0 = jnp.where(in_pivots1 > 0, jnp.where(chained > 0, chained - 1, nb + in_pivots1 - 1), slot)
    second1 = jnp.where(top1_in_pivots0 > 0, top1_in_pivots0 - 1, nb + slot)
    target0 = jnp.where(over_top1 > 0, over_top1, jnp.where(in_pivots1 > 0, nb + in_pivots1 - 1, pivot0))
    target1 = jnp.where(top1_in_pivots0 > 0, top1_in_pivots0 - 1, pivot1)

    def holder(index):
        return lax.rem(lax.div(index, nb), row_devices)

    def local(index):
        return lax.div(index, nb * row_devices) * nb + lax.rem(index, nb)

    def placed(index):
        mine = (holder(index) == row) & (index >= 2 * nb)
        return jnp.where(mine, local(index), rows)

    for k, (source, second, target) in enumerate(((source0, second0, target0), (source1, second1, target1))):
        from_chip = lax.div(holder(source), 2)
        wanted = jnp.where(from_chip == chip, source, second)
        at = (slice(k, k + 1), slice(None))
        fetch[at] = local(wanted)
        join[at] = jnp.where(holder(wanted) == row, lax.rem(slot, nb // 2), nb // 2)
        arrive[at] = placed(source)
        goal[at] = placed(target)
        hops[at] = lax.rem(chip + chips - from_chip, chips)


def copy_rows(count, target, target_at, origin, origin_at):
    def copy(i, carry):
        target[target_at(i)] = origin[origin_at(i)]
        return carry

    lax.fori_loop(0, count, copy, 0, unroll=16)


def first_kernel(tiles, piece, work, sem):
    load = pltpu.make_async_copy(tiles.at[pl.ds(0, piece.shape[0])], work, sem)
    load.start()
    load.wait()
    piece[...] = flat(work[...])[:, : piece.shape[1]]


def gather_kernel(meta, pivots, spread, tiles, *refs):
    *pieces, loaded, send, keep, block0, join, arrive, goal, hops, fetch, fetch_table, load_sem, table_sem = refs
    nb = send.shape[0]
    rows = tiles.shape[0]
    core = meta[1]
    load = pltpu.make_async_copy(tiles, loaded.at[pl.ds(0, rows)], load_sem)
    load.start()
    fill_indices(nb, rows, meta, pivots, spread, fetch, join, arrive, goal, hops)
    table = pltpu.make_async_copy(fetch, fetch_table, table_sem)
    table.start()
    table.wait()
    load.wait()
    begin = nb
    for piece in pieces:
        end = begin + piece.shape[0]
        piece[...] = flat(loaded[begin:end])[:, :nb]
        begin = end
    half, side = nb // 2, lax.rem(meta[2], 2)
    for turn, b in enumerate((1 - side, side)):
        to = lambda i, turn=turn: turn * half + i
        copy_rows(half, send, to, loaded, lambda i, b=b: fetch_table[b, (1 - core) * half + i])
        copy_rows(half, keep, to, loaded, lambda i, b=b: fetch_table[b, core * half + i])
    block0[...] = loaded[0:nb]


def join_kernel(meta, join, keep, came, joined0, joined1, work0, work1):
    half = joined0.shape[0]
    core, side = meta[1], lax.rem(meta[2], 2)
    for turn, (b, work, joined) in enumerate(((1 - side, work0, joined0), (side, work1, joined1))):
        work[0:half] = came[turn * half : (turn + 1) * half]
        copy_rows(
            half, work, lambda i, b=b: join[b, core * half + i], keep, lambda i, turn=turn: turn * half + i
        )
        joined[...] = work[0:half]


def scatter_kernel(meta, arrive, goal, *refs):
    *came, old, old_sibling, tiles, out = refs
    core, side, chip = meta[1], lax.rem(meta[2], 2), meta[0] // 2
    nb = old.shape[0]
    half = nb // 2
    out[...] = tiles[...]

    @pl.when(chip == 0)
    def _():
        copy_rows(nb, out, lambda i: goal[core, i], old, lambda i: i)
        copy_rows(nb, out, lambda i: goal[1 - core, i], old_sibling, lambda i: i)

    @pl.when(chip != 0)
    def _():
        for turn, b in enumerate((1 - side, side)):
            for values, who in ((came[2 * turn], core), (came[2 * turn + 1], 1 - core)):
                copy_rows(half, out, lambda i, b=b, who=who: arrive[b, who * half + i], values, lambda i: i)


def relay_kernel(meta, came, *refs):
    *own, held = refs
    place = lax.div(meta[2], 2)
    for piece in own:

        @pl.when(place == 0)
        def _(piece=piece):
            held[0 : piece.shape[0]] = piece[...]

    @pl.when(place != 0)
    def _():
        count = min(came.shape[0], held.shape[0])
        held[0:count] = came[0:count]


def old_kernel(line, meta, *refs):
    *choices, old = refs
    for h in range(line):

        @pl.when(lax.div(meta[2], 2) == h)
        def _(h=h):
            old[...] = choices[h][0 : old.shape[0]]


def by_chip_kernel(meta, *refs):
    *choices, out = refs
    for h in range(len(choices) // 2):

        @pl.when(meta[0] // 2 == h)
        def _(h=h):
            out[0] = choices[2 * h][...]
            out[1] = choices[2 * h + 1][...]


def by_place_kernel(meta, *refs):
    out = refs[-1]
    for h, choice in enumerate(refs[:-1]):

        @pl.when(lax.div(meta[2], 2) == h)
        def _(choice=choice):
            out[...] = choice[...]


def stack_kernel(*refs):
    *entries, out = refs
    for i, entry in enumerate(entries):
        out[i] = entry[...]


def choose(hop, choices):
    value = flat(choices[0]).astype(F32)
    for h, other in enumerate(choices[1:], 1):
        value = jnp.where(hop == h, flat(other).astype(F32), value)
    return value.astype(BF16)


def fresh_kernel(turn, chips, meta, hops, *refs):
    choices, (fresh, brought, *head) = refs[:chips], refs[chips:]
    half = fresh.shape[0]
    core, side, chip = meta[1], lax.rem(meta[2], 2), meta[0] // 2
    b = side if turn else 1 - side
    hop = jnp.broadcast_to(hops[pl.ds(b, 1), :], (8, 2 * half)).T[:, 0:1]
    hop = jnp.where(core == 0, hop[:half], hop[half:])
    fresh[...] = choose(hop, [c[...] for c in choices])
    if head:
        part, nb = head[0].shape
        head[0][...] = fresh[pl.ds(pl.multiple_of(chip * part, part), part), :nb]
    if chips == 1:
        brought[...] = choices[0][...]
    for h in range(1, chips):

        @pl.when((chip == h) | ((chip == 0) & (h == 1)))
        def _(h=h):
            brought[...] = choices[h][...]


def assemble(meta, b, fresh, work):
    core, side = meta[1], lax.rem(meta[2], 2)
    half = work.shape[0] // 2
    for turn, which in enumerate((1 - side, side)):

        @pl.when(which == b)
        def _(turn=turn):
            work[pl.ds(pl.multiple_of(core * half, half), half)] = fresh[2 * turn][...]
            work[pl.ds(pl.multiple_of((1 - core) * half, half), half)] = fresh[2 * turn + 1][...]


def raw(columns, nb):
    joined = jnp.concatenate(columns, axis=1)
    return joined.reshape(joined.shape[0], len(columns), nb)


def prep0_kernel(meta, lower, *refs):
    *fresh, up0, top, work = refs
    column = meta[2]
    nb = work.shape[0]
    assemble(meta, 0, fresh, work)
    shown = []
    for j in range(work.shape[1] // nb):
        cols = slice(j * nb, (j + 1) * nb)
        product = dot(lower[0], work[:, cols])
        show = product
        if j == 0:
            show = jnp.where(column == 0, work[:, cols].astype(F32), product)
            product = jnp.where(column == 0, 0.0, product)
        up0[:, cols] = product.astype(BF16)
        shown.append(show.astype(BF16))
    top[...] = raw(shown, nb)


def prep1_kernel(chips, meta, lower, upper, up0, heads, heads_sibling, *refs):
    *fresh, up1, up0_panel, top, work, head = refs
    core, column, chip = meta[1], meta[2], meta[0] // 2
    side = lax.rem(column, 2)
    nb, part = work.shape[0], heads.shape[2]
    for who, parts in ((core, heads), (1 - core, heads_sibling)):
        for h in range(chips):
            at = pl.multiple_of((who * chips + lax.rem(chip + chips - h, chips)) * part, part)
            head[1 - side, pl.ds(at, part)] = parts[h, 0]
            head[side, pl.ds(at, part)] = parts[h, 1]
    assemble(meta, 1, fresh, work)
    up0_panel[...] = dot(lower[0], head[0]).astype(BF16)
    factor = dot(head[1], upper[0]).astype(BF16)
    in_panel, next_panel = column == 0, column == 1
    shown = []
    for j in range(work.shape[1] // nb):
        cols = slice(j * nb, (j + 1) * nb)
        updated = (work[:, cols].astype(F32) - dot(factor, up0[:, cols])).astype(BF16)
        last = dot(lower[1], updated)
        show = last
        if j == 0:
            show = jnp.where(next_panel, updated.astype(F32), show)
            show = jnp.where(in_panel, factor.astype(F32), show)
            last = jnp.where(in_panel | next_panel, 0.0, last)
        up1[:, cols] = last.astype(BF16)
        shown.append(show.astype(BF16))
    top[...] = raw(shown, nb)


def update_kernel(
    begin, line, sizes, meta, goal, old, old_sibling, upper, up0, up1, up0_panel, tiles, top0, top1, *rest
):
    spans = len(sizes) * line
    held, other = rest[:spans], rest[spans : 2 * spans]
    out, token, panels, block, result, panel_sem, block_sem, out_sem = rest[-8:]
    row, core, column = meta[0], meta[1], meta[2]
    side, place = lax.rem(column, 2), lax.div(column, 2)
    count, cb, nb = block.shape
    rows_of = pl.ds(begin, count)

    def panel_copy(i, h, which):
        source = (held, other)[which][i * line + h].at[pl.ds(0, sizes[i])]
        target = panels.at[lax.rem(side + which, 2), pl.ds(sum(sizes[:i]), sizes[i])]
        return pltpu.make_async_copy(source, target, panel_sem.at[i, which])

    load = pltpu.make_async_copy(tiles.at[rows_of], block, block_sem)
    load.start()
    for h in range(line):

        @pl.when(place == h)
        def _(h=h):
            for i in range(len(sizes)):
                panel_copy(i, h, 0).start()
                panel_copy(i, h, 1).start()

    def arrived():
        for i in range(len(sizes)):
            panel_copy(i, 0, 0).wait()
            panel_copy(i, 0, 1).wait()

    def from_factors():
        here = begin + lax.broadcasted_iota(I32, (count, nb), 0)
        pick = jnp.where(here == goal[pl.ds(core, 1), :], 1.0, 0.0)
        pick_sibling = jnp.where(here == goal[pl.ds(1 - core, 1), :], 1.0, 0.0)
        moved = jnp.sum(pick + pick_sibling, axis=1, keepdims=True) > 0.5
        pick, pick_sibling = pick.astype(BF16), pick_sibling.astype(BF16)
        arrived()
        whole = []
        for k in range(2):
            which = lax.rem(k + side, 2)
            brought = dot(pick, old[which]) + dot(pick_sibling, old_sibling[which])
            whole.append(jnp.where(moved, brought, panels[k].astype(F32)))
        factor0 = dot(whole[0].astype(BF16), upper[0]).astype(BF16)
        below = (whole[1] - dot(factor0, up0_panel[...])).astype(BF16)
        factor1 = dot(below, upper[1]).astype(BF16)
        load.wait()
        values = flat(block[...])
        columns = []
        for j in range(cb):
            cols = slice(j * nb, (j + 1) * nb)
            value = values[:, cols].astype(F32) - dot(factor0, up0[:, cols])
            value = value.astype(BF16).astype(F32) - dot(factor1, up1[:, cols])
            if j == 0:
                value = jnp.where(column == 0, factor0.astype(F32), value)
                value = jnp.where(column == 1, factor1.astype(F32), value)
            columns.append(value.astype(BF16))
        result[...] = raw(columns, nb)

    def from_top(top):
        arrived()
        load.wait()
        copy = pltpu.make_async_copy(top.at[rows_of], result, block_sem)
        copy.start()
        copy.wait()

    if begin < nb:
        pl.when(row == 0)(lambda: from_top(top0))
        pl.when(row == 1)(lambda: from_top(top1))
        pl.when(row >= 2)(from_factors)
    else:
        from_factors()
    store = pltpu.make_async_copy(result, out.at[rows_of], out_sem)
    store.start()
    token[...] = jnp.zeros(token.shape, F32)
    store.wait()


def body(matrix, pivots, lower, upper):
    rb, nb, cb, _ = matrix.shape
    rows = rb * nb
    sizes = [nb] * (rb - 1) + [nb // 2] * 2
    begins = [sum(sizes[:i]) for i in range(len(sizes))]
    pieces = len(sizes)
    row_devices = lax.axis_size("prow")
    col_devices = lax.axis_size("pcol")
    chips, line = row_devices // 2, col_devices // 2
    row = lax.axis_index("prow").astype(I32)
    column = lax.axis_index("pcol").astype(I32)
    meta = jnp.stack([row, row % 2, column, jnp.int32(row_devices)])
    tiles = matrix.reshape(rows, cb, nb)

    def to_sibling(value):
        return lax.ppermute(value, "prow", [(r, r ^ 1) for r in range(row_devices)])

    def to_neighbour(value):
        return lax.ppermute(value, "pcol", [(c, c ^ 1) for c in range(col_devices)])

    def to_chip(value, h):
        return lax.ppermute(value, "prow", [(r, (r + 2 * h) % row_devices) for r in range(row_devices)])

    def to_next(value):
        return lax.ppermute(value, "pcol", [(c, c + 2) for c in range(col_devices - 2)])

    order = []

    def run(kernel, operands, outs, also=(), **kwargs):
        after = tuple(order[-1:]) + tuple(also)
        results = call(kernel, operands, outs, after=after, **kwargs)
        order.append(results[-1])
        return results

    last_step = pieces + line - 2

    def piece_out(i):
        return (bf16(sizes[i], nb), VMEM)

    def step_out(k):
        return (bf16(max(sizes[k - p] for p in range(line) if 0 <= k - p < pieces), nb), VMEM)

    own, held, other = [], [], []
    state = {}

    def step(k):
        if k == 0:
            own.extend(run(
                first_kernel, [(tiles, ANY)], [piece_out(0)],
                scratch=[pltpu.VMEM((sizes[0], cb, nb), BF16), DMA], mib=60,
            ))
            value = own[0]
        else:
            also = [other[k - 1]] + state.pop('awaited', [])
            operands = [(meta, SMEM), (state["came"], VMEM)] + [(v, VMEM) for v in own[k : k + 1]]
            (value,) = run(relay_kernel, operands, [step_out(k)], also, us=0.2 if k in (2, 3, 5) else 12.0)
        held.append(value)
        if k < last_step:
            sent = max(sizes[k - p] for p in range(line - 1) if 0 <= k - p < pieces)
            state["came"] = to_next(value[:sent])
        other.append(to_neighbour(value))

    def gather():
        lanes = min(nb, 128)
        spread = jnp.broadcast_to(pivots[:, :, None], (2, nb, lanes))
        table = jax.ShapeDtypeStruct((2, nb), I32)
        results = run(
            gather_kernel,
            [(meta, SMEM), (pivots, VMEM), (spread, VMEM), (tiles, ANY)],
            [piece_out(i) for i in range(1, pieces)] + [(bf16(rows + 8, cb, nb), VMEM)]
            + [(bf16(nb, cb, nb), VMEM)] * 3 + [(table, VMEM)] * 4,
            scratch=[pltpu.VMEM((2, nb), I32), pltpu.SMEM((2, nb), I32), DMA, DMA],
            us=8.0, mib=20,
        )
        own.extend(results[: pieces - 1])
        state["loaded"], send, *rest = results[pieces - 1 :]
        state.update(zip(("keep", "block0", "join", "arrive", "goal", "hops"), rest))
        state["sent"] = to_sibling(send)
        state["block0_sibling"] = to_sibling(state["block0"])

    half = nb // 2
    part = half // chips

    def join():
        joined = run(
            join_kernel,
            [(meta, SMEM), (state["join"], SMEM), (state["keep"], VMEM), (state["sent"], VMEM)],
            [(bf16(half, cb, nb), VMEM)] * 2,
            scratch=[pltpu.VMEM((half + 8, cb, nb), BF16)] * 2,
            us=2.0,
        )
        state["choices"] = [[v] + [to_chip(v, h) for h in range(1, chips)] for v in joined]
        state["fresh"], state["brought"] = [], []
        state["awaited"] = [state["block0_sibling"]]

    def fresh(turn):
        new, brought, *head = run(
            functools.partial(fresh_kernel, turn, chips),
            [(meta, SMEM), (state["hops"], VMEM)] + [(c, VMEM) for c in state["choices"][turn]],
            [(bf16(half, cb * nb), VMEM), (bf16(half, cb, nb), VMEM)]
            + [(bf16(part, nb), VMEM)] * (1 - turn),
            us=1.5, mib=16,
        )
        state["fresh"] += [new, to_sibling(new)]
        state["brought"] += [brought, to_sibling(brought)]
        if head:
            state["head"] = head + [
                lax.ppermute(head[0], "pcol", [(0, 2 * h), (1, 2 * h + 1)]) for h in range(1, line)
            ]
            state["awaited"] = state.get("awaited", []) + state["head"][1:]

    def head_here():
        (mine,) = run(
            by_place_kernel, [(meta, SMEM)] + [(v, VMEM) for v in state["head"]], [(bf16(part, nb), VMEM)], us=0.1
        )
        state["head"] = (mine, to_neighbour(mine))

    def head_pair():
        (pair,) = run(stack_kernel, [(v, VMEM) for v in state["head"]], [(bf16(2, part, nb), VMEM)], us=0.1)
        state["head"] = [pair] + [to_chip(pair, h) for h in range(1, chips)]

    def head_all():
        (mine,) = run(
            stack_kernel, [(v, VMEM) for v in state["head"]], [(bf16(chips, 2, part, nb), VMEM)], us=0.1
        )
        state["heads"] = (mine, to_sibling(mine))

    def old(values, name):
        operands = [(meta, SMEM)] + [(v, VMEM) for v in values[:line]]
        (mine,) = run(functools.partial(old_kernel, line), operands, [(bf16(nb, nb), VMEM)], us=0.1)
        state[name] = [mine] + [to_chip(mine, h) for h in range(1, chips)]
        if name == "old_held":
            state["awaited"] = state.get("awaited", []) + state[name][1:]

    def old_here():
        choices = [v for pair in zip(state["old_held"], state["old_other"]) for v in pair]
        (mine,) = run(
            by_chip_kernel, [(meta, SMEM)] + [(v, VMEM) for v in choices], [(bf16(2, nb, nb), VMEM)], us=0.1
        )
        state["old"] = (mine, to_sibling(mine))

    def scatter():
        sources = state["brought"] + [state["block0"], state["block0_sibling"], state["loaded"]]
        (state["moved"],) = run(
            scatter_kernel,
            [(meta, SMEM), (state["arrive"], SMEM), (state["goal"], SMEM)] + [(v, VMEM) for v in sources],
            [(bf16(rows + 8, cb, nb), VMEM)],
            us=0.1, mib=24,
        )

    def prep0():
        state["up0"], state["top0"] = run(
            prep0_kernel,
            [(meta, SMEM), (lower, VMEM)] + [(v, VMEM) for v in state["fresh"]],
            [(bf16(nb, cb * nb), VMEM), (bf16(nb, cb, nb), VMEM)],
            scratch=[pltpu.VMEM((nb, cb * nb), BF16)],
            us=2.0, mib=16,
        )

    def prep1():
        state["up1"], state["up0_panel"], state["top1"] = run(
            functools.partial(prep1_kernel, chips),
            [(meta, SMEM), (lower, VMEM), (upper, VMEM), (state["up0"], VMEM)]
            + [(v, VMEM) for v in state["heads"]] + [(v, VMEM) for v in state["fresh"]],
            [(bf16(nb, cb * nb), VMEM), (bf16(nb, nb), VMEM), (bf16(nb, cb, nb), VMEM)],
            scratch=[pltpu.VMEM((nb, cb * nb), BF16), pltpu.VMEM((2, nb, nb), BF16)],
            us=3.5, mib=16,
        )

    def update(i, group=1):
        operands = [(meta, SMEM), (state["goal"], VMEM)] + [(v, VMEM) for v in state["old"]] + [(upper, VMEM)]
        operands += [(state[name], VMEM) for name in ("up0", "up1", "up0_panel")]
        operands += [(state[name], ANY) for name in ("moved", "top0", "top1")]
        places = [p + h for p in range(i, i + group) for h in range(line)]
        operands += [(values[p], ANY) for values in (held, other) for p in places]
        aliases = {}
        if "result" in state:
            aliases = {len(operands): 0}
            operands.append((state["result"], ANY))
        count = sum(sizes[i : i + group])
        state["result"], _ = run(
            functools.partial(update_kernel, begins[i], line, tuple(sizes[i : i + group])),
            operands,
            [(bf16(rows, cb, nb), ANY), (jax.ShapeDtypeStruct((8, 128), F32), VMEM)],
            scratch=[
                pltpu.VMEM((2, count, nb), BF16), pltpu.VMEM((count, cb, nb), BF16),
                pltpu.VMEM((count, cb, nb), BF16), DMA((group, 2)), DMA, DMA,
            ],
            aliases=aliases,
            us=5.0, mib=24,
        )

    plan = [(0, gather), (1, join), (2, functools.partial(fresh, 0)), (3, head_here), (3, head_pair), (3, functools.partial(fresh, 1)), (line, functools.partial(old, held, "old_held")), (line, functools.partial(old, other, "old_other")), (4, scatter), (4, prep0), (5, head_all), (5, old_here), (5, prep1)]
    for i in range(pieces - 2):
        plan.append((max(6 + i // 2, i + line - 1) if i < 3 else last_step, functools.partial(update, i)))
    plan.append((last_step, functools.partial(update, pieces - 2, 2)))
    for k in range(last_step + 1):
        step(k)
        while plan and (plan[0][0] <= k or k == last_step):
            plan.pop(0)[1]()
    return state["result"].reshape(matrix.shape)


def solution(mesh):
    placed = (P(None, "prow", None, "pcol"), P(), P(), P())
    return jax.shard_map(
        body, mesh=mesh, in_specs=placed, out_specs=P(None, "prow", None, "pcol"), check_vma=False
    )
```

```python
import functools

import jax
import jax.numpy as jnp
from jax import lax
from jax.experimental import pallas as pl
from jax.experimental.pallas import tpu as pltpu
from jax.sharding import PartitionSpec as P

BF16 = jnp.bfloat16
F32 = jnp.float32
I32 = jnp.int32
SMEM = pl.BlockSpec(memory_space=pltpu.SMEM)
VMEM = pl.BlockSpec(memory_space=pltpu.VMEM)
ANY = pl.BlockSpec(memory_space=pl.ANY)
DMA = pltpu.SemaphoreType.DMA


def dot(a, b):
    return jnp.dot(a, b, preferred_element_type=F32)


def flat(rows):
    return rows.reshape(rows.shape[0], rows.shape[1] * rows.shape[2])


def bf16(*shape):
    return jax.ShapeDtypeStruct(shape, BF16)


def call(kernel, operands, outs, after=(), scratch=(), aliases=None, us=1.0, mib=8):
    count = len(operands)

    def ordered(*refs):
        kernel(*refs[:count], *refs[count + len(after) :])

    return pl.pallas_call(
        ordered,
        out_shape=tuple(shape for shape, _ in outs),
        in_specs=[spec for _, spec in operands] + [ANY] * len(after),
        out_specs=tuple(spec for _, spec in outs),
        scratch_shapes=list(scratch),
        input_output_aliases=aliases or {},
        compiler_params=pltpu.CompilerParams(vmem_limit_bytes=mib * 1024 * 1024),
        cost_estimate=pl.CostEstimate(flops=int(us * 1.1e9), bytes_accessed=0, transcendentals=0),
    )(*[array for array, _ in operands], *after)


def fill_indices(nb, rows, meta, pivots, spread, fetch, join, arrive, goal, hops):
    row, row_devices = meta[0], meta[3]
    chip, chips = row // 2, row_devices // 2
    lanes = spread.shape[2]
    tiles = nb // lanes
    slot = lax.broadcasted_iota(I32, (1, nb), 1)
    pivot0, pivot1 = pivots[0:1, :], pivots[1:2, :]

    def lookup(keys, entry, value):
        parts = [keys[:, t * lanes : (t + 1) * lanes] for t in range(tiles)]

        def add(i, totals):
            begin = pl.multiple_of(i * 8, 8)
            at = begin + lax.broadcasted_iota(I32, (8, lanes), 0)
            here, give = entry(begin, at), value(begin, at)
            return tuple(t + jnp.where(p == here, give, 0) for t, p in zip(totals, parts))

        zero = jnp.zeros((8, lanes), I32)
        totals = lax.fori_loop(0, nb // 8, add, (zero,) * tiles, unroll=8)
        return jnp.concatenate([jnp.sum(t, axis=0, keepdims=True) for t in totals], axis=1)

    def pivot_of(panel):
        return lambda begin, at: spread[panel, pl.ds(begin, 8), :]

    place = lambda begin, at: at + 1
    in_pivots0 = lookup(pivot1, pivot_of(0), place)
    in_pivots1 = lookup(pivot0, pivot_of(1), place)
    top1_in_pivots0 = lookup(nb + slot, pivot_of(0), place)
    over_top1 = lookup(pivot0, lambda begin, at: nb + at, pivot_of(1))
    chained = lookup(nb + in_pivots1 - 1, pivot_of(0), place)

    source0 = pivot0
    source1 = jnp.where(in_pivots0 > 0, in_pivots0 - 1, pivot1)
    second0 = jnp.where(in_pivots1 > 0, jnp.where(chained > 0, chained - 1, nb + in_pivots1 - 1), slot)
    second1 = jnp.where(top1_in_pivots0 > 0, top1_in_pivots0 - 1, nb + slot)
    target0 = jnp.where(over_top1 > 0, over_top1, jnp.where(in_pivots1 > 0, nb + in_pivots1 - 1, pivot0))
    target1 = jnp.where(top1_in_pivots0 > 0, top1_in_pivots0 - 1, pivot1)

    def holder(index):
        return lax.rem(lax.div(index, nb), row_devices)

    def local(index):
        return lax.div(index, nb * row_devices) * nb + lax.rem(index, nb)

    def placed(index):
        mine = (holder(index) == row) & (index >= 2 * nb)
        return jnp.where(mine, local(index), rows)

    for k, (source, second, target) in enumerate(((source0, second0, target0), (source1, second1, target1))):
        from_chip = lax.div(holder(source), 2)
        wanted = jnp.where(from_chip == chip, source, second)
        at = (slice(k, k + 1), slice(None))
        fetch[at] = local(wanted)
        join[at] = jnp.where(holder(wanted) == row, lax.rem(slot, nb // 2), nb // 2)
        arrive[at] = placed(source)
        goal[at] = placed(target)
        hops[at] = lax.rem(chip + chips - from_chip, chips)


def copy_rows(count, target, target_at, origin, origin_at):
    def copy(i, carry):
        target[target_at(i)] = origin[origin_at(i)]
        return carry

    lax.fori_loop(0, count, copy, 0, unroll=16)


def first_kernel(tiles, piece, work, sem):
    load = pltpu.make_async_copy(tiles.at[pl.ds(0, piece.shape[0])], work, sem)
    load.start()
    load.wait()
    piece[...] = flat(work[...])[:, : piece.shape[1]]


def gather_kernel(meta, pivots, spread, tiles, *refs):
    *pieces, loaded, send, keep, block0, join, arrive, goal, hops, fetch, fetch_table, load_sem, table_sem = refs
    nb = send.shape[0]
    rows = tiles.shape[0]
    core = meta[1]
    load = pltpu.make_async_copy(tiles, loaded.at[pl.ds(0, rows)], load_sem)
    load.start()
    fill_indices(nb, rows, meta, pivots, spread, fetch, join, arrive, goal, hops)
    table = pltpu.make_async_copy(fetch, fetch_table, table_sem)
    table.start()
    table.wait()
    load.wait()
    begin = nb
    for piece in pieces:
        end = begin + piece.shape[0]
        piece[...] = flat(loaded[begin:end])[:, :nb]
        begin = end
    half, side = nb // 2, lax.rem(meta[2], 2)
    for turn, b in enumerate((1 - side, side)):
        to = lambda i, turn=turn: turn * half + i
        copy_rows(half, send, to, loaded, lambda i, b=b: fetch_table[b, (1 - core) * half + i])
        copy_rows(half, keep, to, loaded, lambda i, b=b: fetch_table[b, core * half + i])
    block0[...] = loaded[0:nb]


def join_kernel(meta, join, keep, came, joined0, joined1, work0, work1):
    half = joined0.shape[0]
    core, side = meta[1], lax.rem(meta[2], 2)
    for turn, (b, work, joined) in enumerate(((1 - side, work0, joined0), (side, work1, joined1))):
        work[0:half] = came[turn * half : (turn + 1) * half]
        copy_rows(
            half, work, lambda i, b=b: join[b, core * half + i], keep, lambda i, turn=turn: turn * half + i
        )
        joined[...] = work[0:half]


def scatter_kernel(meta, arrive, goal, *refs):
    *came, old, old_sibling, tiles, out = refs
    core, side, chip = meta[1], lax.rem(meta[2], 2), meta[0] // 2
    nb = old.shape[0]
    half = nb // 2
    out[...] = tiles[...]

    @pl.when(chip == 0)
    def _():
        copy_rows(nb, out, lambda i: goal[core, i], old, lambda i: i)
        copy_rows(nb, out, lambda i: goal[1 - core, i], old_sibling, lambda i: i)

    @pl.when(chip != 0)
    def _():
        for turn, b in enumerate((1 - side, side)):
            for values, who in ((came[2 * turn], core), (came[2 * turn + 1], 1 - core)):
                copy_rows(half, out, lambda i, b=b, who=who: arrive[b, who * half + i], values, lambda i: i)


def relay_kernel(meta, came, *refs):
    *own, held = refs
    place = lax.div(meta[2], 2)
    for piece in own:

        @pl.when(place == 0)
        def _(piece=piece):
            held[0 : piece.shape[0]] = piece[...]

    @pl.when(place != 0)
    def _():
        count = min(came.shape[0], held.shape[0])
        held[0:count] = came[0:count]


def old_kernel(line, meta, *refs):
    *choices, old = refs
    for h in range(line):

        @pl.when(lax.div(meta[2], 2) == h)
        def _(h=h):
            old[...] = choices[h][0 : old.shape[0]]


def by_chip_kernel(meta, *refs):
    *choices, out = refs
    for h in range(len(choices) // 2):

        @pl.when(meta[0] // 2 == h)
        def _(h=h):
            out[0] = choices[2 * h][...]
            out[1] = choices[2 * h + 1][...]


def by_place_kernel(meta, *refs):
    out = refs[-1]
    for h, choice in enumerate(refs[:-1]):

        @pl.when(lax.div(meta[2], 2) == h)
        def _(choice=choice):
            out[...] = choice[...]


def stack_kernel(*refs):
    *entries, out = refs
    for i, entry in enumerate(entries):
        out[i] = entry[...]


def choose(hop, choices):
    value = flat(choices[0]).astype(F32)
    for h, other in enumerate(choices[1:], 1):
        value = jnp.where(hop == h, flat(other).astype(F32), value)
    return value.astype(BF16)


def fresh_kernel(turn, chips, meta, hops, *refs):
    choices, (fresh, brought, *head) = refs[:chips], refs[chips:]
    half = fresh.shape[0]
    core, side, chip = meta[1], lax.rem(meta[2], 2), meta[0] // 2
    b = side if turn else 1 - side
    hop = jnp.broadcast_to(hops[pl.ds(b, 1), :], (8, 2 * half)).T[:, 0:1]
    hop = jnp.where(core == 0, hop[:half], hop[half:])
    fresh[...] = choose(hop, [c[...] for c in choices])
    if head:
        part, nb = head[0].shape
        head[0][...] = fresh[pl.ds(pl.multiple_of(chip * part, part), part), :nb]
    if chips == 1:
        brought[...] = choices[0][...]
    for h in range(1, chips):

        @pl.when((chip == h) | ((chip == 0) & (h == 1)))
        def _(h=h):
            brought[...] = choices[h][...]


def assemble(meta, b, fresh, work):
    core, side = meta[1], lax.rem(meta[2], 2)
    half = work.shape[0] // 2
    for turn, which in enumerate((1 - side, side)):

        @pl.when(which == b)
        def _(turn=turn):
            work[pl.ds(pl.multiple_of(core * half, half), half)] = fresh[2 * turn][...]
            work[pl.ds(pl.multiple_of((1 - core) * half, half), half)] = fresh[2 * turn + 1][...]


def raw(columns, nb):
    joined = jnp.concatenate(columns, axis=1)
    return joined.reshape(joined.shape[0], len(columns), nb)


def prep0_kernel(meta, lower, *refs):
    *fresh, up0, top, work = refs
    column = meta[2]
    nb = work.shape[0]
    assemble(meta, 0, fresh, work)
    shown = []
    for j in range(work.shape[1] // nb):
        cols = slice(j * nb, (j + 1) * nb)
        product = dot(lower[0], work[:, cols])
        show = product
        if j == 0:
            show = jnp.where(column == 0, work[:, cols].astype(F32), product)
            product = jnp.where(column == 0, 0.0, product)
        up0[:, cols] = product.astype(BF16)
        shown.append(show.astype(BF16))
    top[...] = raw(shown, nb)


def prep1_kernel(chips, meta, lower, upper, up0, heads, heads_sibling, *refs):
    *fresh, up1, up0_panel, top, work, head = refs
    core, column, chip = meta[1], meta[2], meta[0] // 2
    side = lax.rem(column, 2)
    nb, part = work.shape[0], heads.shape[2]
    for who, parts in ((core, heads), (1 - core, heads_sibling)):
        for h in range(chips):
            at = pl.multiple_of((who * chips + lax.rem(chip + chips - h, chips)) * part, part)
            head[1 - side, pl.ds(at, part)] = parts[h, 0]
            head[side, pl.ds(at, part)] = parts[h, 1]
    assemble(meta, 1, fresh, work)
    up0_panel[...] = dot(lower[0], head[0]).astype(BF16)
    factor = dot(head[1], upper[0]).astype(BF16)
    in_panel, next_panel = column == 0, column == 1
    shown = []
    for j in range(work.shape[1] // nb):
        cols = slice(j * nb, (j + 1) * nb)
        updated = (work[:, cols].astype(F32) - dot(factor, up0[:, cols])).astype(BF16)
        last = dot(lower[1], updated)
        show = last
        if j == 0:
            show = jnp.where(next_panel, updated.astype(F32), show)
            show = jnp.where(in_panel, factor.astype(F32), show)
            last = jnp.where(in_panel | next_panel, 0.0, last)
        up1[:, cols] = last.astype(BF16)
        shown.append(show.astype(BF16))
    top[...] = raw(shown, nb)


def update_kernel(
    begin, line, sizes, meta, goal, old, old_sibling, upper, up0, up1, up0_panel, tiles, top0, top1, *rest
):
    spans = len(sizes) * line
    held, other = rest[:spans], rest[spans : 2 * spans]
    out, token, panels, block, result, panel_sem, block_sem, out_sem = rest[-8:]
    row, core, column = meta[0], meta[1], meta[2]
    side, place = lax.rem(column, 2), lax.div(column, 2)
    count, cb, nb = block.shape
    rows_of = pl.ds(begin, count)

    def panel_copy(i, h, which):
        source = (held, other)[which][i * line + h].at[pl.ds(0, sizes[i])]
        target = panels.at[lax.rem(side + which, 2), pl.ds(sum(sizes[:i]), sizes[i])]
        return pltpu.make_async_copy(source, target, panel_sem.at[i, which])

    load = pltpu.make_async_copy(tiles.at[rows_of], block, block_sem)
    load.start()
    for h in range(line):

        @pl.when(place == h)
        def _(h=h):
            for i in range(len(sizes)):
                panel_copy(i, h, 0).start()
                panel_copy(i, h, 1).start()

    def arrived():
        for i in range(len(sizes)):
            panel_copy(i, 0, 0).wait()
            panel_copy(i, 0, 1).wait()

    def from_factors():
        here = begin + lax.broadcasted_iota(I32, (count, nb), 0)
        pick = jnp.where(here == goal[pl.ds(core, 1), :], 1.0, 0.0)
        pick_sibling = jnp.where(here == goal[pl.ds(1 - core, 1), :], 1.0, 0.0)
        pick, pick_sibling = pick.astype(BF16), pick_sibling.astype(BF16)
        lanes = min(nb, 128)
        ones = jnp.ones((nb, lanes), BF16)
        found = dot(pick, ones) + dot(pick_sibling, ones)
        moved = jnp.concatenate([found] * (nb // lanes), axis=1) > 0.5
        arrived()
        whole = []
        for k in range(2):
            which = lax.rem(k + side, 2)
            brought = dot(pick, old[which]) + dot(pick_sibling, old_sibling[which])
            whole.append(jnp.where(moved, brought, panels[k].astype(F32)))
        factor0 = dot(whole[0].astype(BF16), upper[0]).astype(BF16)
        below = (whole[1] - dot(factor0, up0_panel[...])).astype(BF16)
        factor1 = dot(below, upper[1]).astype(BF16)
        load.wait()
        values = flat(block[...])
        columns = []
        for j in range(cb):
            cols = slice(j * nb, (j + 1) * nb)
            value = values[:, cols].astype(F32) - dot(factor0, up0[:, cols])
            value = value.astype(BF16).astype(F32) - dot(factor1, up1[:, cols])
            if j == 0:
                value = jnp.where(column == 0, factor0.astype(F32), value)
                value = jnp.where(column == 1, factor1.astype(F32), value)
            columns.append(value.astype(BF16))
        result[...] = raw(columns, nb)

    def from_top(top):
        arrived()
        load.wait()
        copy = pltpu.make_async_copy(top.at[rows_of], result, block_sem)
        copy.start()
        copy.wait()

    if begin < nb:
        pl.when(row == 0)(lambda: from_top(top0))
        pl.when(row == 1)(lambda: from_top(top1))
        pl.when(row >= 2)(from_factors)
    else:
        from_factors()
    store = pltpu.make_async_copy(result, out.at[rows_of], out_sem)
    store.start()
    token[...] = jnp.zeros(token.shape, F32)
    store.wait()


def body(matrix, pivots, lower, upper):
    rb, nb, cb, _ = matrix.shape
    rows = rb * nb
    sizes = [nb] * (rb - 1) + [nb // 2] * 2
    begins = [sum(sizes[:i]) for i in range(len(sizes))]
    pieces = len(sizes)
    row_devices = lax.axis_size("prow")
    col_devices = lax.axis_size("pcol")
    chips, line = row_devices // 2, col_devices // 2
    row = lax.axis_index("prow").astype(I32)
    column = lax.axis_index("pcol").astype(I32)
    meta = jnp.stack([row, row % 2, column, jnp.int32(row_devices)])
    tiles = matrix.reshape(rows, cb, nb)

    def to_sibling(value):
        return lax.ppermute(value, "prow", [(r, r ^ 1) for r in range(row_devices)])

    def to_neighbour(value):
        return lax.ppermute(value, "pcol", [(c, c ^ 1) for c in range(col_devices)])

    def to_chip(value, h):
        return lax.ppermute(value, "prow", [(r, (r + 2 * h) % row_devices) for r in range(row_devices)])

    def to_next(value):
        return lax.ppermute(value, "pcol", [(c, c + 2) for c in range(col_devices - 2)])

    order = []

    def run(kernel, operands, outs, also=(), **kwargs):
        after = tuple(order[-1:]) + tuple(also)
        results = call(kernel, operands, outs, after=after, **kwargs)
        order.append(results[-1])
        return results

    last_step = pieces + line - 2

    def piece_out(i):
        return (bf16(sizes[i], nb), VMEM)

    def step_out(k):
        return (bf16(max(sizes[k - p] for p in range(line) if 0 <= k - p < pieces), nb), VMEM)

    own, held, other = [], [], []
    state = {}

    def step(k):
        if k == 0:
            own.extend(run(
                first_kernel, [(tiles, ANY)], [piece_out(0)],
                scratch=[pltpu.VMEM((sizes[0], cb, nb), BF16), DMA], mib=60,
            ))
            value = own[0]
        else:
            also = [other[k - 1]] + state.pop('awaited', [])
            operands = [(meta, SMEM), (state["came"], VMEM)] + [(v, VMEM) for v in own[k : k + 1]]
            (value,) = run(relay_kernel, operands, [step_out(k)], also, us=0.2 if k in (2, 3, 5) else 12.0)
        held.append(value)
        if k < last_step:
            sent = max(sizes[k - p] for p in range(line - 1) if 0 <= k - p < pieces)
            state["came"] = to_next(value[:sent])
        other.append(to_neighbour(value))

    def gather():
        lanes = min(nb, 128)
        spread = jnp.broadcast_to(pivots[:, :, None], (2, nb, lanes))
        table = jax.ShapeDtypeStruct((2, nb), I32)
        results = run(
            gather_kernel,
            [(meta, SMEM), (pivots, VMEM), (spread, VMEM), (tiles, ANY)],
            [piece_out(i) for i in range(1, pieces)] + [(bf16(rows + 8, cb, nb), VMEM)]
            + [(bf16(nb, cb, nb), VMEM)] * 3 + [(table, VMEM)] * 4,
            scratch=[pltpu.VMEM((2, nb), I32), pltpu.SMEM((2, nb), I32), DMA, DMA],
            us=8.0, mib=20,
        )
        own.extend(results[: pieces - 1])
        state["loaded"], send, *rest = results[pieces - 1 :]
        state.update(zip(("keep", "block0", "join", "arrive", "goal", "hops"), rest))
        state["sent"] = to_sibling(send)
        state["block0_sibling"] = to_sibling(state["block0"])

    half = nb // 2
    part = half // chips

    def join():
        joined = run(
            join_kernel,
            [(meta, SMEM), (state["join"], SMEM), (state["keep"], VMEM), (state["sent"], VMEM)],
            [(bf16(half, cb, nb), VMEM)] * 2,
            scratch=[pltpu.VMEM((half + 8, cb, nb), BF16)] * 2,
            us=2.0,
        )
        state["choices"] = [[v] + [to_chip(v, h) for h in range(1, chips)] for v in joined]
        state["fresh"], state["brought"] = [], []
        state["awaited"] = [state["block0_sibling"]]

    def fresh(turn):
        new, brought, *head = run(
            functools.partial(fresh_kernel, turn, chips),
            [(meta, SMEM), (state["hops"], VMEM)] + [(c, VMEM) for c in state["choices"][turn]],
            [(bf16(half, cb * nb), VMEM), (bf16(half, cb, nb), VMEM)]
            + [(bf16(part, nb), VMEM)] * (1 - turn),
            us=1.5, mib=16,
        )
        state["fresh"] += [new, to_sibling(new)]
        state["brought"] += [brought, to_sibling(brought)]
        if head:
            state["head"] = head + [
                lax.ppermute(head[0], "pcol", [(0, 2 * h), (1, 2 * h + 1)]) for h in range(1, line)
            ]
            state["awaited"] = state.get("awaited", []) + state["head"][1:]

    def head_here():
        (mine,) = run(
            by_place_kernel, [(meta, SMEM)] + [(v, VMEM) for v in state["head"]], [(bf16(part, nb), VMEM)], us=0.1
        )
        state["head"] = (mine, to_neighbour(mine))

    def head_pair():
        (pair,) = run(stack_kernel, [(v, VMEM) for v in state["head"]], [(bf16(2, part, nb), VMEM)], us=0.1)
        state["head"] = [pair] + [to_chip(pair, h) for h in range(1, chips)]

    def head_all():
        (mine,) = run(
            stack_kernel, [(v, VMEM) for v in state["head"]], [(bf16(chips, 2, part, nb), VMEM)], us=0.1
        )
        state["heads"] = (mine, to_sibling(mine))

    def old(values, name):
        operands = [(meta, SMEM)] + [(v, VMEM) for v in values[:line]]
        (mine,) = run(functools.partial(old_kernel, line), operands, [(bf16(nb, nb), VMEM)], us=0.1)
        state[name] = [mine] + [to_chip(mine, h) for h in range(1, chips)]
        if name == "old_held":
            state["awaited"] = state.get("awaited", []) + state[name][1:]

    def old_here():
        choices = [v for pair in zip(state["old_held"], state["old_other"]) for v in pair]
        (mine,) = run(
            by_chip_kernel, [(meta, SMEM)] + [(v, VMEM) for v in choices], [(bf16(2, nb, nb), VMEM)], us=0.1
        )
        state["old"] = (mine, to_sibling(mine))

    def scatter():
        sources = state["brought"] + [state["block0"], state["block0_sibling"], state["loaded"]]
        (state["moved"],) = run(
            scatter_kernel,
            [(meta, SMEM), (state["arrive"], SMEM), (state["goal"], SMEM)] + [(v, VMEM) for v in sources],
            [(bf16(rows + 8, cb, nb), VMEM)],
            us=0.1, mib=24,
        )

    def prep0():
        state["up0"], state["top0"] = run(
            prep0_kernel,
            [(meta, SMEM), (lower, VMEM)] + [(v, VMEM) for v in state["fresh"]],
            [(bf16(nb, cb * nb), VMEM), (bf16(nb, cb, nb), VMEM)],
            scratch=[pltpu.VMEM((nb, cb * nb), BF16)],
            us=2.0, mib=16,
        )

    def prep1():
        state["up1"], state["up0_panel"], state["top1"] = run(
            functools.partial(prep1_kernel, chips),
            [(meta, SMEM), (lower, VMEM), (upper, VMEM), (state["up0"], VMEM)]
            + [(v, VMEM) for v in state["heads"]] + [(v, VMEM) for v in state["fresh"]],
            [(bf16(nb, cb * nb), VMEM), (bf16(nb, nb), VMEM), (bf16(nb, cb, nb), VMEM)],
            scratch=[pltpu.VMEM((nb, cb * nb), BF16), pltpu.VMEM((2, nb, nb), BF16)],
            us=3.5, mib=16,
        )

    def update(i, group=1):
        operands = [(meta, SMEM), (state["goal"], VMEM)] + [(v, VMEM) for v in state["old"]] + [(upper, VMEM)]
        operands += [(state[name], VMEM) for name in ("up0", "up1", "up0_panel")]
        operands += [(state[name], ANY) for name in ("moved", "top0", "top1")]
        places = [p + h for p in range(i, i + group) for h in range(line)]
        operands += [(values[p], ANY) for values in (held, other) for p in places]
        aliases = {}
        if "result" in state:
            aliases = {len(operands): 0}
            operands.append((state["result"], ANY))
        count = sum(sizes[i : i + group])
        state["result"], _ = run(
            functools.partial(update_kernel, begins[i], line, tuple(sizes[i : i + group])),
            operands,
            [(bf16(rows, cb, nb), ANY), (jax.ShapeDtypeStruct((8, 128), F32), VMEM)],
            scratch=[
                pltpu.VMEM((2, count, nb), BF16), pltpu.VMEM((count, cb, nb), BF16),
                pltpu.VMEM((count, cb, nb), BF16), DMA((group, 2)), DMA, DMA,
            ],
            aliases=aliases,
            us=5.0, mib=24,
        )

    plan = [(0, gather), (1, join), (2, functools.partial(fresh, 0)), (3, head_here), (line - 1, functools.partial(old, held, "old_held")), (3, head_pair), (3, functools.partial(fresh, 1)), (line, functools.partial(old, other, "old_other")), (4, scatter), (4, prep0), (5, head_all), (5, old_here), (5, prep1)]
    for i in range(pieces - 2):
        plan.append((max(6 + i // 2, i + line - 1) if i < 3 else last_step, functools.partial(update, i)))
    plan.append((last_step, functools.partial(update, pieces - 2, 2)))
    for k in range(last_step + 1):
        step(k)
        while plan and (plan[0][0] <= k or k == last_step):
            plan.pop(0)[1]()
    return state["result"].reshape(matrix.shape)


def solution(mesh):
    placed = (P(None, "prow", None, "pcol"), P(), P(), P())
    return jax.shard_map(
        body, mesh=mesh, in_specs=placed, out_specs=P(None, "prow", None, "pcol"), check_vma=False
    )
```
